32 devices in a mesh: gx: 8 (over y, x, core), gy: 4 (over z).
Axes of the slice: x: 2, y: 2, z: 4, core: 2. Of those that a mesh axis runs over, the one named last changes fastest.
Arguments:
- residual_in: bfloat16 [1536, 8192], P('gy', 'gx'), may hold values from -6 to 6
- w_query: bfloat16 [2, 1536, 1536], P(None, 'gx', 'gy'), may hold values from -0.15625 to 0.15625
- w_key: bfloat16 [2, 1536, 256], P(None, 'gx', 'gy'), may hold values from -0.15625 to 0.15625
- w_value: bfloat16 [2, 1536, 256], P(None, 'gx', 'gy'), may hold values from -0.15625 to 0.15625
- b_query: bfloat16 [2, 1536], P(None, 'gy'), may hold values from -1.5 to 1.5
- b_key: bfloat16 [2, 256], P(None, 'gy'), may hold values from -1.5 to 1.5
- b_value: bfloat16 [2, 256], P(None, 'gy'), may hold values from -0.59765625 to 0.59765625
- w_output: bfloat16 [2, 1536, 1536], P(None, 'gx', 'gy'), may hold values from -0.3125 to 0.3125
- gain_attn: bfloat16 [2, 1536], P(None, 'gy'), may hold values from 0.5 to 1.5
- gain_ffn: bfloat16 [2, 1536], P(None, 'gy'), may hold values from 0.5 to 1.5
- w_gate: bfloat16 [2, 1536, 8960], P(None, 'gx', 'gy'), may hold values from -0.15625 to 0.15625
- w_up: bfloat16 [2, 1536, 8960], P(None, 'gx', 'gy'), may hold values from -0.15625 to 0.15625
- w_down: bfloat16 [2, 1536, 8960], P(None, 'gx', 'gy'), may hold values from -0.0625 to 0.0625
- cotangent: bfloat16 [1536, 8192], P('gy', 'gx'), may hold values from -6 to 6
Outputs:
- output: float32 [1536, 8192], P('gy', 'gx')
- grad_input: float32 [1536, 8192], P('gy', 'gx')
- grad_w_query: float32 [2, 1536, 1536], P(None, 'gx', 'gy')
- grad_w_key: float32 [2, 1536, 256], P(None, 'gx', 'gy')
- grad_w_value: float32 [2, 1536, 256], P(None, 'gx', 'gy')
- grad_b_query: float32 [2, 1536], P(None, 'gy')
- grad_b_key: float32 [2, 256], P(None, 'gy')
- grad_b_value: float32 [2, 256], P(None, 'gy')
- grad_w_output: float32 [2, 1536, 1536], P(None, 'gx', 'gy')
- grad_gain_attn: float32 [2, 1536], P(None, 'gy')
- grad_gain_ffn: float32 [2, 1536], P(None, 'gy')
- grad_w_gate: float32 [2, 1536, 8960], P(None, 'gx', 'gy')
- grad_w_up: float32 [2, 1536, 8960], P(None, 'gx', 'gy')
- grad_w_down: float32 [2, 1536, 8960], P(None, 'gx', 'gy')
The draws below stay inside these ranges and needn't reach their ends.
All inputs are finite; a program needn't handle non-finite values.
Results may differ from the reference program's by a relative error of at most 0.018.
Values may be sent and summed in bfloat16 or wider, within the bound.
A program may use at most 384 MiB of HBM per device.

```python
import math
import jax
import jax.numpy as jnp
from jax import lax

D = 1536
FF = 8960
HEADS = 12
KV_HEADS = 2
HEAD_DIM = 128
LEN = 1024
LAYERS = 2
QD = 1536
KVD = 256
TOK_ROW = 1024
TOKENS = 8192
N_GX = 8


def with_spikes(array, rng, source, target, shards_of, factor):
    owner, partner = [(jnp.arange(array.shape[axis_at]) // (array.shape[axis_at] // shards_of)).reshape([-1 if axis == axis_at else 1 for axis in range(array.ndim)]) for axis_at in (source, target)]
    chosen = jax.random.permutation(rng, shards_of)[partner]
    strong = (owner == chosen) | (owner == (partner + shards_of // 2) % shards_of)
    return jnp.where(strong, factor * array, array)


def level_of(own_key, shape, split, low, largest):
    def one(dim, shards_of):
        heights = jax.random.uniform(jax.random.fold_in(jax.random.fold_in(own_key, 6), dim), (shards_of,), jnp.float32, low / len(split), largest / len(split))
        return jnp.repeat(jnp.exp(heights), shape[dim] // shards_of).reshape((-1,) + (1,) * (len(shape) - dim - 1))

    factor_of = one(*split[0])
    for cut in split[1:]:
        factor_of = factor_of * one(*cut)
    return factor_of


def bell_draw(rng, dims, spread, bound, cuts=(), kind=jnp.bfloat16):
    array = spread * jax.random.normal(rng, dims, jnp.float32)
    if cuts:
        array = array * level_of(rng, dims, cuts, -0.22, 0.18)
    return jnp.clip(array, -bound, bound).astype(kind)


def heavy_noise(rng, shape, width, reach, pieces, heavy, kind=jnp.bfloat16):
    entries = width * jax.random.normal(rng, shape, jnp.float32)
    if pieces:
        entries = entries * level_of(rng, shape, pieces, -0.22, 0.18)
    return jnp.clip(with_spikes(entries, jax.random.fold_in(rng, 3), *heavy), -reach, reach).astype(kind)


def setup_inputs(seed: int = 0) -> dict:
    key_of = jax.random.split(jax.random.key(seed), 15)
    return {
        "residual_in": heavy_noise(key_of[0], (D, TOKENS), 1.0, 6.0, ((0, 4), (1, 8)), (1, 0, 8, 2.0)),
        "w_query": bell_draw(key_of[1], (LAYERS, D, QD), D ** -0.5, 0.15625, ((1, 8), (2, 4))),
        "w_key": bell_draw(key_of[2], (LAYERS, D, KVD), D ** -0.5, 0.15625, ((1, 8), (2, 4))),
        "w_value": bell_draw(key_of[3], (LAYERS, D, KVD), D ** -0.5, 0.15625, ((1, 8), (2, 4))),
        "b_query": bell_draw(key_of[4], (LAYERS, QD), 0.25, 1.5, ((1, 4),)),
        "b_key": bell_draw(key_of[5], (LAYERS, KVD), 0.25, 1.5, ((1, 4),)),
        "b_value": bell_draw(key_of[6], (LAYERS, KVD), 0.1, 0.59765625, ((1, 4),)),
        "w_output": bell_draw(key_of[7], (LAYERS, D, QD), (QD // 4) ** -0.5, 0.3125, ((1, 8), (2, 4))),
        "gain_attn": jnp.clip(1.0 + 0.1 * jax.random.normal(key_of[8], (LAYERS, D), jnp.float32), 0.5, 1.5).astype(jnp.bfloat16),
        "gain_ffn": jnp.clip(1.0 + 0.1 * jax.random.normal(key_of[9], (LAYERS, D), jnp.float32), 0.5, 1.5).astype(jnp.bfloat16),
        "w_gate": bell_draw(key_of[10], (LAYERS, D, FF), D ** -0.5, 0.15625, ((1, 8), (2, 4))),
        "w_up": bell_draw(key_of[11], (LAYERS, D, FF), D ** -0.5, 0.15625, ((1, 8), (2, 4))),
        "w_down": bell_draw(key_of[12], (LAYERS, D, FF), FF ** -0.5, 0.0625, ((1, 8), (2, 4))),
        "cotangent": heavy_noise(key_of[13], (D, TOKENS), 1.0, 6.0, ((0, 4), (1, 8)), (1, 0, 8, 2.0)),
    }


@jax.custom_vjp
def low(v):
    return lax.optimization_barrier(v.astype(jnp.bfloat16)).astype(jnp.float32)

@jax.custom_vjp
def low_back(v):
    return v

def low_keep(v):
    return (low(v), None)

def low_pass(kept, grad):
    return (grad,)

def back_keep(v):
    return (v, None)

def back_low(kept, grad):
    return (low(grad),)
low.defvjp(low_keep, low_pass)
low_back.defvjp(back_keep, back_low)
epsilon = 1e-06
rope_base = 1000000.0
penalty = 0.25
highest = lax.Precision.HIGHEST

def matmul(left, right):
    return jnp.dot(left, right, precision=highest, preferred_element_type=jnp.float32)

def rms_scale(resid, gain):
    scale = lax.rsqrt(lax.optimization_barrier(jnp.mean(resid * resid, axis=-1, keepdims=True)) + epsilon)
    return resid * scale * gain

def rope_tables(positions):
    freqs = rope_base ** (-jnp.arange(0, HEAD_DIM, 2).astype(jnp.float32) / HEAD_DIM)
    angles = positions.astype(jnp.float32)[:, None] * freqs[None, :]
    cosine = jnp.cos(angles)
    sine_table = jnp.sin(angles)
    return (jnp.concatenate([cosine, cosine], -1)[:, None, :], jnp.concatenate([sine_table, sine_table], -1)[:, None, :])

def rotate(tensor, cosine, sine_table):
    half = HEAD_DIM // 2
    turned = jnp.concatenate([-tensor[..., half:], tensor[..., :half]], -1)
    return tensor * cosine + turned * sine_table

def block_forward(resid, params, cosine, sine_table, allowed):
    w_query, w_key, w_value, b_query, b_key, b_value, w_output, gain_attn, gain_ffn, w_gate, w_up, w_down = params
    count = resid.shape[0]
    group = HEADS // KV_HEADS
    scale_factor = 1.0 / math.sqrt(HEAD_DIM)
    normed = low(rms_scale(resid, gain_attn))
    queries = low_back(matmul(normed, w_query) + b_query)
    keys = low_back(matmul(normed, w_key) + b_key)
    values = low(low_back(matmul(normed, w_value) + b_value))
    q_rot = low(rotate(queries.reshape(count, HEADS, HEAD_DIM), cosine, sine_table)).reshape(count, KV_HEADS, group, HEAD_DIM)
    k_rot = low(rotate(keys.reshape(count, KV_HEADS, HEAD_DIM), cosine, sine_table))
    v_heads = values.reshape(count, KV_HEADS, HEAD_DIM)
    scores = low_back(jnp.einsum('qkgd,skd->kgqs', q_rot, k_rot, precision=highest) * scale_factor)
    scores = jnp.where(allowed, scores, -1e+30)
    top = lax.optimization_barrier(jnp.max(scores, axis=-1, keepdims=True))
    expo = jnp.exp(scores - top)
    soft = low(expo / lax.optimization_barrier(jnp.sum(expo, axis=-1, keepdims=True)))
    mixed = jnp.einsum('kgqs,skd->qkgd', soft, v_heads, precision=highest).reshape(count, HEADS * HEAD_DIM)
    mixed = low(low_back(mixed))
    middle = resid + low_back(matmul(mixed, w_output.T))
    normed_two = low(rms_scale(middle, gain_ffn))
    gate_value = low_back(matmul(normed_two, w_gate))
    up_value = low_back(matmul(normed_two, w_up))
    hidden = low(gate_value * lax.logistic(gate_value) * up_value)
    return middle + low_back(matmul(hidden, w_down.T))

def forward(resid, params, cosine, sine_table, allowed):
    for layer_index in range(LAYERS):
        layer_params = tuple((weight[layer_index] for weight in params))
        resid = jax.checkpoint(block_forward)(resid, layer_params, cosine, sine_table, allowed)
    return resid

def reference(residual_in, w_query, w_key, w_value, b_query, b_key, b_value, w_output, gain_attn, gain_ffn, w_gate, w_up, w_down, cotangent):
    params = tuple((weight.astype(jnp.float32) for weight in (w_query, w_key, w_value, b_query, b_key, b_value, w_output, gain_attn, gain_ffn, w_gate, w_up, w_down)))
    index = jnp.arange(TOK_ROW, dtype=jnp.int32)
    cosine, sine_table = rope_tables(index % LEN)
    allowed = (index[:, None] // LEN == index[None, :] // LEN) & (index[None, :] <= index[:, None])
    rows_in = residual_in.astype(jnp.float32).T.reshape(N_GX, TOK_ROW, D)
    rows_cot = cotangent.astype(jnp.float32).T.reshape(N_GX, TOK_ROW, D)

    def step(totals, item):
        resid, weight_rows = item

        def run(params_in, resid_in):
            result = forward(resid_in, params_in, cosine, sine_table, allowed)
            loss = jnp.sum(weight_rows * result) + penalty * jnp.sum(result * result)
            return (loss, result)
        loss, pull, result = jax.vjp(run, params, resid, has_aux=True)
        grad_params, grad_resid = pull(jnp.ones_like(loss))
        new_totals = tuple((total + grad for total, grad in zip(totals, grad_params)))
        return (new_totals, (result, grad_resid))
    zeros = tuple((jnp.zeros_like(weight) for weight in params))
    totals, (results, grads_in) = lax.scan(step, zeros, (rows_in, rows_cot))
    return (results.reshape(TOKENS, D).T, grads_in.reshape(TOKENS, D).T, totals[0], totals[1], totals[2], totals[3], totals[4], totals[5], totals[6], totals[7], totals[8], totals[9], totals[10], totals[11])
```

```python
import math

import jax
import jax.numpy as jnp
from jax import lax
from jax.sharding import PartitionSpec as P

D = 1536
HEADS = 12
KV_HEADS = 2
HEAD_DIM = 128
LEN = 1024
LAYERS = 2
GROUP = HEADS // KV_HEADS

epsilon = 1e-06
rope_base = 1000000.0
penalty = 0.25
bf16 = jnp.bfloat16
f32 = jnp.float32


def rope_tables(positions, head_size):
    freqs = rope_base ** (-jnp.arange(0, head_size, 2).astype(f32) / head_size)
    angles = positions.astype(f32)[:, None] * freqs[None, :]
    cosine = jnp.cos(angles)
    sine_table = jnp.sin(angles)
    return (
        jnp.concatenate([cosine, cosine], -1)[:, None, :],
        jnp.concatenate([sine_table, sine_table], -1)[:, None, :],
    )


def rotate(tensor, cosine, sine_table):
    half = tensor.shape[-1] // 2
    turned = jnp.concatenate([-tensor[..., half:], tensor[..., :half]], -1)
    return tensor * cosine + turned * sine_table


def rotate_back(tensor, cosine, sine_table):
    half = tensor.shape[-1] // 2
    moved = tensor * sine_table
    return tensor * cosine + jnp.concatenate([moved[..., half:], -moved[..., :half]], -1)


def dot(pattern, left, right):
    return jnp.einsum(pattern, left, right, preferred_element_type=f32)


def rms_parts(resid):
    scale = lax.rsqrt(jnp.mean(resid * resid, axis=1, keepdims=True) + epsilon)
    return resid * scale, scale


def norm_backward(grad_normed, normed, scale, gain):
    grad_gain = jnp.sum(grad_normed * normed, axis=0)
    scaled = grad_normed * gain
    project = jnp.mean(scaled * normed, axis=1, keepdims=True)
    return scale * (scaled - normed * project), grad_gain


def gather_attention(w_query, w_key, w_value, w_output):
    sizes = (w_query.shape[1], w_key.shape[1], w_value.shape[1], w_output.shape[1])
    pack = jnp.concatenate([w_query, w_key, w_value, w_output], axis=1)
    pack = lax.all_gather(pack, "gy", axis=0)
    pack = lax.all_gather(pack, "gx", axis=0)
    full, start = [], 0
    for size in sizes:
        part = pack[..., start : start + size].transpose(0, 2, 1, 3)
        full.append(part.reshape(D, -1))
        start += size
    return full


def scatter_attention(grads, devices_x, devices_y):
    parts = [
        grad.reshape(devices_x, D // devices_x, devices_y, -1).transpose(0, 2, 1, 3)
        for grad in grads
    ]
    sizes = [part.shape[-1] for part in parts]
    pack = jnp.concatenate(parts, axis=-1)
    pack = lax.psum_scatter(pack, "gx", scatter_dimension=0)
    pack = lax.psum_scatter(pack, "gy", scatter_dimension=0).astype(f32)
    out, start = [], 0
    for size in sizes:
        out.append(pack[:, start : start + size])
        start += size
    return out


def score_block(q_rot, k_rot, allowed):
    scores = dot("qkgd,skd->kgqs", q_rot, k_rot) * (1.0 / math.sqrt(HEAD_DIM))
    return jnp.where(allowed, scores, -1e30)


def on_device(
    residual_in,
    w_query,
    w_key,
    w_value,
    b_query,
    b_key,
    b_value,
    w_output,
    gain_attn,
    gain_ffn,
    w_gate,
    w_up,
    w_down,
    cotangent,
):
    devices_x = lax.axis_size("gx")
    devices_y = lax.axis_size("gy")
    rows_tok = residual_in.shape[1]
    count = rows_tok // devices_y
    q_index = lax.axis_index("gy") * count + jnp.arange(count, dtype=jnp.int32)
    k_index = jnp.arange(rows_tok, dtype=jnp.int32)
    allowed = (q_index[:, None] // LEN == k_index[None, :] // LEN) & (
        k_index[None, :] <= q_index[:, None]
    )
    cosine, sine = rope_tables(q_index % LEN, HEAD_DIM)

    small = jnp.concatenate([gain_attn, gain_ffn, b_query, b_key, b_value], axis=1)
    small_sizes = [v.shape[1] for v in (gain_attn, gain_ffn, b_query, b_key, b_value)]
    small = lax.all_gather(small, "gy", axis=1).astype(f32)
    vectors, start = [], 0
    for size in small_sizes:
        vectors.append(small[:, :, start : start + size].reshape(LAYERS, -1))
        start += size
    gains_one, gains_two, bias_q, bias_k, bias_v = vectors

    resid = lax.all_to_all(residual_in, "gy", split_axis=1, concat_axis=0, tiled=True)
    resid = resid.astype(f32).T
    attn_full, ffn_full = [], []
    for l in range(LAYERS):
        attn_full.append(gather_attention(w_query[l], w_key[l], w_value[l], w_output[l]))
        ffn_full.append(
            tuple(lax.all_gather(w[l], "gx", axis=0, tiled=True) for w in (w_gate, w_up, w_down))
        )
    cot = lax.all_to_all(cotangent, "gy", split_axis=1, concat_axis=0, tiled=True)

    kept = []
    for l in range(LAYERS):
        wq, wk, wv, wo = attn_full[l]
        wg, wu, wd = ffn_full[l]
        normed_one, scale_one = rms_parts(resid)
        acts_one = (normed_one * gains_one[l]).astype(bf16)
        queries = dot("td,dq->tq", acts_one, wq) + bias_q[l]
        keys = dot("td,dq->tq", acts_one, wk) + bias_k[l]
        values = (dot("td,dq->tq", acts_one, wv) + bias_v[l]).astype(bf16)
        q_rot = rotate(queries.reshape(count, HEADS, HEAD_DIM), cosine, sine).astype(bf16)
        q_rot = q_rot.reshape(count, KV_HEADS, GROUP, HEAD_DIM)
        k_rot = rotate(keys.reshape(count, KV_HEADS, HEAD_DIM), cosine, sine).astype(bf16)
        both = jnp.concatenate([k_rot.reshape(count, -1), values], axis=1)
        both = lax.all_gather(both, "gy", axis=0, tiled=True)
        half = both.shape[1] // 2
        k_rot = both[:, :half].reshape(rows_tok, KV_HEADS, HEAD_DIM)
        v_heads = both[:, half:].reshape(rows_tok, KV_HEADS, HEAD_DIM)
        scores = score_block(q_rot, k_rot, allowed)
        top = jnp.max(scores, axis=-1, keepdims=True)
        expo = jnp.exp(scores - top)
        total = jnp.sum(expo, axis=-1, keepdims=True)
        soft = (expo / total).astype(bf16)
        log_total = top + jnp.log(total)
        mixed = dot("kgqs,skd->qkgd", soft, v_heads).reshape(count, -1).astype(bf16)
        middle = resid + dot("tq,dq->td", mixed, wo)
        normed_two, scale_two = rms_parts(middle)
        acts_two = (normed_two * gains_two[l]).astype(bf16)
        acts_two = lax.all_gather(acts_two, "gy", axis=0, tiled=True)
        gate = dot("td,df->tf", acts_two, wg)
        up = dot("td,df->tf", acts_two, wu)
        hidden = (gate * lax.logistic(gate) * up).astype(bf16)
        part = dot("tf,df->td", hidden, wd).astype(bf16)
        part = lax.psum_scatter(part, "gy", scatter_dimension=0, tiled=True)
        kept.append(
            (
                normed_one,
                scale_one,
                acts_one,
                q_rot,
                k_rot,
                v_heads,
                log_total,
                mixed,
                normed_two,
                scale_two,
                acts_two,
                gate.astype(bf16),
                up.astype(bf16),
                hidden,
            )
        )
        resid = middle + part.astype(f32)

    def to_blocks(tokens_major):
        flipped = tokens_major.astype(bf16).T
        out = lax.all_to_all(flipped, "gy", split_axis=0, concat_axis=1, tiled=True)
        return out.astype(f32)

    output = to_blocks(resid)
    grad = cot.astype(f32).T + 2.0 * penalty * resid
    attn_grads = [None] * LAYERS
    ffn_grads = [None] * LAYERS
    small_grads = [None] * LAYERS

    def scatter_x(weight_grad):
        return lax.psum_scatter(
            weight_grad.astype(bf16), "gx", scatter_dimension=0, tiled=True
        ).astype(f32)

    for l in reversed(range(LAYERS)):
        (
            normed_one,
            scale_one,
            acts_one,
            q_rot,
            k_rot,
            v_heads,
            log_total,
            mixed,
            normed_two,
            scale_two,
            acts_two,
            gate,
            up,
            hidden,
        ) = kept[l]
        wq, wk, wv, wo = attn_full[l]
        wg, wu, wd = ffn_full[l]
        grad_out = lax.all_gather(grad.astype(bf16), "gy", axis=0, tiled=True)
        grad_hidden = dot("td,df->tf", grad_out, wd)
        gate = gate.astype(f32)
        up = up.astype(f32)
        sigma = lax.logistic(gate)
        grad_gate = (grad_hidden * up * sigma * (1.0 + gate * (1.0 - sigma))).astype(bf16)
        grad_up = (grad_hidden * gate * sigma).astype(bf16)
        part = dot("tf,df->td", grad_gate, wg) + dot("tf,df->td", grad_up, wu)
        grad_acts_two = lax.psum_scatter(
            part.astype(bf16), "gy", scatter_dimension=0, tiled=True
        ).astype(f32)
        ffn_grads[l] = (
            scatter_x(dot("td,tf->df", acts_two, grad_gate)),
            scatter_x(dot("td,tf->df", acts_two, grad_up)),
            scatter_x(dot("td,tf->df", grad_out, hidden)),
        )
        grad_norm, grad_gain_two = norm_backward(
            grad_acts_two, normed_two, scale_two, gains_two[l]
        )
        grad_mid = grad + grad_norm
        grad_branch = grad_mid.astype(bf16)
        grad_wo = dot("td,tq->dq", grad_branch, mixed)
        grad_mixed = dot("td,dq->tq", grad_branch, wo).astype(bf16)
        grad_heads = grad_mixed.reshape(count, KV_HEADS, GROUP, HEAD_DIM)
        scores = score_block(q_rot, k_rot, allowed)
        soft_full = jnp.exp(scores - log_total)
        soft = soft_full.astype(bf16)
        grad_soft = dot("qkgd,skd->kgqs", grad_heads, v_heads)
        inner = jnp.sum(soft_full * grad_soft, axis=-1, keepdims=True)
        grad_scores = (soft_full * (grad_soft - inner)).astype(bf16)
        grad_values = dot("kgqs,qkgd->skd", soft, grad_heads)
        factor = 1.0 / math.sqrt(HEAD_DIM)
        grad_qrot = dot("kgqs,skd->qkgd", grad_scores, k_rot) * factor
        grad_krot = dot("kgqs,qkgd->skd", grad_scores, q_rot) * factor
        grad_q = rotate_back(grad_qrot.reshape(count, HEADS, HEAD_DIM), cosine, sine)
        grad_q = grad_q.reshape(count, -1).astype(bf16)
        both = jnp.concatenate(
            [grad_krot.reshape(rows_tok, -1), grad_values.reshape(rows_tok, -1)], axis=1
        ).astype(bf16)
        both = lax.psum_scatter(both, "gy", scatter_dimension=0, tiled=True).astype(f32)
        half = both.shape[1] // 2
        grad_k = rotate_back(both[:, :half].reshape(count, KV_HEADS, HEAD_DIM), cosine, sine)
        grad_k = grad_k.reshape(count, -1).astype(bf16)
        grad_v = both[:, half:].astype(bf16)
        grad_acts_one = (
            dot("tq,dq->td", grad_q, wq)
            + dot("tq,dq->td", grad_k, wk)
            + dot("tq,dq->td", grad_v, wv)
        )
        attn_grads[l] = scatter_attention(
            [
                g.astype(bf16)
                for g in (
                    dot("td,tq->dq", acts_one, grad_q),
                    dot("td,tq->dq", acts_one, grad_k),
                    dot("td,tq->dq", acts_one, grad_v),
                    grad_wo,
                )
            ],
            devices_x,
            devices_y,
        )
        grad_norm, grad_gain_one = norm_backward(
            grad_acts_one, normed_one, scale_one, gains_one[l]
        )
        grad = grad_mid + grad_norm
        small_grads[l] = [
            v.reshape(devices_y, -1)
            for v in (
                grad_gain_one,
                grad_gain_two,
                jnp.sum(grad_q.astype(f32), axis=0),
                jnp.sum(grad_k.astype(f32), axis=0),
                jnp.sum(grad_v.astype(f32), axis=0),
            )
        ]
    small = jnp.stack([jnp.concatenate(v, axis=1) for v in small_grads], axis=1)
    small = lax.psum(small, ("gx", "gy"))
    small = lax.dynamic_index_in_dim(small, lax.axis_index("gy"), 0, keepdims=False)
    small_out, start = [], 0
    for size in small_sizes:
        small_out.append(small[:, start : start + size])
        start += size

    def stack(parts, k):
        return jnp.stack([part[k] for part in parts])

    return (
        output,
        to_blocks(grad),
        stack(attn_grads, 0),
        stack(attn_grads, 1),
        stack(attn_grads, 2),
        small_out[2],
        small_out[3],
        small_out[4],
        stack(attn_grads, 3),
        small_out[0],
        small_out[1],
        stack(ffn_grads, 0),
        stack(ffn_grads, 1),
        stack(ffn_grads, 2),
    )


def solution(mesh):
    tokens = P("gy", "gx")
    weight = P(None, "gx", "gy")
    vector = P(None, "gy")
    return jax.shard_map(
        on_device,
        mesh=mesh,
        in_specs=(
            tokens,
            weight,
            weight,
            weight,
            vector,
            vector,
            vector,
            weight,
            vector,
            vector,
            weight,
            weight,
            weight,
            tokens,
        ),
        out_specs=(
            tokens,
            tokens,
            weight,
            weight,
            weight,
            vector,
            vector,
            vector,
            weight,
            vector,
            vector,
            weight,
            weight,
            weight,
        ),
        check_vma=False,
    )
```

```python
import math

import jax
import jax.numpy as jnp
from jax import lax
from jax.experimental import pallas as pl
from jax.experimental.pallas import tpu as pltpu
from jax.sharding import PartitionSpec as P

D = 1536
HEADS = 12
KV_HEADS = 2
HEAD_DIM = 128
LEN = 1024
LAYERS = 2
GROUP = HEADS // KV_HEADS

epsilon = 1e-06
rope_base = 1000000.0
penalty = 0.25
bf16 = jnp.bfloat16
f32 = jnp.float32
MESH = pl.DeviceIdType.MESH
VMEM_LIMIT = 60 << 20


def rope_tables(positions, head_size):
    freqs = rope_base ** (-jnp.arange(0, head_size, 2).astype(f32) / head_size)
    angles = positions.astype(f32)[:, None] * freqs[None, :]
    cosine = jnp.cos(angles)
    sine_table = jnp.sin(angles)
    return (
        jnp.concatenate([cosine, cosine], -1)[:, None, :],
        jnp.concatenate([sine_table, sine_table], -1)[:, None, :],
    )


def rotate(tensor, cosine, sine_table):
    half = tensor.shape[-1] // 2
    turned = jnp.concatenate([-tensor[..., half:], tensor[..., :half]], -1)
    return tensor * cosine + turned * sine_table


def rotate_back(tensor, cosine, sine_table):
    half = tensor.shape[-1] // 2
    moved = tensor * sine_table
    return tensor * cosine + jnp.concatenate([moved[..., half:], -moved[..., :half]], -1)


def dot(pattern, left, right):
    return jnp.einsum(pattern, left, right, preferred_element_type=f32)


def rms_parts(resid):
    scale = lax.rsqrt(jnp.mean(resid * resid, axis=1, keepdims=True) + epsilon)
    return resid * scale, scale


def norm_backward(grad_normed, normed, scale, gain):
    grad_gain = jnp.sum(grad_normed * normed, axis=0)
    scaled = grad_normed * gain
    project = jnp.mean(scaled * normed, axis=1, keepdims=True)
    return scale * (scaled - normed * project), grad_gain


def gather_attention(w_query, w_key, w_value, w_output):
    sizes = (w_query.shape[1], w_key.shape[1], w_value.shape[1], w_output.shape[1])
    pack = jnp.concatenate([w_query, w_key, w_value, w_output], axis=1)
    pack = lax.all_gather(pack, "gy", axis=0)
    pack = lax.all_gather(pack, "gx", axis=0)
    full, start = [], 0
    for size in sizes:
        part = pack[..., start : start + size].transpose(0, 2, 1, 3)
        full.append(part.reshape(D, -1))
        start += size
    return full


def scatter_attention(grads, devices_x, devices_y):
    parts = [
        grad.reshape(devices_x, D // devices_x, devices_y, -1).transpose(0, 2, 1, 3)
        for grad in grads
    ]
    sizes = [part.shape[-1] for part in parts]
    pack = jnp.concatenate(parts, axis=-1)
    pack = lax.psum_scatter(pack, "gx", scatter_dimension=0)
    pack = lax.psum_scatter(pack, "gy", scatter_dimension=0).astype(f32)
    out, start = [], 0
    for size in sizes:
        out.append(pack[:, start : start + size])
        start += size
    return out


def score_block(q_rot, k_rot, allowed):
    scores = dot("qkgd,skd->kgqs", q_rot, k_rot) * (1.0 / math.sqrt(HEAD_DIM))
    return jnp.where(allowed, scores, -1e30)


FF_CHUNK = 512
PIECES = 4


def spans(total):
    return [(start, min(FF_CHUNK, total - start)) for start in range(0, total, FF_CHUNK)]


def nn(left, right):
    return lax.dot_general(left, right, (((1,), (0,)), ((), ())), preferred_element_type=f32)


def nt(left, right):
    return lax.dot_general(left, right, (((1,), (1,)), ((), ())), preferred_element_type=f32)


def line_pass(own_ref, sum_ref, gathered, part, own, outb, inb, sems, load, finish):
    own_sem, ag_send, ag_recv, rs_send, rs_recv = sems
    gx, me, size = lax.axis_index("gx"), lax.axis_index("gy"), lax.axis_size("gy")
    rows = own.shape[0]
    piece = rows // PIECES
    last = size - 1
    inner = jnp.logical_and(me > 0, me < last)

    first = pltpu.make_async_copy(own_ref, gathered.at[me], own_sem)
    first.start()
    barrier = pltpu.get_barrier_semaphore()

    @pl.when(me > 0)
    def _():
        pl.semaphore_signal(barrier, inc=1, device_id=(gx, me - 1), device_id_type=MESH)

    @pl.when(me < last)
    def _():
        pl.semaphore_signal(barrier, inc=1, device_id=(gx, me + 1), device_id_type=MESH)

    pl.semaphore_wait(barrier, jnp.where(inner, 2, 1))
    first.wait()

    def gather_copy(b, s, way):
        here = gathered.at[b, pl.ds(s * piece, piece)]
        return pltpu.make_async_remote_copy(
            src_ref=here,
            dst_ref=here,
            send_sem=ag_send.at[b, way, s],
            recv_sem=ag_recv.at[b, s],
            device_id=(gx, me - 1 + 2 * way),
            device_id_type=MESH,
        )

    def sum_copy(b, s):
        towards = jnp.where(b > me, me + 1, me - 1)
        slot = jnp.where(jnp.logical_and(towards == b, me > b), size, b)
        return pltpu.make_async_remote_copy(
            src_ref=outb.at[b, pl.ds(s * piece, piece)],
            dst_ref=inb.at[slot, pl.ds(s * piece, piece)],
            send_sem=rs_send.at[b, s],
            recv_sem=rs_recv.at[slot, s],
            device_id=(gx, towards),
            device_id_type=MESH,
        )

    def sum_arrived(slot, s):
        here = inb.at[slot, pl.ds(s * piece, piece)]
        pltpu.make_async_copy(here, here, rs_recv.at[slot, s]).wait()

    def step(t, carry):
        short = jnp.minimum(me, last - me)
        even = lax.rem(t, 2) == 0
        near = jnp.where(even, me - t // 2, me + (t + 1) // 2)
        far = jnp.where(me < last - me, me + (t - short), me - (t - short))
        b = jnp.where(t <= 2 * short, near, far)
        for s in range(PIECES):

            @pl.when(t > 0)
            def _():
                gather_copy(b, s, 0).wait_recv()

            @pl.when(jnp.logical_and(b <= me, me < last))
            def _():
                gather_copy(b, s, 1).start()

            @pl.when(jnp.logical_and(b >= me, me > 0))
            def _():
                gather_copy(b, s, 0).start()

        @pl.when(t == 0)
        def _():
            load()

        finish(b)

        @pl.when(b == me)
        def _():
            own[...] = part[...]

        @pl.when(b != me)
        def _():
            outb[b] = part[...].astype(bf16)

            @pl.when(jnp.logical_not(inner))
            def _():
                for s in range(PIECES):
                    sum_copy(b, s).start()

        return carry

    lax.fori_loop(0, size, step, 0)

    def relay(t, carry):
        above, below = last - me, me
        low = jnp.where(t < above, me + 1 + t, me - 1 - (t - above))
        high = jnp.where(t < below, me - 1 - t, me + 1 + (t - below))
        b = jnp.where(2 * me < size, low, high)

        @pl.when(inner)
        def _():
            for s in range(PIECES):
                at = pl.ds(s * piece, piece)
                sum_arrived(b, s)
                outb[b, at] = (outb[b, at].astype(f32) + inb[b, at].astype(f32)).astype(bf16)
                sum_copy(b, s).start()

        return carry

    lax.fori_loop(0, last, relay, 0)

    @pl.when(me > 0)
    def _():
        for s in range(PIECES):
            sum_arrived(me, s)
        own[...] += inb[me].astype(f32)

    @pl.when(me < last)
    def _():
        for s in range(PIECES):
            sum_arrived(size, s)
        own[...] += inb[size].astype(f32)

    sum_ref[...] = own[...]

    def drain(b, carry):
        for s in range(PIECES):

            @pl.when(jnp.logical_and(b <= me, me < last))
            def _():
                gather_copy(b, s, 1).wait_send()

            @pl.when(jnp.logical_and(b >= me, me > 0))
            def _():
                gather_copy(b, s, 0).wait_send()

            @pl.when(b != me)
            def _():
                sum_copy(b, s).wait_send()

        return carry

    lax.fori_loop(0, size, drain, 0)


def line_scratch(size, rows, width):
    return [
        pltpu.VMEM((size, rows, width), bf16),
        pltpu.VMEM((rows, width), f32),
        pltpu.VMEM((rows, width), f32),
        pltpu.VMEM((size, rows, width), bf16),
        pltpu.VMEM((size + 1, rows, width), bf16),
        pltpu.SemaphoreType.DMA,
        pltpu.SemaphoreType.DMA((size, 2, PIECES)),
        pltpu.SemaphoreType.DMA((size, PIECES)),
        pltpu.SemaphoreType.DMA((size, PIECES)),
        pltpu.SemaphoreType.DMA((size + 1, PIECES)),
    ]


LINE = 10


def forward_kernel(
    acts_ref, wg_ref, wu_ref, wd_ref, sum_ref, full_ref, gate_ref, up_ref, hidden_ref, *scratch
):
    gathered, part, own, outb, inb = scratch[:5]
    sems = scratch[5:LINE]
    wg, wu, wd, gate, up, hidden, w_sem, out_sem = scratch[LINE:]
    loads = [
        pltpu.make_async_copy(src, dst, w_sem.at[k])
        for k, (src, dst) in enumerate(((wg_ref, wg), (wu_ref, wu), (wd_ref, wd)))
    ]
    for copy in loads:
        copy.start()

    def load():
        for copy in loads:
            copy.wait()

    def results(b):
        pairs = ((gathered, full_ref), (gate, gate_ref), (up, up_ref), (hidden, hidden_ref))
        return [
            pltpu.make_async_copy(src.at[b], dst.at[b], out_sem.at[b, k])
            for k, (src, dst) in enumerate(pairs)
        ]

    def finish(b):
        block = gathered[b]
        for start, width in spans(wg.shape[1]):
            at = slice(start, start + width)
            g = nn(block, wg[:, at])
            u = nn(block, wu[:, at])
            h = (g * lax.logistic(g) * u).astype(bf16)
            gate[b, :, at] = g.astype(bf16)
            up[b, :, at] = u.astype(bf16)
            hidden[b, :, at] = h
            p = nt(h, wd[:, at])
            if start == 0:
                part[...] = p
            else:
                part[...] += p
        for copy in results(b):
            copy.start()

    line_pass(acts_ref, sum_ref, gathered, part, own, outb, inb, sems, load, finish)

    def settle(b, carry):
        for copy in results(b):
            copy.wait()
        return carry

    lax.fori_loop(0, gathered.shape[0], settle, 0)


ANY = pl.BlockSpec(memory_space=pl.ANY)


def forward_ffn(acts, wg, wu, wd):
    rows, width = acts.shape
    size, hidden = lax.axis_size("gy"), wg.shape[1]
    wide = jax.ShapeDtypeStruct((size, rows, hidden), bf16)
    return pl.pallas_call(
        forward_kernel,
        out_shape=[
            jax.ShapeDtypeStruct((rows, width), f32),
            jax.ShapeDtypeStruct((size, rows, width), bf16),
            wide,
            wide,
            wide,
        ],
        in_specs=[ANY] * 4,
        out_specs=[pl.BlockSpec(memory_space=pltpu.VMEM)] + [ANY] * 4,
        scratch_shapes=line_scratch(size, rows, width)
        + [pltpu.VMEM((width, hidden), bf16)] * 3
        + [pltpu.VMEM((size, rows, hidden), bf16)] * 3
        + [pltpu.SemaphoreType.DMA((3,)), pltpu.SemaphoreType.DMA((size, 4))],
        compiler_params=pltpu.CompilerParams(
            collective_id=0, has_side_effects=True, vmem_limit_bytes=VMEM_LIMIT
        ),
        cost_estimate=pl.CostEstimate(
            flops=6 * size * rows * width * hidden, bytes_accessed=40 << 20, transcendentals=0
        ),
        name="ffn_forward",
    )(acts, wg, wu, wd)


def backward_kernel(
    grad_ref, gate_ref, up_ref, wg_ref, wu_ref, wd_ref, sum_ref, full_ref, dg_ref, du_ref, *scratch
):
    gathered, part, own, outb, inb = scratch[:5]
    sems = scratch[5:LINE]
    wg, wu, wd, gate, up, w_sem, out_sem = scratch[LINE:]
    operands = ((wd_ref, wd), (gate_ref, gate), (up_ref, up), (wg_ref, wg), (wu_ref, wu))
    loads = [
        pltpu.make_async_copy(src, dst, w_sem.at[k]) for k, (src, dst) in enumerate(operands)
    ]
    for copy in loads:
        copy.start()

    def load():
        for copy in loads:
            copy.wait()

    def results(b):
        pairs = ((gathered, full_ref), (gate, dg_ref), (up, du_ref))
        return [
            pltpu.make_async_copy(src.at[b], dst.at[b], out_sem.at[b, k])
            for k, (src, dst) in enumerate(pairs)
        ]

    def finish(b):
        block = gathered[b]
        for start, width in spans(wg.shape[1]):
            at = slice(start, start + width)
            d = nn(block, wd[:, at])
            g = gate[b, :, at].astype(f32)
            u = up[b, :, at].astype(f32)
            sigma = lax.logistic(g)
            ds = d * sigma
            dg = (ds * u * (1.0 + g * (1.0 - sigma))).astype(bf16)
            du = (ds * g).astype(bf16)
            gate[b, :, at] = dg
            up[b, :, at] = du
            p = nt(dg, wg[:, at]) + nt(du, wu[:, at])
            if start == 0:
                part[...] = p
            else:
                part[...] += p
        for copy in results(b):
            copy.start()

    line_pass(grad_ref, sum_ref, gathered, part, own, outb, inb, sems, load, finish)

    def settle(b, carry):
        for copy in results(b):
            copy.wait()
        return carry

    lax.fori_loop(0, gathered.shape[0], settle, 0)


def backward_ffn(grad, gate, up, wg, wu, wd):
    rows, width = grad.shape
    size, hidden = lax.axis_size("gy"), wg.shape[1]
    wide = jax.ShapeDtypeStruct((size, rows, hidden), bf16)
    return pl.pallas_call(
        backward_kernel,
        out_shape=[
            jax.ShapeDtypeStruct((rows, width), f32),
            jax.ShapeDtypeStruct((size, rows, width), bf16),
            wide,
            wide,
        ],
        in_specs=[ANY] * 6,
        out_specs=[pl.BlockSpec(memory_space=pltpu.VMEM)] + [ANY] * 3,
        scratch_shapes=line_scratch(size, rows, width)
        + [pltpu.VMEM((width, hidden), bf16)] * 3
        + [pltpu.VMEM((size, rows, hidden), bf16)] * 2
        + [pltpu.SemaphoreType.DMA((5,)), pltpu.SemaphoreType.DMA((size, 3))],
        compiler_params=pltpu.CompilerParams(
            collective_id=1, has_side_effects=True, vmem_limit_bytes=VMEM_LIMIT
        ),
        cost_estimate=pl.CostEstimate(
            flops=6 * size * rows * width * hidden, bytes_accessed=40 << 20, transcendentals=0
        ),
        name="ffn_backward",
    )(grad, gate, up, wg, wu, wd)


def on_device(
    residual_in,
    w_query,
    w_key,
    w_value,
    b_query,
    b_key,
    b_value,
    w_output,
    gain_attn,
    gain_ffn,
    w_gate,
    w_up,
    w_down,
    cotangent,
):
    devices_x = lax.axis_size("gx")
    devices_y = lax.axis_size("gy")
    rows_tok = residual_in.shape[1]
    count = rows_tok // devices_y
    q_index = lax.axis_index("gy") * count + jnp.arange(count, dtype=jnp.int32)
    k_index = jnp.arange(rows_tok, dtype=jnp.int32)
    allowed = (q_index[:, None] // LEN == k_index[None, :] // LEN) & (
        k_index[None, :] <= q_index[:, None]
    )
    cosine, sine = rope_tables(q_index % LEN, HEAD_DIM)

    small = jnp.concatenate([gain_attn, gain_ffn, b_query, b_key, b_value], axis=1)
    small_sizes = [v.shape[1] for v in (gain_attn, gain_ffn, b_query, b_key, b_value)]
    small = lax.all_gather(small, "gy", axis=1).astype(f32)
    vectors, start = [], 0
    for size in small_sizes:
        vectors.append(small[:, :, start : start + size].reshape(LAYERS, -1))
        start += size
    gains_one, gains_two, bias_q, bias_k, bias_v = vectors

    resid = lax.all_to_all(residual_in, "gy", split_axis=1, concat_axis=0, tiled=True)
    resid = resid.astype(f32).T
    attn_full, ffn_full = [], []
    for l in range(LAYERS):
        attn_full.append(gather_attention(w_query[l], w_key[l], w_value[l], w_output[l]))
        ffn_full.append(
            tuple(lax.all_gather(w[l], "gx", axis=0, tiled=True) for w in (w_gate, w_up, w_down))
        )
    cot = lax.all_to_all(cotangent, "gy", split_axis=1, concat_axis=0, tiled=True)

    kept = []
    for l in range(LAYERS):
        wq, wk, wv, wo = attn_full[l]
        wg, wu, wd = ffn_full[l]
        normed_one, scale_one = rms_parts(resid)
        acts_one = (normed_one * gains_one[l]).astype(bf16)
        queries = dot("td,dq->tq", acts_one, wq) + bias_q[l]
        keys = dot("td,dq->tq", acts_one, wk) + bias_k[l]
        values = (dot("td,dq->tq", acts_one, wv) + bias_v[l]).astype(bf16)
        q_rot = rotate(queries.reshape(count, HEADS, HEAD_DIM), cosine, sine).astype(bf16)
        q_rot = q_rot.reshape(count, KV_HEADS, GROUP, HEAD_DIM)
        k_rot = rotate(keys.reshape(count, KV_HEADS, HEAD_DIM), cosine, sine).astype(bf16)
        both = jnp.concatenate([k_rot.reshape(count, -1), values], axis=1)
        both = lax.all_gather(both, "gy", axis=0, tiled=True)
        half = both.shape[1] // 2
        k_rot = both[:, :half].reshape(rows_tok, KV_HEADS, HEAD_DIM)
        v_heads = both[:, half:].reshape(rows_tok, KV_HEADS, HEAD_DIM)
        scores = score_block(q_rot, k_rot, allowed)
        top = jnp.max(scores, axis=-1, keepdims=True)
        expo = jnp.exp(scores - top)
        total = jnp.sum(expo, axis=-1, keepdims=True)
        soft = (expo / total).astype(bf16)
        log_total = top + jnp.log(total)
        mixed = dot("kgqs,skd->qkgd", soft, v_heads).reshape(count, -1).astype(bf16)
        middle = resid + dot("tq,dq->td", mixed, wo)
        normed_two, scale_two = rms_parts(middle)
        acts_two = (normed_two * gains_two[l]).astype(bf16)
        part, acts_two, gate, up, hidden = forward_ffn(acts_two, wg, wu, wd)
        kept.append(
            (
                normed_one,
                scale_one,
                acts_one,
                q_rot,
                k_rot,
                v_heads,
                log_total,
                mixed,
                normed_two,
                scale_two,
                acts_two,
                gate,
                up,
                hidden,
            )
        )
        resid = middle + part

    def to_blocks(tokens_major):
        flipped = tokens_major.astype(bf16).T
        out = lax.all_to_all(flipped, "gy", split_axis=0, concat_axis=1, tiled=True)
        return out.astype(f32)

    output = to_blocks(resid)
    grad = cot.astype(f32).T + 2.0 * penalty * resid
    attn_grads = [None] * LAYERS
    ffn_grads = [None] * LAYERS
    small_grads = [None] * LAYERS

    def scatter_x(weight_grad):
        return lax.psum_scatter(
            weight_grad.astype(bf16), "gx", scatter_dimension=0, tiled=True
        ).astype(f32)

    for l in reversed(range(LAYERS)):
        (
            normed_one,
            scale_one,
            acts_one,
            q_rot,
            k_rot,
            v_heads,
            log_total,
            mixed,
            normed_two,
            scale_two,
            acts_two,
            gate,
            up,
            hidden,
        ) = kept[l]
        wq, wk, wv, wo = attn_full[l]
        wg, wu, wd = ffn_full[l]
        grad_acts_two, grad_out, grad_gate, grad_up = backward_ffn(
            grad.astype(bf16), gate, up, wg, wu, wd
        )
        ffn_grads[l] = (
            scatter_x(dot("ztd,ztf->df", acts_two, grad_gate)),
            scatter_x(dot("ztd,ztf->df", acts_two, grad_up)),
            scatter_x(dot("ztd,ztf->df", grad_out, hidden)),
        )
        grad_norm, grad_gain_two = norm_backward(
            grad_acts_two, normed_two, scale_two, gains_two[l]
        )
        grad_mid = grad + grad_norm
        grad_branch = grad_mid.astype(bf16)
        grad_wo = dot("td,tq->dq", grad_branch, mixed)
        grad_mixed = dot("td,dq->tq", grad_branch, wo).astype(bf16)
        grad_heads = grad_mixed.reshape(count, KV_HEADS, GROUP, HEAD_DIM)
        scores = score_block(q_rot, k_rot, allowed)
        soft_full = jnp.exp(scores - log_total)
        soft = soft_full.astype(bf16)
        grad_soft = dot("qkgd,skd->kgqs", grad_heads, v_heads)
        inner = jnp.sum(soft_full * grad_soft, axis=-1, keepdims=True)
        grad_scores = (soft_full * (grad_soft - inner)).astype(bf16)
        grad_values = dot("kgqs,qkgd->skd", soft, grad_heads)
        factor = 1.0 / math.sqrt(HEAD_DIM)
        grad_qrot = dot("kgqs,skd->qkgd", grad_scores, k_rot) * factor
        grad_krot = dot("kgqs,qkgd->skd", grad_scores, q_rot) * factor
        grad_q = rotate_back(grad_qrot.reshape(count, HEADS, HEAD_DIM), cosine, sine)
        grad_q = grad_q.reshape(count, -1).astype(bf16)
        both = jnp.concatenate(
            [grad_krot.reshape(rows_tok, -1), grad_values.reshape(rows_tok, -1)], axis=1
        ).astype(bf16)
        both = lax.psum_scatter(both, "gy", scatter_dimension=0, tiled=True).astype(f32)
        half = both.shape[1] // 2
        grad_k = rotate_back(both[:, :half].reshape(count, KV_HEADS, HEAD_DIM), cosine, sine)
        grad_k = grad_k.reshape(count, -1).astype(bf16)
        grad_v = both[:, half:].astype(bf16)
        grad_acts_one = (
            dot("tq,dq->td", grad_q, wq)
            + dot("tq,dq->td", grad_k, wk)
            + dot("tq,dq->td", grad_v, wv)
        )
        attn_grads[l] = scatter_attention(
            [
                g.astype(bf16)
                for g in (
                    dot("td,tq->dq", acts_one, grad_q),
                    dot("td,tq->dq", acts_one, grad_k),
                    dot("td,tq->dq", acts_one, grad_v),
                    grad_wo,
                )
            ],
            devices_x,
            devices_y,
        )
        grad_norm, grad_gain_one = norm_backward(
            grad_acts_one, normed_one, scale_one, gains_one[l]
        )
        grad = grad_mid + grad_norm
        small_grads[l] = [
            v.reshape(devices_y, -1)
            for v in (
                grad_gain_one,
                grad_gain_two,
                jnp.sum(grad_q.astype(f32), axis=0),
                jnp.sum(grad_k.astype(f32), axis=0),
                jnp.sum(grad_v.astype(f32), axis=0),
            )
        ]
    small = jnp.stack([jnp.concatenate(v, axis=1) for v in small_grads], axis=1)
    small = lax.psum(small, ("gx", "gy"))
    small = lax.dynamic_index_in_dim(small, lax.axis_index("gy"), 0, keepdims=False)
    small_out, start = [], 0
    for size in small_sizes:
        small_out.append(small[:, start : start + size])
        start += size

    def stack(parts, k):
        return jnp.stack([part[k] for part in parts])

    return (
        output,
        to_blocks(grad),
        stack(attn_grads, 0),
        stack(attn_grads, 1),
        stack(attn_grads, 2),
        small_out[2],
        small_out[3],
        small_out[4],
        stack(attn_grads, 3),
        small_out[0],
        small_out[1],
        stack(ffn_grads, 0),
        stack(ffn_grads, 1),
        stack(ffn_grads, 2),
    )


def solution(mesh):
    tokens = P("gy", "gx")
    weight = P(None, "gx", "gy")
    vector = P(None, "gy")
    return jax.shard_map(
        on_device,
        mesh=mesh,
        in_specs=(
            tokens,
            weight,
            weight,
            weight,
            vector,
            vector,
            vector,
            weight,
            vector,
            vector,
            weight,
            weight,
            weight,
            tokens,
        ),
        out_specs=(
            tokens,
            tokens,
            weight,
            weight,
            weight,
            vector,
            vector,
            vector,
            weight,
            vector,
            vector,
            weight,
            weight,
            weight,
        ),
        check_vma=False,
    )
```

```python
import functools
import math

import jax
import jax.numpy as jnp
from jax import lax
from jax.experimental import pallas as pl
from jax.experimental.pallas import tpu as pltpu
from jax.sharding import PartitionSpec as P

D = 1536
HEADS = 12
KV_HEADS = 2
HEAD_DIM = 128
LEN = 1024
LAYERS = 2
GROUP = HEADS // KV_HEADS

epsilon = 1e-06
rope_base = 1000000.0
penalty = 0.25
bf16 = jnp.bfloat16
f32 = jnp.float32
MESH = pl.DeviceIdType.MESH
VMEM_LIMIT = 62 << 20
ANY = pl.BlockSpec(memory_space=pl.ANY)


def rope_tables(positions, head_size):
    freqs = rope_base ** (-jnp.arange(0, head_size, 2).astype(f32) / head_size)
    angles = positions.astype(f32)[:, None] * freqs[None, :]
    cosine = jnp.cos(angles)
    sine_table = jnp.sin(angles)
    return (
        jnp.concatenate([cosine, cosine], -1)[:, None, :],
        jnp.concatenate([sine_table, sine_table], -1)[:, None, :],
    )


def rotate(tensor, cosine, sine_table):
    half = tensor.shape[-1] // 2
    turned = jnp.concatenate([-tensor[..., half:], tensor[..., :half]], -1)
    return tensor * cosine + turned * sine_table


def rotate_back(tensor, cosine, sine_table):
    half = tensor.shape[-1] // 2
    moved = tensor * sine_table
    return tensor * cosine + jnp.concatenate([moved[..., half:], -moved[..., :half]], -1)


def dot(pattern, left, right):
    return jnp.einsum(pattern, left, right, preferred_element_type=f32)


def rms_parts(resid):
    scale = lax.rsqrt(jnp.mean(resid * resid, axis=1, keepdims=True) + epsilon)
    return resid * scale, scale


def norm_backward(grad_normed, normed, scale, gain):
    grad_gain = jnp.sum(grad_normed * normed, axis=0)
    scaled = grad_normed * gain
    project = jnp.mean(scaled * normed, axis=1, keepdims=True)
    return scale * (scaled - normed * project), grad_gain


def unpack_attention(pack, sizes):
    full, start = [], 0
    for size in sizes:
        part = pack[..., start : start + size].transpose(0, 2, 1, 3)
        full.append(part.reshape(D, -1))
        start += size
    return full


def scatter_attention(grads, devices_x, devices_y):
    parts = [
        grad.reshape(devices_x, D // devices_x, devices_y, -1).transpose(0, 2, 1, 3)
        for grad in grads
    ]
    sizes = [part.shape[-1] for part in parts]
    pack = jnp.concatenate(parts, axis=-1)
    pack = lax.psum_scatter(pack, "gx", scatter_dimension=0)
    pack = lax.psum_scatter(pack, "gy", scatter_dimension=0).astype(f32)
    out, start = [], 0
    for size in sizes:
        out.append(pack[:, start : start + size])
        start += size
    return out


def score_block(q_rot, k_rot, allowed):
    scores = dot("qkgd,skd->kgqs", q_rot, k_rot) * (1.0 / math.sqrt(HEAD_DIM))
    return jnp.where(allowed, scores, -1e30)


FF_CHUNK = 512
PIECES = 4


def spans(total):
    return [(start, min(FF_CHUNK, total - start)) for start in range(0, total, FF_CHUNK)]


def nn(left, right):
    return lax.dot_general(left, right, (((1,), (0,)), ((), ())), preferred_element_type=f32)


def nt(left, right):
    return lax.dot_general(left, right, (((1,), (1,)), ((), ())), preferred_element_type=f32)


def wait_for(ref, sem):
    pltpu.make_async_copy(ref, ref, sem).wait()


def places():
    gx, devices = lax.axis_index("gx"), lax.axis_size("gx")
    chips = devices // 2
    chip, core = gx // 2, lax.rem(gx, 2)
    partner = gx + 1 - 2 * core
    others = [lax.rem(chip + k, chips) * 2 + core for k in range(1, chips)]
    return partner, others


def square():
    gx = lax.axis_index("gx")
    chip, core = gx // 2, lax.rem(gx, 2)
    side = gx + 2 - 4 * lax.rem(chip, 2)
    along = gx + 4 - 8 * (chip // 2)
    return side, along, (3 - chip) * 2 + core


def spread_slots():
    chips = lax.axis_size("gx") // 2
    return 14 if chips == 4 else 2 * chips + 2 * (chips - 1)


def spread_scratch(count):
    devices = lax.axis_size("gx")
    return [
        pltpu.SemaphoreType.DMA((count,)),
        pltpu.SemaphoreType.DMA((count, spread_slots())),
        pltpu.SemaphoreType.DMA((count, devices, 2)),
    ]


def greet(gx_peers, gy_peers):
    gx, gy = lax.axis_index("gx"), lax.axis_index("gy")
    barrier = pltpu.get_barrier_semaphore()
    for peer in gx_peers:
        pl.semaphore_signal(barrier, inc=1, device_id=(peer, gy), device_id_type=MESH)
    for peer in gy_peers:
        pl.semaphore_signal(barrier, inc=1, device_id=(gx, peer), device_id_type=MESH)
    pl.semaphore_wait(barrier, len(gx_peers) + len(gy_peers))


class Spread:
    def __init__(self, items, sems):
        self.items, (self.local, self.send_sem, self.recv_sem) = items, sems
        self.partner, self.others = places()
        self.four = lax.axis_size("gx") // 2 == 4
        self.near = list(square()[:2]) if self.four else self.others

    def part(self, i, k, h):
        full = self.items[i][1]
        half = full.shape[1] // 2
        return full.at[k, pl.ds(h * half, half)]

    def send(self, i, k, h, target, slot, first=False):
        here = self.part(i, k, h)
        half = here.shape[0]
        source = self.items[i][0].at[pl.ds(h * half, half)] if first else here
        pltpu.make_async_remote_copy(
            src_ref=source,
            dst_ref=here,
            send_sem=self.send_sem.at[i, slot],
            recv_sem=self.recv_sem.at[i, k, h],
            device_id=(target, lax.axis_index("gy")),
            device_id_type=MESH,
        ).start()

    def arrived(self, i, k, h):
        wait_for(self.part(i, k, h), self.recv_sem.at[i, k, h])

    def place(self, i):
        own, full = self.items[i]
        return pltpu.make_async_copy(own, full.at[lax.axis_index("gx")], self.local.at[i])

    def begin(self, i):
        gx = lax.axis_index("gx")
        self.place(i).start()
        slot = 0
        for target in self.near + [self.partner]:
            for h in range(2):
                self.send(i, gx, h, target, slot, True)
                slot += 1

    def relay(self, i):
        slot = 2 * len(self.near) + 2
        if self.four:
            side, along, _ = square()
            steps = [(side, 0, along), (along, 1, side), (side, 1, None), (along, 0, None)]
        else:
            steps = [(k, h, None) for k in self.others for h in range(2)]
        for k, h, target in steps:
            self.arrived(i, k, h)
            for to in [self.partner] if target is None else [target, self.partner]:
                self.send(i, k, h, to, slot)
                slot += 1

    def finish(self, i):
        if self.four:
            for h in range(2):
                self.arrived(i, square()[2], h)
                self.send(i, square()[2], h, self.partner, 12 + h)

    def close(self, i):
        core = lax.rem(lax.axis_index("gx"), 2)
        for k in [self.partner] + [k + 1 - 2 * core for k in self.others]:
            for h in range(2):
                self.arrived(i, k, h)
        for slot in range(spread_slots()):
            wait_for(self.part(i, 0, 0), self.send_sem.at[i, slot])
        self.place(i).wait()


def line_order(t, me, last):
    short = jnp.minimum(me, last - me)
    near = jnp.where(lax.rem(t, 2) == 0, me - t // 2, me + (t + 1) // 2)
    far = jnp.where(me < last - me, me + (t - short), me - (t - short))
    return jnp.where(t <= 2 * short, near, far)


class Chain:
    def __init__(self, own, full, sems):
        self.own, self.full, (self.local, self.send_sem, self.recv_sem) = own, full, sems

    def copy(self, b, way, first=False):
        me = lax.axis_index("gy")
        return pltpu.make_async_remote_copy(
            src_ref=self.own if first else self.full.at[b],
            dst_ref=self.full.at[b],
            send_sem=self.send_sem.at[b, way],
            recv_sem=self.recv_sem.at[b],
            device_id=(lax.axis_index("gx"), me - 1 + 2 * way),
            device_id_type=MESH,
        )

    def each(self, b, act, first=False):
        me, last = lax.axis_index("gy"), lax.axis_size("gy") - 1

        @pl.when(jnp.logical_and(b <= me, me < last))
        def _():
            act(self.copy(b, 1, first))

        @pl.when(jnp.logical_and(b >= me, me > 0))
        def _():
            act(self.copy(b, 0, first))

    def begin(self):
        me = lax.axis_index("gy")
        self.place = pltpu.make_async_copy(self.own, self.full.at[me], self.local)
        self.place.start()
        self.each(me, lambda copy: copy.start(), True)

    def relay(self, t):
        b = line_order(t, lax.axis_index("gy"), lax.axis_size("gy") - 1)
        wait_for(self.full.at[b], self.recv_sem.at[b])
        self.each(b, lambda copy: copy.start())

    def close(self):
        self.place.wait()
        for b in range(lax.axis_size("gy")):
            self.each(b, lambda copy: copy.wait_send())


class Exchange:
    def __init__(self, own, full, sems):
        self.own, self.full, (self.local, self.send_sem, self.recv_sem) = own, full, sems

    def begin(self):
        gx, me, size = lax.axis_index("gx"), lax.axis_index("gy"), lax.axis_size("gy")
        width = self.full.shape[2]

        def columns(k):
            return self.own.at[:, pl.ds(pl.multiple_of(k * width, width), width)]

        self.place = pltpu.make_async_copy(columns(me), self.full.at[me], self.local)
        self.place.start()
        self.sent = []
        for d in range(1, size):
            target = lax.rem(me + d, size)
            copy = pltpu.make_async_remote_copy(
                src_ref=columns(target),
                dst_ref=self.full.at[me],
                send_sem=self.send_sem.at[d],
                recv_sem=self.recv_sem.at[me],
                device_id=(gx, target),
                device_id_type=MESH,
            )
            copy.start()
            self.sent.append(copy)

    def close(self):
        me, size = lax.axis_index("gy"), lax.axis_size("gy")
        self.place.wait()
        for copy in self.sent:
            copy.wait_send()
        for d in range(1, size):
            k = lax.rem(me + d, size)
            wait_for(self.full.at[k], self.recv_sem.at[k])


def chain_scratch():
    size = lax.axis_size("gy")
    return [
        pltpu.SemaphoreType.DMA,
        pltpu.SemaphoreType.DMA((size, 2)),
        pltpu.SemaphoreType.DMA((size,)),
    ]


def exchange_scratch():
    size = lax.axis_size("gy")
    return [
        pltpu.SemaphoreType.DMA,
        pltpu.SemaphoreType.DMA((size,)),
        pltpu.SemaphoreType.DMA((size,)),
    ]


def opening_kernel(*refs):
    ins, outs, sems = refs[:8], refs[8:17], refs[17:]
    resid, cot, small, pack_a, pack_b, wg, wu, wd = ins
    resid_out, cot_out, small_out, line_a, line_b, attn, gate, up, down = outs
    me, size = lax.axis_index("gy"), lax.axis_size("gy")
    partner, others = places()
    near = list(square()[:2]) if lax.axis_size("gx") == 8 else others
    chains = [
        Chain(own, full, sems[3 * k : 3 * k + 3])
        for k, (own, full) in enumerate(((pack_a, line_a), (pack_b, line_b), (small, small_out)))
    ]
    swaps = [
        Exchange(own, full, sems[9 + 3 * k : 12 + 3 * k])
        for k, (own, full) in enumerate(((resid, resid_out), (cot, cot_out)))
    ]
    spread = Spread(
        [(line_a, attn), (wg.at[0], gate), (wu.at[0], up), (wd.at[0], down)], sems[15:18]
    )
    greet([partner] + near, [lax.rem(me + d, size) for d in range(1, size)])
    chains[0].begin()
    chains[2].begin()
    spread.begin(1)
    for t in range(1, size):
        chains[0].relay(t)
    chains[0].close()
    spread.begin(0)
    swaps[0].begin()
    for t in range(1, size):
        chains[2].relay(t)
    spread.begin(2)
    chains[1].begin()
    spread.relay(1)
    for t in range(1, size):
        chains[1].relay(t)
    spread.begin(3)
    swaps[1].begin()
    spread.relay(0)
    spread.finish(1)
    spread.relay(2)
    spread.finish(0)
    spread.relay(3)
    spread.finish(2)
    spread.finish(3)
    for i in (1, 2, 3, 0):
        spread.close(i)
    for part in chains[1:] + swaps:
        part.close()


def opening(resid, cot, small, pack_a, pack_b, wg, wu, wd):
    devices, size = lax.axis_size("gx"), lax.axis_size("gy")
    count = resid.shape[1] // size

    def shape(*dims, kind=bf16):
        return jax.ShapeDtypeStruct(dims, kind)

    blocks = shape(size, resid.shape[0], count)
    line = shape(size, *pack_a.shape)
    weight = shape(devices, *wg.shape[1:])
    packed = shape(devices, size, *pack_a.shape)
    out = [blocks, blocks, shape(size, *small.shape, kind=f32), line, line, packed] + [weight] * 3

    return pl.pallas_call(
        opening_kernel,
        out_shape=out,
        in_specs=[ANY] * 8,
        out_specs=[ANY] * 9,
        scratch_shapes=chain_scratch() * 3 + exchange_scratch() * 2 + spread_scratch(4),
        compiler_params=pltpu.CompilerParams(collective_id=2, has_side_effects=True),
        name="opening",
    )(resid, cot, small, pack_a, pack_b, wg, wu, wd)


def line_pass(own_ref, own, gathered, part, outb, inb, sems, load, finish, peers=(), plan={}):
    own_sem, ag_send, ag_recv, rs_send, rs_recv = sems
    gx, me, size = lax.axis_index("gx"), lax.axis_index("gy"), lax.axis_size("gy")
    rows = own.shape[0]
    piece = rows // PIECES
    last = size - 1
    inner = jnp.logical_and(me > 0, me < last)

    first = pltpu.make_async_copy(own_ref, gathered.at[me], own_sem)
    first.start()
    barrier = pltpu.get_barrier_semaphore()

    @pl.when(me > 0)
    def _():
        pl.semaphore_signal(barrier, inc=1, device_id=(gx, me - 1), device_id_type=MESH)

    @pl.when(me < last)
    def _():
        pl.semaphore_signal(barrier, inc=1, device_id=(gx, me + 1), device_id_type=MESH)

    for peer in peers:
        pl.semaphore_signal(barrier, inc=1, device_id=(peer, me), device_id_type=MESH)
    pl.semaphore_wait(barrier, jnp.where(inner, 2, 1) + len(peers))
    first.wait()

    def planned(name, t):
        for (key, when), act in plan.items():
            if key == name:
                pl.when(t == when)(act)


    def gather_copy(b, s, way):
        here = gathered.at[b, pl.ds(s * piece, piece)]
        return pltpu.make_async_remote_copy(
            src_ref=here,
            dst_ref=here,
            send_sem=ag_send.at[b, way, s],
            recv_sem=ag_recv.at[b, s],
            device_id=(gx, me - 1 + 2 * way),
            device_id_type=MESH,
        )

    def sum_copy(b, s):
        towards = jnp.where(b > me, me + 1, me - 1)
        slot = jnp.where(jnp.logical_and(towards == b, me > b), size, b)
        return pltpu.make_async_remote_copy(
            src_ref=outb.at[b, pl.ds(s * piece, piece)],
            dst_ref=inb.at[slot, pl.ds(s * piece, piece)],
            send_sem=rs_send.at[b, s],
            recv_sem=rs_recv.at[slot, s],
            device_id=(gx, towards),
            device_id_type=MESH,
        )

    def sum_arrived(slot, s):
        here = inb.at[slot, pl.ds(s * piece, piece)]
        pltpu.make_async_copy(here, here, rs_recv.at[slot, s]).wait()

    def step(t, carry):
        b = line_order(t, me, last)
        for s in range(PIECES):

            @pl.when(t > 0)
            def _():
                gather_copy(b, s, 0).wait_recv()

            @pl.when(jnp.logical_and(b <= me, me < last))
            def _():
                gather_copy(b, s, 1).start()

            @pl.when(jnp.logical_and(b >= me, me > 0))
            def _():
                gather_copy(b, s, 0).start()

        @pl.when(t == 0)
        def _():
            load()

        planned("step", t)
        finish(b)

        @pl.when(b == me)
        def _():
            own[...] = part[...]

        @pl.when(b != me)
        def _():
            outb[b] = part[...].astype(bf16)

            @pl.when(jnp.logical_not(inner))
            def _():
                for s in range(PIECES):
                    sum_copy(b, s).start()

        return carry

    lax.fori_loop(0, size, step, 0)

    def relay(t, carry):
        above, below = last - me, me
        low = jnp.where(t < above, me + 1 + t, me - 1 - (t - above))
        high = jnp.where(t < below, me - 1 - t, me + 1 + (t - below))
        b = jnp.where(2 * me < size, low, high)
        planned("hop", t)

        @pl.when(inner)
        def _():
            for s in range(PIECES):
                at = pl.ds(s * piece, piece)
                sum_arrived(b, s)
                outb[b, at] = (outb[b, at].astype(f32) + inb[b, at].astype(f32)).astype(bf16)
                sum_copy(b, s).start()

        return carry

    lax.fori_loop(0, last, relay, 0)

    @pl.when(me > 0)
    def _():
        for s in range(PIECES):
            sum_arrived(me, s)
        own[...] += inb[me].astype(f32)

    @pl.when(me < last)
    def _():
        for s in range(PIECES):
            sum_arrived(size, s)
        own[...] += inb[size].astype(f32)

    def drain(b, carry):
        for s in range(PIECES):

            @pl.when(jnp.logical_and(b <= me, me < last))
            def _():
                gather_copy(b, s, 1).wait_send()

            @pl.when(jnp.logical_and(b >= me, me > 0))
            def _():
                gather_copy(b, s, 0).wait_send()

            @pl.when(b != me)
            def _():
                sum_copy(b, s).wait_send()

        return carry

    lax.fori_loop(0, size, drain, 0)


def line_scratch(size, rows, width):
    return [
        pltpu.VMEM((size, rows, width), bf16),
        pltpu.VMEM((rows, width), f32),
        pltpu.VMEM((size, rows, width), bf16),
        pltpu.VMEM((size + 1, rows, width), bf16),
        pltpu.SemaphoreType.DMA,
        pltpu.SemaphoreType.DMA((size, 2, PIECES)),
        pltpu.SemaphoreType.DMA((size, PIECES)),
        pltpu.SemaphoreType.DMA((size, PIECES)),
        pltpu.SemaphoreType.DMA((size + 1, PIECES)),
    ]


LINE = 9


ORDER = {
    ("step", 0): "b0",
    ("step", 2): "b1",
    ("hop", 0): "r0 r1 b2",
    ("hop", 1): "f0 f1 b3",
}
REST = "r2 r3 f2 f3 c0 c1 c2 c3"
VERBS = {"b": "begin", "r": "relay", "f": "finish", "c": "close"}


def schedule(spread, size):
    def run(text):
        def act():
            for word in text.split():
                getattr(spread, VERBS[word[0]])(int(word[1]))

        return act

    plan = {key: run(text) for key, text in ORDER.items()}
    return plan, [(VERBS[word[0]], int(word[1])) for word in REST.split()]


def forward_kernel(extra, *refs):
    acts_ref, wg_ref, wu_ref, wd_ref = refs[:4]
    shards, refs = refs[4 : 4 + extra], refs[4 + extra :]
    sum_ref, turned_ref, gate_ref, up_ref, hidden_ref = refs[:5]
    wholes, scratch = refs[5 : 5 + extra], refs[5 + extra :]
    gathered, part, outb, inb = scratch[:4]
    sems = scratch[4:LINE]
    wg, wu, wd, gate, up, hidden, turned, w_sem, out_sem = scratch[LINE : LINE + 9]
    peers, spread = [], None
    if extra:
        items = [(r if r.shape == w.shape[1:] else r.at[1], w) for r, w in zip(shards, wholes)]
        spread = Spread(items, scratch[LINE + 9 :])
        partner, others = places()
        peers = [partner] + (list(square()[:2]) if spread.four else others)

    plan, rest = schedule(spread, lax.axis_size("gy")) if extra else ({}, ())
    loads = [
        pltpu.make_async_copy(src, dst, w_sem.at[k])
        for k, (src, dst) in enumerate(((wg_ref, wg), (wu_ref, wu), (wd_ref, wd)))
    ]
    for copy in loads:
        copy.start()

    def load():
        for copy in loads:
            copy.wait()

    def results(b):
        pairs = ((gate, gate_ref), (up, up_ref), (hidden, hidden_ref))
        return [
            pltpu.make_async_copy(src.at[b], dst.at[b], out_sem.at[b, k])
            for k, (src, dst) in enumerate(pairs)
        ]

    def finish(b):
        block = gathered[b]
        store_turned(block, turned, b)
        for start, width in spans(wg.shape[1]):
            at = slice(start, start + width)
            g = nn(block, wg[:, at])
            u = nn(block, wu[:, at])
            h = (g * lax.logistic(g) * u).astype(bf16)
            gate[b, :, at] = g.astype(bf16)
            up[b, :, at] = u.astype(bf16)
            hidden[b, :, at] = h
            p = nt(h, wd[:, at])
            if start == 0:
                part[...] = p
            else:
                part[...] += p
        for copy in results(b):
            copy.start()

    line_pass(
        acts_ref, sum_ref, gathered, part, outb, inb, sems, load, finish, peers, plan
    )
    keep = pltpu.make_async_copy(turned, turned_ref, w_sem.at[0])
    keep.start()
    for act, i in rest:
        getattr(spread, act)(i)

    def settle(b, carry):
        for copy in results(b):
            copy.wait()
        return carry

    lax.fori_loop(0, gathered.shape[0], settle, 0)
    keep.wait()


def forward_ffn(acts, wg, wu, wd, shards=()):
    rows, width = acts.shape
    devices, size, hidden = lax.axis_size("gx"), lax.axis_size("gy"), wg.shape[1]
    wide = jax.ShapeDtypeStruct((size, rows, hidden), bf16)
    extra = len(shards)
    wholes = [
        jax.ShapeDtypeStruct((devices,) + (s.shape if k == 0 else s.shape[1:]), bf16)
        for k, s in enumerate(shards)
    ]
    return pl.pallas_call(
        functools.partial(forward_kernel, extra),
        out_shape=[
            jax.ShapeDtypeStruct((rows, width), f32),
            jax.ShapeDtypeStruct((2, width // 2, size * rows), bf16),
            wide,
            wide,
            wide,
        ]
        + wholes,
        in_specs=[ANY] * (4 + extra),
        out_specs=[pl.BlockSpec(memory_space=pltpu.VMEM)] + [ANY] * (4 + extra),
        scratch_shapes=line_scratch(size, rows, width)
        + [pltpu.VMEM((width, hidden), bf16)] * 3
        + [pltpu.VMEM((size, rows, hidden), bf16)] * 3
        + [pltpu.VMEM((2, width // 2, size * rows), bf16)]
        + [pltpu.SemaphoreType.DMA((3,)), pltpu.SemaphoreType.DMA((size, 3))]
        + (spread_scratch(extra) if extra else []),
        compiler_params=pltpu.CompilerParams(
            collective_id=3 if extra else 0, has_side_effects=True, vmem_limit_bytes=VMEM_LIMIT
        ),
        cost_estimate=pl.CostEstimate(
            flops=6 * size * rows * width * hidden, bytes_accessed=40 << 20, transcendentals=0
        ),
        name="ffn_forward",
    )(acts, wg, wu, wd, *shards)


class Reduce:
    def __init__(self, lhs, rhs, bufs, abuf, fbuf, ftail, a_all, r_all, c_all, outs, sems):
        self.lhs, self.rhs, self.bufs, self.outs = lhs, rhs, bufs, outs
        self.abuf, self.fbuf, self.ftail = abuf, fbuf, ftail
        self.a_all, self.r_all, self.c_all = a_all, r_all, c_all
        (
            self.a_send,
            self.a_recv,
            self.r_send,
            self.r_recv,
            self.c_send,
            self.c_recv,
            self.local,
        ) = sems
        gx, self.gy = lax.axis_index("gx"), lax.axis_index("gy")
        self.chip, self.core = gx // 2, lax.rem(gx, 2)
        self.chips = lax.axis_size("gx") // 2
        self.half, self.wide = bufs[0].shape[0] // 2, bufs[0].shape[1]
        self.r = self.half // self.chips
        self.four = self.chips == 4
        self.partner, self.others = places()
        self.near = list(square()[:2]) if self.four else self.others

    def product(self, m, which, at):
        z, n, _ = self.rhs[m].shape
        right = self.rhs[m][:, :, at].reshape(z * n, at.stop - at.start)
        return nn(self.lhs[which], right)

    def remote(self, src, dst, send, recv, target):
        return pltpu.make_async_remote_copy(
            src_ref=src,
            dst_ref=dst,
            send_sem=send,
            recv_sem=recv,
            device_id=(target, self.gy),
            device_id_type=MESH,
        )

    def columns(self):
        return [(j, slice(s, s + w)) for j, (s, w) in enumerate(spans(self.wide))]

    def swap(self, m, j, at):
        here = (slice(0, self.half), at)
        return self.remote(
            self.bufs[m].at[here],
            self.a_all.at[m, :, at],
            self.a_send.at[m, j],
            self.a_recv.at[m, j],
            self.partner,
        )

    def block(self, m, device, start=0, size=None):
        size = self.r if size is None else size
        first = self.half + (device // 2) * self.r + start
        return self.bufs[m].at[pl.ds(pl.multiple_of(first, 16), size)]

    def first(self, m):
        for j, at in self.columns():
            self.bufs[m][: self.half, at] = self.product(m, 1 - self.core, at).astype(bf16)
            self.swap(m, j, at).start()

    def corner(self, m, h):
        side, along, across = square()
        half = self.r // 2
        return self.remote(
            self.block(m, across, h * half, half),
            self.r_all.at[m, h],
            self.r_send.at[m, h],
            self.r_recv.at[m, h],
            along if h else side,
        )

    def second(self, m):
        for j, at in self.columns():
            self.swap(m, j, at).wait_recv()
            landed = self.abuf.at[:, at]
            fetch = pltpu.make_async_copy(self.a_all.at[m, :, at], landed, self.local.at[0])
            fetch.start()
            mine = self.product(m, self.core, at)
            fetch.wait()
            self.bufs[m][self.half :, at] = (mine + landed[...].astype(f32)).astype(bf16)
        if self.four:
            for h in range(2):
                self.corner(m, h).start()

    def hand(self, m, k):
        target = self.near[k]
        return self.remote(
            self.block(m, target),
            self.c_all.at[m, k],
            self.c_send.at[m, k],
            self.c_recv.at[m, k],
            target,
        )

    def third(self, m):
        if self.four:
            side, along, _ = square()
            half = self.r // 2
            for h, device in ((0, along), (1, side)):
                self.corner(m, h).wait_recv()
                here = self.block(m, device, h * half, half)
                landed = self.abuf.at[h * half : (h + 1) * half]
                fetch = pltpu.make_async_copy(self.r_all.at[m, h], landed, self.local.at[0])
                fetch.start()
                fetch.wait()
                here[...] = (here[...].astype(f32) + landed[...].astype(f32)).astype(bf16)
        for k in range(len(self.near)):
            self.hand(m, k).start()

    def fourth(self, m):
        for j, at in self.columns():
            self.swap(m, j, at).wait_send()
        fetches = []
        for k in range(len(self.near)):
            self.hand(m, k).wait_recv()
            here = self.bufs[m].at[pl.ds(k * self.r, self.r)]
            fetch = pltpu.make_async_copy(self.c_all.at[m, k], here, self.local.at[k])
            fetch.start()
            fetches.append(fetch)
        for fetch in fetches:
            fetch.wait()
        first = pl.multiple_of(self.half + self.chip * self.r, 16)
        for _, at in self.columns():
            total = self.bufs[m][pl.ds(first, self.r), at].astype(f32)
            for k in range(len(self.near)):
                total = total + self.bufs[m][k * self.r : (k + 1) * self.r, at].astype(f32)
            stage = self.fbuf if total.shape[1] == FF_CHUNK else self.ftail
            stage[...] = total
            store = pltpu.make_async_copy(stage, self.outs[m].at[:, at], self.local.at[0])
            store.start()
            store.wait()

    def drain(self, m):
        if self.four:
            for h in range(2):
                self.corner(m, h).wait_send()
        for k in range(len(self.near)):
            self.hand(m, k).wait_send()


def reduce_scratch(width, hidden, count=3):
    devices = lax.axis_size("gx")
    rows, parts = width // devices, len(spans(hidden))
    near = 2 if devices == 8 else devices // 2 - 1
    dma = pltpu.SemaphoreType.DMA
    return [
        pltpu.VMEM((width // 2, hidden), bf16),
        pltpu.VMEM((rows, FF_CHUNK), f32),
        pltpu.VMEM((rows, hidden % FF_CHUNK), f32),
        dma((count, parts)),
        dma((count, parts)),
        dma((count, 2)),
        dma((count, 2)),
        dma((count, near)),
        dma((count, near)),
        dma((near,)),
    ]


def store_turned(block, turned, b):
    count, width = block.shape
    _, chips_rows, _ = turned.shape
    devices = lax.axis_size("gx")
    r = width // devices
    flipped = block.T
    at = pl.ds(pl.multiple_of(b * count, count), count)
    for k in range(devices):
        q = k // 2
        turned[k % 2, q * r : (q + 1) * r, at] = flipped[k * r : (k + 1) * r]


AFTER = (
    ("hop", 0, "first", 0),
    ("hop", 1, "second", 0),
    ("hop", 1, "first", 1),
    ("hop", 2, "third", 0),
    ("hop", 2, "second", 1),
)


def backward_kernel(
    grad_ref, gate_ref, up_ref, hidden_ref, turned_ref, wg_ref, wu_ref, wd_ref, *refs
):
    sum_ref, og, ou, od, a_all, r_all, c_all = refs[:7]
    scratch = refs[7:]
    gathered, part, outb, inb = scratch[:4]
    sems = scratch[4:LINE]
    wg, wu, wd, gate, up, hidden, turned, w_sem = scratch[LINE : LINE + 8]
    abuf, fbuf, ftail = scratch[LINE + 8 : LINE + 11]
    operands = (
        (wd_ref, wd),
        (gate_ref, gate),
        (up_ref, up),
        (wg_ref, wg),
        (wu_ref, wu),
        (hidden_ref, hidden),
    )
    loads = [
        pltpu.make_async_copy(src, dst, w_sem.at[k]) for k, (src, dst) in enumerate(operands)
    ]
    for copy in loads:
        copy.start()

    def load():
        for copy in loads:
            copy.wait()

    reduce = Reduce(
        turned,
        (hidden, gate, up),
        (wd, wg, wu),
        abuf,
        fbuf,
        ftail,
        a_all,
        r_all,
        c_all,
        (od, og, ou),
        scratch[LINE + 11 :],
    )

    def finish(b):
        block = gathered[b]
        store_turned(block, turned, b)
        for start, width in spans(wg.shape[1]):
            at = slice(start, start + width)
            d = nn(block, wd[:, at])
            g = gate[b, :, at].astype(f32)
            u = up[b, :, at].astype(f32)
            sigma = lax.logistic(g)
            ds = d * sigma
            dg = (ds * u * (1.0 + g * (1.0 - sigma))).astype(bf16)
            du = (ds * g).astype(bf16)
            gate[b, :, at] = dg
            up[b, :, at] = du
            p = nt(dg, wg[:, at]) + nt(du, wu[:, at])
            if start == 0:
                part[...] = p
            else:
                part[...] += p

    def swap_operand():
        copy = pltpu.make_async_copy(turned_ref, turned, w_sem.at[0])
        copy.start()
        copy.wait()

    def work(when):
        def act():
            for name, t, verb, m in AFTER:
                if t == when:
                    getattr(reduce, verb)(m)
                    if verb == "second" and m == 0:
                        swap_operand()

        return act

    peers = [reduce.partner] + reduce.near
    plan = {("hop", t): work(t) for t in range(3)}
    line_pass(grad_ref, sum_ref, gathered, part, outb, inb, sems, load, finish, peers, plan)
    reduce.first(2)
    reduce.third(1)
    reduce.second(2)
    reduce.fourth(0)
    reduce.third(2)
    reduce.fourth(1)
    reduce.fourth(2)
    for m in range(3):
        reduce.drain(m)


def backward_ffn(grad, gate, up, hidden, turned, wg, wu, wd):
    rows, width = grad.shape
    devices, size, wide = lax.axis_size("gx"), lax.axis_size("gy"), wg.shape[1]
    near = 2 if devices == 8 else devices // 2 - 1
    mine = jax.ShapeDtypeStruct((width // devices, wide), f32)
    return pl.pallas_call(
        backward_kernel,
        out_shape=[
            jax.ShapeDtypeStruct((rows, width), f32),
            mine,
            mine,
            mine,
            jax.ShapeDtypeStruct((3, width // 2, wide), bf16),
            jax.ShapeDtypeStruct((3, 2, width // devices // 2, wide), bf16),
            jax.ShapeDtypeStruct((3, near, width // devices, wide), bf16),
        ],
        in_specs=[ANY] * 8,
        out_specs=[pl.BlockSpec(memory_space=pltpu.VMEM)] + [ANY] * 6,
        scratch_shapes=line_scratch(size, rows, width)
        + [pltpu.VMEM((width, wide), bf16)] * 3
        + [pltpu.VMEM((size, rows, wide), bf16)] * 3
        + [pltpu.VMEM((2, width // 2, size * rows), bf16), pltpu.SemaphoreType.DMA((6,))]
        + reduce_scratch(width, wide),
        compiler_params=pltpu.CompilerParams(
            collective_id=1, has_side_effects=True, vmem_limit_bytes=VMEM_LIMIT
        ),
        cost_estimate=pl.CostEstimate(
            flops=12 * size * rows * width * wide, bytes_accessed=40 << 20, transcendentals=0
        ),
        name="ffn_backward",
    )(grad, gate, up, hidden, turned, wg, wu, wd)


def on_device(
    residual_in,
    w_query,
    w_key,
    w_value,
    b_query,
    b_key,
    b_value,
    w_output,
    gain_attn,
    gain_ffn,
    w_gate,
    w_up,
    w_down,
    cotangent,
):
    devices_x = lax.axis_size("gx")
    devices_y = lax.axis_size("gy")
    rows_tok = residual_in.shape[1]
    count = rows_tok // devices_y
    q_index = lax.axis_index("gy") * count + jnp.arange(count, dtype=jnp.int32)
    k_index = jnp.arange(rows_tok, dtype=jnp.int32)
    allowed = (q_index[:, None] // LEN == k_index[None, :] // LEN) & (
        k_index[None, :] <= q_index[:, None]
    )
    cosine, sine = rope_tables(q_index % LEN, HEAD_DIM)

    small = jnp.concatenate([gain_attn, gain_ffn, b_query, b_key, b_value], axis=1)
    small_sizes = [v.shape[1] for v in (gain_attn, gain_ffn, b_query, b_key, b_value)]
    small = jnp.pad(small.astype(f32), ((0, 8 - LAYERS), (0, 0)))
    packs = [
        jnp.concatenate([w[l] for w in (w_query, w_key, w_value, w_output)], axis=1)
        for l in range(LAYERS)
    ]
    pack_sizes = [w.shape[2] for w in (w_query, w_key, w_value, w_output)]
    opened = opening(residual_in, cotangent, small, *packs, w_gate, w_up, w_down)
    resid, cot, small, _, line_next, attn_pack = opened[:6]
    ffn_full = [[w.reshape(D, -1) for w in opened[6:]], None]
    small = small[:, :LAYERS].transpose(1, 0, 2)
    vectors, start = [], 0
    for size in small_sizes:
        vectors.append(small[:, :, start : start + size].reshape(LAYERS, -1))
        start += size
    gains_one, gains_two, bias_q, bias_k, bias_v = vectors

    resid = resid.reshape(D, count).astype(f32).T
    cot = cot.reshape(D, count)
    attn_full = [unpack_attention(attn_pack, pack_sizes), None]

    kept = []
    for l in range(LAYERS):
        wq, wk, wv, wo = attn_full[l]
        wg, wu, wd = ffn_full[l]
        normed_one, scale_one = rms_parts(resid)
        acts_one = (normed_one * gains_one[l]).astype(bf16)
        queries = dot("td,dq->tq", acts_one, wq) + bias_q[l]
        keys = dot("td,dq->tq", acts_one, wk) + bias_k[l]
        values = (dot("td,dq->tq", acts_one, wv) + bias_v[l]).astype(bf16)
        q_rot = rotate(queries.reshape(count, HEADS, HEAD_DIM), cosine, sine).astype(bf16)
        q_rot = q_rot.reshape(count, KV_HEADS, GROUP, HEAD_DIM)
        k_rot = rotate(keys.reshape(count, KV_HEADS, HEAD_DIM), cosine, sine).astype(bf16)
        both = jnp.concatenate([k_rot.reshape(count, -1), values], axis=1)
        both = lax.all_gather(both, "gy", axis=0, tiled=True)
        half = both.shape[1] // 2
        k_rot = both[:, :half].reshape(rows_tok, KV_HEADS, HEAD_DIM)
        v_heads = both[:, half:].reshape(rows_tok, KV_HEADS, HEAD_DIM)
        scores = score_block(q_rot, k_rot, allowed)
        top = jnp.max(scores, axis=-1, keepdims=True)
        expo = jnp.exp(scores - top)
        total = jnp.sum(expo, axis=-1, keepdims=True)
        soft = (expo / total).astype(bf16)
        log_total = top + jnp.log(total)
        mixed = dot("kgqs,skd->qkgd", soft, v_heads).reshape(count, -1).astype(bf16)
        middle = resid + dot("tq,dq->td", mixed, wo)
        normed_two, scale_two = rms_parts(middle)
        acts_two = (normed_two * gains_two[l]).astype(bf16)
        if l == 0:
            shards = (line_next, w_gate, w_up, w_down)
            done = forward_ffn(acts_two, wg, wu, wd, shards)
            attn_full[1] = unpack_attention(done[5], pack_sizes)
            ffn_full[1] = [w.reshape(D, -1) for w in done[6:]]
        else:
            done = forward_ffn(acts_two, wg, wu, wd)
        part, acts_two, gate, up, hidden = done[:5]
        kept.append(
            (
                normed_one,
                scale_one,
                acts_one,
                q_rot,
                k_rot,
                v_heads,
                log_total,
                mixed,
                normed_two,
                scale_two,
                acts_two,
                gate,
                up,
                hidden,
            )
        )
        resid = middle + part

    def to_blocks(tokens_major):
        flipped = tokens_major.astype(bf16).T
        out = lax.all_to_all(flipped, "gy", split_axis=0, concat_axis=1, tiled=True)
        return out.astype(f32)

    output = to_blocks(resid)
    grad = cot.astype(f32).T + 2.0 * penalty * resid
    attn_grads = [None] * LAYERS
    ffn_grads = [None] * LAYERS
    small_grads = [None] * LAYERS

    for l in reversed(range(LAYERS)):
        (
            normed_one,
            scale_one,
            acts_one,
            q_rot,
            k_rot,
            v_heads,
            log_total,
            mixed,
            normed_two,
            scale_two,
            acts_two,
            gate,
            up,
            hidden,
        ) = kept[l]
        wq, wk, wv, wo = attn_full[l]
        wg, wu, wd = ffn_full[l]
        done = backward_ffn(grad.astype(bf16), gate, up, hidden, acts_two, wg, wu, wd)
        grad_acts_two, ffn_grads[l] = done[0], done[1:4]
        grad_norm, grad_gain_two = norm_backward(
            grad_acts_two, normed_two, scale_two, gains_two[l]
        )
        grad_mid = grad + grad_norm
        grad_branch = grad_mid.astype(bf16)
        grad_wo = dot("td,tq->dq", grad_branch, mixed)
        grad_mixed = dot("td,dq->tq", grad_branch, wo).astype(bf16)
        grad_heads = grad_mixed.reshape(count, KV_HEADS, GROUP, HEAD_DIM)
        scores = score_block(q_rot, k_rot, allowed)
        soft_full = jnp.exp(scores - log_total)
        soft = soft_full.astype(bf16)
        grad_soft = dot("qkgd,skd->kgqs", grad_heads, v_heads)
        inner = jnp.sum(soft_full * grad_soft, axis=-1, keepdims=True)
        grad_scores = (soft_full * (grad_soft - inner)).astype(bf16)
        grad_values = dot("kgqs,qkgd->skd", soft, grad_heads)
        factor = 1.0 / math.sqrt(HEAD_DIM)
        grad_qrot = dot("kgqs,skd->qkgd", grad_scores, k_rot) * factor
        grad_krot = dot("kgqs,qkgd->skd", grad_scores, q_rot) * factor
        grad_q = rotate_back(grad_qrot.reshape(count, HEADS, HEAD_DIM), cosine, sine)
        grad_q = grad_q.reshape(count, -1).astype(bf16)
        both = jnp.concatenate(
            [grad_krot.reshape(rows_tok, -1), grad_values.reshape(rows_tok, -1)], axis=1
        ).astype(bf16)
        both = lax.psum_scatter(both, "gy", scatter_dimension=0, tiled=True).astype(f32)
        half = both.shape[1] // 2
        grad_k = rotate_back(both[:, :half].reshape(count, KV_HEADS, HEAD_DIM), cosine, sine)
        grad_k = grad_k.reshape(count, -1).astype(bf16)
        grad_v = both[:, half:].astype(bf16)
        grad_acts_one = (
            dot("tq,dq->td", grad_q, wq)
            + dot("tq,dq->td", grad_k, wk)
            + dot("tq,dq->td", grad_v, wv)
        )
        attn_grads[l] = scatter_attention(
            [
                g.astype(bf16)
                for g in (
                    dot("td,tq->dq", acts_one, grad_q),
                    dot("td,tq->dq", acts_one, grad_k),
                    dot("td,tq->dq", acts_one, grad_v),
                    grad_wo,
                )
            ],
            devices_x,
            devices_y,
        )
        grad_norm, grad_gain_one = norm_backward(
            grad_acts_one, normed_one, scale_one, gains_one[l]
        )
        grad = grad_mid + grad_norm
        small_grads[l] = [
            v.reshape(devices_y, -1)
            for v in (
                grad_gain_one,
                grad_gain_two,
                jnp.sum(grad_q.astype(f32), axis=0),
                jnp.sum(grad_k.astype(f32), axis=0),
                jnp.sum(grad_v.astype(f32), axis=0),
            )
        ]
    small = jnp.stack([jnp.concatenate(v, axis=1) for v in small_grads], axis=1)
    small = lax.psum(small, ("gx", "gy"))
    small = lax.dynamic_index_in_dim(small, lax.axis_index("gy"), 0, keepdims=False)
    small_out, start = [], 0
    for size in small_sizes:
        small_out.append(small[:, start : start + size])
        start += size

    def stack(parts, k):
        return jnp.stack([part[k] for part in parts])

    return (
        output,
        to_blocks(grad),
        stack(attn_grads, 0),
        stack(attn_grads, 1),
        stack(attn_grads, 2),
        small_out[2],
        small_out[3],
        small_out[4],
        stack(attn_grads, 3),
        small_out[0],
        small_out[1],
        stack(ffn_grads, 0),
        stack(ffn_grads, 1),
        stack(ffn_grads, 2),
    )


def solution(mesh):
    tokens = P("gy", "gx")
    weight = P(None, "gx", "gy")
    vector = P(None, "gy")
    return jax.shard_map(
        on_device,
        mesh=mesh,
        in_specs=(
            tokens,
            weight,
            weight,
            weight,
            vector,
            vector,
            vector,
            weight,
            vector,
            vector,
            weight,
            weight,
            weight,
            tokens,
        ),
        out_specs=(
            tokens,
            tokens,
            weight,
            weight,
            weight,
            vector,
            vector,
            vector,
            weight,
            vector,
            vector,
            weight,
            weight,
            weight,
        ),
        check_vma=False,
    )
```

```python
import functools
import math

import jax
import jax.numpy as jnp
from jax import lax
from jax.experimental import pallas as pl
from jax.experimental.pallas import tpu as pltpu
from jax.sharding import PartitionSpec as P

D = 1536
HEADS = 12
KV_HEADS = 2
HEAD_DIM = 128
LEN = 1024
LAYERS = 2
GROUP = HEADS // KV_HEADS

epsilon = 1e-06
rope_base = 1000000.0
penalty = 0.25
bf16 = jnp.bfloat16
f32 = jnp.float32
MESH = pl.DeviceIdType.MESH
VMEM_LIMIT = 62 << 20
ANY = pl.BlockSpec(memory_space=pl.ANY)


def rope_tables(positions, head_size):
    freqs = rope_base ** (-jnp.arange(0, head_size, 2).astype(f32) / head_size)
    angles = positions.astype(f32)[:, None] * freqs[None, :]
    cosine = jnp.cos(angles)
    sine_table = jnp.sin(angles)
    return (
        jnp.concatenate([cosine, cosine], -1)[:, None, :],
        jnp.concatenate([sine_table, sine_table], -1)[:, None, :],
    )


def rotate(tensor, cosine, sine_table):
    half = tensor.shape[-1] // 2
    turned = jnp.concatenate([-tensor[..., half:], tensor[..., :half]], -1)
    return tensor * cosine + turned * sine_table


def rotate_back(tensor, cosine, sine_table):
    half = tensor.shape[-1] // 2
    moved = tensor * sine_table
    return tensor * cosine + jnp.concatenate([moved[..., half:], -moved[..., :half]], -1)


def dot(pattern, left, right):
    return jnp.einsum(pattern, left, right, preferred_element_type=f32)


def rms_parts(resid):
    scale = lax.rsqrt(jnp.mean(resid * resid, axis=1, keepdims=True) + epsilon)
    return resid * scale, scale


def norm_backward(grad_normed, normed, scale, gain):
    grad_gain = jnp.sum(grad_normed * normed, axis=0)
    scaled = grad_normed * gain
    project = jnp.mean(scaled * normed, axis=1, keepdims=True)
    return scale * (scaled - normed * project), grad_gain


def split_columns(blocks, sizes):
    out, start = [], 0
    for size in sizes:
        out.append(blocks[:, :, start : start + size].reshape(blocks.shape[0], -1))
        start += size
    return out


def turn(tokens_major):
    count, width = tokens_major.shape
    devices = lax.axis_size("gx")
    blocks = tokens_major.T.reshape(devices // 2, 2, width // devices, count)
    return blocks.transpose(1, 0, 2, 3).reshape(2, width // 2, count)


def score_block(q_rot, k_rot, allowed):
    scores = dot("qkgd,skd->kgqs", q_rot, k_rot) * (1.0 / math.sqrt(HEAD_DIM))
    return jnp.where(allowed, scores, -1e30)


def wait_for(ref, sem):
    pltpu.make_async_copy(ref, ref, sem).wait()


def places():
    gx, devices = lax.axis_index("gx"), lax.axis_size("gx")
    chips = devices // 2
    chip, core = gx // 2, lax.rem(gx, 2)
    partner = gx + 1 - 2 * core
    others = [lax.rem(chip + k, chips) * 2 + core for k in range(1, chips)]
    return partner, others


def square():
    gx = lax.axis_index("gx")
    chip, core = gx // 2, lax.rem(gx, 2)
    side = gx + 2 - 4 * lax.rem(chip, 2)
    along = gx + 4 - 8 * (chip // 2)
    return side, along, (3 - chip) * 2 + core


def spread_slots():
    chips = lax.axis_size("gx") // 2
    return 14 if chips == 4 else 2 * chips + 2 * (chips - 1)


def spread_scratch(count):
    devices = lax.axis_size("gx")
    return [
        pltpu.SemaphoreType.DMA((count,)),
        pltpu.SemaphoreType.DMA((count, spread_slots())),
        pltpu.SemaphoreType.DMA((count, devices, 2)),
    ]


def greet(gx_peers, gy_peers):
    gx, gy = lax.axis_index("gx"), lax.axis_index("gy")
    barrier = pltpu.get_barrier_semaphore()
    for peer in gx_peers:
        pl.semaphore_signal(barrier, inc=1, device_id=(peer, gy), device_id_type=MESH)
    for peer in gy_peers:
        pl.semaphore_signal(barrier, inc=1, device_id=(gx, peer), device_id_type=MESH)
    pl.semaphore_wait(barrier, len(gx_peers) + len(gy_peers))


class Spread:
    def __init__(self, items, sems):
        self.items, (self.local, self.send_sem, self.recv_sem) = items, sems
        self.partner, self.others = places()
        self.four = lax.axis_size("gx") // 2 == 4
        self.near = list(square()[:2]) if self.four else self.others

    def part(self, i, k, h):
        full = self.items[i][1]
        if len(full.shape) == 4:
            half = full.shape[0] // 2
            return full.at[pl.ds(h * half, half), k]
        half = full.shape[1] // 2
        return full.at[k, pl.ds(h * half, half)]

    def send(self, i, k, h, target, slot, first=False):
        here = self.part(i, k, h)
        half = here.shape[0]
        source = self.items[i][0].at[pl.ds(h * half, half)] if first else here
        pltpu.make_async_remote_copy(
            src_ref=source,
            dst_ref=here,
            send_sem=self.send_sem.at[i, slot],
            recv_sem=self.recv_sem.at[i, k, h],
            device_id=(target, lax.axis_index("gy")),
            device_id_type=MESH,
        ).start()

    def arrived(self, i, k, h):
        wait_for(self.part(i, k, h), self.recv_sem.at[i, k, h])

    def place(self, i):
        own, full = self.items[i]
        gx = lax.axis_index("gx")
        here = full.at[:, gx] if len(full.shape) == 4 else full.at[gx]
        return pltpu.make_async_copy(own, here, self.local.at[i])

    def begin(self, i):
        gx = lax.axis_index("gx")
        self.place(i).start()
        slot = 0
        for target in self.near + [self.partner]:
            for h in range(2):
                self.send(i, gx, h, target, slot, True)
                slot += 1

    def relay(self, i):
        slot = 2 * len(self.near) + 2
        if self.four:
            side, along, _ = square()
            steps = [(side, 0, along), (along, 1, side), (side, 1, None), (along, 0, None)]
        else:
            steps = [(k, h, None) for k in self.others for h in range(2)]
        for k, h, target in steps:
            self.arrived(i, k, h)
            for to in [self.partner] if target is None else [target, self.partner]:
                self.send(i, k, h, to, slot)
                slot += 1

    def finish(self, i):
        if self.four:
            for h in range(2):
                self.arrived(i, square()[2], h)
                self.send(i, square()[2], h, self.partner, 12 + h)

    def close(self, i):
        core = lax.rem(lax.axis_index("gx"), 2)
        for k in [self.partner] + [k + 1 - 2 * core for k in self.others]:
            for h in range(2):
                self.arrived(i, k, h)
        for slot in range(spread_slots()):
            wait_for(self.part(i, 0, 0), self.send_sem.at[i, slot])
        self.place(i).wait()


def line_order(t, me, last):
    short = jnp.minimum(me, last - me)
    near = jnp.where(lax.rem(t, 2) == 0, me - t // 2, me + (t + 1) // 2)
    far = jnp.where(me < last - me, me + (t - short), me - (t - short))
    return jnp.where(t <= 2 * short, near, far)


class Chain:
    def __init__(self, own, full, sems):
        self.own, self.full, (self.local, self.send_sem, self.recv_sem) = own, full, sems

    def copy(self, b, way, first=False):
        me = lax.axis_index("gy")
        return pltpu.make_async_remote_copy(
            src_ref=self.own if first else self.full.at[b],
            dst_ref=self.full.at[b],
            send_sem=self.send_sem.at[b, way],
            recv_sem=self.recv_sem.at[b],
            device_id=(lax.axis_index("gx"), me - 1 + 2 * way),
            device_id_type=MESH,
        )

    def each(self, b, act, first=False):
        me, last = lax.axis_index("gy"), lax.axis_size("gy") - 1

        @pl.when(jnp.logical_and(b <= me, me < last))
        def _():
            act(self.copy(b, 1, first))

        @pl.when(jnp.logical_and(b >= me, me > 0))
        def _():
            act(self.copy(b, 0, first))

    def begin(self):
        me = lax.axis_index("gy")
        self.place = pltpu.make_async_copy(self.own, self.full.at[me], self.local)
        self.place.start()
        self.each(me, lambda copy: copy.start(), True)

    def relay(self, t):
        b = line_order(t, lax.axis_index("gy"), lax.axis_size("gy") - 1)
        wait_for(self.full.at[b], self.recv_sem.at[b])
        self.each(b, lambda copy: copy.start())

    def close(self):
        self.place.wait()
        for b in range(lax.axis_size("gy")):
            self.each(b, lambda copy: copy.wait_send())


class Exchange:
    def __init__(self, own, full, sems, apart=False):
        self.own, self.full, (self.local, self.send_sem, self.recv_sem) = own, full, sems
        self.apart = apart

    def begin(self):
        gx, me, size = lax.axis_index("gx"), lax.axis_index("gy"), lax.axis_size("gy")
        width = self.full.shape[2]

        def columns(k):
            if self.apart:
                return self.own.at[k]
            return self.own.at[:, pl.ds(pl.multiple_of(k * width, width), width)]

        self.place = pltpu.make_async_copy(columns(me), self.full.at[me], self.local)
        self.place.start()
        self.sent = []
        for d in range(1, size):
            target = lax.rem(me + d, size)
            copy = pltpu.make_async_remote_copy(
                src_ref=columns(target),
                dst_ref=self.full.at[me],
                send_sem=self.send_sem.at[d],
                recv_sem=self.recv_sem.at[me],
                device_id=(gx, target),
                device_id_type=MESH,
            )
            copy.start()
            self.sent.append(copy)

    def close(self):
        me, size = lax.axis_index("gy"), lax.axis_size("gy")
        self.place.wait()
        for copy in self.sent:
            copy.wait_send()
        for d in range(1, size):
            k = lax.rem(me + d, size)
            wait_for(self.full.at[k], self.recv_sem.at[k])


def chain_scratch():
    size = lax.axis_size("gy")
    return [
        pltpu.SemaphoreType.DMA,
        pltpu.SemaphoreType.DMA((size, 2)),
        pltpu.SemaphoreType.DMA((size,)),
    ]


def exchange_scratch():
    size = lax.axis_size("gy")
    return [
        pltpu.SemaphoreType.DMA,
        pltpu.SemaphoreType.DMA((size,)),
        pltpu.SemaphoreType.DMA((size,)),
    ]


def opening_kernel(*refs):
    ins, outs, sems = refs[:10], refs[10:22], refs[22:]
    resid, cot, small, qkv_a, o_a, qkv_b, o_b, wg, wu, wd = ins
    resid_out, cot_out, small_out = outs[:3]
    lines, (qkv, o, gate, up, down) = outs[3:7], outs[7:]
    me, size = lax.axis_index("gy"), lax.axis_size("gy")
    owns = (qkv_a, o_a, qkv_b, o_b, small)
    chains = [
        Chain(own, full, sems[3 * k : 3 * k + 3])
        for k, (own, full) in enumerate(zip(owns, list(lines) + [small_out]))
    ]
    swaps = [
        Exchange(own, full, sems[15 + 3 * k : 18 + 3 * k])
        for k, (own, full) in enumerate(((resid, resid_out), (cot, cot_out)))
    ]
    items = [(lines[0], qkv), (lines[1], o), (wg.at[0], gate), (wu.at[0], up), (wd.at[0], down)]
    spread = Spread(items, sems[21:24])
    greet([spread.partner] + spread.near, [lax.rem(me + d, size) for d in range(1, size)])
    for k in (0, 1, 4):
        chains[k].begin()
    spread.begin(2)
    for t in range(1, size):
        chains[0].relay(t)
        chains[1].relay(t)
    chains[0].close()
    spread.begin(0)
    chains[1].close()
    spread.begin(1)
    swaps[0].begin()
    for t in range(1, size):
        chains[4].relay(t)
    spread.begin(3)
    chains[2].begin()
    chains[3].begin()
    spread.relay(2)
    for t in range(1, size):
        chains[2].relay(t)
        chains[3].relay(t)
    spread.begin(4)
    swaps[1].begin()
    for i in (0, 1):
        spread.relay(i)
    spread.finish(2)
    spread.relay(3)
    for i in (0, 1):
        spread.finish(i)
    spread.relay(4)
    for i in (3, 4):
        spread.finish(i)
    for i in range(5):
        spread.close(i)
    for part in chains[2:] + swaps:
        part.close()


def opening(resid, cot, small, lines, wg, wu, wd):
    devices, size = lax.axis_size("gx"), lax.axis_size("gy")
    count = resid.shape[1] // size

    def shape(*dims, kind=bf16):
        return jax.ShapeDtypeStruct(dims, kind)

    blocks = shape(size, resid.shape[0], count)
    weight = shape(devices, *wg.shape[1:])
    out = [blocks, blocks, shape(size, *small.shape, kind=f32)]
    out += [shape(size, *line.shape) for line in lines]
    out += [shape(size, devices, *line.shape) for line in lines[:2]] + [weight] * 3
    return pl.pallas_call(
        opening_kernel,
        out_shape=out,
        in_specs=[ANY] * 10,
        out_specs=[ANY] * 12,
        scratch_shapes=chain_scratch() * 5 + exchange_scratch() * 2 + spread_scratch(5),
        compiler_params=pltpu.CompilerParams(collective_id=2, has_side_effects=True),
        name="opening",
    )(resid, cot, small, *lines, wg, wu, wd)


FF_CHUNK = 512
PIECES = 4


def spans(total):
    return [(start, min(FF_CHUNK, total - start)) for start in range(0, total, FF_CHUNK)]


def nn(left, right):
    return lax.dot_general(left, right, (((1,), (0,)), ((), ())), preferred_element_type=f32)


def nt(left, right):
    return lax.dot_general(left, right, (((1,), (1,)), ((), ())), preferred_element_type=f32)


def line_pass(own_ref, own, gathered, part, outb, inb, sems, load, finish, peers=(), plan={}):
    own_sem, ag_send, ag_recv, rs_send, rs_recv = sems
    gx, me, size = lax.axis_index("gx"), lax.axis_index("gy"), lax.axis_size("gy")
    rows = own.shape[0]
    piece = rows // PIECES
    last = size - 1
    inner = jnp.logical_and(me > 0, me < last)

    first = pltpu.make_async_copy(own_ref, gathered.at[me], own_sem)
    first.start()
    barrier = pltpu.get_barrier_semaphore()

    @pl.when(me > 0)
    def _():
        pl.semaphore_signal(barrier, inc=1, device_id=(gx, me - 1), device_id_type=MESH)

    @pl.when(me < last)
    def _():
        pl.semaphore_signal(barrier, inc=1, device_id=(gx, me + 1), device_id_type=MESH)

    for peer in peers:
        pl.semaphore_signal(barrier, inc=1, device_id=(peer, me), device_id_type=MESH)
    pl.semaphore_wait(barrier, jnp.where(inner, 2, 1) + len(peers))
    first.wait()

    def planned(name, t):
        for (key, when), act in plan.items():
            if key == name:
                pl.when(t == when)(act)


    def gather_copy(b, s, way):
        here = gathered.at[b, pl.ds(s * piece, piece)]
        return pltpu.make_async_remote_copy(
            src_ref=here,
            dst_ref=here,
            send_sem=ag_send.at[b, way, s],
            recv_sem=ag_recv.at[b, s],
            device_id=(gx, me - 1 + 2 * way),
            device_id_type=MESH,
        )

    def sum_copy(b, s):
        towards = jnp.where(b > me, me + 1, me - 1)
        slot = jnp.where(jnp.logical_and(towards == b, me > b), size, b)
        return pltpu.make_async_remote_copy(
            src_ref=outb.at[b, pl.ds(s * piece, piece)],
            dst_ref=inb.at[slot, pl.ds(s * piece, piece)],
            send_sem=rs_send.at[b, s],
            recv_sem=rs_recv.at[slot, s],
            device_id=(gx, towards),
            device_id_type=MESH,
        )

    def sum_arrived(slot, s):
        here = inb.at[slot, pl.ds(s * piece, piece)]
        pltpu.make_async_copy(here, here, rs_recv.at[slot, s]).wait()

    def step(t, carry):
        b = line_order(t, me, last)
        for s in range(PIECES):

            @pl.when(t > 0)
            def _():
                gather_copy(b, s, 0).wait_recv()

            @pl.when(jnp.logical_and(b <= me, me < last))
            def _():
                gather_copy(b, s, 1).start()

            @pl.when(jnp.logical_and(b >= me, me > 0))
            def _():
                gather_copy(b, s, 0).start()

        @pl.when(t == 0)
        def _():
            load()

        planned("step", t)
        finish(b)

        @pl.when(b == me)
        def _():
            own[...] = part[...]

        @pl.when(b != me)
        def _():
            outb[b] = part[...].astype(bf16)

            @pl.when(jnp.logical_not(inner))
            def _():
                for s in range(PIECES):
                    sum_copy(b, s).start()

        return carry

    lax.fori_loop(0, size, step, 0)

    def relay(t, carry):
        above, below = last - me, me
        low = jnp.where(t < above, me + 1 + t, me - 1 - (t - above))
        high = jnp.where(t < below, me - 1 - t, me + 1 + (t - below))
        b = jnp.where(2 * me < size, low, high)
        planned("hop", t)

        @pl.when(inner)
        def _():
            for s in range(PIECES):
                at = pl.ds(s * piece, piece)
                sum_arrived(b, s)
                outb[b, at] = (outb[b, at].astype(f32) + inb[b, at].astype(f32)).astype(bf16)
                sum_copy(b, s).start()

        return carry

    lax.fori_loop(0, last, relay, 0)

    @pl.when(me > 0)
    def _():
        for s in range(PIECES):
            sum_arrived(me, s)
        own[...] += inb[me].astype(f32)

    @pl.when(me < last)
    def _():
        for s in range(PIECES):
            sum_arrived(size, s)
        own[...] += inb[size].astype(f32)

    def drain(b, carry):
        for s in range(PIECES):

            @pl.when(jnp.logical_and(b <= me, me < last))
            def _():
                gather_copy(b, s, 1).wait_send()

            @pl.when(jnp.logical_and(b >= me, me > 0))
            def _():
                gather_copy(b, s, 0).wait_send()

            @pl.when(b != me)
            def _():
                sum_copy(b, s).wait_send()

        return carry

    lax.fori_loop(0, size, drain, 0)


def line_scratch(size, rows, width):
    return [
        pltpu.VMEM((size, rows, width), bf16),
        pltpu.VMEM((rows, width), f32),
        pltpu.VMEM((size, rows, width), bf16),
        pltpu.VMEM((size + 1, rows, width), bf16),
        pltpu.SemaphoreType.DMA,
        pltpu.SemaphoreType.DMA((size, 2, PIECES)),
        pltpu.SemaphoreType.DMA((size, PIECES)),
        pltpu.SemaphoreType.DMA((size, PIECES)),
        pltpu.SemaphoreType.DMA((size + 1, PIECES)),
    ]


LINE = 9


ORDER = {
    ("step", 0): (("begin", 0), ("begin", 1)),
    ("step", 2): (("begin", 2),),
    ("hop", 0): (("relay", 0), ("relay", 1), ("relay", 2), ("begin", 3)),
    ("hop", 1): (("finish", 0), ("finish", 1), ("finish", 2), ("begin", 4)),
}
REST = (("relay", 3), ("relay", 4), ("finish", 3), ("finish", 4))


def schedule(spread):
    def run(steps):
        def act():
            for verb, i in steps:
                getattr(spread, verb)(i)

        return act

    plan = {key: run(steps) for key, steps in ORDER.items()}
    return plan, REST + tuple(("close", i) for i in range(len(spread.items)))


def forward_kernel(extra, *refs):
    acts_ref, wg_ref, wu_ref, wd_ref = refs[:4]
    shards, refs = refs[4 : 4 + extra], refs[4 + extra :]
    sum_ref, turned_ref, gate_ref, up_ref, hidden_ref = refs[:5]
    wholes, scratch = refs[5 : 5 + extra], refs[5 + extra :]
    gathered, part, outb, inb = scratch[:4]
    sems = scratch[4:LINE]
    wg, wu, wd, gate, up, hidden, turned, w_sem, out_sem = scratch[LINE : LINE + 9]
    peers, spread = [], None
    if extra:
        items = [(r if len(w.shape) == 4 else r.at[1], w) for r, w in zip(shards, wholes)]
        spread = Spread(items, scratch[LINE + 9 :])
        partner, others = places()
        peers = [partner] + (list(square()[:2]) if spread.four else others)

    plan, rest = schedule(spread) if extra else ({}, ())
    loads = [
        pltpu.make_async_copy(src, dst, w_sem.at[k])
        for k, (src, dst) in enumerate(((wg_ref, wg), (wu_ref, wu), (wd_ref, wd)))
    ]
    for copy in loads:
        copy.start()

    def load():
        for copy in loads:
            copy.wait()

    def results(b):
        pairs = ((gate, gate_ref), (up, up_ref), (hidden, hidden_ref))
        return [
            pltpu.make_async_copy(src.at[b], dst.at[b], out_sem.at[b, k])
            for k, (src, dst) in enumerate(pairs)
        ]

    def finish(b):
        block = gathered[b]
        store_turned(block, turned, b)
        for start, width in spans(wg.shape[1]):
            at = slice(start, start + width)
            g = nn(block, wg[:, at])
            u = nn(block, wu[:, at])
            h = (g * lax.logistic(g) * u).astype(bf16)
            gate[b, :, at] = g.astype(bf16)
            up[b, :, at] = u.astype(bf16)
            hidden[b, :, at] = h
            p = nt(h, wd[:, at])
            if start == 0:
                part[...] = p
            else:
                part[...] += p
        for copy in results(b):
            copy.start()

    line_pass(
        acts_ref, sum_ref, gathered, part, outb, inb, sems, load, finish, peers, plan
    )
    keep = pltpu.make_async_copy(turned, turned_ref, w_sem.at[0])
    keep.start()
    for act, i in rest:
        getattr(spread, act)(i)

    def settle(b, carry):
        for copy in results(b):
            copy.wait()
        return carry

    lax.fori_loop(0, gathered.shape[0], settle, 0)
    keep.wait()


def forward_ffn(acts, wg, wu, wd, shards=()):
    rows, width = acts.shape
    devices, size, hidden = lax.axis_size("gx"), lax.axis_size("gy"), wg.shape[1]
    wide = jax.ShapeDtypeStruct((size, rows, hidden), bf16)
    extra = len(shards)
    wholes = [
        jax.ShapeDtypeStruct(
            (size, devices) + s.shape[1:] if k < 2 else (devices,) + s.shape[1:], bf16
        )
        for k, s in enumerate(shards)
    ]
    return pl.pallas_call(
        functools.partial(forward_kernel, extra),
        out_shape=[
            jax.ShapeDtypeStruct((rows, width), f32),
            jax.ShapeDtypeStruct((2, width // 2, size * rows), bf16),
            wide,
            wide,
            wide,
        ]
        + wholes,
        in_specs=[ANY] * (4 + extra),
        out_specs=[pl.BlockSpec(memory_space=pltpu.VMEM)] + [ANY] * (4 + extra),
        scratch_shapes=line_scratch(size, rows, width)
        + [pltpu.VMEM((width, hidden), bf16)] * 3
        + [pltpu.VMEM((size, rows, hidden), bf16)] * 3
        + [pltpu.VMEM((2, width // 2, size * rows), bf16)]
        + [pltpu.SemaphoreType.DMA((3,)), pltpu.SemaphoreType.DMA((size, 3))]
        + (spread_scratch(extra) if extra else []),
        compiler_params=pltpu.CompilerParams(
            collective_id=3 if extra else 0, has_side_effects=True, vmem_limit_bytes=VMEM_LIMIT
        ),
        cost_estimate=pl.CostEstimate(
            flops=6 * size * rows * width * hidden, bytes_accessed=40 << 20, transcendentals=0
        ),
        name="ffn_forward",
    )(acts, wg, wu, wd, *shards)


class Reduce:
    def __init__(self, lhs, rhs, bufs, abuf, fbuf, ftail, a_all, r_all, c_all, outs, sems):
        self.lhs, self.rhs, self.bufs, self.outs = lhs, rhs, bufs, outs
        self.abuf, self.fbuf, self.ftail = abuf, fbuf, ftail
        self.a_all, self.r_all, self.c_all = a_all, r_all, c_all
        (
            self.a_send,
            self.a_recv,
            self.r_send,
            self.r_recv,
            self.c_send,
            self.c_recv,
            self.local,
        ) = sems
        gx, self.gy = lax.axis_index("gx"), lax.axis_index("gy")
        self.chip, self.core = gx // 2, lax.rem(gx, 2)
        self.chips = lax.axis_size("gx") // 2
        self.half, self.wide = bufs[0].shape[0] // 2, bufs[0].shape[1]
        self.r = self.half // self.chips
        self.four = self.chips == 4
        self.partner, self.others = places()
        self.near = list(square()[:2]) if self.four else self.others

    def product(self, m, which, at):
        z, n, _ = self.rhs[m].shape
        right = self.rhs[m][:, :, at].reshape(z * n, at.stop - at.start)
        return nn(self.lhs[which], right)

    def remote(self, src, dst, send, recv, target):
        return pltpu.make_async_remote_copy(
            src_ref=src,
            dst_ref=dst,
            send_sem=send,
            recv_sem=recv,
            device_id=(target, self.gy),
            device_id_type=MESH,
        )

    def columns(self):
        return [(j, slice(s, s + w)) for j, (s, w) in enumerate(spans(self.wide))]

    def swap(self, m, j, at):
        here = (slice(0, self.half), at)
        return self.remote(
            self.bufs[m].at[here],
            self.a_all.at[m, :, at],
            self.a_send.at[m, j],
            self.a_recv.at[m, j],
            self.partner,
        )

    def block(self, m, device, start=0, size=None):
        size = self.r if size is None else size
        first = self.half + (device // 2) * self.r + start
        return self.bufs[m].at[pl.ds(pl.multiple_of(first, 16), size)]

    def first(self, m):
        for j, at in self.columns():
            self.bufs[m][: self.half, at] = self.product(m, 1 - self.core, at).astype(bf16)
            self.swap(m, j, at).start()

    def corner(self, m, h):
        side, along, across = square()
        half = self.r // 2
        return self.remote(
            self.block(m, across, h * half, half),
            self.r_all.at[m, h],
            self.r_send.at[m, h],
            self.r_recv.at[m, h],
            along if h else side,
        )

    def second(self, m):
        for j, at in self.columns():
            self.swap(m, j, at).wait_recv()
            landed = self.abuf.at[:, at]
            fetch = pltpu.make_async_copy(self.a_all.at[m, :, at], landed, self.local.at[0])
            fetch.start()
            mine = self.product(m, self.core, at)
            fetch.wait()
            self.bufs[m][self.half :, at] = (mine + landed[...].astype(f32)).astype(bf16)
        if self.four:
            for h in range(2):
                self.corner(m, h).start()

    def hand(self, m, k):
        target = self.near[k]
        return self.remote(
            self.block(m, target),
            self.c_all.at[m, k],
            self.c_send.at[m, k],
            self.c_recv.at[m, k],
            target,
        )

    def third(self, m):
        if self.four:
            side, along, _ = square()
            half = self.r // 2
            for h, device in ((0, along), (1, side)):
                self.corner(m, h).wait_recv()
                here = self.block(m, device, h * half, half)
                landed = self.abuf.at[h * half : (h + 1) * half]
                fetch = pltpu.make_async_copy(self.r_all.at[m, h], landed, self.local.at[0])
                fetch.start()
                fetch.wait()
                here[...] = (here[...].astype(f32) + landed[...].astype(f32)).astype(bf16)
        for k in range(len(self.near)):
            self.hand(m, k).start()

    def fourth(self, m):
        for j, at in self.columns():
            self.swap(m, j, at).wait_send()
        fetches = []
        for k in range(len(self.near)):
            self.hand(m, k).wait_recv()
            here = self.bufs[m].at[pl.ds(k * self.r, self.r)]
            fetch = pltpu.make_async_copy(self.c_all.at[m, k], here, self.local.at[k])
            fetch.start()
            fetches.append(fetch)
        for fetch in fetches:
            fetch.wait()
        first = pl.multiple_of(self.half + self.chip * self.r, 16)
        for _, at in self.columns():
            total = self.bufs[m][pl.ds(first, self.r), at].astype(f32)
            for k in range(len(self.near)):
                total = total + self.bufs[m][k * self.r : (k + 1) * self.r, at].astype(f32)
            stage = self.fbuf if total.shape[1] == FF_CHUNK else self.ftail
            stage[...] = total
            store = pltpu.make_async_copy(stage, self.outs[m].at[:, at], self.local.at[0])
            store.start()
            store.wait()

    def drain(self, m):
        if self.four:
            for h in range(2):
                self.corner(m, h).wait_send()
        for k in range(len(self.near)):
            self.hand(m, k).wait_send()


def reduce_scratch(width, hidden, count=3):
    devices = lax.axis_size("gx")
    rows, parts = width // devices, len(spans(hidden))
    near = 2 if devices == 8 else devices // 2 - 1
    dma = pltpu.SemaphoreType.DMA
    return [
        pltpu.VMEM((width // 2, hidden), bf16),
        pltpu.VMEM((rows, FF_CHUNK), f32),
        pltpu.VMEM((rows, hidden % FF_CHUNK), f32),
        dma((count, parts)),
        dma((count, parts)),
        dma((count, 2)),
        dma((count, 2)),
        dma((count, near)),
        dma((count, near)),
        dma((near,)),
    ]


def store_turned(block, turned, b):
    count, width = block.shape
    _, chips_rows, _ = turned.shape
    devices = lax.axis_size("gx")
    r = width // devices
    flipped = block.T
    at = pl.ds(pl.multiple_of(b * count, count), count)
    for k in range(devices):
        q = k // 2
        turned[k % 2, q * r : (q + 1) * r, at] = flipped[k * r : (k + 1) * r]


AFTER = (
    ("hop", 0, "first", 0),
    ("hop", 1, "second", 0),
    ("hop", 1, "first", 1),
    ("hop", 2, "third", 0),
    ("hop", 2, "second", 1),
)


def backward_kernel(
    grad_ref, gate_ref, up_ref, hidden_ref, turned_ref, wg_ref, wu_ref, wd_ref, *refs
):
    sum_ref, og, ou, od, a_all, r_all, c_all = refs[:7]
    scratch = refs[7:]
    gathered, part, outb, inb = scratch[:4]
    sems = scratch[4:LINE]
    wg, wu, wd, gate, up, hidden, turned, w_sem = scratch[LINE : LINE + 8]
    abuf, fbuf, ftail = scratch[LINE + 8 : LINE + 11]
    operands = (
        (wd_ref, wd),
        (gate_ref, gate),
        (up_ref, up),
        (wg_ref, wg),
        (wu_ref, wu),
        (hidden_ref, hidden),
    )
    loads = [
        pltpu.make_async_copy(src, dst, w_sem.at[k]) for k, (src, dst) in enumerate(operands)
    ]
    for copy in loads:
        copy.start()

    def load():
        for copy in loads:
            copy.wait()

    reduce = Reduce(
        turned,
        (hidden, gate, up),
        (wd, wg, wu),
        abuf,
        fbuf,
        ftail,
        a_all,
        r_all,
        c_all,
        (od, og, ou),
        scratch[LINE + 11 :],
    )

    def finish(b):
        block = gathered[b]
        store_turned(block, turned, b)
        for start, width in spans(wg.shape[1]):
            at = slice(start, start + width)
            d = nn(block, wd[:, at])
            g = gate[b, :, at].astype(f32)
            u = up[b, :, at].astype(f32)
            sigma = lax.logistic(g)
            ds = d * sigma
            dg = (ds * u * (1.0 + g * (1.0 - sigma))).astype(bf16)
            du = (ds * g).astype(bf16)
            gate[b, :, at] = dg
            up[b, :, at] = du
            p = nt(dg, wg[:, at]) + nt(du, wu[:, at])
            if start == 0:
                part[...] = p
            else:
                part[...] += p

    def swap_operand():
        copy = pltpu.make_async_copy(turned_ref, turned, w_sem.at[0])
        copy.start()
        copy.wait()

    def work(when):
        def act():
            for name, t, verb, m in AFTER:
                if t == when:
                    getattr(reduce, verb)(m)
                    if verb == "second" and m == 0:
                        swap_operand()

        return act

    peers = [reduce.partner] + reduce.near
    plan = {("hop", t): work(t) for t in range(3)}
    line_pass(grad_ref, sum_ref, gathered, part, outb, inb, sems, load, finish, peers, plan)
    reduce.first(2)
    reduce.third(1)
    reduce.second(2)
    reduce.fourth(0)
    reduce.third(2)
    reduce.fourth(1)
    reduce.fourth(2)
    for m in range(3):
        reduce.drain(m)


def backward_ffn(grad, gate, up, hidden, turned, wg, wu, wd):
    rows, width = grad.shape
    devices, size, wide = lax.axis_size("gx"), lax.axis_size("gy"), wg.shape[1]
    near = 2 if devices == 8 else devices // 2 - 1
    mine = jax.ShapeDtypeStruct((width // devices, wide), f32)
    return pl.pallas_call(
        backward_kernel,
        out_shape=[
            jax.ShapeDtypeStruct((rows, width), f32),
            mine,
            mine,
            mine,
            jax.ShapeDtypeStruct((3, width // 2, wide), bf16),
            jax.ShapeDtypeStruct((3, 2, width // devices // 2, wide), bf16),
            jax.ShapeDtypeStruct((3, near, width // devices, wide), bf16),
        ],
        in_specs=[ANY] * 8,
        out_specs=[pl.BlockSpec(memory_space=pltpu.VMEM)] + [ANY] * 6,
        scratch_shapes=line_scratch(size, rows, width)
        + [pltpu.VMEM((width, wide), bf16)] * 3
        + [pltpu.VMEM((size, rows, wide), bf16)] * 3
        + [pltpu.VMEM((2, width // 2, size * rows), bf16), pltpu.SemaphoreType.DMA((6,))]
        + reduce_scratch(width, wide),
        compiler_params=pltpu.CompilerParams(
            collective_id=1, has_side_effects=True, vmem_limit_bytes=VMEM_LIMIT
        ),
        cost_estimate=pl.CostEstimate(
            flops=12 * size * rows * width * wide, bytes_accessed=40 << 20, transcendentals=0
        ),
        name="ffn_backward",
    )(grad, gate, up, hidden, turned, wg, wu, wd)


class Fold:
    def __init__(self, lhs, rhs, bufs, sems):
        self.lhs, self.rhs = lhs, rhs
        self.up, self.low, self.a_in, self.r_in, self.c_in, self.z_out, self.z_in = bufs
        (
            self.a_send,
            self.a_recv,
            self.r_send,
            self.r_recv,
            self.c_send,
            self.c_recv,
            self.z_send,
            self.z_recv,
        ) = sems
        self.gx, self.gy = lax.axis_index("gx"), lax.axis_index("gy")
        self.core, self.size = lax.rem(self.gx, 2), lax.axis_size("gy")
        self.chips = lax.axis_size("gx") // 2
        self.r = self.low.shape[2] // self.chips
        self.four = self.chips == 4
        self.partner, self.others = places()
        self.near = list(square()[:2]) if self.four else self.others

    def product(self, m, which, z):
        return [nn(left[which], right[z]) for left, right in zip(self.lhs[m], self.rhs[m])]

    def remote(self, src, dst, send, recv, gx, gy):
        return pltpu.make_async_remote_copy(
            src_ref=src,
            dst_ref=dst,
            send_sem=send,
            recv_sem=recv,
            device_id=(gx, gy),
            device_id_type=MESH,
        )

    def block(self, m, device, start=0, size=None):
        size = self.r if size is None else size
        first = (device // 2) * self.r + start
        return self.low.at[m, :, pl.ds(pl.multiple_of(first, 16), size)]

    def swap(self, m, z):
        return self.remote(
            self.up.at[m, z],
            self.a_in.at[m, z],
            self.a_send.at[m, z],
            self.a_recv.at[m, z],
            self.partner,
            self.gy,
        )

    def first(self, m):
        for z in range(self.size):
            left, right = self.product(m, 1 - self.core, z)
            edge = left.shape[1]
            self.up[m, z, :, :edge] = left.astype(bf16)
            self.up[m, z, :, edge:] = right.astype(bf16)
            self.swap(m, z).start()

    def corner(self, m, h):
        side, along, across = square()
        half = self.r // 2
        return self.remote(
            self.block(m, across, h * half, half),
            self.r_in.at[m, h],
            self.r_send.at[m, h],
            self.r_recv.at[m, h],
            along if h else side,
            self.gy,
        )

    def second(self, m):
        for z in range(self.size):
            left, right = self.product(m, self.core, z)
            edge = left.shape[1]
            self.swap(m, z).wait_recv()
            came = self.a_in[m, z].astype(f32)
            self.low[m, z, :, :edge] = (left + came[:, :edge]).astype(bf16)
            self.low[m, z, :, edge:] = (right + came[:, edge:]).astype(bf16)
        if self.four:
            for h in range(2):
                self.corner(m, h).start()

    def hand(self, m, k):
        return self.remote(
            self.block(m, self.near[k]),
            self.c_in.at[m, k],
            self.c_send.at[m, k],
            self.c_recv.at[m, k],
            self.near[k],
            self.gy,
        )

    def third(self, m):
        if self.four:
            side, along, _ = square()
            half = self.r // 2
            for h, device in ((0, along), (1, side)):
                self.corner(m, h).wait_recv()
                here = self.block(m, device, h * half, half)
                here[...] = (here[...].astype(f32) + self.r_in[m, h].astype(f32)).astype(bf16)
        for k in range(len(self.near)):
            self.hand(m, k).start()

    def down_line(self, m, d):
        target = lax.rem(self.gy + d, self.size)
        return self.remote(
            self.z_out.at[m, target],
            self.z_in.at[m, self.gy],
            self.z_send.at[m, d],
            self.z_recv.at[m, self.gy],
            self.gx,
            target,
        )

    def fourth(self, m):
        for k in range(len(self.near)):
            self.hand(m, k).wait_recv()
        mine = self.block(m, self.gx)
        for z in range(self.size):
            total = mine[z].astype(f32)
            for k in range(len(self.near)):
                total = total + self.c_in[m, k, z].astype(f32)
            self.z_out[m, z] = total.astype(bf16)
        for d in range(1, self.size):
            self.down_line(m, d).start()

    def fifth(self, m, out):
        total = self.z_out[m, self.gy].astype(f32)
        for d in range(1, self.size):
            z = lax.rem(self.gy + d, self.size)
            wait_for(self.z_in.at[m, z], self.z_recv.at[m, z])
            total = total + self.z_in[m, z].astype(f32)
        out[m] = total

    def drain(self, m):
        for z in range(self.size):
            self.swap(m, z).wait_send()
        if self.four:
            for h in range(2):
                self.corner(m, h).wait_send()
        for k in range(len(self.near)):
            self.hand(m, k).wait_send()
        for d in range(1, self.size):
            self.down_line(m, d).wait_send()


class Total:
    def __init__(self, own, line_in, pair, pair_in, chip_in, sems):
        self.own, self.line_in, self.pair = own, line_in, pair
        self.pair_in, self.chip_in = pair_in, chip_in
        self.l_send, self.l_recv, self.p_send, self.p_recv, self.g_send, self.g_recv = sems
        self.gx, self.gy = lax.axis_index("gx"), lax.axis_index("gy")
        self.size, self.chips = lax.axis_size("gy"), lax.axis_size("gx") // 2
        self.partner, self.others = places()

    def remote(self, src, dst, send, recv, gx, gy):
        return pltpu.make_async_remote_copy(
            src_ref=src,
            dst_ref=dst,
            send_sem=send,
            recv_sem=recv,
            device_id=(gx, gy),
            device_id_type=MESH,
        )

    def line(self, d):
        target = lax.rem(self.gy + d, self.size)
        return self.remote(
            self.own.at[target],
            self.line_in.at[self.gy],
            self.l_send.at[d],
            self.l_recv.at[self.gy],
            self.gx,
            target,
        )

    def across(self):
        return self.remote(
            self.pair.at[0], self.pair_in, self.p_send, self.p_recv, self.partner, self.gy
        )

    def chip(self, k):
        return self.remote(
            self.pair.at[1],
            self.chip_in.at[self.gx // 2],
            self.g_send.at[k],
            self.g_recv.at[self.gx // 2],
            self.others[k],
            self.gy,
        )

    def begin(self):
        for d in range(1, self.size):
            self.line(d).start()

    def middle(self):
        total = self.own[self.gy]
        for d in range(1, self.size):
            z = lax.rem(self.gy + d, self.size)
            wait_for(self.line_in.at[z], self.l_recv.at[z])
            total = total + self.line_in[z]
        self.pair[0] = total
        self.across().start()

    def later(self):
        self.across().wait_recv()
        self.pair[1] = self.pair[0] + self.pair_in[...]
        self.chip_in[self.gx // 2] = self.pair[1]
        for k in range(self.chips - 1):
            self.chip(k).start()

    def close(self, out):
        for k in range(self.chips - 1):
            q = self.others[k] // 2
            wait_for(self.chip_in.at[q], self.g_recv.at[q])
        total = self.chip_in[0]
        for q in range(1, self.chips):
            total = total + self.chip_in[q]
        out[...] = total
        for d in range(1, self.size):
            self.line(d).wait_send()
        self.across().wait_send()
        for k in range(self.chips - 1):
            self.chip(k).wait_send()


def closing_kernel(layers, *refs):
    operands, refs = refs[: 4 * layers], refs[4 * layers :]
    small, out_rows, grad_rows = refs[:3]
    grads, small_out, out_blocks, grad_blocks = refs[3:7]
    scratch = refs[7:]
    lhs = [operands[4 * m : 4 * m + 2] for m in range(layers)]
    rhs = [operands[4 * m + 2 : 4 * m + 4] for m in range(layers)]
    fold = Fold(lhs, rhs, scratch[:7], scratch[7:15])
    total = Total(small, *scratch[15:19], scratch[19:25])
    swaps = [
        Exchange(own, full, scratch[25 + 3 * k : 28 + 3 * k], True)
        for k, (own, full) in enumerate(((grad_rows, grad_blocks), (out_rows, out_blocks)))
    ]
    me, size = lax.axis_index("gy"), lax.axis_size("gy")
    greet([fold.partner] + fold.others, [lax.rem(me + d, size) for d in range(1, size)])
    total.begin()
    for m in range(layers):
        fold.first(m)
    for swap in swaps:
        swap.begin()
    fold.second(0)
    total.middle()
    for m in range(1, layers):
        fold.second(m)
    total.later()
    for m in range(layers):
        fold.third(m)
    for m in range(layers):
        fold.fourth(m)
    total.close(small_out)
    for m in range(layers):
        fold.fifth(m, grads)
    for m in range(layers):
        fold.drain(m)
    for swap in swaps:
        swap.close()


def closing(operands, small, out_rows, grad_rows):
    layers = len(operands) // 4
    devices, size = lax.axis_size("gx"), lax.axis_size("gy")
    half = operands[0].shape[1]
    chips = devices // 2
    r, near = half // chips, 2 if chips == 4 else chips - 1
    c = operands[2].shape[2] + operands[3].shape[2]
    vmem, dma = pltpu.VMEM, pltpu.SemaphoreType.DMA
    row = small.shape[1:]
    local = pl.BlockSpec(memory_space=pltpu.VMEM)
    blocks = jax.ShapeDtypeStruct(out_rows.shape, bf16)
    return pl.pallas_call(
        functools.partial(closing_kernel, layers),
        out_shape=[
            jax.ShapeDtypeStruct((layers, r, c), f32),
            jax.ShapeDtypeStruct(row, f32),
            blocks,
            blocks,
        ],
        in_specs=[local] * (len(operands) + 1) + [ANY] * 2,
        out_specs=[local] * 2 + [ANY] * 2,
        scratch_shapes=[
            vmem((layers, size, half, c), bf16),
            vmem((layers, size, half, c), bf16),
            vmem((layers, size, half, c), bf16),
            vmem((layers, 2, size, r // 2, c), bf16),
            vmem((layers, near, size, r, c), bf16),
            vmem((layers, size, r, c), bf16),
            vmem((layers, size, r, c), bf16),
            dma((layers, size)),
            dma((layers, size)),
            dma((layers, 2)),
            dma((layers, 2)),
            dma((layers, near)),
            dma((layers, near)),
            dma((layers, size)),
            dma((layers, size)),
            vmem((size,) + row, f32),
            vmem((2,) + row, f32),
            vmem(row, f32),
            vmem((chips,) + row, f32),
            dma((size,)),
            dma((size,)),
            dma,
            dma,
            dma((chips,)),
            dma((chips,)),
        ]
        + exchange_scratch() * 2,
        compiler_params=pltpu.CompilerParams(
            collective_id=4, has_side_effects=True, vmem_limit_bytes=VMEM_LIMIT
        ),
        name="closing",
    )(*operands, small, out_rows, grad_rows)


def on_device(
    residual_in,
    w_query,
    w_key,
    w_value,
    b_query,
    b_key,
    b_value,
    w_output,
    gain_attn,
    gain_ffn,
    w_gate,
    w_up,
    w_down,
    cotangent,
):
    devices_y = lax.axis_size("gy")
    rows_tok = residual_in.shape[1]
    count = rows_tok // devices_y
    q_index = lax.axis_index("gy") * count + jnp.arange(count, dtype=jnp.int32)
    k_index = jnp.arange(rows_tok, dtype=jnp.int32)
    allowed = (q_index[:, None] // LEN == k_index[None, :] // LEN) & (
        k_index[None, :] <= q_index[:, None]
    )
    cosine, sine = rope_tables(q_index % LEN, HEAD_DIM)

    small = jnp.concatenate([gain_attn, gain_ffn, b_query, b_key, b_value], axis=1)
    small_sizes = [v.shape[1] for v in (gain_attn, gain_ffn, b_query, b_key, b_value)]
    small = jnp.pad(small.astype(f32), ((0, 8 - LAYERS), (0, 0)))
    lines = []
    for l in range(LAYERS):
        lines += [jnp.concatenate([w_query[l], w_key[l], w_value[l]], axis=1), w_output[l]]
    part_sizes = (w_query.shape[2], w_key.shape[2], w_value.shape[2])
    opened = opening(residual_in, cotangent, small, lines, w_gate, w_up, w_down)
    resid, cot, small = opened[:3]
    lines_next = opened[5:7]
    attn_full = [[w.reshape(devices_y, D, -1) for w in opened[7:9]], None]
    ffn_full = [[w.reshape(D, -1) for w in opened[9:]], None]
    small = small[:, :LAYERS].transpose(1, 0, 2)
    vectors, start = [], 0
    for size in small_sizes:
        vectors.append(small[:, :, start : start + size].reshape(LAYERS, -1))
        start += size
    gains_one, gains_two, bias_q, bias_k, bias_v = vectors

    resid = resid.reshape(D, count).astype(f32).T
    cot = cot.reshape(D, count)

    kept = []
    for l in range(LAYERS):
        w_qkv, w_out = attn_full[l]
        wg, wu, wd = ffn_full[l]
        normed_one, scale_one = rms_parts(resid)
        acts_one = (normed_one * gains_one[l]).astype(bf16)
        queries, keys, values = split_columns(
            jnp.stack([dot("td,dq->tq", acts_one, w_qkv[z]) for z in range(devices_y)], axis=1),
            part_sizes,
        )
        queries = queries + bias_q[l]
        keys = keys + bias_k[l]
        values = (values + bias_v[l]).astype(bf16)
        q_rot = rotate(queries.reshape(count, HEADS, HEAD_DIM), cosine, sine).astype(bf16)
        q_rot = q_rot.reshape(count, KV_HEADS, GROUP, HEAD_DIM)
        k_rot = rotate(keys.reshape(count, KV_HEADS, HEAD_DIM), cosine, sine).astype(bf16)
        both = jnp.concatenate([k_rot.reshape(count, -1), values], axis=1)
        both = lax.all_gather(both, "gy", axis=0, tiled=True)
        half = both.shape[1] // 2
        k_rot = both[:, :half].reshape(rows_tok, KV_HEADS, HEAD_DIM)
        v_heads = both[:, half:].reshape(rows_tok, KV_HEADS, HEAD_DIM)
        scores = score_block(q_rot, k_rot, allowed)
        top = jnp.max(scores, axis=-1, keepdims=True)
        expo = jnp.exp(scores - top)
        total = jnp.sum(expo, axis=-1, keepdims=True)
        soft = (expo / total).astype(bf16)
        log_total = top + jnp.log(total)
        mixed = dot("kgqs,skd->qkgd", soft, v_heads).reshape(count, -1).astype(bf16)
        mixed = mixed.reshape(count, devices_y, -1)
        middle = resid
        for z in range(devices_y):
            middle = middle + dot("tq,dq->td", mixed[:, z], w_out[z])
        normed_two, scale_two = rms_parts(middle)
        acts_two = (normed_two * gains_two[l]).astype(bf16)
        if l == 0:
            shards = (*lines_next, w_gate, w_up, w_down)
            done = forward_ffn(acts_two, wg, wu, wd, shards)
            attn_full[1] = [w.reshape(devices_y, D, -1) for w in done[5:7]]
            ffn_full[1] = [w.reshape(D, -1) for w in done[7:]]
        else:
            done = forward_ffn(acts_two, wg, wu, wd)
        part, acts_two, gate, up, hidden = done[:5]
        kept.append(
            (
                normed_one,
                scale_one,
                acts_one,
                q_rot,
                k_rot,
                v_heads,
                log_total,
                mixed,
                normed_two,
                scale_two,
                acts_two,
                gate,
                up,
                hidden,
            )
        )
        resid = middle + part

    grad = cot.astype(f32).T + 2.0 * penalty * resid
    attn_grads = [None] * LAYERS
    ffn_grads = [None] * LAYERS
    small_grads = [None] * LAYERS

    for l in reversed(range(LAYERS)):
        (
            normed_one,
            scale_one,
            acts_one,
            q_rot,
            k_rot,
            v_heads,
            log_total,
            mixed,
            normed_two,
            scale_two,
            acts_two,
            gate,
            up,
            hidden,
        ) = kept[l]
        w_qkv, w_out = attn_full[l]
        wg, wu, wd = ffn_full[l]
        done = backward_ffn(grad.astype(bf16), gate, up, hidden, acts_two, wg, wu, wd)
        grad_acts_two, ffn_grads[l] = done[0], done[1:4]
        grad_norm, grad_gain_two = norm_backward(
            grad_acts_two, normed_two, scale_two, gains_two[l]
        )
        grad_mid = grad + grad_norm
        grad_branch = grad_mid.astype(bf16)
        grad_mixed = jnp.concatenate(
            [dot("td,dq->tq", grad_branch, w_out[z]) for z in range(devices_y)], axis=1
        ).astype(bf16)
        grad_heads = grad_mixed.reshape(count, KV_HEADS, GROUP, HEAD_DIM)
        scores = score_block(q_rot, k_rot, allowed)
        soft_full = jnp.exp(scores - log_total)
        soft = soft_full.astype(bf16)
        grad_soft = dot("qkgd,skd->kgqs", grad_heads, v_heads)
        inner = jnp.sum(soft_full * grad_soft, axis=-1, keepdims=True)
        grad_scores = (soft_full * (grad_soft - inner)).astype(bf16)
        grad_values = dot("kgqs,qkgd->skd", soft, grad_heads)
        factor = 1.0 / math.sqrt(HEAD_DIM)
        grad_qrot = dot("kgqs,skd->qkgd", grad_scores, k_rot) * factor
        grad_krot = dot("kgqs,qkgd->skd", grad_scores, q_rot) * factor
        grad_q = rotate_back(grad_qrot.reshape(count, HEADS, HEAD_DIM), cosine, sine)
        grad_q = grad_q.reshape(count, -1).astype(bf16)
        both = jnp.concatenate(
            [grad_krot.reshape(rows_tok, -1), grad_values.reshape(rows_tok, -1)], axis=1
        ).astype(bf16)
        both = lax.psum_scatter(both, "gy", scatter_dimension=0, tiled=True).astype(f32)
        half = both.shape[1] // 2
        grad_k = rotate_back(both[:, :half].reshape(count, KV_HEADS, HEAD_DIM), cosine, sine)
        grad_k = grad_k.reshape(count, -1).astype(bf16)
        grad_v = both[:, half:].astype(bf16)
        grad_qkv = jnp.concatenate(
            [g.reshape(count, devices_y, -1) for g in (grad_q, grad_k, grad_v)], axis=2
        ).transpose(1, 0, 2)
        grad_acts_one = dot("tq,dq->td", grad_qkv[0], w_qkv[0])
        for z in range(1, devices_y):
            grad_acts_one = grad_acts_one + dot("tq,dq->td", grad_qkv[z], w_qkv[z])
        attn_grads[l] = [
            turn(acts_one),
            turn(grad_branch),
            grad_qkv,
            mixed.transpose(1, 0, 2),
        ]
        grad_norm, grad_gain_one = norm_backward(
            grad_acts_one, normed_one, scale_one, gains_one[l]
        )
        grad = grad_mid + grad_norm
        small_grads[l] = [
            v.reshape(devices_y, -1)
            for v in (
                grad_gain_one,
                grad_gain_two,
                jnp.sum(grad_q.astype(f32), axis=0),
                jnp.sum(grad_k.astype(f32), axis=0),
                jnp.sum(grad_v.astype(f32), axis=0),
            )
        ]
    small = jnp.stack([jnp.concatenate(v, axis=1) for v in small_grads], axis=1)
    small = jnp.pad(small, ((0, 0), (0, 8 - LAYERS), (0, 0)))

    def to_rows(tokens_major):
        return tokens_major.astype(bf16).T.reshape(devices_y, -1, count)

    def from_blocks(blocks):
        return blocks.transpose(1, 0, 2).reshape(-1, rows_tok).astype(f32)

    attn_sums, small, output, grad_input = closing(
        attn_grads[0] + attn_grads[1], small, to_rows(resid), to_rows(grad)
    )
    small = small[:LAYERS]
    attn_out, start = [], 0
    for size in part_sizes + (w_output.shape[2],):
        attn_out.append(attn_sums[:, :, start : start + size])
        start += size
    small_out, start = [], 0
    for size in small_sizes:
        small_out.append(small[:, start : start + size])
        start += size

    def stack(parts, k):
        return jnp.stack([part[k] for part in parts])

    return (
        from_blocks(output),
        from_blocks(grad_input),
        attn_out[0],
        attn_out[1],
        attn_out[2],
        small_out[2],
        small_out[3],
        small_out[4],
        attn_out[3],
        small_out[0],
        small_out[1],
        stack(ffn_grads, 0),
        stack(ffn_grads, 1),
        stack(ffn_grads, 2),
    )


def solution(mesh):
    tokens = P("gy", "gx")
    weight = P(None, "gx", "gy")
    vector = P(None, "gy")
    return jax.shard_map(
        on_device,
        mesh=mesh,
        in_specs=(
            tokens,
            weight,
            weight,
            weight,
            vector,
            vector,
            vector,
            weight,
            vector,
            vector,
            weight,
            weight,
            weight,
            tokens,
        ),
        out_specs=(
            tokens,
            tokens,
            weight,
            weight,
            weight,
            vector,
            vector,
            vector,
            weight,
            vector,
            vector,
            weight,
            weight,
            weight,
        ),
        check_vma=False,
    )
```

```python
import functools
import math

import jax
import jax.numpy as jnp
from jax import lax
from jax.experimental import pallas as pl
from jax.experimental.pallas import tpu as pltpu
from jax.sharding import PartitionSpec as P

D = 1536
HEADS = 12
KV_HEADS = 2
HEAD_DIM = 128
LEN = 1024
LAYERS = 2
GROUP = HEADS // KV_HEADS

epsilon = 1e-06
rope_base = 1000000.0
penalty = 0.25
bf16 = jnp.bfloat16
f32 = jnp.float32
MESH = pl.DeviceIdType.MESH
VMEM_LIMIT = 62 << 20
ANY = pl.BlockSpec(memory_space=pl.ANY)


def rope_tables(positions, head_size):
    freqs = rope_base ** (-jnp.arange(0, head_size, 2).astype(f32) / head_size)
    angles = positions.astype(f32)[:, None] * freqs[None, :]
    cosine = jnp.cos(angles)
    sine_table = jnp.sin(angles)
    return (
        jnp.concatenate([cosine, cosine], -1)[:, None, :],
        jnp.concatenate([sine_table, sine_table], -1)[:, None, :],
    )


def rotate(tensor, cosine, sine_table):
    half = tensor.shape[-1] // 2
    turned = jnp.concatenate([-tensor[..., half:], tensor[..., :half]], -1)
    return tensor * cosine + turned * sine_table


def dot(pattern, left, right):
    return jnp.einsum(pattern, left, right, preferred_element_type=f32)


def rms_parts(resid):
    scale = lax.rsqrt(jnp.mean(resid * resid, axis=1, keepdims=True) + epsilon)
    return resid * scale, scale


def split_columns(blocks, sizes):
    out, start = [], 0
    for size in sizes:
        out.append(blocks[:, :, start : start + size].reshape(blocks.shape[0], -1))
        start += size
    return out


def score_block(q_rot, k_rot, allowed):
    scores = dot("qkgd,skd->kgqs", q_rot, k_rot) * (1.0 / math.sqrt(HEAD_DIM))
    return jnp.where(allowed, scores, -1e30)


def wait_for(ref, sem):
    pltpu.make_async_copy(ref, ref, sem).wait()


def places():
    gx, devices = lax.axis_index("gx"), lax.axis_size("gx")
    chips = devices // 2
    chip, core = gx // 2, lax.rem(gx, 2)
    partner = gx + 1 - 2 * core
    others = [lax.rem(chip + k, chips) * 2 + core for k in range(1, chips)]
    return partner, others


def square():
    gx = lax.axis_index("gx")
    chip, core = gx // 2, lax.rem(gx, 2)
    side = gx + 2 - 4 * lax.rem(chip, 2)
    along = gx + 4 - 8 * (chip // 2)
    return side, along, (3 - chip) * 2 + core


def spread_slots():
    chips = lax.axis_size("gx") // 2
    return 14 if chips == 4 else 2 * chips + 2 * (chips - 1)


def spread_scratch(count):
    devices = lax.axis_size("gx")
    return [
        pltpu.SemaphoreType.DMA((count,)),
        pltpu.SemaphoreType.DMA((count, spread_slots())),
        pltpu.SemaphoreType.DMA((count, devices, 2)),
    ]


def greet(gx_peers, gy_peers):
    gx, gy = lax.axis_index("gx"), lax.axis_index("gy")
    barrier = pltpu.get_barrier_semaphore()
    for peer in gx_peers:
        pl.semaphore_signal(barrier, inc=1, device_id=(peer, gy), device_id_type=MESH)
    for peer in gy_peers:
        pl.semaphore_signal(barrier, inc=1, device_id=(gx, peer), device_id_type=MESH)
    pl.semaphore_wait(barrier, len(gx_peers) + len(gy_peers))


class Spread:
    def __init__(self, items, sems):
        self.items, (self.local, self.send_sem, self.recv_sem) = items, sems
        self.partner, self.others = places()
        self.four = lax.axis_size("gx") // 2 == 4
        self.near = list(square()[:2]) if self.four else self.others

    def part(self, i, k, h):
        full = self.items[i][1]
        if len(full.shape) == 4:
            half = full.shape[0] // 2
            return full.at[pl.ds(h * half, half), k]
        half = full.shape[1] // 2
        return full.at[k, pl.ds(h * half, half)]

    def send(self, i, k, h, target, slot, first=False):
        here = self.part(i, k, h)
        half = here.shape[0]
        source = self.items[i][0].at[pl.ds(h * half, half)] if first else here
        pltpu.make_async_remote_copy(
            src_ref=source,
            dst_ref=here,
            send_sem=self.send_sem.at[i, slot],
            recv_sem=self.recv_sem.at[i, k, h],
            device_id=(target, lax.axis_index("gy")),
            device_id_type=MESH,
        ).start()

    def arrived(self, i, k, h):
        wait_for(self.part(i, k, h), self.recv_sem.at[i, k, h])

    def place(self, i):
        own, full = self.items[i]
        gx = lax.axis_index("gx")
        here = full.at[:, gx] if len(full.shape) == 4 else full.at[gx]
        return pltpu.make_async_copy(own, here, self.local.at[i])

    def begin(self, i):
        gx = lax.axis_index("gx")
        self.place(i).start()
        slot = 0
        for target in self.near + [self.partner]:
            for h in range(2):
                self.send(i, gx, h, target, slot, True)
                slot += 1

    def relay(self, i):
        slot = 2 * len(self.near) + 2
        if self.four:
            side, along, _ = square()
            steps = [(side, 0, along), (along, 1, side), (side, 1, None), (along, 0, None)]
        else:
            steps = [(k, h, None) for k in self.others for h in range(2)]
        for k, h, target in steps:
            self.arrived(i, k, h)
            for to in [self.partner] if target is None else [target, self.partner]:
                self.send(i, k, h, to, slot)
                slot += 1

    def finish(self, i):
        if self.four:
            for h in range(2):
                self.arrived(i, square()[2], h)
                self.send(i, square()[2], h, self.partner, 12 + h)

    def close(self, i):
        core = lax.rem(lax.axis_index("gx"), 2)
        for k in [self.partner] + [k + 1 - 2 * core for k in self.others]:
            for h in range(2):
                self.arrived(i, k, h)
        for slot in range(spread_slots()):
            wait_for(self.part(i, 0, 0), self.send_sem.at[i, slot])
        self.place(i).wait()


def line_order(t, me, last):
    short = jnp.minimum(me, last - me)
    near = jnp.where(lax.rem(t, 2) == 0, me - t // 2, me + (t + 1) // 2)
    far = jnp.where(me < last - me, me + (t - short), me - (t - short))
    return jnp.where(t <= 2 * short, near, far)


class Chain:
    def __init__(self, own, full, sems):
        self.own, self.full, (self.local, self.send_sem, self.recv_sem) = own, full, sems

    def copy(self, b, way, first=False):
        me = lax.axis_index("gy")
        return pltpu.make_async_remote_copy(
            src_ref=self.own if first else self.full.at[b],
            dst_ref=self.full.at[b],
            send_sem=self.send_sem.at[b, way],
            recv_sem=self.recv_sem.at[b],
            device_id=(lax.axis_index("gx"), me - 1 + 2 * way),
            device_id_type=MESH,
        )

    def each(self, b, act, first=False):
        me, last = lax.axis_index("gy"), lax.axis_size("gy") - 1

        @pl.when(jnp.logical_and(b <= me, me < last))
        def _():
            act(self.copy(b, 1, first))

        @pl.when(jnp.logical_and(b >= me, me > 0))
        def _():
            act(self.copy(b, 0, first))

    def begin(self):
        me = lax.axis_index("gy")
        self.place = pltpu.make_async_copy(self.own, self.full.at[me], self.local)
        self.place.start()
        self.each(me, lambda copy: copy.start(), True)

    def relay(self, t):
        b = line_order(t, lax.axis_index("gy"), lax.axis_size("gy") - 1)
        wait_for(self.full.at[b], self.recv_sem.at[b])
        self.each(b, lambda copy: copy.start())

    def close(self):
        self.place.wait()
        for b in range(lax.axis_size("gy")):
            self.each(b, lambda copy: copy.wait_send())


class Exchange:
    def __init__(self, own, full, sems, apart=False):
        self.own, self.full, (self.local, self.send_sem, self.recv_sem) = own, full, sems
        self.apart = apart

    def begin(self):
        gx, me, size = lax.axis_index("gx"), lax.axis_index("gy"), lax.axis_size("gy")
        width = self.full.shape[2]

        def columns(k):
            if self.apart:
                return self.own.at[k]
            return self.own.at[:, pl.ds(pl.multiple_of(k * width, width), width)]

        self.place = pltpu.make_async_copy(columns(me), self.full.at[me], self.local)
        self.place.start()
        self.sent = []
        for d in range(1, size):
            target = lax.rem(me + d, size)
            copy = pltpu.make_async_remote_copy(
                src_ref=columns(target),
                dst_ref=self.full.at[me],
                send_sem=self.send_sem.at[d],
                recv_sem=self.recv_sem.at[me],
                device_id=(gx, target),
                device_id_type=MESH,
            )
            copy.start()
            self.sent.append(copy)

    def close(self):
        me, size = lax.axis_index("gy"), lax.axis_size("gy")
        self.place.wait()
        for copy in self.sent:
            copy.wait_send()
        for d in range(1, size):
            k = lax.rem(me + d, size)
            wait_for(self.full.at[k], self.recv_sem.at[k])


def chain_scratch():
    size = lax.axis_size("gy")
    return [
        pltpu.SemaphoreType.DMA,
        pltpu.SemaphoreType.DMA((size, 2)),
        pltpu.SemaphoreType.DMA((size,)),
    ]


def exchange_scratch():
    size = lax.axis_size("gy")
    return [
        pltpu.SemaphoreType.DMA,
        pltpu.SemaphoreType.DMA((size,)),
        pltpu.SemaphoreType.DMA((size,)),
    ]


def opening_kernel(*refs):
    ins, outs, sems = refs[:10], refs[10:22], refs[22:]
    resid, cot, small, qkv_a, o_a, qkv_b, o_b, wg, wu, wd = ins
    resid_out, cot_out, small_out = outs[:3]
    lines, (qkv, o, gate, up, down) = outs[3:7], outs[7:]
    me, size = lax.axis_index("gy"), lax.axis_size("gy")
    owns = (qkv_a, o_a, qkv_b, o_b, small)
    chains = [
        Chain(own, full, sems[3 * k : 3 * k + 3])
        for k, (own, full) in enumerate(zip(owns, list(lines) + [small_out]))
    ]
    swaps = [
        Exchange(own, full, sems[15 + 3 * k : 18 + 3 * k])
        for k, (own, full) in enumerate(((resid, resid_out), (cot, cot_out)))
    ]
    items = [(lines[0], qkv), (lines[1], o), (wg.at[0], gate), (wu.at[0], up), (wd.at[0], down)]
    spread = Spread(items, sems[21:24])
    greet([spread.partner] + spread.near, [lax.rem(me + d, size) for d in range(1, size)])
    for k in (0, 1, 4):
        chains[k].begin()
    spread.begin(2)
    for t in range(1, size):
        chains[0].relay(t)
        chains[1].relay(t)
    chains[0].close()
    spread.begin(0)
    chains[1].close()
    spread.begin(1)
    swaps[0].begin()
    for t in range(1, size):
        chains[4].relay(t)
    spread.begin(3)
    chains[2].begin()
    chains[3].begin()
    spread.relay(2)
    for t in range(1, size):
        chains[2].relay(t)
        chains[3].relay(t)
    spread.begin(4)
    swaps[1].begin()
    for i in (0, 1):
        spread.relay(i)
    spread.finish(2)
    spread.relay(3)
    for i in (0, 1):
        spread.finish(i)
    spread.relay(4)
    for i in (3, 4):
        spread.finish(i)
    for i in range(5):
        spread.close(i)
    for part in chains[2:] + swaps:
        part.close()


def opening(resid, cot, small, lines, wg, wu, wd):
    devices, size = lax.axis_size("gx"), lax.axis_size("gy")
    count = resid.shape[1] // size

    def shape(*dims, kind=bf16):
        return jax.ShapeDtypeStruct(dims, kind)

    blocks = shape(size, resid.shape[0], count)
    weight = shape(devices, *wg.shape[1:])
    out = [blocks, blocks, shape(size, *small.shape, kind=f32)]
    out += [shape(size, *line.shape) for line in lines]
    out += [shape(size, devices, *line.shape) for line in lines[:2]] + [weight] * 3
    return pl.pallas_call(
        opening_kernel,
        out_shape=out,
        in_specs=[ANY] * 10,
        out_specs=[ANY] * 12,
        scratch_shapes=chain_scratch() * 5 + exchange_scratch() * 2 + spread_scratch(5),
        compiler_params=pltpu.CompilerParams(collective_id=2, has_side_effects=True),
        name="opening",
    )(resid, cot, small, *lines, wg, wu, wd)


FF_CHUNK = 512
PIECES = 4


def spans(total):
    return [(start, min(FF_CHUNK, total - start)) for start in range(0, total, FF_CHUNK)]


def nn(left, right):
    return lax.dot_general(left, right, (((1,), (0,)), ((), ())), preferred_element_type=f32)


def nt(left, right):
    return lax.dot_general(left, right, (((1,), (1,)), ((), ())), preferred_element_type=f32)


def line_pass(own_ref, own, gathered, part, outb, inb, sems, load, finish, peers=(), plan={}):
    own_sem, ag_send, ag_recv, rs_send, rs_recv = sems
    gx, me, size = lax.axis_index("gx"), lax.axis_index("gy"), lax.axis_size("gy")
    rows = own.shape[0]
    piece = rows // PIECES
    last = size - 1
    inner = jnp.logical_and(me > 0, me < last)

    first = pltpu.make_async_copy(own_ref, gathered.at[me], own_sem)
    first.start()
    barrier = pltpu.get_barrier_semaphore()

    @pl.when(me > 0)
    def _():
        pl.semaphore_signal(barrier, inc=1, device_id=(gx, me - 1), device_id_type=MESH)

    @pl.when(me < last)
    def _():
        pl.semaphore_signal(barrier, inc=1, device_id=(gx, me + 1), device_id_type=MESH)

    for peer in peers:
        pl.semaphore_signal(barrier, inc=1, device_id=(peer, me), device_id_type=MESH)
    pl.semaphore_wait(barrier, jnp.where(inner, 2, 1) + len(peers))
    first.wait()

    def planned(name, t):
        for (key, when), act in plan.items():
            if key == name:
                pl.when(t == when)(act)


    def gather_copy(b, s, way):
        here = gathered.at[b, pl.ds(s * piece, piece)]
        return pltpu.make_async_remote_copy(
            src_ref=here,
            dst_ref=here,
            send_sem=ag_send.at[b, way, s],
            recv_sem=ag_recv.at[b, s],
            device_id=(gx, me - 1 + 2 * way),
            device_id_type=MESH,
        )

    def sum_copy(b, s):
        towards = jnp.where(b > me, me + 1, me - 1)
        slot = jnp.where(jnp.logical_and(towards == b, me > b), size, b)
        return pltpu.make_async_remote_copy(
            src_ref=outb.at[b, pl.ds(s * piece, piece)],
            dst_ref=inb.at[slot, pl.ds(s * piece, piece)],
            send_sem=rs_send.at[b, s],
            recv_sem=rs_recv.at[slot, s],
            device_id=(gx, towards),
            device_id_type=MESH,
        )

    def sum_arrived(slot, s):
        here = inb.at[slot, pl.ds(s * piece, piece)]
        pltpu.make_async_copy(here, here, rs_recv.at[slot, s]).wait()

    def step(t, carry):
        b = line_order(t, me, last)
        for s in range(PIECES):

            @pl.when(t > 0)
            def _():
                gather_copy(b, s, 0).wait_recv()

            @pl.when(jnp.logical_and(b <= me, me < last))
            def _():
                gather_copy(b, s, 1).start()

            @pl.when(jnp.logical_and(b >= me, me > 0))
            def _():
                gather_copy(b, s, 0).start()

        @pl.when(t == 0)
        def _():
            load()

        planned("step", t)
        finish(b)

        @pl.when(b == me)
        def _():
            own[...] = part[...]

        @pl.when(b != me)
        def _():
            outb[b] = part[...].astype(bf16)

            @pl.when(jnp.logical_not(inner))
            def _():
                for s in range(PIECES):
                    sum_copy(b, s).start()

        return carry

    lax.fori_loop(0, size, step, 0)

    def relay(t, carry):
        above, below = last - me, me
        low = jnp.where(t < above, me + 1 + t, me - 1 - (t - above))
        high = jnp.where(t < below, me - 1 - t, me + 1 + (t - below))
        b = jnp.where(2 * me < size, low, high)
        planned("hop", t)

        @pl.when(inner)
        def _():
            for s in range(PIECES):
                at = pl.ds(s * piece, piece)
                sum_arrived(b, s)
                outb[b, at] = (outb[b, at].astype(f32) + inb[b, at].astype(f32)).astype(bf16)
                sum_copy(b, s).start()

        return carry

    lax.fori_loop(0, last, relay, 0)

    @pl.when(me > 0)
    def _():
        for s in range(PIECES):
            sum_arrived(me, s)
        own[...] += inb[me].astype(f32)

    @pl.when(me < last)
    def _():
        for s in range(PIECES):
            sum_arrived(size, s)
        own[...] += inb[size].astype(f32)

    def drain(b, carry):
        for s in range(PIECES):

            @pl.when(jnp.logical_and(b <= me, me < last))
            def _():
                gather_copy(b, s, 1).wait_send()

            @pl.when(jnp.logical_and(b >= me, me > 0))
            def _():
                gather_copy(b, s, 0).wait_send()

            @pl.when(b != me)
            def _():
                sum_copy(b, s).wait_send()

        return carry

    lax.fori_loop(0, size, drain, 0)


def line_scratch(size, rows, width):
    return [
        pltpu.VMEM((size, rows, width), bf16),
        pltpu.VMEM((rows, width), f32),
        pltpu.VMEM((size, rows, width), bf16),
        pltpu.VMEM((size + 1, rows, width), bf16),
        pltpu.SemaphoreType.DMA,
        pltpu.SemaphoreType.DMA((size, 2, PIECES)),
        pltpu.SemaphoreType.DMA((size, PIECES)),
        pltpu.SemaphoreType.DMA((size, PIECES)),
        pltpu.SemaphoreType.DMA((size + 1, PIECES)),
    ]


LINE = 9


ORDER = {
    ("step", 0): (("begin", 0), ("begin", 1)),
    ("step", 2): (("begin", 2),),
    ("hop", 0): (("relay", 0), ("relay", 1), ("relay", 2), ("begin", 3)),
    ("hop", 1): (("finish", 0), ("finish", 1), ("finish", 2), ("begin", 4)),
}
REST = (("relay", 3), ("relay", 4), ("finish", 3), ("finish", 4))


def schedule(spread):
    def run(steps):
        def act():
            for verb, i in steps:
                getattr(spread, verb)(i)

        return act

    plan = {key: run(steps) for key, steps in ORDER.items()}
    return plan, REST + tuple(("close", i) for i in range(len(spread.items)))


def forward_kernel(extra, *refs):
    acts_ref, wg_ref, wu_ref, wd_ref = refs[:4]
    shards, refs = refs[4 : 4 + extra], refs[4 + extra :]
    sum_ref, turned_ref, gate_ref, up_ref, hidden_ref = refs[:5]
    wholes, scratch = refs[5 : 5 + extra], refs[5 + extra :]
    gathered, part, outb, inb = scratch[:4]
    sems = scratch[4:LINE]
    wg, wu, wd, gate, up, hidden, turned, w_sem, out_sem = scratch[LINE : LINE + 9]
    peers, spread = [], None
    if extra:
        items = [(r if len(w.shape) == 4 else r.at[1], w) for r, w in zip(shards, wholes)]
        spread = Spread(items, scratch[LINE + 9 :])
        partner, others = places()
        peers = [partner] + (list(square()[:2]) if spread.four else others)

    plan, rest = schedule(spread) if extra else ({}, ())
    loads = [
        pltpu.make_async_copy(src, dst, w_sem.at[k])
        for k, (src, dst) in enumerate(((wg_ref, wg), (wu_ref, wu), (wd_ref, wd)))
    ]
    for copy in loads:
        copy.start()

    def load():
        for copy in loads:
            copy.wait()

    def results(b):
        pairs = ((gate, gate_ref), (up, up_ref), (hidden, hidden_ref))
        return [
            pltpu.make_async_copy(src.at[b], dst.at[b], out_sem.at[b, k])
            for k, (src, dst) in enumerate(pairs)
        ]

    def finish(b):
        block = gathered[b]
        store_turned(block, turned, b)
        for start, width in spans(wg.shape[1]):
            at = slice(start, start + width)
            g = nn(block, wg[:, at])
            u = nn(block, wu[:, at])
            h = (g * lax.logistic(g) * u).astype(bf16)
            gate[b, :, at] = g.astype(bf16)
            up[b, :, at] = u.astype(bf16)
            hidden[b, :, at] = h
            p = nt(h, wd[:, at])
            if start == 0:
                part[...] = p
            else:
                part[...] += p
        for copy in results(b):
            copy.start()

    line_pass(
        acts_ref, sum_ref, gathered, part, outb, inb, sems, load, finish, peers, plan
    )
    keep = pltpu.make_async_copy(turned, turned_ref, w_sem.at[0])
    keep.start()
    for act, i in rest:
        getattr(spread, act)(i)

    def settle(b, carry):
        for copy in results(b):
            copy.wait()
        return carry

    lax.fori_loop(0, gathered.shape[0], settle, 0)
    keep.wait()


def forward_ffn(acts, wg, wu, wd, shards=()):
    rows, width = acts.shape
    devices, size, hidden = lax.axis_size("gx"), lax.axis_size("gy"), wg.shape[1]
    wide = jax.ShapeDtypeStruct((size, rows, hidden), bf16)
    extra = len(shards)
    wholes = [
        jax.ShapeDtypeStruct(
            (size, devices) + s.shape[1:] if k < 2 else (devices,) + s.shape[1:], bf16
        )
        for k, s in enumerate(shards)
    ]
    return pl.pallas_call(
        functools.partial(forward_kernel, extra),
        out_shape=[
            jax.ShapeDtypeStruct((rows, width), f32),
            jax.ShapeDtypeStruct((2, width // 2, size * rows), bf16),
            wide,
            wide,
            wide,
        ]
        + wholes,
        in_specs=[ANY] * (4 + extra),
        out_specs=[pl.BlockSpec(memory_space=pltpu.VMEM)] + [ANY] * (4 + extra),
        scratch_shapes=line_scratch(size, rows, width)
        + [pltpu.VMEM((width, hidden), bf16)] * 3
        + [pltpu.VMEM((size, rows, hidden), bf16)] * 3
        + [pltpu.VMEM((2, width // 2, size * rows), bf16)]
        + [pltpu.SemaphoreType.DMA((3,)), pltpu.SemaphoreType.DMA((size, 3))]
        + (spread_scratch(extra) if extra else []),
        compiler_params=pltpu.CompilerParams(
            collective_id=3 if extra else 0, has_side_effects=True, vmem_limit_bytes=VMEM_LIMIT
        ),
        cost_estimate=pl.CostEstimate(
            flops=6 * size * rows * width * hidden, bytes_accessed=40 << 20, transcendentals=0
        ),
        name="ffn_forward",
    )(acts, wg, wu, wd, *shards)


class Reduce:
    def __init__(self, lhs, rhs, bufs, abuf, fbuf, ftail, a_all, r_all, c_all, outs, late, sems):
        self.late = late
        self.lhs, self.rhs, self.bufs, self.outs = lhs, rhs, bufs, outs
        self.abuf, self.fbuf, self.ftail = abuf, fbuf, ftail
        self.a_all, self.r_all, self.c_all = a_all, r_all, c_all
        (
            self.a_send,
            self.a_recv,
            self.r_send,
            self.r_recv,
            self.c_send,
            self.c_recv,
            self.local,
        ) = sems
        gx, self.gy = lax.axis_index("gx"), lax.axis_index("gy")
        self.chip, self.core = gx // 2, lax.rem(gx, 2)
        self.chips = lax.axis_size("gx") // 2
        self.half, self.wide = bufs[0].shape[0] // 2, bufs[0].shape[1]
        self.r = self.half // self.chips
        self.four = self.chips == 4
        self.partner, self.others = places()
        self.near = list(square()[:2]) if self.four else self.others

    def product(self, m, which, at):
        z, n, _ = self.rhs[m].shape
        right = self.rhs[m][:, :, at].reshape(z * n, at.stop - at.start)
        return nn(self.lhs[which], right)

    def remote(self, src, dst, send, recv, target):
        return pltpu.make_async_remote_copy(
            src_ref=src,
            dst_ref=dst,
            send_sem=send,
            recv_sem=recv,
            device_id=(target, self.gy),
            device_id_type=MESH,
        )

    def columns(self):
        return [(j, slice(s, s + w)) for j, (s, w) in enumerate(spans(self.wide))]

    def swap(self, m, j, at):
        here = (slice(0, self.half), at)
        return self.remote(
            self.bufs[m].at[here],
            self.a_all.at[m, :, at],
            self.a_send.at[m, j],
            self.a_recv.at[m, j],
            self.partner,
        )

    def block(self, m, device, start=0, size=None):
        size = self.r if size is None else size
        first = self.half + (device // 2) * self.r + start
        return self.bufs[m].at[pl.ds(pl.multiple_of(first, 16), size)]

    def first(self, m):
        for j, at in self.columns():
            self.bufs[m][: self.half, at] = self.product(m, 1 - self.core, at).astype(bf16)
            self.swap(m, j, at).start()

    def corner(self, m, h):
        side, along, across = square()
        half = self.r // 2
        return self.remote(
            self.block(m, across, h * half, half),
            self.r_all.at[m, h],
            self.r_send.at[m, h],
            self.r_recv.at[m, h],
            along if h else side,
        )

    def second(self, m):
        for j, at in self.columns():
            self.swap(m, j, at).wait_recv()
            landed = self.abuf.at[:, at]
            fetch = pltpu.make_async_copy(self.a_all.at[m, :, at], landed, self.local.at[0])
            fetch.start()
            mine = self.product(m, self.core, at)
            fetch.wait()
            self.bufs[m][self.half :, at] = (mine + landed[...].astype(f32)).astype(bf16)
        if m in self.late:
            self.keep(m).start()
        elif self.four:
            for h in range(2):
                self.corner(m, h).start()

    def keep(self, m):
        kept = self.outs[m]
        return pltpu.make_async_copy(
            self.bufs[m].at[pl.ds(self.half, self.half)], kept, self.local.at[max(len(self.near), 2)]
        )

    def hand(self, m, k):
        target = self.near[k]
        return self.remote(
            self.block(m, target),
            self.c_all.at[m, k],
            self.c_send.at[m, k],
            self.c_recv.at[m, k],
            target,
        )

    def third(self, m):
        if self.four:
            side, along, _ = square()
            half = self.r // 2
            for h, device in ((0, along), (1, side)):
                self.corner(m, h).wait_recv()
                here = self.block(m, device, h * half, half)
                landed = self.abuf.at[h * half : (h + 1) * half]
                fetch = pltpu.make_async_copy(self.r_all.at[m, h], landed, self.local.at[0])
                fetch.start()
                fetch.wait()
                here[...] = (here[...].astype(f32) + landed[...].astype(f32)).astype(bf16)
        for k in range(len(self.near)):
            self.hand(m, k).start()

    def fourth(self, m):
        for j, at in self.columns():
            self.swap(m, j, at).wait_send()
        fetches = []
        for k in range(len(self.near)):
            self.hand(m, k).wait_recv()
            here = self.bufs[m].at[pl.ds(k * self.r, self.r)]
            fetch = pltpu.make_async_copy(self.c_all.at[m, k], here, self.local.at[k])
            fetch.start()
            fetches.append(fetch)
        for fetch in fetches:
            fetch.wait()
        first = pl.multiple_of(self.half + self.chip * self.r, 16)
        for _, at in self.columns():
            total = self.bufs[m][pl.ds(first, self.r), at].astype(f32)
            for k in range(len(self.near)):
                total = total + self.bufs[m][k * self.r : (k + 1) * self.r, at].astype(f32)
            stage = self.fbuf if total.shape[1] == FF_CHUNK else self.ftail
            stage[...] = total
            store = pltpu.make_async_copy(stage, self.outs[m].at[:, at], self.local.at[0])
            store.start()
            store.wait()

    def drain(self, m):
        if self.four:
            for h in range(2):
                self.corner(m, h).wait_send()
        for k in range(len(self.near)):
            self.hand(m, k).wait_send()


def reduce_scratch(width, hidden, count=3):
    devices = lax.axis_size("gx")
    rows, parts = width // devices, len(spans(hidden))
    near = 2 if devices == 8 else devices // 2 - 1
    dma = pltpu.SemaphoreType.DMA
    return [
        pltpu.VMEM((width // 2, hidden), bf16),
        pltpu.VMEM((rows, FF_CHUNK), f32),
        pltpu.VMEM((rows, hidden % FF_CHUNK), f32),
        dma((count, parts)),
        dma((count, parts)),
        dma((count, 2)),
        dma((count, 2)),
        dma((count, near)),
        dma((count, near)),
        dma((max(near, 2) + 1,)),
    ]


class Tail:
    def __init__(self, b_all, r_all, c_all, outs, abuf, fbuf, ftail, sems):
        self.b_all, self.r_all, self.c_all, self.outs = b_all, r_all, c_all, outs
        self.abuf, self.fbuf, self.ftail = abuf, fbuf, ftail
        self.r_send, self.r_recv, self.c_send, self.c_recv, self.local = sems
        gx, self.gy = lax.axis_index("gx"), lax.axis_index("gy")
        self.chip, chips = gx // 2, lax.axis_size("gx") // 2
        self.r = b_all.shape[1] // chips
        self.part = self.r // 2
        self.space = b_all.shape[1] // b_all.shape[0]
        self.four = chips == 4
        self.near = list(square()[:2]) if self.four else places()[1]

    def remote(self, src, dst, send, recv, target):
        return pltpu.make_async_remote_copy(
            src_ref=src,
            dst_ref=dst,
            send_sem=send,
            recv_sem=recv,
            device_id=(target, self.gy),
            device_id_type=MESH,
        )

    def held(self, i, chip, h):
        first = pl.multiple_of(chip * self.r + h * self.part, 16)
        return self.b_all.at[i, pl.ds(first, self.part)]

    def slot(self, i, k):
        return self.abuf.at[pl.ds(i * self.space + k * self.part, self.part)]

    def corner(self, i, h):
        side, along, across = square()
        return self.remote(
            self.held(i, across // 2, h),
            self.r_all.at[i, h],
            self.r_send.at[i, h],
            self.r_recv.at[i, h],
            along if h else side,
        )

    def hand(self, i, k, h):
        target = self.near[k]
        summed = self.four and k != h
        return self.remote(
            self.slot(i, 2 + h) if summed else self.held(i, target // 2, h),
            self.c_all.at[i, k, h],
            self.c_send.at[i, k, h],
            self.c_recv.at[i, k, h],
            target,
        )

    def hands(self):
        return [(k, h) for k in range(len(self.near)) for h in range(2)]

    def begin(self, i):
        if self.four:
            for h in range(2):
                self.corner(i, h).start()

    def middle(self, i):
        if self.four:
            side, along, _ = square()
            for h, device in ((0, along), (1, side)):
                self.corner(i, h).wait_recv()
                came, mine = self.slot(i, h), self.slot(i, 2 + h)
                fetches = [
                    pltpu.make_async_copy(self.r_all.at[i, h], came, self.local.at[0]),
                    pltpu.make_async_copy(self.held(i, device // 2, h), mine, self.local.at[1]),
                ]
                for fetch in fetches:
                    fetch.start()
                for fetch in fetches:
                    fetch.wait()
                mine[...] = (mine[...].astype(f32) + came[...].astype(f32)).astype(bf16)
        for k, h in self.hands():
            self.hand(i, k, h).start()

    def close(self, i):
        if self.four:
            for h in range(2):
                self.corner(i, h).wait_send()
        for k, h in self.hands():
            self.hand(i, k, h).wait_send()
        count = len(self.near)
        for h in range(2):
            fetches = [
                pltpu.make_async_copy(
                    self.held(i, self.chip, h), self.slot(i, count), self.local.at[count]
                )
            ]
            for k in range(count):
                self.hand(i, k, h).wait_recv()
                fetches.append(
                    pltpu.make_async_copy(
                        self.c_all.at[i, k, h], self.slot(i, k), self.local.at[k]
                    )
                )
            for fetch in fetches:
                fetch.start()
            for fetch in fetches:
                fetch.wait()
            for start, width in spans(self.abuf.shape[1]):
                at = slice(start, start + width)
                total = self.slot(i, 0)[:, at].astype(f32)
                for k in range(1, count + 1):
                    total = total + self.slot(i, k)[:, at].astype(f32)
                stage = self.fbuf if width == FF_CHUNK else self.ftail
                stage[: self.part] = total
                store = pltpu.make_async_copy(
                    stage.at[pl.ds(0, self.part)],
                    self.outs[i].at[pl.ds(h * self.part, self.part), at],
                    self.local.at[0],
                )
                store.start()
                store.wait()


def tail_scratch(count):
    devices = lax.axis_size("gx")
    near = 2 if devices == 8 else devices // 2 - 1
    dma = pltpu.SemaphoreType.DMA
    return [
        dma((count, 2)),
        dma((count, 2)),
        dma((count, near, 2)),
        dma((count, near, 2)),
        dma((near + 1,)),
    ]


def store_turned(block, turned, b):
    count, width = block.shape
    _, chips_rows, _ = turned.shape
    devices = lax.axis_size("gx")
    r = width // devices
    flipped = block.T
    at = pl.ds(pl.multiple_of(b * count, count), count)
    for k in range(devices):
        q = k // 2
        turned[k % 2, q * r : (q + 1) * r, at] = flipped[k * r : (k + 1) * r]


AFTER = {
    0: (("first", 0),),
    1: (("second", 0), ("swap", 0), ("first", 1)),
    2: (("third", 0), ("second", 1)),
}
WHOLE_END = (("first", 2), ("third", 1), ("second", 2), ("fourth", 0), ("third", 2))
WHOLE_END += (("fourth", 1), ("fourth", 2), ("drain", 0), ("drain", 1), ("drain", 2))
LATE_END = (("kept", 1), ("first", 2), ("second", 2), ("fourth", 0), ("kept", 2))
LATE_END += (("sent", 1), ("sent", 2), ("drain", 0))


TAIL_BEGIN, TAIL_MIDDLE = ("step", 0), ("step", 2)


def both(one, other):
    def act():
        one()
        other()

    return act


def backward_kernel(late, tails, *refs):
    grad_ref, gate_ref, up_ref, hidden_ref, turned_ref, wg_ref, wu_ref, wd_ref = refs[:8]
    held, refs = refs[8 : 8 + (tails > 0)], refs[8 + (tails > 0) :]
    sum_ref, refs = refs[0], refs[1:]
    if late:
        od, b_all, a_all, r_all, c_all = refs[:5]
        outs, refs = (od, b_all.at[0], b_all.at[1]), refs[5:]
    else:
        og, ou, od, a_all, r_all, c_all = refs[:6]
        outs, refs = (od, og, ou), refs[6:]
    tail_refs, scratch = refs[: tails + 2 * (tails > 0)], refs[tails + 2 * (tails > 0) :]
    gathered, part, outb, inb = scratch[:4]
    sems = scratch[4:LINE]
    wg, wu, wd, gate, up, hidden, turned, w_sem = scratch[LINE : LINE + 8]
    abuf, fbuf, ftail = scratch[LINE + 8 : LINE + 11]
    operands = (
        (wd_ref, wd),
        (gate_ref, gate),
        (up_ref, up),
        (wg_ref, wg),
        (wu_ref, wu),
        (hidden_ref, hidden),
    )
    loads = [
        pltpu.make_async_copy(src, dst, w_sem.at[k]) for k, (src, dst) in enumerate(operands)
    ]
    for copy in loads:
        copy.start()

    def load():
        for copy in loads:
            copy.wait()

    reduce = Reduce(
        turned,
        (hidden, gate, up),
        (wd, wg, wu),
        abuf,
        fbuf,
        ftail,
        a_all,
        r_all,
        c_all,
        outs,
        late,
        scratch[LINE + 11 : LINE + 18],
    )
    tail = None
    if tails:
        tail = Tail(
            held[0],
            tail_refs[tails],
            tail_refs[tails + 1],
            tail_refs[:tails],
            abuf,
            fbuf,
            ftail,
            scratch[LINE + 18 :],
        )

    def finish(b):
        block = gathered[b]
        store_turned(block, turned, b)
        for start, width in spans(wg.shape[1]):
            at = slice(start, start + width)
            d = nn(block, wd[:, at])
            g = gate[b, :, at].astype(f32)
            u = up[b, :, at].astype(f32)
            sigma = lax.logistic(g)
            ds = d * sigma
            dg = (ds * u * (1.0 + g * (1.0 - sigma))).astype(bf16)
            du = (ds * g).astype(bf16)
            gate[b, :, at] = dg
            up[b, :, at] = du
            p = nt(dg, wg[:, at]) + nt(du, wu[:, at])
            if start == 0:
                part[...] = p
            else:
                part[...] += p

    def run(verb, m):
        if verb == "swap":
            copy = pltpu.make_async_copy(turned_ref, turned, w_sem.at[0])
            copy.start()
            copy.wait()
        elif verb == "kept":
            reduce.keep(m).wait()
        elif verb == "sent":
            for j, at in reduce.columns():
                reduce.swap(m, j, at).wait_send()
        else:
            getattr(reduce, verb)(m)

    def work(t):
        def act():
            if tail is not None and t == 1:
                for i in range(tails):
                    tail.close(i)
            for verb, m in AFTER[t]:
                run(verb, m)

        return act

    def each(verb):
        def act():
            for i in range(tails):
                getattr(tail, verb)(i)

        return act

    peers = [reduce.partner] + reduce.near
    plan = {("hop", t): work(t) for t in range(3)}
    if tails:
        for key, act in ((TAIL_BEGIN, each("begin")), (TAIL_MIDDLE, each("middle"))):
            old = plan.get(key)
            plan[key] = act if old is None else both(act, old)
    line_pass(grad_ref, sum_ref, gathered, part, outb, inb, sems, load, finish, peers, plan)
    for verb, m in LATE_END if late else WHOLE_END:
        run(verb, m)


def backward_ffn(grad, gate, up, hidden, turned, wg, wu, wd, late=False, held=None):
    rows, width = grad.shape
    devices, size, wide = lax.axis_size("gx"), lax.axis_size("gy"), wg.shape[1]
    near = 2 if devices == 8 else devices // 2 - 1
    r = width // devices
    mine = jax.ShapeDtypeStruct((r, wide), f32)

    def between(*dims):
        return jax.ShapeDtypeStruct(dims + (wide,), bf16)

    count = 1 if late else 3
    out = [jax.ShapeDtypeStruct((rows, width), f32)]
    out += [mine, between(2, width // 2)] if late else [mine] * 3
    out += [between(3, width // 2), between(count, 2, r // 2), between(count, near, r)]
    tails = 0 if held is None else held.shape[0]
    if tails:
        out += [mine] * tails
        out += [between(tails, 2, r // 2), between(tails, near, 2, r // 2)]
    extra = [held] if tails else []
    return pl.pallas_call(
        functools.partial(backward_kernel, (1, 2) if late else (), tails),
        out_shape=out,
        in_specs=[ANY] * (8 + len(extra)),
        out_specs=[pl.BlockSpec(memory_space=pltpu.VMEM)] + [ANY] * (len(out) - 1),
        scratch_shapes=line_scratch(size, rows, width)
        + [pltpu.VMEM((width, wide), bf16)] * 3
        + [pltpu.VMEM((size, rows, wide), bf16)] * 3
        + [pltpu.VMEM((2, width // 2, size * rows), bf16), pltpu.SemaphoreType.DMA((6,))]
        + reduce_scratch(width, wide)
        + (tail_scratch(tails) if tails else []),
        compiler_params=pltpu.CompilerParams(
            collective_id=1 if late else 5, has_side_effects=True, vmem_limit_bytes=VMEM_LIMIT
        ),
        cost_estimate=pl.CostEstimate(
            flops=12 * size * rows * width * wide, bytes_accessed=40 << 20, transcendentals=0
        ),
        name="ffn_backward",
    )(grad, gate, up, hidden, turned, wg, wu, wd, *extra)


class Fold:
    def __init__(self, lhs, rhs, bufs, sems):
        self.lhs, self.rhs = lhs, rhs
        self.up, self.low, self.a_in, self.r_in, self.c_in, self.z_out, self.z_in = bufs
        (
            self.a_send,
            self.a_recv,
            self.r_send,
            self.r_recv,
            self.c_send,
            self.c_recv,
            self.z_send,
            self.z_recv,
        ) = sems
        self.gx, self.gy = lax.axis_index("gx"), lax.axis_index("gy")
        self.core, self.size = lax.rem(self.gx, 2), lax.axis_size("gy")
        self.chips = lax.axis_size("gx") // 2
        self.r = self.low.shape[2] // self.chips
        self.four = self.chips == 4
        self.partner, self.others = places()
        self.near = list(square()[:2]) if self.four else self.others

    def product(self, m, which, z):
        return [nn(left[which], right[z]) for left, right in zip(self.lhs[m], self.rhs[m])]

    def remote(self, src, dst, send, recv, gx, gy):
        return pltpu.make_async_remote_copy(
            src_ref=src,
            dst_ref=dst,
            send_sem=send,
            recv_sem=recv,
            device_id=(gx, gy),
            device_id_type=MESH,
        )

    def block(self, m, device, start=0, size=None):
        size = self.r if size is None else size
        first = (device // 2) * self.r + start
        return self.low.at[m, :, pl.ds(pl.multiple_of(first, 16), size)]

    def swap(self, m, z):
        return self.remote(
            self.up.at[m, z],
            self.a_in.at[m, z],
            self.a_send.at[m, z],
            self.a_recv.at[m, z],
            self.partner,
            self.gy,
        )

    def first(self, m):
        for z in range(self.size):
            left, right = self.product(m, 1 - self.core, z)
            edge = left.shape[1]
            self.up[m, z, :, :edge] = left.astype(bf16)
            self.up[m, z, :, edge:] = right.astype(bf16)
            self.swap(m, z).start()

    def corner(self, m, h):
        side, along, across = square()
        half = self.r // 2
        return self.remote(
            self.block(m, across, h * half, half),
            self.r_in.at[m, h],
            self.r_send.at[m, h],
            self.r_recv.at[m, h],
            along if h else side,
            self.gy,
        )

    def second(self, m):
        for z in range(self.size):
            left, right = self.product(m, self.core, z)
            edge = left.shape[1]
            self.swap(m, z).wait_recv()
            came = self.a_in[m, z].astype(f32)
            self.low[m, z, :, :edge] = (left + came[:, :edge]).astype(bf16)
            self.low[m, z, :, edge:] = (right + came[:, edge:]).astype(bf16)
        if self.four:
            for h in range(2):
                self.corner(m, h).start()

    def hand(self, m, k):
        return self.remote(
            self.block(m, self.near[k]),
            self.c_in.at[m, k],
            self.c_send.at[m, k],
            self.c_recv.at[m, k],
            self.near[k],
            self.gy,
        )

    def third(self, m):
        if self.four:
            side, along, _ = square()
            half = self.r // 2
            for h, device in ((0, along), (1, side)):
                self.corner(m, h).wait_recv()
                here = self.block(m, device, h * half, half)
                here[...] = (here[...].astype(f32) + self.r_in[m, h].astype(f32)).astype(bf16)
        for k in range(len(self.near)):
            self.hand(m, k).start()

    def down_line(self, m, d):
        target = lax.rem(self.gy + d, self.size)
        return self.remote(
            self.z_out.at[m, target],
            self.z_in.at[m, self.gy],
            self.z_send.at[m, d],
            self.z_recv.at[m, self.gy],
            self.gx,
            target,
        )

    def fourth(self, m):
        for k in range(len(self.near)):
            self.hand(m, k).wait_recv()
        mine = self.block(m, self.gx)
        for z in range(self.size):
            total = mine[z].astype(f32)
            for k in range(len(self.near)):
                total = total + self.c_in[m, k, z].astype(f32)
            self.z_out[m, z] = total.astype(bf16)
        for d in range(1, self.size):
            self.down_line(m, d).start()

    def fifth(self, m, out):
        total = self.z_out[m, self.gy].astype(f32)
        for d in range(1, self.size):
            z = lax.rem(self.gy + d, self.size)
            wait_for(self.z_in.at[m, z], self.z_recv.at[m, z])
            total = total + self.z_in[m, z].astype(f32)
        out[m] = total

    def drain(self, m):
        for z in range(self.size):
            self.swap(m, z).wait_send()
        if self.four:
            for h in range(2):
                self.corner(m, h).wait_send()
        for k in range(len(self.near)):
            self.hand(m, k).wait_send()
        for d in range(1, self.size):
            self.down_line(m, d).wait_send()


class Total:
    def __init__(self, own, line_in, pair, pair_in, chip_in, sems):
        self.own, self.line_in, self.pair = own, line_in, pair
        self.pair_in, self.chip_in = pair_in, chip_in
        self.l_send, self.l_recv, self.p_send, self.p_recv, self.g_send, self.g_recv = sems
        self.gx, self.gy = lax.axis_index("gx"), lax.axis_index("gy")
        self.size, self.chips = lax.axis_size("gy"), lax.axis_size("gx") // 2
        self.partner, self.others = places()

    def remote(self, src, dst, send, recv, gx, gy):
        return pltpu.make_async_remote_copy(
            src_ref=src,
            dst_ref=dst,
            send_sem=send,
            recv_sem=recv,
            device_id=(gx, gy),
            device_id_type=MESH,
        )

    def line(self, d):
        target = lax.rem(self.gy + d, self.size)
        return self.remote(
            self.own.at[target],
            self.line_in.at[self.gy],
            self.l_send.at[d],
            self.l_recv.at[self.gy],
            self.gx,
            target,
        )

    def across(self):
        return self.remote(
            self.pair.at[0], self.pair_in, self.p_send, self.p_recv, self.partner, self.gy
        )

    def chip(self, k):
        return self.remote(
            self.pair.at[1],
            self.chip_in.at[self.gx // 2],
            self.g_send.at[k],
            self.g_recv.at[self.gx // 2],
            self.others[k],
            self.gy,
        )

    def begin(self):
        for d in range(1, self.size):
            self.line(d).start()

    def middle(self):
        total = self.own[self.gy]
        for d in range(1, self.size):
            z = lax.rem(self.gy + d, self.size)
            wait_for(self.line_in.at[z], self.l_recv.at[z])
            total = total + self.line_in[z]
        self.pair[0] = total
        self.across().start()

    def later(self):
        self.across().wait_recv()
        self.pair[1] = self.pair[0] + self.pair_in[...]
        self.chip_in[self.gx // 2] = self.pair[1]
        for k in range(self.chips - 1):
            self.chip(k).start()

    def close(self, out):
        for k in range(self.chips - 1):
            q = self.others[k] // 2
            wait_for(self.chip_in.at[q], self.g_recv.at[q])
        total = self.chip_in[0]
        for q in range(1, self.chips):
            total = total + self.chip_in[q]
        out[...] = total
        for d in range(1, self.size):
            self.line(d).wait_send()
        self.across().wait_send()
        for k in range(self.chips - 1):
            self.chip(k).wait_send()


def closing_kernel(layers, *refs):
    operands, refs = refs[: 4 * layers], refs[4 * layers :]
    small, out_rows, grad_rows = refs[:3]
    grads, small_out, out_blocks, grad_blocks = refs[3:7]
    scratch = refs[7:]
    lhs = [operands[4 * m : 4 * m + 2] for m in range(layers)]
    rhs = [operands[4 * m + 2 : 4 * m + 4] for m in range(layers)]
    fold = Fold(lhs, rhs, scratch[:7], scratch[7:15])
    total = Total(small, *scratch[15:19], scratch[19:25])
    swaps = [
        Exchange(own, full, scratch[25 + 3 * k : 28 + 3 * k], True)
        for k, (own, full) in enumerate(((grad_rows, grad_blocks), (out_rows, out_blocks)))
    ]
    me, size = lax.axis_index("gy"), lax.axis_size("gy")
    greet([fold.partner] + fold.others, [lax.rem(me + d, size) for d in range(1, size)])
    total.begin()
    for m in range(layers):
        fold.first(m)
    for swap in swaps:
        swap.begin()
    fold.second(0)
    total.middle()
    for m in range(1, layers):
        fold.second(m)
    total.later()
    for m in range(layers):
        fold.third(m)
    for m in range(layers):
        fold.fourth(m)
    total.close(small_out)
    for m in range(layers):
        fold.fifth(m, grads)
    for m in range(layers):
        fold.drain(m)
    for swap in swaps:
        swap.close()


def closing(operands, small, out_rows, grad_rows):
    layers = len(operands) // 4
    devices, size = lax.axis_size("gx"), lax.axis_size("gy")
    half = operands[0].shape[1]
    chips = devices // 2
    r, near = half // chips, 2 if chips == 4 else chips - 1
    c = operands[2].shape[2] + operands[3].shape[2]
    vmem, dma = pltpu.VMEM, pltpu.SemaphoreType.DMA
    row = small.shape[1:]
    local = pl.BlockSpec(memory_space=pltpu.VMEM)
    blocks = jax.ShapeDtypeStruct(out_rows.shape, bf16)
    return pl.pallas_call(
        functools.partial(closing_kernel, layers),
        out_shape=[
            jax.ShapeDtypeStruct((layers, r, c), f32),
            jax.ShapeDtypeStruct(row, f32),
            blocks,
            blocks,
        ],
        in_specs=[local] * (len(operands) + 1) + [ANY] * 2,
        out_specs=[local] * 2 + [ANY] * 2,
        scratch_shapes=[
            vmem((layers, size, half, c), bf16),
            vmem((layers, size, half, c), bf16),
            vmem((layers, size, half, c), bf16),
            vmem((layers, 2, size, r // 2, c), bf16),
            vmem((layers, near, size, r, c), bf16),
            vmem((layers, size, r, c), bf16),
            vmem((layers, size, r, c), bf16),
            dma((layers, size)),
            dma((layers, size)),
            dma((layers, 2)),
            dma((layers, 2)),
            dma((layers, near)),
            dma((layers, near)),
            dma((layers, size)),
            dma((layers, size)),
            vmem((size,) + row, f32),
            vmem((2,) + row, f32),
            vmem(row, f32),
            vmem((chips,) + row, f32),
            dma((size,)),
            dma((size,)),
            dma,
            dma,
            dma((chips,)),
            dma((chips,)),
        ]
        + exchange_scratch() * 2,
        compiler_params=pltpu.CompilerParams(
            collective_id=4, has_side_effects=True, vmem_limit_bytes=VMEM_LIMIT
        ),
        name="closing",
    )(*operands, small, out_rows, grad_rows)


def swing(value, cosine, turned_sine):
    return value * cosine + pltpu.roll(value, HEAD_DIM // 2, 1) * turned_sine


def tile_columns(value, tables):
    heads = value.shape[1] // HEAD_DIM
    parts = [swing(value[:, k * HEAD_DIM : (k + 1) * HEAD_DIM], *tables) for k in range(heads)]
    return jnp.concatenate(parts, axis=1)


def store_split(block, turned):
    width = block.shape[1]
    devices = lax.axis_size("gx")
    r = width // devices
    flipped = block.T
    for k in range(devices):
        q = k // 2
        turned[k % 2, q * r : (q + 1) * r] = flipped[k * r : (k + 1) * r]


def norm_pull(grad, normed, scale, gain):
    row = jnp.sum(grad * normed, axis=0, keepdims=True)
    scaled = grad * gain
    project = jnp.mean(scaled * normed, axis=1, keepdims=True)
    return row, scale * (scaled - normed * project)


def attention_pull_kernel(*refs):
    (grad, grad_ffn, norm_b, scale_b, gain_b, norm_a, scale_a, gain_a) = refs[:8]
    acts, q, k, v, lse, cosine, sine, qkv_ref, out_ref = refs[8:17]
    grad_out, grad_low, acts_turned, branch_turned, gqkv, small = refs[17:23]
    qkv, wout, heads, branch, dq, dk_sum, dv_sum, kv_out, kv_in, total = refs[23:33]
    w_sem, kv_send, kv_recv = refs[33:]
    gx, me, size = lax.axis_index("gx"), lax.axis_index("gy"), lax.axis_size("gy")
    count, rows = q.shape[0], k.shape[0]
    loads = [
        pltpu.make_async_copy(out_ref, wout, w_sem.at[0]),
        pltpu.make_async_copy(qkv_ref, qkv, w_sem.at[1]),
    ]
    for load in loads:
        load.start()
    greet([], [lax.rem(me + d, size) for d in range(1, size)])
    small[...] = jnp.zeros_like(small)
    row, pulled = norm_pull(grad_ffn[...], norm_b[...], scale_b[...], gain_b[...])
    small[1:2] = row
    branch[...] = grad[...] + pulled
    low = branch[...].astype(bf16)
    store_split(low, branch_turned)
    store_split(acts[...], acts_turned)
    loads[0].wait()
    cq = wout.shape[2]
    heads[...] = jnp.concatenate([nn(low, wout[z]) for z in range(size)], axis=1).astype(bf16)

    query = me * count + lax.broadcasted_iota(jnp.int32, (rows, count), 1)
    key = lax.broadcasted_iota(jnp.int32, (rows, count), 0)
    allowed = key <= query
    if rows > LEN:
        allowed = jnp.logical_and(allowed, key // LEN == query // LEN)
    factor = 1.0 / math.sqrt(HEAD_DIM)
    tables = (cosine[...], sine[...])

    def kv_copy(g, d):
        target = lax.rem(me + d, size)
        return pltpu.make_async_remote_copy(
            src_ref=kv_out.at[g, target],
            dst_ref=kv_in.at[g, me],
            send_sem=kv_send.at[g, d],
            recv_sem=kv_recv.at[g, me],
            device_id=(gx, target),
            device_id_type=MESH,
        )

    for g in range(KV_HEADS):
        span = slice(g * HEAD_DIM, (g + 1) * HEAD_DIM)
        kg, vg = k[:, span], v[:, span]
        turned_k = kg.T
        dk_sum[...] = jnp.zeros_like(dk_sum)
        dv_sum[...] = jnp.zeros_like(dv_sum)

        def head(i, carry):
            h = g * GROUP + i
            at = pl.ds(pl.multiple_of(h * HEAD_DIM, HEAD_DIM), HEAD_DIM)
            qh, dh = q[:, at], heads[:, at]
            scores = jnp.where(allowed, nt(kg, qh) * factor, -1e30)
            p = jnp.exp(scores - lse[pl.ds(h, 1), :])
            dp = nt(vg, dh)
            inner = jnp.sum(p * dp, axis=0, keepdims=True)
            ds = (p * (dp - inner)).astype(bf16)
            dv_sum[...] += nn(p.astype(bf16), dh)
            dk_sum[...] += nn(ds, qh)
            dq[:, at] = swing(nn(turned_k, ds).T * factor, *tables).astype(bf16)
            return carry

        lax.fori_loop(0, GROUP, head, 0)
        for z in range(size):
            at = slice(z * count, (z + 1) * count)
            kv_out[g, z, :, :HEAD_DIM] = (dk_sum[at] * factor).astype(bf16)
            kv_out[g, z, :, HEAD_DIM:] = dv_sum[at].astype(bf16)
        for d in range(1, size):
            kv_copy(g, d).start()

    loads[1].wait()
    apart = cq % HEAD_DIM == 0
    if apart:
        for z in range(size):
            p = nt(dq[:, z * cq : (z + 1) * cq], qkv[z, :, :cq])
            if z == 0:
                total[...] = p
            else:
                total[...] += p
    dks, dvs = [], []
    for g in range(KV_HEADS):
        summed = kv_out[g, me].astype(f32)
        for d in range(1, size):
            z = lax.rem(me + d, size)
            wait_for(kv_in.at[g, z], kv_recv.at[g, z])
            summed = summed + kv_in[g, z].astype(f32)
        dks.append(swing(summed[:, :HEAD_DIM], *tables).astype(bf16).astype(f32))
        dvs.append(summed[:, HEAD_DIM:].astype(bf16).astype(f32))
    dk, dv = jnp.concatenate(dks, axis=1), jnp.concatenate(dvs, axis=1)
    ck = dk.shape[1] // size
    for z in range(size):
        at = slice(z * ck, (z + 1) * ck)
        kv = jnp.concatenate([dk[:, at], dv[:, at]], axis=1)
        if apart:
            kv = kv.astype(bf16)
            gqkv[z, :, :cq] = dq[:, z * cq : (z + 1) * cq]
            gqkv[z, :, cq:] = kv
            total[...] += nt(kv, qkv[z, :, cq:])
        else:
            mine = dq[:, z * cq : (z + 1) * cq].astype(f32)
            gqkv[z] = jnp.concatenate([mine, kv], axis=1).astype(bf16)
            p = nt(gqkv[z], qkv[z])
            if z == 0:
                total[...] = p
            else:
                total[...] += p
    row, pulled = norm_pull(total[...], norm_a[...], scale_a[...], gain_a[...])
    small[0:1] = row
    small[2:3] = jnp.sum(dq[...].astype(f32), axis=0, keepdims=True)
    width = dk.shape[1]
    small[3:4, :width] = jnp.sum(dk, axis=0, keepdims=True)
    small[4:5, :width] = jnp.sum(dv, axis=0, keepdims=True)
    final = branch[...] + pulled
    grad_out[...] = final
    grad_low[...] = final.astype(bf16)
    for g in range(KV_HEADS):
        for d in range(1, size):
            kv_copy(g, d).wait_send()


def attention_pull(vectors, acts, q, k, v, lse, tables, qkv, wout):
    count, width = acts.shape
    size, rows = lax.axis_size("gy"), k.shape[0]
    local = pl.BlockSpec(memory_space=pltpu.VMEM)
    vmem, dma = pltpu.VMEM, pltpu.SemaphoreType.DMA
    turned = jax.ShapeDtypeStruct((2, width // 2, count), bf16)
    return pl.pallas_call(
        attention_pull_kernel,
        out_shape=[
            jax.ShapeDtypeStruct((count, width), f32),
            jax.ShapeDtypeStruct((count, width), bf16),
            turned,
            turned,
            jax.ShapeDtypeStruct((size, count, qkv.shape[2]), bf16),
            jax.ShapeDtypeStruct((8, width), f32),
        ],
        in_specs=[local] * 15 + [ANY] * 2,
        out_specs=[local] * 6,
        scratch_shapes=[
            vmem(qkv.shape, bf16),
            vmem(wout.shape, bf16),
            vmem((count, width), bf16),
            vmem((count, width), f32),
            vmem((count, width), bf16),
            vmem((rows, HEAD_DIM), f32),
            vmem((rows, HEAD_DIM), f32),
            vmem((KV_HEADS, size, count, 2 * HEAD_DIM), bf16),
            vmem((KV_HEADS, size, count, 2 * HEAD_DIM), bf16),
            vmem((count, width), f32),
            dma((2,)),
            dma((KV_HEADS, size)),
            dma((KV_HEADS, size)),
        ],
        compiler_params=pltpu.CompilerParams(
            collective_id=6, has_side_effects=True, vmem_limit_bytes=VMEM_LIMIT
        ),
        name="attention_pull",
    )(*vectors, acts, q, k, v, lse, *tables, qkv, wout)


def on_device(
    residual_in,
    w_query,
    w_key,
    w_value,
    b_query,
    b_key,
    b_value,
    w_output,
    gain_attn,
    gain_ffn,
    w_gate,
    w_up,
    w_down,
    cotangent,
):
    devices_y = lax.axis_size("gy")
    rows_tok = residual_in.shape[1]
    count = rows_tok // devices_y
    q_index = lax.axis_index("gy") * count + jnp.arange(count, dtype=jnp.int32)
    k_index = jnp.arange(rows_tok, dtype=jnp.int32)
    allowed = (q_index[:, None] // LEN == k_index[None, :] // LEN) & (
        k_index[None, :] <= q_index[:, None]
    )
    cosine, sine = rope_tables(q_index % LEN, HEAD_DIM)

    small = jnp.concatenate([gain_attn, gain_ffn, b_query, b_key, b_value], axis=1)
    small_sizes = [v.shape[1] for v in (gain_attn, gain_ffn, b_query, b_key, b_value)]
    small = jnp.pad(small.astype(f32), ((0, 8 - LAYERS), (0, 0)))
    lines = []
    for l in range(LAYERS):
        lines += [jnp.concatenate([w_query[l], w_key[l], w_value[l]], axis=1), w_output[l]]
    part_sizes = (w_query.shape[2], w_key.shape[2], w_value.shape[2])
    opened = opening(residual_in, cotangent, small, lines, w_gate, w_up, w_down)
    resid, cot, small = opened[:3]
    lines_next = opened[5:7]
    attn_full = [[w.reshape(devices_y, D, -1) for w in opened[7:9]], None]
    ffn_full = [[w.reshape(D, -1) for w in opened[9:]], None]
    small = small[:, :LAYERS].transpose(1, 0, 2)
    vectors, start = [], 0
    for size in small_sizes:
        vectors.append(small[:, :, start : start + size].reshape(LAYERS, -1))
        start += size
    gains_one, gains_two, bias_q, bias_k, bias_v = vectors

    resid = resid.reshape(D, count).astype(f32).T
    cot = cot.reshape(D, count)

    kept = []
    for l in range(LAYERS):
        w_qkv, w_out = attn_full[l]
        wg, wu, wd = ffn_full[l]
        normed_one, scale_one = rms_parts(resid)
        acts_one = (normed_one * gains_one[l]).astype(bf16)
        queries, keys, values = split_columns(
            jnp.stack([dot("td,dq->tq", acts_one, w_qkv[z]) for z in range(devices_y)], axis=1),
            part_sizes,
        )
        queries = queries + bias_q[l]
        keys = keys + bias_k[l]
        values = (values + bias_v[l]).astype(bf16)
        q_rot = rotate(queries.reshape(count, HEADS, HEAD_DIM), cosine, sine).astype(bf16)
        q_flat = q_rot.reshape(count, -1)
        q_rot = q_rot.reshape(count, KV_HEADS, GROUP, HEAD_DIM)
        k_rot = rotate(keys.reshape(count, KV_HEADS, HEAD_DIM), cosine, sine).astype(bf16)
        both = jnp.concatenate([k_rot.reshape(count, -1), values], axis=1)
        both = lax.all_gather(both, "gy", axis=0, tiled=True)
        half = both.shape[1] // 2
        k_rot = both[:, :half].reshape(rows_tok, KV_HEADS, HEAD_DIM)
        v_heads = both[:, half:].reshape(rows_tok, KV_HEADS, HEAD_DIM)
        scores = score_block(q_rot, k_rot, allowed)
        top = jnp.max(scores, axis=-1, keepdims=True)
        expo = jnp.exp(scores - top)
        total = jnp.sum(expo, axis=-1, keepdims=True)
        soft = (expo / total).astype(bf16)
        log_total = top + jnp.log(total)
        mixed = dot("kgqs,skd->qkgd", soft, v_heads).reshape(count, -1).astype(bf16)
        mixed = mixed.reshape(count, devices_y, -1)
        middle = resid
        for z in range(devices_y):
            middle = middle + dot("tq,dq->td", mixed[:, z], w_out[z])
        normed_two, scale_two = rms_parts(middle)
        acts_two = (normed_two * gains_two[l]).astype(bf16)
        if l == 0:
            shards = (*lines_next, w_gate, w_up, w_down)
            done = forward_ffn(acts_two, wg, wu, wd, shards)
            attn_full[1] = [w.reshape(devices_y, D, -1) for w in done[5:7]]
            ffn_full[1] = [w.reshape(D, -1) for w in done[7:]]
        else:
            done = forward_ffn(acts_two, wg, wu, wd)
        part, acts_two, gate, up, hidden = done[:5]
        kept.append(
            (
                normed_one,
                scale_one,
                acts_one,
                q_flat,
                both[:, :half],
                both[:, half:],
                log_total.reshape(HEADS, count),
                mixed,
                normed_two,
                scale_two,
                acts_two,
                gate,
                up,
                hidden,
            )
        )
        resid = middle + part

    grad = cot.astype(f32).T + 2.0 * penalty * resid
    grad_low = grad.astype(bf16)
    side = cosine[:, 0, : HEAD_DIM // 2], sine[:, 0, : HEAD_DIM // 2]
    tables = (
        jnp.concatenate([side[0], side[0]], axis=1),
        jnp.concatenate([side[1], -side[1]], axis=1),
    )
    attn_grads = [None] * LAYERS
    ffn_grads = [None] * LAYERS
    small_grads = [None] * LAYERS

    for l in reversed(range(LAYERS)):
        (
            normed_one,
            scale_one,
            acts_one,
            q_rot,
            k_rot,
            v_heads,
            log_total,
            mixed,
            normed_two,
            scale_two,
            acts_two,
            gate,
            up,
            hidden,
        ) = kept[l]
        w_qkv, w_out = attn_full[l]
        wg, wu, wd = ffn_full[l]
        operands = (grad_low, gate, up, hidden, acts_two, wg, wu, wd)
        if l == LAYERS - 1:
            done = backward_ffn(*operands, late=True)
            grad_down, held = done[1:3]
        else:
            done = backward_ffn(*operands, held=held)
            ffn_grads[l] = done[1:4]
            ffn_grads[l + 1] = [*done[7:9], grad_down]
        grad_acts_two = done[0]
        vectors = [grad, grad_acts_two, normed_two, scale_two, gains_two[l][None]]
        vectors += [normed_one, scale_one, gains_one[l][None]]
        done = attention_pull(
            vectors, acts_one, q_rot, k_rot, v_heads, log_total, tables, w_qkv, w_out
        )
        grad, grad_low = done[:2]
        attn_grads[l] = [*done[2:5], mixed.transpose(1, 0, 2)]
        rows = done[5]
        width = k_rot.shape[1]
        small_grads[l] = [
            v.reshape(devices_y, -1)
            for v in (rows[0], rows[1], rows[2], rows[3, :width], rows[4, :width])
        ]
    small = jnp.stack([jnp.concatenate(v, axis=1) for v in small_grads], axis=1)
    small = jnp.pad(small, ((0, 0), (0, 8 - LAYERS), (0, 0)))

    def to_rows(tokens_major):
        return tokens_major.astype(bf16).T.reshape(devices_y, -1, count)

    def from_blocks(blocks):
        return blocks.transpose(1, 0, 2).reshape(-1, rows_tok).astype(f32)

    attn_sums, small, output, grad_input = closing(
        attn_grads[0] + attn_grads[1], small, to_rows(resid), to_rows(grad_low)
    )
    small = small[:LAYERS]
    attn_out, start = [], 0
    for size in part_sizes + (w_output.shape[2],):
        attn_out.append(attn_sums[:, :, start : start + size])
        start += size
    small_out, start = [], 0
    for size in small_sizes:
        small_out.append(small[:, start : start + size])
        start += size

    def stack(parts, k):
        return jnp.stack([part[k] for part in parts])

    return (
        from_blocks(output),
        from_blocks(grad_input),
        attn_out[0],
        attn_out[1],
        attn_out[2],
        small_out[2],
        small_out[3],
        small_out[4],
        attn_out[3],
        small_out[0],
        small_out[1],
        stack(ffn_grads, 0),
        stack(ffn_grads, 1),
        stack(ffn_grads, 2),
    )


def solution(mesh):
    tokens = P("gy", "gx")
    weight = P(None, "gx", "gy")
    vector = P(None, "gy")
    return jax.shard_map(
        on_device,
        mesh=mesh,
        in_specs=(
            tokens,
            weight,
            weight,
            weight,
            vector,
            vector,
            vector,
            weight,
            vector,
            vector,
            weight,
            weight,
            weight,
            tokens,
        ),
        out_specs=(
            tokens,
            tokens,
            weight,
            weight,
            weight,
            vector,
            vector,
            vector,
            weight,
            vector,
            vector,
            weight,
            weight,
            weight,
        ),
        check_vma=False,
    )
```

```python
import functools
import math

import jax
import jax.numpy as jnp
from jax import lax
from jax.experimental import pallas as pl
from jax.experimental.pallas import tpu as pltpu
from jax.sharding import PartitionSpec as P

D = 1536
HEADS = 12
KV_HEADS = 2
HEAD_DIM = 128
LEN = 1024
LAYERS = 2
GROUP = HEADS // KV_HEADS

epsilon = 1e-06
rope_base = 1000000.0
penalty = 0.25
bf16 = jnp.bfloat16
f32 = jnp.float32
MESH = pl.DeviceIdType.MESH
VMEM_LIMIT = 62 << 20
ANY = pl.BlockSpec(memory_space=pl.ANY)


def rope_tables(positions, head_size):
    freqs = rope_base ** (-jnp.arange(0, head_size, 2).astype(f32) / head_size)
    angles = positions.astype(f32)[:, None] * freqs[None, :]
    cosine = jnp.cos(angles)
    sine_table = jnp.sin(angles)
    return (
        jnp.concatenate([cosine, cosine], -1),
        jnp.concatenate([sine_table, -sine_table], -1),
    )


def wait_for(ref, sem):
    pltpu.make_async_copy(ref, ref, sem).wait()


def places():
    gx, devices = lax.axis_index("gx"), lax.axis_size("gx")
    chips = devices // 2
    chip, core = gx // 2, lax.rem(gx, 2)
    partner = gx + 1 - 2 * core
    others = [lax.rem(chip + k, chips) * 2 + core for k in range(1, chips)]
    return partner, others


def square():
    gx = lax.axis_index("gx")
    chip, core = gx // 2, lax.rem(gx, 2)
    side = gx + 2 - 4 * lax.rem(chip, 2)
    along = gx + 4 - 8 * (chip // 2)
    return side, along, (3 - chip) * 2 + core


def spread_slots():
    chips = lax.axis_size("gx") // 2
    return 14 if chips == 4 else 2 * chips + 2 * (chips - 1)


def spread_scratch(count):
    devices = lax.axis_size("gx")
    return [
        pltpu.SemaphoreType.DMA((count,)),
        pltpu.SemaphoreType.DMA((count, spread_slots())),
        pltpu.SemaphoreType.DMA((count, devices, 2)),
    ]


def greet(gx_peers, gy_peers):
    gx, gy = lax.axis_index("gx"), lax.axis_index("gy")
    barrier = pltpu.get_barrier_semaphore()
    for peer in gx_peers:
        pl.semaphore_signal(barrier, inc=1, device_id=(peer, gy), device_id_type=MESH)
    for peer in gy_peers:
        pl.semaphore_signal(barrier, inc=1, device_id=(gx, peer), device_id_type=MESH)
    pl.semaphore_wait(barrier, len(gx_peers) + len(gy_peers))


class Spread:
    def __init__(self, items, sems):
        self.items, (self.local, self.send_sem, self.recv_sem) = items, sems
        self.partner, self.others = places()
        self.four = lax.axis_size("gx") // 2 == 4
        self.near = list(square()[:2]) if self.four else self.others

    def part(self, i, k, h):
        full = self.items[i][1]
        if len(full.shape) == 4:
            half = full.shape[0] // 2
            return full.at[pl.ds(h * half, half), k]
        half = full.shape[1] // 2
        return full.at[k, pl.ds(h * half, half)]

    def send(self, i, k, h, target, slot, first=False):
        here = self.part(i, k, h)
        half = here.shape[0]
        source = self.items[i][0].at[pl.ds(h * half, half)] if first else here
        pltpu.make_async_remote_copy(
            src_ref=source,
            dst_ref=here,
            send_sem=self.send_sem.at[i, slot],
            recv_sem=self.recv_sem.at[i, k, h],
            device_id=(target, lax.axis_index("gy")),
            device_id_type=MESH,
        ).start()

    def arrived(self, i, k, h):
        wait_for(self.part(i, k, h), self.recv_sem.at[i, k, h])

    def place(self, i):
        own, full = self.items[i]
        gx = lax.axis_index("gx")
        here = full.at[:, gx] if len(full.shape) == 4 else full.at[gx]
        return pltpu.make_async_copy(own, here, self.local.at[i])

    def begin(self, i):
        gx = lax.axis_index("gx")
        self.place(i).start()
        slot = 0
        for target in self.near + [self.partner]:
            for h in range(2):
                self.send(i, gx, h, target, slot, True)
                slot += 1

    def relay(self, i):
        slot = 2 * len(self.near) + 2
        if self.four:
            side, along, _ = square()
            steps = [(side, 0, along), (along, 1, side), (side, 1, None), (along, 0, None)]
        else:
            steps = [(k, h, None) for k in self.others for h in range(2)]
        for k, h, target in steps:
            self.arrived(i, k, h)
            for to in [self.partner] if target is None else [target, self.partner]:
                self.send(i, k, h, to, slot)
                slot += 1

    def finish(self, i):
        if self.four:
            for h in range(2):
                self.arrived(i, square()[2], h)
                self.send(i, square()[2], h, self.partner, 12 + h)

    def close(self, i):
        core = lax.rem(lax.axis_index("gx"), 2)
        for k in [self.partner] + [k + 1 - 2 * core for k in self.others]:
            for h in range(2):
                self.arrived(i, k, h)
        for slot in range(spread_slots()):
            wait_for(self.part(i, 0, 0), self.send_sem.at[i, slot])
        self.place(i).wait()


def line_order(t, me, last):
    short = jnp.minimum(me, last - me)
    near = jnp.where(lax.rem(t, 2) == 0, me - t // 2, me + (t + 1) // 2)
    far = jnp.where(me < last - me, me + (t - short), me - (t - short))
    return jnp.where(t <= 2 * short, near, far)


class Chain:
    def __init__(self, own, full, sems):
        self.own, self.full, (self.local, self.send_sem, self.recv_sem) = own, full, sems

    def copy(self, b, way, first=False):
        me = lax.axis_index("gy")
        return pltpu.make_async_remote_copy(
            src_ref=self.own if first else self.full.at[b],
            dst_ref=self.full.at[b],
            send_sem=self.send_sem.at[b, way],
            recv_sem=self.recv_sem.at[b],
            device_id=(lax.axis_index("gx"), me - 1 + 2 * way),
            device_id_type=MESH,
        )

    def each(self, b, act, first=False):
        me, last = lax.axis_index("gy"), lax.axis_size("gy") - 1

        @pl.when(jnp.logical_and(b <= me, me < last))
        def _():
            act(self.copy(b, 1, first))

        @pl.when(jnp.logical_and(b >= me, me > 0))
        def _():
            act(self.copy(b, 0, first))

    def begin(self):
        me = lax.axis_index("gy")
        self.place = pltpu.make_async_copy(self.own, self.full.at[me], self.local)
        self.place.start()
        self.each(me, lambda copy: copy.start(), True)

    def relay(self, t):
        b = line_order(t, lax.axis_index("gy"), lax.axis_size("gy") - 1)
        wait_for(self.full.at[b], self.recv_sem.at[b])
        self.each(b, lambda copy: copy.start())

    def close(self):
        self.place.wait()
        for b in range(lax.axis_size("gy")):
            self.each(b, lambda copy: copy.wait_send())


class Exchange:
    def __init__(self, own, full, sems, apart=False):
        self.own, self.full, (self.local, self.send_sem, self.recv_sem) = own, full, sems
        self.apart = apart

    def begin(self):
        gx, me, size = lax.axis_index("gx"), lax.axis_index("gy"), lax.axis_size("gy")
        width = self.full.shape[2]

        def columns(k):
            if self.apart:
                return self.own.at[k]
            return self.own.at[:, pl.ds(pl.multiple_of(k * width, width), width)]

        self.place = pltpu.make_async_copy(columns(me), self.full.at[me], self.local)
        self.place.start()
        self.sent = []
        for d in range(1, size):
            target = lax.rem(me + d, size)
            copy = pltpu.make_async_remote_copy(
                src_ref=columns(target),
                dst_ref=self.full.at[me],
                send_sem=self.send_sem.at[d],
                recv_sem=self.recv_sem.at[me],
                device_id=(gx, target),
                device_id_type=MESH,
            )
            copy.start()
            self.sent.append(copy)

    def close(self):
        me, size = lax.axis_index("gy"), lax.axis_size("gy")
        self.place.wait()
        for copy in self.sent:
            copy.wait_send()
        for d in range(1, size):
            k = lax.rem(me + d, size)
            wait_for(self.full.at[k], self.recv_sem.at[k])


def chain_scratch():
    size = lax.axis_size("gy")
    return [
        pltpu.SemaphoreType.DMA,
        pltpu.SemaphoreType.DMA((size, 2)),
        pltpu.SemaphoreType.DMA((size,)),
    ]


def exchange_scratch():
    size = lax.axis_size("gy")
    return [
        pltpu.SemaphoreType.DMA,
        pltpu.SemaphoreType.DMA((size,)),
        pltpu.SemaphoreType.DMA((size,)),
    ]


def opening_kernel(*refs):
    ins, outs, sems = refs[:10], refs[10:22], refs[22:]
    resid, cot, small, qkv_a, o_a, qkv_b, o_b, wg, wu, wd = ins
    resid_out, cot_out, small_out = outs[:3]
    lines, (qkv, o, gate, up, down) = outs[3:7], outs[7:]
    me, size = lax.axis_index("gy"), lax.axis_size("gy")
    owns = (qkv_a, o_a, qkv_b, o_b, small)
    chains = [
        Chain(own, full, sems[3 * k : 3 * k + 3])
        for k, (own, full) in enumerate(zip(owns, list(lines) + [small_out]))
    ]
    swaps = [
        Exchange(own, full, sems[15 + 3 * k : 18 + 3 * k])
        for k, (own, full) in enumerate(((resid, resid_out), (cot, cot_out)))
    ]
    items = [(lines[0], qkv), (lines[1], o), (wg.at[0], gate), (wu.at[0], up), (wd.at[0], down)]
    spread = Spread(items, sems[21:24])
    greet([spread.partner] + spread.near, [lax.rem(me + d, size) for d in range(1, size)])
    for k in (0, 1, 4):
        chains[k].begin()
    spread.begin(2)
    for t in range(1, size):
        chains[0].relay(t)
        chains[1].relay(t)
    chains[0].close()
    spread.begin(0)
    chains[1].close()
    spread.begin(1)
    swaps[0].begin()
    for t in range(1, size):
        chains[4].relay(t)
    spread.begin(3)
    chains[2].begin()
    chains[3].begin()
    spread.relay(2)
    for t in range(1, size):
        chains[2].relay(t)
        chains[3].relay(t)
    spread.begin(4)
    swaps[1].begin()
    for i in (0, 1):
        spread.relay(i)
    spread.finish(2)
    spread.relay(3)
    for i in (0, 1):
        spread.finish(i)
    spread.relay(4)
    for i in (3, 4):
        spread.finish(i)
    for i in range(5):
        spread.close(i)
    for part in chains[2:] + swaps:
        part.close()


def opening(resid, cot, small, lines, wg, wu, wd):
    devices, size = lax.axis_size("gx"), lax.axis_size("gy")
    count = resid.shape[1] // size

    def shape(*dims, kind=bf16):
        return jax.ShapeDtypeStruct(dims, kind)

    blocks = shape(size, resid.shape[0], count)
    weight = shape(devices, *wg.shape[1:])
    out = [blocks, blocks, shape(size, *small.shape, kind=f32)]
    out += [shape(size, *line.shape) for line in lines]
    out += [shape(size, devices, *line.shape) for line in lines[:2]] + [weight] * 3
    return pl.pallas_call(
        opening_kernel,
        out_shape=out,
        in_specs=[ANY] * 10,
        out_specs=[ANY] * 12,
        scratch_shapes=chain_scratch() * 5 + exchange_scratch() * 2 + spread_scratch(5),
        compiler_params=pltpu.CompilerParams(collective_id=2, has_side_effects=True),
        name="opening",
    )(resid, cot, small, *lines, wg, wu, wd)


FF_CHUNK = 512
PIECES = 4


def spans(total):
    return [(start, min(FF_CHUNK, total - start)) for start in range(0, total, FF_CHUNK)]


def nn(left, right):
    return lax.dot_general(left, right, (((1,), (0,)), ((), ())), preferred_element_type=f32)


def nt(left, right):
    return lax.dot_general(left, right, (((1,), (1,)), ((), ())), preferred_element_type=f32)


def line_pass(own_ref, own, gathered, part, outb, inb, sems, load, finish, peers=(), plan={}):
    own_sem, ag_send, ag_recv, rs_send, rs_recv = sems
    gx, me, size = lax.axis_index("gx"), lax.axis_index("gy"), lax.axis_size("gy")
    rows = own.shape[0]
    piece = rows // PIECES
    last = size - 1
    inner = jnp.logical_and(me > 0, me < last)

    first = pltpu.make_async_copy(own_ref, gathered.at[me], own_sem)
    first.start()
    barrier = pltpu.get_barrier_semaphore()

    @pl.when(me > 0)
    def _():
        pl.semaphore_signal(barrier, inc=1, device_id=(gx, me - 1), device_id_type=MESH)

    @pl.when(me < last)
    def _():
        pl.semaphore_signal(barrier, inc=1, device_id=(gx, me + 1), device_id_type=MESH)

    for peer in peers:
        pl.semaphore_signal(barrier, inc=1, device_id=(peer, me), device_id_type=MESH)
    pl.semaphore_wait(barrier, jnp.where(inner, 2, 1) + len(peers))
    first.wait()

    def planned(name, t):
        for (key, when), act in plan.items():
            if key == name:
                pl.when(t == when)(act)


    def gather_copy(b, s, way):
        here = gathered.at[b, pl.ds(s * piece, piece)]
        return pltpu.make_async_remote_copy(
            src_ref=here,
            dst_ref=here,
            send_sem=ag_send.at[b, way, s],
            recv_sem=ag_recv.at[b, s],
            device_id=(gx, me - 1 + 2 * way),
            device_id_type=MESH,
        )

    def sum_copy(b, s):
        towards = jnp.where(b > me, me + 1, me - 1)
        slot = jnp.where(jnp.logical_and(towards == b, me > b), size, b)
        return pltpu.make_async_remote_copy(
            src_ref=outb.at[b, pl.ds(s * piece, piece)],
            dst_ref=inb.at[slot, pl.ds(s * piece, piece)],
            send_sem=rs_send.at[b, s],
            recv_sem=rs_recv.at[slot, s],
            device_id=(gx, towards),
            device_id_type=MESH,
        )

    def sum_arrived(slot, s):
        here = inb.at[slot, pl.ds(s * piece, piece)]
        pltpu.make_async_copy(here, here, rs_recv.at[slot, s]).wait()

    def step(t, carry):
        b = line_order(t, me, last)
        for s in range(PIECES):

            @pl.when(t > 0)
            def _():
                gather_copy(b, s, 0).wait_recv()

            @pl.when(jnp.logical_and(b <= me, me < last))
            def _():
                gather_copy(b, s, 1).start()

            @pl.when(jnp.logical_and(b >= me, me > 0))
            def _():
                gather_copy(b, s, 0).start()

        @pl.when(t == 0)
        def _():
            load()

        planned("step", t)
        finish(b)

        @pl.when(b == me)
        def _():
            own[...] = part[...]

        @pl.when(b != me)
        def _():
            outb[b] = part[...].astype(bf16)

            @pl.when(jnp.logical_not(inner))
            def _():
                for s in range(PIECES):
                    sum_copy(b, s).start()

        return carry

    lax.fori_loop(0, size, step, 0)

    def relay(t, carry):
        above, below = last - me, me
        low = jnp.where(t < above, me + 1 + t, me - 1 - (t - above))
        high = jnp.where(t < below, me - 1 - t, me + 1 + (t - below))
        b = jnp.where(2 * me < size, low, high)
        planned("hop", t)

        @pl.when(inner)
        def _():
            for s in range(PIECES):
                at = pl.ds(s * piece, piece)
                sum_arrived(b, s)
                outb[b, at] = (outb[b, at].astype(f32) + inb[b, at].astype(f32)).astype(bf16)
                sum_copy(b, s).start()

        return carry

    lax.fori_loop(0, last, relay, 0)

    @pl.when(me > 0)
    def _():
        for s in range(PIECES):
            sum_arrived(me, s)
        own[...] += inb[me].astype(f32)

    @pl.when(me < last)
    def _():
        for s in range(PIECES):
            sum_arrived(size, s)
        own[...] += inb[size].astype(f32)

    def drain(b, carry):
        for s in range(PIECES):

            @pl.when(jnp.logical_and(b <= me, me < last))
            def _():
                gather_copy(b, s, 1).wait_send()

            @pl.when(jnp.logical_and(b >= me, me > 0))
            def _():
                gather_copy(b, s, 0).wait_send()

            @pl.when(b != me)
            def _():
                sum_copy(b, s).wait_send()

        return carry

    lax.fori_loop(0, size, drain, 0)


def line_scratch(size, rows, width):
    return [
        pltpu.VMEM((size, rows, width), bf16),
        pltpu.VMEM((rows, width), f32),
        pltpu.VMEM((size, rows, width), bf16),
        pltpu.VMEM((size + 1, rows, width), bf16),
        pltpu.SemaphoreType.DMA,
        pltpu.SemaphoreType.DMA((size, 2, PIECES)),
        pltpu.SemaphoreType.DMA((size, PIECES)),
        pltpu.SemaphoreType.DMA((size, PIECES)),
        pltpu.SemaphoreType.DMA((size + 1, PIECES)),
    ]


LINE = 9


ORDER = {
    ("step", 0): (("begin", 0), ("begin", 1)),
    ("step", 2): (("begin", 2),),
    ("hop", 0): (("relay", 0), ("relay", 1), ("relay", 2), ("begin", 3)),
    ("hop", 1): (("finish", 0), ("finish", 1), ("finish", 2), ("begin", 4)),
}
REST = (("relay", 3), ("relay", 4), ("finish", 3), ("finish", 4))


def schedule(spread):
    def run(steps):
        def act():
            for verb, i in steps:
                getattr(spread, verb)(i)

        return act

    plan = {key: run(steps) for key, steps in ORDER.items()}
    return plan, REST + tuple(("close", i) for i in range(len(spread.items)))


def forward_kernel(extra, *refs):
    acts_ref, wg_ref, wu_ref, wd_ref = refs[:4]
    shards, refs = refs[4 : 4 + extra], refs[4 + extra :]
    sum_ref, turned_ref, gate_ref, up_ref, hidden_ref = refs[:5]
    wholes, scratch = refs[5 : 5 + extra], refs[5 + extra :]
    gathered, part, outb, inb = scratch[:4]
    sems = scratch[4:LINE]
    wg, wu, wd, gate, up, hidden, turned, w_sem, out_sem = scratch[LINE : LINE + 9]
    peers, spread = [], None
    if extra:
        items = [(r if len(w.shape) == 4 else r.at[1], w) for r, w in zip(shards, wholes)]
        spread = Spread(items, scratch[LINE + 9 :])
        partner, others = places()
        peers = [partner] + (list(square()[:2]) if spread.four else others)

    plan, rest = schedule(spread) if extra else ({}, ())
    loads = [
        pltpu.make_async_copy(src, dst, w_sem.at[k])
        for k, (src, dst) in enumerate(((wg_ref, wg), (wu_ref, wu), (wd_ref, wd)))
    ]
    for copy in loads:
        copy.start()

    def load():
        for copy in loads:
            copy.wait()

    def results(b):
        pairs = ((gate, gate_ref), (up, up_ref), (hidden, hidden_ref))
        return [
            pltpu.make_async_copy(src.at[b], dst.at[b], out_sem.at[b, k])
            for k, (src, dst) in enumerate(pairs)
        ]

    def finish(b):
        block = gathered[b]
        store_turned(block, turned, b)
        for start, width in spans(wg.shape[1]):
            at = slice(start, start + width)
            g = nn(block, wg[:, at])
            u = nn(block, wu[:, at])
            h = (g * lax.logistic(g) * u).astype(bf16)
            gate[b, :, at] = g.astype(bf16)
            up[b, :, at] = u.astype(bf16)
            hidden[b, :, at] = h
            p = nt(h, wd[:, at])
            if start == 0:
                part[...] = p
            else:
                part[...] += p
        for copy in results(b):
            copy.start()

    line_pass(
        acts_ref, sum_ref, gathered, part, outb, inb, sems, load, finish, peers, plan
    )
    keep = pltpu.make_async_copy(turned, turned_ref, w_sem.at[0])
    keep.start()
    for act, i in rest:
        getattr(spread, act)(i)

    def settle(b, carry):
        for copy in results(b):
            copy.wait()
        return carry

    lax.fori_loop(0, gathered.shape[0], settle, 0)
    keep.wait()


def forward_ffn(acts, wg, wu, wd, shards=()):
    rows, width = acts.shape
    devices, size, hidden = lax.axis_size("gx"), lax.axis_size("gy"), wg.shape[1]
    wide = jax.ShapeDtypeStruct((size, rows, hidden), bf16)
    extra = len(shards)
    wholes = [
        jax.ShapeDtypeStruct(
            (size, devices) + s.shape[1:] if k < 2 else (devices,) + s.shape[1:], bf16
        )
        for k, s in enumerate(shards)
    ]
    return pl.pallas_call(
        functools.partial(forward_kernel, extra),
        out_shape=[
            jax.ShapeDtypeStruct((rows, width), f32),
            jax.ShapeDtypeStruct((2, width // 2, size * rows), bf16),
            wide,
            wide,
            wide,
        ]
        + wholes,
        in_specs=[ANY] * (4 + extra),
        out_specs=[pl.BlockSpec(memory_space=pltpu.VMEM)] + [ANY] * (4 + extra),
        scratch_shapes=line_scratch(size, rows, width)
        + [pltpu.VMEM((width, hidden), bf16)] * 3
        + [pltpu.VMEM((size, rows, hidden), bf16)] * 3
        + [pltpu.VMEM((2, width // 2, size * rows), bf16)]
        + [pltpu.SemaphoreType.DMA((3,)), pltpu.SemaphoreType.DMA((size, 3))]
        + (spread_scratch(extra) if extra else []),
        compiler_params=pltpu.CompilerParams(
            collective_id=3 if extra else 0, has_side_effects=True, vmem_limit_bytes=VMEM_LIMIT
        ),
        cost_estimate=pl.CostEstimate(
            flops=6 * size * rows * width * hidden, bytes_accessed=40 << 20, transcendentals=0
        ),
        name="ffn_forward",
    )(acts, wg, wu, wd, *shards)


class Reduce:
    def __init__(self, lhs, rhs, bufs, abuf, fbuf, ftail, a_all, r_all, c_all, outs, late, sems):
        self.late = late
        self.lhs, self.rhs, self.bufs, self.outs = lhs, rhs, bufs, outs
        self.abuf, self.fbuf, self.ftail = abuf, fbuf, ftail
        self.a_all, self.r_all, self.c_all = a_all, r_all, c_all
        (
            self.a_send,
            self.a_recv,
            self.r_send,
            self.r_recv,
            self.c_send,
            self.c_recv,
            self.local,
        ) = sems
        gx, self.gy = lax.axis_index("gx"), lax.axis_index("gy")
        self.chip, self.core = gx // 2, lax.rem(gx, 2)
        self.chips = lax.axis_size("gx") // 2
        self.half, self.wide = bufs[0].shape[0] // 2, bufs[0].shape[1]
        self.r = self.half // self.chips
        self.four = self.chips == 4
        self.partner, self.others = places()
        self.near = list(square()[:2]) if self.four else self.others

    def product(self, m, which, at):
        z, n, _ = self.rhs[m].shape
        right = self.rhs[m][:, :, at].reshape(z * n, at.stop - at.start)
        return nn(self.lhs[which], right)

    def remote(self, src, dst, send, recv, target):
        return pltpu.make_async_remote_copy(
            src_ref=src,
            dst_ref=dst,
            send_sem=send,
            recv_sem=recv,
            device_id=(target, self.gy),
            device_id_type=MESH,
        )

    def columns(self):
        return [(j, slice(s, s + w)) for j, (s, w) in enumerate(spans(self.wide))]

    def swap(self, m, j, at):
        here = (slice(0, self.half), at)
        return self.remote(
            self.bufs[m].at[here],
            self.a_all.at[m, :, at],
            self.a_send.at[m, j],
            self.a_recv.at[m, j],
            self.partner,
        )

    def block(self, m, device, start=0, size=None):
        size = self.r if size is None else size
        first = self.half + (device // 2) * self.r + start
        return self.bufs[m].at[pl.ds(pl.multiple_of(first, 16), size)]

    def first(self, m):
        for j, at in self.columns():
            self.bufs[m][: self.half, at] = self.product(m, 1 - self.core, at).astype(bf16)
            self.swap(m, j, at).start()

    def corner(self, m, h):
        side, along, across = square()
        half = self.r // 2
        return self.remote(
            self.block(m, across, h * half, half),
            self.r_all.at[m, h],
            self.r_send.at[m, h],
            self.r_recv.at[m, h],
            along if h else side,
        )

    def second(self, m):
        for j, at in self.columns():
            self.swap(m, j, at).wait_recv()
            landed = self.abuf.at[:, at]
            fetch = pltpu.make_async_copy(self.a_all.at[m, :, at], landed, self.local.at[0])
            fetch.start()
            mine = self.product(m, self.core, at)
            fetch.wait()
            self.bufs[m][self.half :, at] = (mine + landed[...].astype(f32)).astype(bf16)
        if m in self.late:
            self.keep(m).start()
        elif self.four:
            for h in range(2):
                self.corner(m, h).start()

    def keep(self, m):
        kept = self.outs[m]
        return pltpu.make_async_copy(
            self.bufs[m].at[pl.ds(self.half, self.half)], kept, self.local.at[max(len(self.near), 2)]
        )

    def hand(self, m, k):
        target = self.near[k]
        return self.remote(
            self.block(m, target),
            self.c_all.at[m, k],
            self.c_send.at[m, k],
            self.c_recv.at[m, k],
            target,
        )

    def third(self, m):
        if self.four:
            side, along, _ = square()
            half = self.r // 2
            for h, device in ((0, along), (1, side)):
                self.corner(m, h).wait_recv()
                here = self.block(m, device, h * half, half)
                landed = self.abuf.at[h * half : (h + 1) * half]
                fetch = pltpu.make_async_copy(self.r_all.at[m, h], landed, self.local.at[0])
                fetch.start()
                fetch.wait()
                here[...] = (here[...].astype(f32) + landed[...].astype(f32)).astype(bf16)
        for k in range(len(self.near)):
            self.hand(m, k).start()

    def fourth(self, m):
        for j, at in self.columns():
            self.swap(m, j, at).wait_send()
        fetches = []
        for k in range(len(self.near)):
            self.hand(m, k).wait_recv()
            here = self.bufs[m].at[pl.ds(k * self.r, self.r)]
            fetch = pltpu.make_async_copy(self.c_all.at[m, k], here, self.local.at[k])
            fetch.start()
            fetches.append(fetch)
        for fetch in fetches:
            fetch.wait()
        first = pl.multiple_of(self.half + self.chip * self.r, 16)
        for _, at in self.columns():
            total = self.bufs[m][pl.ds(first, self.r), at].astype(f32)
            for k in range(len(self.near)):
                total = total + self.bufs[m][k * self.r : (k + 1) * self.r, at].astype(f32)
            stage = self.fbuf if total.shape[1] == FF_CHUNK else self.ftail
            stage[...] = total
            store = pltpu.make_async_copy(stage, self.outs[m].at[:, at], self.local.at[0])
            store.start()
            store.wait()

    def drain(self, m):
        if self.four:
            for h in range(2):
                self.corner(m, h).wait_send()
        for k in range(len(self.near)):
            self.hand(m, k).wait_send()


def reduce_scratch(width, hidden, count=3):
    devices = lax.axis_size("gx")
    rows, parts = width // devices, len(spans(hidden))
    near = 2 if devices == 8 else devices // 2 - 1
    dma = pltpu.SemaphoreType.DMA
    return [
        pltpu.VMEM((width // 2, hidden), bf16),
        pltpu.VMEM((rows, FF_CHUNK), f32),
        pltpu.VMEM((rows, hidden % FF_CHUNK), f32),
        dma((count, parts)),
        dma((count, parts)),
        dma((count, 2)),
        dma((count, 2)),
        dma((count, near)),
        dma((count, near)),
        dma((max(near, 2) + 1,)),
    ]


class Tail:
    def __init__(self, b_all, r_all, c_all, outs, abuf, fbuf, ftail, sems):
        self.b_all, self.r_all, self.c_all, self.outs = b_all, r_all, c_all, outs
        self.abuf, self.fbuf, self.ftail = abuf, fbuf, ftail
        self.r_send, self.r_recv, self.c_send, self.c_recv, self.local = sems
        gx, self.gy = lax.axis_index("gx"), lax.axis_index("gy")
        self.chip, chips = gx // 2, lax.axis_size("gx") // 2
        self.r = b_all.shape[1] // chips
        self.part = self.r // 2
        self.space = b_all.shape[1] // b_all.shape[0]
        self.four = chips == 4
        self.near = list(square()[:2]) if self.four else places()[1]

    def remote(self, src, dst, send, recv, target):
        return pltpu.make_async_remote_copy(
            src_ref=src,
            dst_ref=dst,
            send_sem=send,
            recv_sem=recv,
            device_id=(target, self.gy),
            device_id_type=MESH,
        )

    def held(self, i, chip, h):
        first = pl.multiple_of(chip * self.r + h * self.part, 16)
        return self.b_all.at[i, pl.ds(first, self.part)]

    def slot(self, i, k):
        return self.abuf.at[pl.ds(i * self.space + k * self.part, self.part)]

    def corner(self, i, h):
        side, along, across = square()
        return self.remote(
            self.held(i, across // 2, h),
            self.r_all.at[i, h],
            self.r_send.at[i, h],
            self.r_recv.at[i, h],
            along if h else side,
        )

    def hand(self, i, k, h):
        target = self.near[k]
        summed = self.four and k != h
        return self.remote(
            self.slot(i, 2 + h) if summed else self.held(i, target // 2, h),
            self.c_all.at[i, k, h],
            self.c_send.at[i, k, h],
            self.c_recv.at[i, k, h],
            target,
        )

    def hands(self):
        return [(k, h) for k in range(len(self.near)) for h in range(2)]

    def begin(self, i):
        if self.four:
            for h in range(2):
                self.corner(i, h).start()

    def middle(self, i):
        if self.four:
            side, along, _ = square()
            for h, device in ((0, along), (1, side)):
                self.corner(i, h).wait_recv()
                came, mine = self.slot(i, h), self.slot(i, 2 + h)
                fetches = [
                    pltpu.make_async_copy(self.r_all.at[i, h], came, self.local.at[0]),
                    pltpu.make_async_copy(self.held(i, device // 2, h), mine, self.local.at[1]),
                ]
                for fetch in fetches:
                    fetch.start()
                for fetch in fetches:
                    fetch.wait()
                mine[...] = (mine[...].astype(f32) + came[...].astype(f32)).astype(bf16)
        for k, h in self.hands():
            self.hand(i, k, h).start()

    def close(self, i):
        if self.four:
            for h in range(2):
                self.corner(i, h).wait_send()
        for k, h in self.hands():
            self.hand(i, k, h).wait_send()
        count = len(self.near)
        for h in range(2):
            fetches = [
                pltpu.make_async_copy(
                    self.held(i, self.chip, h), self.slot(i, count), self.local.at[count]
                )
            ]
            for k in range(count):
                self.hand(i, k, h).wait_recv()
                fetches.append(
                    pltpu.make_async_copy(
                        self.c_all.at[i, k, h], self.slot(i, k), self.local.at[k]
                    )
                )
            for fetch in fetches:
                fetch.start()
            for fetch in fetches:
                fetch.wait()
            for start, width in spans(self.abuf.shape[1]):
                at = slice(start, start + width)
                total = self.slot(i, 0)[:, at].astype(f32)
                for k in range(1, count + 1):
                    total = total + self.slot(i, k)[:, at].astype(f32)
                stage = self.fbuf if width == FF_CHUNK else self.ftail
                stage[: self.part] = total
                store = pltpu.make_async_copy(
                    stage.at[pl.ds(0, self.part)],
                    self.outs[i].at[pl.ds(h * self.part, self.part), at],
                    self.local.at[0],
                )
                store.start()
                store.wait()


def tail_scratch(count):
    devices = lax.axis_size("gx")
    near = 2 if devices == 8 else devices // 2 - 1
    dma = pltpu.SemaphoreType.DMA
    return [
        dma((count, 2)),
        dma((count, 2)),
        dma((count, near, 2)),
        dma((count, near, 2)),
        dma((near + 1,)),
    ]


def store_turned(block, turned, b):
    count, width = block.shape
    _, chips_rows, _ = turned.shape
    devices = lax.axis_size("gx")
    r = width // devices
    flipped = block.T
    at = pl.ds(pl.multiple_of(b * count, count), count)
    for k in range(devices):
        q = k // 2
        turned[k % 2, q * r : (q + 1) * r, at] = flipped[k * r : (k + 1) * r]


AFTER = {
    0: (("first", 0),),
    1: (("second", 0), ("swap", 0), ("first", 1)),
    2: (("third", 0), ("second", 1)),
}
WHOLE_END = (("first", 2), ("third", 1), ("second", 2), ("fourth", 0), ("third", 2))
WHOLE_END += (("fourth", 1), ("fourth", 2), ("drain", 0), ("drain", 1), ("drain", 2))
LATE_END = (("kept", 1), ("first", 2), ("second", 2), ("fourth", 0), ("kept", 2))
LATE_END += (("sent", 1), ("sent", 2), ("drain", 0))


TAIL_BEGIN, TAIL_MIDDLE = ("step", 0), ("step", 2)


def both(one, other):
    def act():
        one()
        other()

    return act


def backward_kernel(late, tails, *refs):
    grad_ref, gate_ref, up_ref, hidden_ref, turned_ref, wg_ref, wu_ref, wd_ref = refs[:8]
    held, refs = refs[8 : 8 + (tails > 0)], refs[8 + (tails > 0) :]
    sum_ref, refs = refs[0], refs[1:]
    if late:
        od, b_all, a_all, r_all, c_all = refs[:5]
        outs, refs = (od, b_all.at[0], b_all.at[1]), refs[5:]
    else:
        og, ou, od, a_all, r_all, c_all = refs[:6]
        outs, refs = (od, og, ou), refs[6:]
    tail_refs, scratch = refs[: tails + 2 * (tails > 0)], refs[tails + 2 * (tails > 0) :]
    gathered, part, outb, inb = scratch[:4]
    sems = scratch[4:LINE]
    wg, wu, wd, gate, up, hidden, turned, w_sem = scratch[LINE : LINE + 8]
    abuf, fbuf, ftail = scratch[LINE + 8 : LINE + 11]
    operands = (
        (wd_ref, wd),
        (gate_ref, gate),
        (up_ref, up),
        (wg_ref, wg),
        (wu_ref, wu),
        (hidden_ref, hidden),
    )
    loads = [
        pltpu.make_async_copy(src, dst, w_sem.at[k]) for k, (src, dst) in enumerate(operands)
    ]
    for copy in loads:
        copy.start()

    def load():
        for copy in loads:
            copy.wait()

    reduce = Reduce(
        turned,
        (hidden, gate, up),
        (wd, wg, wu),
        abuf,
        fbuf,
        ftail,
        a_all,
        r_all,
        c_all,
        outs,
        late,
        scratch[LINE + 11 : LINE + 18],
    )
    tail = None
    if tails:
        tail = Tail(
            held[0],
            tail_refs[tails],
            tail_refs[tails + 1],
            tail_refs[:tails],
            abuf,
            fbuf,
            ftail,
            scratch[LINE + 18 :],
        )

    def finish(b):
        block = gathered[b]
        store_turned(block, turned, b)
        for start, width in spans(wg.shape[1]):
            at = slice(start, start + width)
            d = nn(block, wd[:, at])
            g = gate[b, :, at].astype(f32)
            u = up[b, :, at].astype(f32)
            sigma = lax.logistic(g)
            ds = d * sigma
            dg = (ds * u * (1.0 + g * (1.0 - sigma))).astype(bf16)
            du = (ds * g).astype(bf16)
            gate[b, :, at] = dg
            up[b, :, at] = du
            p = nt(dg, wg[:, at]) + nt(du, wu[:, at])
            if start == 0:
                part[...] = p
            else:
                part[...] += p

    def run(verb, m):
        if verb == "swap":
            copy = pltpu.make_async_copy(turned_ref, turned, w_sem.at[0])
            copy.start()
            copy.wait()
        elif verb == "kept":
            reduce.keep(m).wait()
        elif verb == "sent":
            for j, at in reduce.columns():
                reduce.swap(m, j, at).wait_send()
        else:
            getattr(reduce, verb)(m)

    def work(t):
        def act():
            if tail is not None and t == 1:
                for i in range(tails):
                    tail.close(i)
            for verb, m in AFTER[t]:
                run(verb, m)

        return act

    def each(verb):
        def act():
            for i in range(tails):
                getattr(tail, verb)(i)

        return act

    peers = [reduce.partner] + reduce.near
    plan = {("hop", t): work(t) for t in range(3)}
    if tails:
        for key, act in ((TAIL_BEGIN, each("begin")), (TAIL_MIDDLE, each("middle"))):
            old = plan.get(key)
            plan[key] = act if old is None else both(act, old)
    line_pass(grad_ref, sum_ref, gathered, part, outb, inb, sems, load, finish, peers, plan)
    for verb, m in LATE_END if late else WHOLE_END:
        run(verb, m)


def backward_ffn(grad, gate, up, hidden, turned, wg, wu, wd, late=False, held=None):
    rows, width = grad.shape
    devices, size, wide = lax.axis_size("gx"), lax.axis_size("gy"), wg.shape[1]
    near = 2 if devices == 8 else devices // 2 - 1
    r = width // devices
    mine = jax.ShapeDtypeStruct((r, wide), f32)

    def between(*dims):
        return jax.ShapeDtypeStruct(dims + (wide,), bf16)

    count = 1 if late else 3
    out = [jax.ShapeDtypeStruct((rows, width), f32)]
    out += [mine, between(2, width // 2)] if late else [mine] * 3
    out += [between(3, width // 2), between(count, 2, r // 2), between(count, near, r)]
    tails = 0 if held is None else held.shape[0]
    if tails:
        out += [mine] * tails
        out += [between(tails, 2, r // 2), between(tails, near, 2, r // 2)]
    extra = [held] if tails else []
    return pl.pallas_call(
        functools.partial(backward_kernel, (1, 2) if late else (), tails),
        out_shape=out,
        in_specs=[ANY] * (8 + len(extra)),
        out_specs=[pl.BlockSpec(memory_space=pltpu.VMEM)] + [ANY] * (len(out) - 1),
        scratch_shapes=line_scratch(size, rows, width)
        + [pltpu.VMEM((width, wide), bf16)] * 3
        + [pltpu.VMEM((size, rows, wide), bf16)] * 3
        + [pltpu.VMEM((2, width // 2, size * rows), bf16), pltpu.SemaphoreType.DMA((6,))]
        + reduce_scratch(width, wide)
        + (tail_scratch(tails) if tails else []),
        compiler_params=pltpu.CompilerParams(
            collective_id=1 if late else 5, has_side_effects=True, vmem_limit_bytes=VMEM_LIMIT
        ),
        cost_estimate=pl.CostEstimate(
            flops=12 * size * rows * width * wide, bytes_accessed=40 << 20, transcendentals=0
        ),
        name="ffn_backward",
    )(grad, gate, up, hidden, turned, wg, wu, wd, *extra)


class Fold:
    def __init__(self, lhs, rhs, bufs, sems):
        self.lhs, self.rhs = lhs, rhs
        self.up, self.low, self.a_in, self.r_in, self.c_in, self.z_out, self.z_in = bufs
        (
            self.a_send,
            self.a_recv,
            self.r_send,
            self.r_recv,
            self.c_send,
            self.c_recv,
            self.z_send,
            self.z_recv,
        ) = sems
        self.gx, self.gy = lax.axis_index("gx"), lax.axis_index("gy")
        self.core, self.size = lax.rem(self.gx, 2), lax.axis_size("gy")
        self.chips = lax.axis_size("gx") // 2
        self.r = self.low.shape[2] // self.chips
        self.four = self.chips == 4
        self.partner, self.others = places()
        self.near = list(square()[:2]) if self.four else self.others

    def product(self, m, which, z):
        return [nn(left[which], right[z]) for left, right in zip(self.lhs[m], self.rhs[m])]

    def remote(self, src, dst, send, recv, gx, gy):
        return pltpu.make_async_remote_copy(
            src_ref=src,
            dst_ref=dst,
            send_sem=send,
            recv_sem=recv,
            device_id=(gx, gy),
            device_id_type=MESH,
        )

    def block(self, m, device, start=0, size=None):
        size = self.r if size is None else size
        first = (device // 2) * self.r + start
        return self.low.at[m, :, pl.ds(pl.multiple_of(first, 16), size)]

    def swap(self, m, z):
        return self.remote(
            self.up.at[m, z],
            self.a_in.at[m, z],
            self.a_send.at[m, z],
            self.a_recv.at[m, z],
            self.partner,
            self.gy,
        )

    def first(self, m):
        for z in range(self.size):
            left, right = self.product(m, 1 - self.core, z)
            edge = left.shape[1]
            self.up[m, z, :, :edge] = left.astype(bf16)
            self.up[m, z, :, edge:] = right.astype(bf16)
            self.swap(m, z).start()

    def corner(self, m, h):
        side, along, across = square()
        half = self.r // 2
        return self.remote(
            self.block(m, across, h * half, half),
            self.r_in.at[m, h],
            self.r_send.at[m, h],
            self.r_recv.at[m, h],
            along if h else side,
            self.gy,
        )

    def second(self, m):
        for z in range(self.size):
            left, right = self.product(m, self.core, z)
            edge = left.shape[1]
            self.swap(m, z).wait_recv()
            came = self.a_in[m, z].astype(f32)
            self.low[m, z, :, :edge] = (left + came[:, :edge]).astype(bf16)
            self.low[m, z, :, edge:] = (right + came[:, edge:]).astype(bf16)
        if self.four:
            for h in range(2):
                self.corner(m, h).start()

    def hand(self, m, k):
        return self.remote(
            self.block(m, self.near[k]),
            self.c_in.at[m, k],
            self.c_send.at[m, k],
            self.c_recv.at[m, k],
            self.near[k],
            self.gy,
        )

    def third(self, m):
        if self.four:
            side, along, _ = square()
            half = self.r // 2
            for h, device in ((0, along), (1, side)):
                self.corner(m, h).wait_recv()
                here = self.block(m, device, h * half, half)
                here[...] = (here[...].astype(f32) + self.r_in[m, h].astype(f32)).astype(bf16)
        for k in range(len(self.near)):
            self.hand(m, k).start()

    def down_line(self, m, d):
        target = lax.rem(self.gy + d, self.size)
        return self.remote(
            self.z_out.at[m, target],
            self.z_in.at[m, self.gy],
            self.z_send.at[m, d],
            self.z_recv.at[m, self.gy],
            self.gx,
            target,
        )

    def fourth(self, m):
        for k in range(len(self.near)):
            self.hand(m, k).wait_recv()
        mine = self.block(m, self.gx)
        for z in range(self.size):
            total = mine[z].astype(f32)
            for k in range(len(self.near)):
                total = total + self.c_in[m, k, z].astype(f32)
            self.z_out[m, z] = total.astype(bf16)
        for d in range(1, self.size):
            self.down_line(m, d).start()

    def fifth(self, m, out):
        total = self.z_out[m, self.gy].astype(f32)
        for d in range(1, self.size):
            z = lax.rem(self.gy + d, self.size)
            wait_for(self.z_in.at[m, z], self.z_recv.at[m, z])
            total = total + self.z_in[m, z].astype(f32)
        out[m] = total

    def drain(self, m):
        for z in range(self.size):
            self.swap(m, z).wait_send()
        if self.four:
            for h in range(2):
                self.corner(m, h).wait_send()
        for k in range(len(self.near)):
            self.hand(m, k).wait_send()
        for d in range(1, self.size):
            self.down_line(m, d).wait_send()


class Total:
    def __init__(self, own, line_in, pair, pair_in, chip_in, sems):
        self.own, self.line_in, self.pair = own, line_in, pair
        self.pair_in, self.chip_in = pair_in, chip_in
        self.l_send, self.l_recv, self.p_send, self.p_recv, self.g_send, self.g_recv = sems
        self.gx, self.gy = lax.axis_index("gx"), lax.axis_index("gy")
        self.size, self.chips = lax.axis_size("gy"), lax.axis_size("gx") // 2
        self.partner, self.others = places()

    def remote(self, src, dst, send, recv, gx, gy):
        return pltpu.make_async_remote_copy(
            src_ref=src,
            dst_ref=dst,
            send_sem=send,
            recv_sem=recv,
            device_id=(gx, gy),
            device_id_type=MESH,
        )

    def line(self, d):
        target = lax.rem(self.gy + d, self.size)
        return self.remote(
            self.own.at[target],
            self.line_in.at[self.gy],
            self.l_send.at[d],
            self.l_recv.at[self.gy],
            self.gx,
            target,
        )

    def across(self):
        return self.remote(
            self.pair.at[0], self.pair_in, self.p_send, self.p_recv, self.partner, self.gy
        )

    def chip(self, k):
        return self.remote(
            self.pair.at[1],
            self.chip_in.at[self.gx // 2],
            self.g_send.at[k],
            self.g_recv.at[self.gx // 2],
            self.others[k],
            self.gy,
        )

    def begin(self):
        for d in range(1, self.size):
            self.line(d).start()

    def middle(self):
        total = self.own[self.gy]
        for d in range(1, self.size):
            z = lax.rem(self.gy + d, self.size)
            wait_for(self.line_in.at[z], self.l_recv.at[z])
            total = total + self.line_in[z]
        self.pair[0] = total
        self.across().start()

    def later(self):
        self.across().wait_recv()
        self.pair[1] = self.pair[0] + self.pair_in[...]
        self.chip_in[self.gx // 2] = self.pair[1]
        for k in range(self.chips - 1):
            self.chip(k).start()

    def close(self, out):
        for k in range(self.chips - 1):
            q = self.others[k] // 2
            wait_for(self.chip_in.at[q], self.g_recv.at[q])
        total = self.chip_in[0]
        for q in range(1, self.chips):
            total = total + self.chip_in[q]
        out[...] = total
        for d in range(1, self.size):
            self.line(d).wait_send()
        self.across().wait_send()
        for k in range(self.chips - 1):
            self.chip(k).wait_send()


def closing_kernel(layers, *refs):
    operands, refs = refs[: 4 * layers], refs[4 * layers :]
    small, out_rows, grad_rows = refs[:3]
    grads, small_out, out_blocks, grad_blocks = refs[3:7]
    scratch = refs[7:]
    lhs = [operands[4 * m : 4 * m + 2] for m in range(layers)]
    rhs = [operands[4 * m + 2 : 4 * m + 4] for m in range(layers)]
    fold = Fold(lhs, rhs, scratch[:7], scratch[7:15])
    total = Total(small, *scratch[15:19], scratch[19:25])
    swaps = [
        Exchange(own, full, scratch[25 + 3 * k : 28 + 3 * k], True)
        for k, (own, full) in enumerate(((grad_rows, grad_blocks), (out_rows, out_blocks)))
    ]
    me, size = lax.axis_index("gy"), lax.axis_size("gy")
    greet([fold.partner] + fold.others, [lax.rem(me + d, size) for d in range(1, size)])
    total.begin()
    for m in range(layers):
        fold.first(m)
    for swap in swaps:
        swap.begin()
    fold.second(0)
    total.middle()
    for m in range(1, layers):
        fold.second(m)
    total.later()
    for m in range(layers):
        fold.third(m)
    for m in range(layers):
        fold.fourth(m)
    total.close(small_out)
    for m in range(layers):
        fold.fifth(m, grads)
    for m in range(layers):
        fold.drain(m)
    for swap in swaps:
        swap.close()


def closing(operands, small, out_rows, grad_rows):
    layers = len(operands) // 4
    devices, size = lax.axis_size("gx"), lax.axis_size("gy")
    half = operands[0].shape[1]
    chips = devices // 2
    r, near = half // chips, 2 if chips == 4 else chips - 1
    c = operands[2].shape[2] + operands[3].shape[2]
    vmem, dma = pltpu.VMEM, pltpu.SemaphoreType.DMA
    row = small.shape[1:]
    local = pl.BlockSpec(memory_space=pltpu.VMEM)
    blocks = jax.ShapeDtypeStruct(out_rows.shape, bf16)
    return pl.pallas_call(
        functools.partial(closing_kernel, layers),
        out_shape=[
            jax.ShapeDtypeStruct((layers, r, c), f32),
            jax.ShapeDtypeStruct(row, f32),
            blocks,
            blocks,
        ],
        in_specs=[local] * (len(operands) + 1) + [ANY] * 2,
        out_specs=[local] * 2 + [ANY] * 2,
        scratch_shapes=[
            vmem((layers, size, half, c), bf16),
            vmem((layers, size, half, c), bf16),
            vmem((layers, size, half, c), bf16),
            vmem((layers, 2, size, r // 2, c), bf16),
            vmem((layers, near, size, r, c), bf16),
            vmem((layers, size, r, c), bf16),
            vmem((layers, size, r, c), bf16),
            dma((layers, size)),
            dma((layers, size)),
            dma((layers, 2)),
            dma((layers, 2)),
            dma((layers, near)),
            dma((layers, near)),
            dma((layers, size)),
            dma((layers, size)),
            vmem((size,) + row, f32),
            vmem((2,) + row, f32),
            vmem(row, f32),
            vmem((chips,) + row, f32),
            dma((size,)),
            dma((size,)),
            dma,
            dma,
            dma((chips,)),
            dma((chips,)),
        ]
        + exchange_scratch() * 2,
        compiler_params=pltpu.CompilerParams(
            collective_id=4, has_side_effects=True, vmem_limit_bytes=VMEM_LIMIT
        ),
        name="closing",
    )(*operands, small, out_rows, grad_rows)


def swing(value, cosine, turned_sine):
    return value * cosine + pltpu.roll(value, HEAD_DIM // 2, 1) * turned_sine


def tile_columns(value, tables):
    heads = value.shape[1] // HEAD_DIM
    parts = [swing(value[:, k * HEAD_DIM : (k + 1) * HEAD_DIM], *tables) for k in range(heads)]
    return jnp.concatenate(parts, axis=1)


def store_split(block, turned):
    width = block.shape[1]
    devices = lax.axis_size("gx")
    r = width // devices
    flipped = block.T
    for k in range(devices):
        q = k // 2
        turned[k % 2, q * r : (q + 1) * r] = flipped[k * r : (k + 1) * r]


def norm_pull(grad, normed, scale, gain):
    row = jnp.sum(grad * normed, axis=0, keepdims=True)
    scaled = grad * gain
    project = jnp.mean(scaled * normed, axis=1, keepdims=True)
    return row, scale * (scaled - normed * project)


def attention_pull_kernel(*refs):
    (grad, grad_ffn, norm_b, scale_b, gain_b, norm_a, scale_a, gain_a) = refs[:8]
    acts, q, k, v, lse, cosine, sine, qkv_ref, out_ref = refs[8:17]
    grad_out, grad_low, acts_turned, branch_turned, gqkv, small = refs[17:23]
    qkv, wout, heads, branch, dq, dk_sum, dv_sum, kv_out, kv_in, total = refs[23:33]
    w_sem, kv_send, kv_recv = refs[33:]
    gx, me, size = lax.axis_index("gx"), lax.axis_index("gy"), lax.axis_size("gy")
    count, rows = q.shape[0], k.shape[0]
    loads = [
        pltpu.make_async_copy(out_ref, wout, w_sem.at[0]),
        pltpu.make_async_copy(qkv_ref, qkv, w_sem.at[1]),
    ]
    for load in loads:
        load.start()
    greet([], [lax.rem(me + d, size) for d in range(1, size)])
    small[...] = jnp.zeros_like(small)
    row, pulled = norm_pull(grad_ffn[...], norm_b[...], scale_b[...], gain_b[...])
    small[1:2] = row
    branch[...] = grad[...] + pulled
    low = branch[...].astype(bf16)
    store_split(low, branch_turned)
    store_split(acts[...], acts_turned)
    loads[0].wait()
    cq = wout.shape[2]
    heads[...] = jnp.concatenate([nn(low, wout[z]) for z in range(size)], axis=1).astype(bf16)

    query = me * count + lax.broadcasted_iota(jnp.int32, (rows, count), 1)
    key = lax.broadcasted_iota(jnp.int32, (rows, count), 0)
    allowed = key <= query
    if rows > LEN:
        allowed = jnp.logical_and(allowed, key // LEN == query // LEN)
    factor = 1.0 / math.sqrt(HEAD_DIM)
    tables = (cosine[...], sine[...])

    def kv_copy(g, d):
        target = lax.rem(me + d, size)
        return pltpu.make_async_remote_copy(
            src_ref=kv_out.at[g, target],
            dst_ref=kv_in.at[g, me],
            send_sem=kv_send.at[g, d],
            recv_sem=kv_recv.at[g, me],
            device_id=(gx, target),
            device_id_type=MESH,
        )

    for g in range(KV_HEADS):
        span = slice(g * HEAD_DIM, (g + 1) * HEAD_DIM)
        kg, vg = k[:, span], v[:, span]
        turned_k = kg.T
        dk_sum[...] = jnp.zeros_like(dk_sum)
        dv_sum[...] = jnp.zeros_like(dv_sum)

        def head(i, carry):
            h = g * GROUP + i
            at = pl.ds(pl.multiple_of(h * HEAD_DIM, HEAD_DIM), HEAD_DIM)
            qh, dh = q[:, at], heads[:, at]
            scores = jnp.where(allowed, nt(kg, qh) * factor, -1e30)
            p = jnp.exp(scores - lse[pl.ds(h, 1), :])
            dp = nt(vg, dh)
            inner = jnp.sum(p * dp, axis=0, keepdims=True)
            ds = (p * (dp - inner)).astype(bf16)
            dv_sum[...] += nn(p.astype(bf16), dh)
            dk_sum[...] += nn(ds, qh)
            dq[:, at] = swing(nn(turned_k, ds).T * factor, *tables).astype(bf16)
            return carry

        lax.fori_loop(0, GROUP, head, 0)
        for z in range(size):
            at = slice(z * count, (z + 1) * count)
            kv_out[g, z, :, :HEAD_DIM] = (dk_sum[at] * factor).astype(bf16)
            kv_out[g, z, :, HEAD_DIM:] = dv_sum[at].astype(bf16)
        for d in range(1, size):
            kv_copy(g, d).start()

    loads[1].wait()
    apart = cq % HEAD_DIM == 0
    if apart:
        for z in range(size):
            p = nt(dq[:, z * cq : (z + 1) * cq], qkv[z, :, :cq])
            if z == 0:
                total[...] = p
            else:
                total[...] += p
    dks, dvs = [], []
    for g in range(KV_HEADS):
        summed = kv_out[g, me].astype(f32)
        for d in range(1, size):
            z = lax.rem(me + d, size)
            wait_for(kv_in.at[g, z], kv_recv.at[g, z])
            summed = summed + kv_in[g, z].astype(f32)
        dks.append(swing(summed[:, :HEAD_DIM], *tables).astype(bf16).astype(f32))
        dvs.append(summed[:, HEAD_DIM:].astype(bf16).astype(f32))
    dk, dv = jnp.concatenate(dks, axis=1), jnp.concatenate(dvs, axis=1)
    ck = dk.shape[1] // size
    for z in range(size):
        at = slice(z * ck, (z + 1) * ck)
        kv = jnp.concatenate([dk[:, at], dv[:, at]], axis=1)
        if apart:
            kv = kv.astype(bf16)
            gqkv[z, :, :cq] = dq[:, z * cq : (z + 1) * cq]
            gqkv[z, :, cq:] = kv
            total[...] += nt(kv, qkv[z, :, cq:])
        else:
            mine = dq[:, z * cq : (z + 1) * cq].astype(f32)
            gqkv[z] = jnp.concatenate([mine, kv], axis=1).astype(bf16)
            p = nt(gqkv[z], qkv[z])
            if z == 0:
                total[...] = p
            else:
                total[...] += p
    row, pulled = norm_pull(total[...], norm_a[...], scale_a[...], gain_a[...])
    small[0:1] = row
    small[2:3] = jnp.sum(dq[...].astype(f32), axis=0, keepdims=True)
    width = dk.shape[1]
    small[3:4, :width] = jnp.sum(dk, axis=0, keepdims=True)
    small[4:5, :width] = jnp.sum(dv, axis=0, keepdims=True)
    final = branch[...] + pulled
    grad_out[...] = final
    grad_low[...] = final.astype(bf16)
    for g in range(KV_HEADS):
        for d in range(1, size):
            kv_copy(g, d).wait_send()


def attention_pull(vectors, acts, q, k, v, lse, tables, qkv, wout):
    count, width = acts.shape
    size, rows = lax.axis_size("gy"), k.shape[0]
    local = pl.BlockSpec(memory_space=pltpu.VMEM)
    vmem, dma = pltpu.VMEM, pltpu.SemaphoreType.DMA
    turned = jax.ShapeDtypeStruct((2, width // 2, count), bf16)
    return pl.pallas_call(
        attention_pull_kernel,
        out_shape=[
            jax.ShapeDtypeStruct((count, width), f32),
            jax.ShapeDtypeStruct((count, width), bf16),
            turned,
            turned,
            jax.ShapeDtypeStruct((size, count, qkv.shape[2]), bf16),
            jax.ShapeDtypeStruct((8, width), f32),
        ],
        in_specs=[local] * 15 + [ANY] * 2,
        out_specs=[local] * 6,
        scratch_shapes=[
            vmem(qkv.shape, bf16),
            vmem(wout.shape, bf16),
            vmem((count, width), bf16),
            vmem((count, width), f32),
            vmem((count, width), bf16),
            vmem((rows, HEAD_DIM), f32),
            vmem((rows, HEAD_DIM), f32),
            vmem((KV_HEADS, size, count, 2 * HEAD_DIM), bf16),
            vmem((KV_HEADS, size, count, 2 * HEAD_DIM), bf16),
            vmem((count, width), f32),
            dma((2,)),
            dma((KV_HEADS, size)),
            dma((KV_HEADS, size)),
        ],
        compiler_params=pltpu.CompilerParams(
            collective_id=6, has_side_effects=True, vmem_limit_bytes=VMEM_LIMIT
        ),
        name="attention_pull",
    )(*vectors, acts, q, k, v, lse, *tables, qkv, wout)


def greet_line():
    gx, me, last = lax.axis_index("gx"), lax.axis_index("gy"), lax.axis_size("gy") - 1
    barrier = pltpu.get_barrier_semaphore()

    @pl.when(me > 0)
    def _():
        pl.semaphore_signal(barrier, inc=1, device_id=(gx, me - 1), device_id_type=MESH)

    @pl.when(me < last)
    def _():
        pl.semaphore_signal(barrier, inc=1, device_id=(gx, me + 1), device_id_type=MESH)

    pl.semaphore_wait(barrier, jnp.where(jnp.logical_and(me > 0, me < last), 2, 1))


def attention_push_kernel(*refs):
    x, gain_a, gain_b, bq, bk, bv, cosine, sine, qkv_ref, out_ref = refs[:10]
    middle, norm_a, scale_a, acts_a, q, k_all, v_all, lse = refs[10:18]
    mixed, norm_b, scale_b, acts_b = refs[18:22]
    qkv, wout, kv_own, kv_all, flat, w_sem = refs[22:28]
    me, size = lax.axis_index("gy"), lax.axis_size("gy")
    count, rows = x.shape[0], k_all.shape[0]
    loads = [
        pltpu.make_async_copy(qkv_ref, qkv, w_sem.at[0]),
        pltpu.make_async_copy(out_ref, wout, w_sem.at[1]),
    ]
    for load in loads:
        load.start()
    chain = Chain(kv_own, kv_all, refs[28:31])
    greet_line()
    value = x[...]
    scale = lax.rsqrt(jnp.mean(value * value, axis=1, keepdims=True) + epsilon)
    scale_a[...] = scale
    norm_a[...] = value * scale
    acts_a[...] = (norm_a[...] * gain_a[...]).astype(bf16)
    loads[0].wait()
    cq, width = wout.shape[2], k_all.shape[1]
    ck = width // size
    tables = (cosine[...], sine[...])
    apart = cq % HEAD_DIM == 0
    if apart:
        kv = [nn(acts_a[...], qkv[z, :, cq:]) for z in range(size)]
    else:
        both = [nn(acts_a[...], qkv[z]) for z in range(size)]
        kv = [part[:, cq:] for part in both]
    keys = jnp.concatenate([part[:, :ck] for part in kv], axis=1) + bk[...]
    values = jnp.concatenate([part[:, ck:] for part in kv], axis=1) + bv[...]
    kv_own[:, :width] = tile_columns(keys, tables).astype(bf16)
    kv_own[:, width:] = values.astype(bf16)
    chain.begin()
    if apart:
        for z in range(size):
            at = slice(z * cq, (z + 1) * cq)
            mine = nn(acts_a[...], qkv[z, :, :cq]) + bq[:, at]
            q[:, at] = tile_columns(mine, tables).astype(bf16)
            if z:
                chain.relay(z)
    else:
        mine = jnp.concatenate([part[:, :cq] for part in both], axis=1) + bq[...]
        q[...] = tile_columns(mine, tables).astype(bf16)
        for t in range(1, size):
            chain.relay(t)
    chain.close()
    k_all[...] = kv_all[:, :, :width].reshape(rows, width)
    v_all[...] = kv_all[:, :, width:].reshape(rows, width)

    query = me * count + lax.broadcasted_iota(jnp.int32, (rows, count), 1)
    key = lax.broadcasted_iota(jnp.int32, (rows, count), 0)
    allowed = key <= query
    if rows > LEN:
        allowed = jnp.logical_and(allowed, key // LEN == query // LEN)
    factor = 1.0 / math.sqrt(HEAD_DIM)
    for g in range(KV_HEADS):
        span = slice(g * HEAD_DIM, (g + 1) * HEAD_DIM)
        kg, turned_v = k_all[:, span], v_all[:, span].T

        def head(i, carry):
            h = g * GROUP + i
            at = pl.ds(pl.multiple_of(h * HEAD_DIM, HEAD_DIM), HEAD_DIM)
            scores = jnp.where(allowed, nt(kg, q[:, at]) * factor, -1e30)
            top = jnp.max(scores, axis=0, keepdims=True)
            expo = jnp.exp(scores - top)
            total = jnp.sum(expo, axis=0, keepdims=True)
            lse[pl.ds(h, 1), :] = top + jnp.log(total)
            soft = (expo * (1.0 / total)).astype(bf16)
            flat[:, at] = nn(turned_v, soft).T.astype(bf16)
            return carry

        lax.fori_loop(0, GROUP, head, 0)
    loads[1].wait()
    middle[...] = x[...]
    for z in range(size):
        at = slice(z * cq, (z + 1) * cq)
        if apart:
            mixed[z] = flat[:, at]
        else:
            mixed[z] = flat[:, at].astype(f32).astype(bf16)
        middle[...] += nt(mixed[z], wout[z])
    value = middle[...]
    scale = lax.rsqrt(jnp.mean(value * value, axis=1, keepdims=True) + epsilon)
    scale_b[...] = scale
    norm_b[...] = value * scale
    acts_b[...] = (norm_b[...] * gain_b[...]).astype(bf16)


def attention_push(x, vectors, tables, qkv, wout, rows):
    count, width = x.shape
    size = lax.axis_size("gy")
    kvd = KV_HEADS * HEAD_DIM
    local = pl.BlockSpec(memory_space=pltpu.VMEM)
    vmem = pltpu.VMEM

    def shape(*dims, kind=bf16):
        return jax.ShapeDtypeStruct(dims, kind)

    normed = [shape(count, width, kind=f32), shape(count, 1, kind=f32), shape(count, width)]
    out = [shape(count, width, kind=f32), *normed, shape(count, HEADS * HEAD_DIM)]
    out += [shape(rows, kvd), shape(rows, kvd), shape(HEADS, count, kind=f32)]
    out += [shape(size, count, wout.shape[2]), *normed]
    return pl.pallas_call(
        attention_push_kernel,
        out_shape=out,
        in_specs=[local] * 8 + [ANY] * 2,
        out_specs=[local] * 12,
        scratch_shapes=[
            vmem(qkv.shape, bf16),
            vmem(wout.shape, bf16),
            vmem((count, 2 * kvd), bf16),
            vmem((size, count, 2 * kvd), bf16),
            vmem((count, HEADS * HEAD_DIM), bf16),
            pltpu.SemaphoreType.DMA((2,)),
        ]
        + chain_scratch(),
        compiler_params=pltpu.CompilerParams(
            collective_id=7, has_side_effects=True, vmem_limit_bytes=VMEM_LIMIT
        ),
        name="attention_push",
    )(x, *vectors, *tables, qkv, wout)


def on_device(
    residual_in,
    w_query,
    w_key,
    w_value,
    b_query,
    b_key,
    b_value,
    w_output,
    gain_attn,
    gain_ffn,
    w_gate,
    w_up,
    w_down,
    cotangent,
):
    devices_y = lax.axis_size("gy")
    rows_tok = residual_in.shape[1]
    count = rows_tok // devices_y
    q_index = lax.axis_index("gy") * count + jnp.arange(count, dtype=jnp.int32)
    cos_table, sin_table = rope_tables(q_index % LEN, HEAD_DIM)

    small = jnp.concatenate([gain_attn, gain_ffn, b_query, b_key, b_value], axis=1)
    small_sizes = [v.shape[1] for v in (gain_attn, gain_ffn, b_query, b_key, b_value)]
    small = jnp.pad(small.astype(f32), ((0, 8 - LAYERS), (0, 0)))
    lines = []
    for l in range(LAYERS):
        lines += [jnp.concatenate([w_query[l], w_key[l], w_value[l]], axis=1), w_output[l]]
    part_sizes = (w_query.shape[2], w_key.shape[2], w_value.shape[2])
    opened = opening(residual_in, cotangent, small, lines, w_gate, w_up, w_down)
    resid, cot, small = opened[:3]
    lines_next = opened[5:7]
    attn_full = [[w.reshape(devices_y, D, -1) for w in opened[7:9]], None]
    ffn_full = [[w.reshape(D, -1) for w in opened[9:]], None]
    small = small[:, :LAYERS].transpose(1, 0, 2)
    vectors, start = [], 0
    for size in small_sizes:
        vectors.append(small[:, :, start : start + size].reshape(LAYERS, -1))
        start += size
    gains_one, gains_two, bias_q, bias_k, bias_v = vectors

    resid = resid.reshape(D, count).astype(f32).T
    cot = cot.reshape(D, count)

    kept = []
    for l in range(LAYERS):
        w_qkv, w_out = attn_full[l]
        wg, wu, wd = ffn_full[l]
        vectors = [v[l][None] for v in (gains_one, gains_two, bias_q, bias_k, bias_v)]
        done = attention_push(resid, vectors, (cos_table, -sin_table), w_qkv, w_out, rows_tok)
        middle, normed_one, scale_one, acts_one, q_rot, k_rot, v_heads, log_total = done[:8]
        mixed, normed_two, scale_two, acts_two = done[8:]
        if l == 0:
            shards = (*lines_next, w_gate, w_up, w_down)
            done = forward_ffn(acts_two, wg, wu, wd, shards)
            attn_full[1] = [w.reshape(devices_y, D, -1) for w in done[5:7]]
            ffn_full[1] = [w.reshape(D, -1) for w in done[7:]]
        else:
            done = forward_ffn(acts_two, wg, wu, wd)
        part, acts_two, gate, up, hidden = done[:5]
        kept.append(
            (
                normed_one,
                scale_one,
                acts_one,
                q_rot,
                k_rot,
                v_heads,
                log_total,
                mixed,
                normed_two,
                scale_two,
                acts_two,
                gate,
                up,
                hidden,
            )
        )
        resid = middle + part

    grad = cot.astype(f32).T + 2.0 * penalty * resid
    grad_low = grad.astype(bf16)
    attn_grads = [None] * LAYERS
    ffn_grads = [None] * LAYERS
    small_grads = [None] * LAYERS

    for l in reversed(range(LAYERS)):
        (
            normed_one,
            scale_one,
            acts_one,
            q_rot,
            k_rot,
            v_heads,
            log_total,
            mixed,
            normed_two,
            scale_two,
            acts_two,
            gate,
            up,
            hidden,
        ) = kept[l]
        w_qkv, w_out = attn_full[l]
        wg, wu, wd = ffn_full[l]
        operands = (grad_low, gate, up, hidden, acts_two, wg, wu, wd)
        if l == LAYERS - 1:
            done = backward_ffn(*operands, late=True)
            grad_down, held = done[1:3]
        else:
            done = backward_ffn(*operands, held=held)
            ffn_grads[l] = done[1:4]
            ffn_grads[l + 1] = [*done[7:9], grad_down]
        grad_acts_two = done[0]
        vectors = [grad, grad_acts_two, normed_two, scale_two, gains_two[l][None]]
        vectors += [normed_one, scale_one, gains_one[l][None]]
        done = attention_pull(
            vectors, acts_one, q_rot, k_rot, v_heads, log_total, (cos_table, sin_table), w_qkv, w_out
        )
        grad, grad_low = done[:2]
        attn_grads[l] = [*done[2:5], mixed]
        rows = done[5]
        width = k_rot.shape[1]
        small_grads[l] = [
            v.reshape(devices_y, -1)
            for v in (rows[0], rows[1], rows[2], rows[3, :width], rows[4, :width])
        ]
    small = jnp.stack([jnp.concatenate(v, axis=1) for v in small_grads], axis=1)
    small = jnp.pad(small, ((0, 0), (0, 8 - LAYERS), (0, 0)))

    def to_rows(tokens_major):
        return tokens_major.astype(bf16).T.reshape(devices_y, -1, count)

    def from_blocks(blocks):
        return blocks.transpose(1, 0, 2).reshape(-1, rows_tok).astype(f32)

    attn_sums, small, output, grad_input = closing(
        attn_grads[0] + attn_grads[1], small, to_rows(resid), to_rows(grad_low)
    )
    small = small[:LAYERS]
    attn_out, start = [], 0
    for size in part_sizes + (w_output.shape[2],):
        attn_out.append(attn_sums[:, :, start : start + size])
        start += size
    small_out, start = [], 0
    for size in small_sizes:
        small_out.append(small[:, start : start + size])
        start += size

    def stack(parts, k):
        return jnp.stack([part[k] for part in parts])

    return (
        from_blocks(output),
        from_blocks(grad_input),
        attn_out[0],
        attn_out[1],
        attn_out[2],
        small_out[2],
        small_out[3],
        small_out[4],
        attn_out[3],
        small_out[0],
        small_out[1],
        stack(ffn_grads, 0),
        stack(ffn_grads, 1),
        stack(ffn_grads, 2),
    )


def solution(mesh):
    tokens = P("gy", "gx")
    weight = P(None, "gx", "gy")
    vector = P(None, "gy")
    return jax.shard_map(
        on_device,
        mesh=mesh,
        in_specs=(
            tokens,
            weight,
            weight,
            weight,
            vector,
            vector,
            vector,
            weight,
            vector,
            vector,
            weight,
            weight,
            weight,
            tokens,
        ),
        out_specs=(
            tokens,
            tokens,
            weight,
            weight,
            weight,
            vector,
            vector,
            vector,
            weight,
            vector,
            vector,
            weight,
            weight,
            weight,
        ),
        check_vma=False,
    )
```

```python
import functools
import math

import jax
import jax.numpy as jnp
from jax import lax
from jax.experimental import pallas as pl
from jax.experimental.pallas import tpu as pltpu
from jax.sharding import PartitionSpec as P

D = 1536
HEADS = 12
KV_HEADS = 2
HEAD_DIM = 128
LEN = 1024
LAYERS = 2
GROUP = HEADS // KV_HEADS

epsilon = 1e-06
rope_base = 1000000.0
penalty = 0.25
bf16 = jnp.bfloat16
f32 = jnp.float32
MESH = pl.DeviceIdType.MESH
VMEM_LIMIT = 62 << 20
ANY = pl.BlockSpec(memory_space=pl.ANY)


def rope_tables(positions, head_size):
    freqs = rope_base ** (-jnp.arange(0, head_size, 2).astype(f32) / head_size)
    angles = positions.astype(f32)[:, None] * freqs[None, :]
    cosine = jnp.cos(angles)
    sine_table = jnp.sin(angles)
    return (
        jnp.concatenate([cosine, cosine], -1),
        jnp.concatenate([sine_table, -sine_table], -1),
    )


def wait_for(ref, sem):
    pltpu.make_async_copy(ref, ref, sem).wait()


def places():
    gx, devices = lax.axis_index("gx"), lax.axis_size("gx")
    chips = devices // 2
    chip, core = gx // 2, lax.rem(gx, 2)
    partner = gx + 1 - 2 * core
    others = [lax.rem(chip + k, chips) * 2 + core for k in range(1, chips)]
    return partner, others


def square():
    gx = lax.axis_index("gx")
    chip, core = gx // 2, lax.rem(gx, 2)
    side = gx + 2 - 4 * lax.rem(chip, 2)
    along = gx + 4 - 8 * (chip // 2)
    return side, along, (3 - chip) * 2 + core


def spread_slots():
    chips = lax.axis_size("gx") // 2
    return 14 if chips == 4 else 2 * chips + 2 * (chips - 1)


def spread_scratch(count):
    devices = lax.axis_size("gx")
    return [
        pltpu.SemaphoreType.DMA((count,)),
        pltpu.SemaphoreType.DMA((count, spread_slots())),
        pltpu.SemaphoreType.DMA((count, devices, 2)),
    ]


def greet(gx_peers, gy_peers):
    gx, gy = lax.axis_index("gx"), lax.axis_index("gy")
    barrier = pltpu.get_barrier_semaphore()
    for peer in gx_peers:
        pl.semaphore_signal(barrier, inc=1, device_id=(peer, gy), device_id_type=MESH)
    for peer in gy_peers:
        pl.semaphore_signal(barrier, inc=1, device_id=(gx, peer), device_id_type=MESH)
    pl.semaphore_wait(barrier, len(gx_peers) + len(gy_peers))


class Spread:
    def __init__(self, items, sems):
        self.items, (self.local, self.send_sem, self.recv_sem) = items, sems
        self.partner, self.others = places()
        self.four = lax.axis_size("gx") // 2 == 4
        self.near = list(square()[:2]) if self.four else self.others

    def part(self, i, k, h):
        full = self.items[i][1]
        if len(full.shape) == 4:
            half = full.shape[0] // 2
            return full.at[pl.ds(h * half, half), k]
        half = full.shape[1] // 2
        return full.at[k, pl.ds(h * half, half)]

    def send(self, i, k, h, target, slot, first=False):
        here = self.part(i, k, h)
        half = here.shape[0]
        source = self.items[i][0].at[pl.ds(h * half, half)] if first else here
        pltpu.make_async_remote_copy(
            src_ref=source,
            dst_ref=here,
            send_sem=self.send_sem.at[i, slot],
            recv_sem=self.recv_sem.at[i, k, h],
            device_id=(target, lax.axis_index("gy")),
            device_id_type=MESH,
        ).start()

    def arrived(self, i, k, h):
        wait_for(self.part(i, k, h), self.recv_sem.at[i, k, h])

    def place(self, i):
        own, full = self.items[i]
        gx = lax.axis_index("gx")
        here = full.at[:, gx] if len(full.shape) == 4 else full.at[gx]
        return pltpu.make_async_copy(own, here, self.local.at[i])

    def begin(self, i):
        gx = lax.axis_index("gx")
        self.place(i).start()
        slot = 0
        for target in self.near + [self.partner]:
            for h in range(2):
                self.send(i, gx, h, target, slot, True)
                slot += 1

    def relay(self, i):
        slot = 2 * len(self.near) + 2
        if self.four:
            side, along, _ = square()
            steps = [(side, 0, along), (along, 1, side), (side, 1, None), (along, 0, None)]
        else:
            steps = [(k, h, None) for k in self.others for h in range(2)]
        for k, h, target in steps:
            self.arrived(i, k, h)
            for to in [self.partner] if target is None else [target, self.partner]:
                self.send(i, k, h, to, slot)
                slot += 1

    def finish(self, i):
        if self.four:
            for h in range(2):
                self.arrived(i, square()[2], h)
                self.send(i, square()[2], h, self.partner, 12 + h)

    def close(self, i):
        core = lax.rem(lax.axis_index("gx"), 2)
        for k in [self.partner] + [k + 1 - 2 * core for k in self.others]:
            for h in range(2):
                self.arrived(i, k, h)
        for slot in range(spread_slots()):
            wait_for(self.part(i, 0, 0), self.send_sem.at[i, slot])
        self.place(i).wait()


def line_order(t, me, last):
    short = jnp.minimum(me, last - me)
    near = jnp.where(lax.rem(t, 2) == 0, me - t // 2, me + (t + 1) // 2)
    far = jnp.where(me < last - me, me + (t - short), me - (t - short))
    return jnp.where(t <= 2 * short, near, far)


class Chain:
    def __init__(self, own, full, sems):
        self.own, self.full, (self.local, self.send_sem, self.recv_sem) = own, full, sems

    def copy(self, b, way, first=False):
        me = lax.axis_index("gy")
        return pltpu.make_async_remote_copy(
            src_ref=self.own if first else self.full.at[b],
            dst_ref=self.full.at[b],
            send_sem=self.send_sem.at[b, way],
            recv_sem=self.recv_sem.at[b],
            device_id=(lax.axis_index("gx"), me - 1 + 2 * way),
            device_id_type=MESH,
        )

    def each(self, b, act, first=False):
        me, last = lax.axis_index("gy"), lax.axis_size("gy") - 1

        @pl.when(jnp.logical_and(b <= me, me < last))
        def _():
            act(self.copy(b, 1, first))

        @pl.when(jnp.logical_and(b >= me, me > 0))
        def _():
            act(self.copy(b, 0, first))

    def begin(self):
        me = lax.axis_index("gy")
        self.place = pltpu.make_async_copy(self.own, self.full.at[me], self.local)
        self.place.start()
        self.each(me, lambda copy: copy.start(), True)

    def relay(self, t):
        b = line_order(t, lax.axis_index("gy"), lax.axis_size("gy") - 1)
        wait_for(self.full.at[b], self.recv_sem.at[b])
        self.each(b, lambda copy: copy.start())

    def close(self):
        self.place.wait()
        for b in range(lax.axis_size("gy")):
            self.each(b, lambda copy: copy.wait_send())


class Exchange:
    def __init__(self, own, full, sems, apart=False):
        self.own, self.full, (self.local, self.send_sem, self.recv_sem) = own, full, sems
        self.apart = apart

    def begin(self):
        gx, me, size = lax.axis_index("gx"), lax.axis_index("gy"), lax.axis_size("gy")
        width = self.full.shape[2]

        def columns(k):
            if self.apart:
                return self.own.at[k]
            return self.own.at[:, pl.ds(pl.multiple_of(k * width, width), width)]

        self.place = pltpu.make_async_copy(columns(me), self.full.at[me], self.local)
        self.place.start()
        self.sent = []
        for d in range(1, size):
            target = lax.rem(me + d, size)
            copy = pltpu.make_async_remote_copy(
                src_ref=columns(target),
                dst_ref=self.full.at[me],
                send_sem=self.send_sem.at[d],
                recv_sem=self.recv_sem.at[me],
                device_id=(gx, target),
                device_id_type=MESH,
            )
            copy.start()
            self.sent.append(copy)

    def close(self):
        me, size = lax.axis_index("gy"), lax.axis_size("gy")
        self.place.wait()
        for copy in self.sent:
            copy.wait_send()
        for d in range(1, size):
            k = lax.rem(me + d, size)
            wait_for(self.full.at[k], self.recv_sem.at[k])


def chain_scratch():
    size = lax.axis_size("gy")
    return [
        pltpu.SemaphoreType.DMA,
        pltpu.SemaphoreType.DMA((size, 2)),
        pltpu.SemaphoreType.DMA((size,)),
    ]


def exchange_scratch():
    size = lax.axis_size("gy")
    return [
        pltpu.SemaphoreType.DMA,
        pltpu.SemaphoreType.DMA((size,)),
        pltpu.SemaphoreType.DMA((size,)),
    ]


def opening_kernel(*refs):
    ins, outs, sems = refs[:9], refs[9:20], refs[20:]
    resid, cot, small, qkv_a, o_a, qkv_b, o_b, wg, wu = ins
    resid_out, cot_out, small_out = outs[:3]
    lines, (qkv, o, gate, up) = outs[3:7], outs[7:]
    me, size = lax.axis_index("gy"), lax.axis_size("gy")
    owns = (qkv_a, o_a, qkv_b, o_b, small)
    chains = [
        Chain(own, full, sems[3 * k : 3 * k + 3])
        for k, (own, full) in enumerate(zip(owns, list(lines) + [small_out]))
    ]
    swaps = [
        Exchange(own, full, sems[15 + 3 * k : 18 + 3 * k])
        for k, (own, full) in enumerate(((resid, resid_out), (cot, cot_out)))
    ]
    items = [(lines[0], qkv), (lines[1], o), (wg.at[0], gate), (wu.at[0], up)]
    spread = Spread(items, sems[21:24])
    greet([spread.partner] + spread.near, [lax.rem(me + d, size) for d in range(1, size)])
    for k in (0, 1, 4):
        chains[k].begin()
    spread.begin(2)
    for t in range(1, size):
        chains[0].relay(t)
        chains[1].relay(t)
    chains[0].close()
    spread.begin(0)
    chains[1].close()
    spread.begin(1)
    swaps[0].begin()
    for t in range(1, size):
        chains[4].relay(t)
    spread.relay(2)
    spread.begin(3)
    chains[2].begin()
    chains[3].begin()
    for i in (0, 1):
        spread.relay(i)
    swaps[1].begin()
    for t in range(1, size):
        chains[2].relay(t)
        chains[3].relay(t)
    spread.finish(2)
    for i in (0, 1):
        spread.finish(i)
    spread.relay(3)
    spread.finish(3)
    for i in range(4):
        spread.close(i)
    for part in chains[2:] + swaps:
        part.close()


def opening(resid, cot, small, lines, wg, wu):
    devices, size = lax.axis_size("gx"), lax.axis_size("gy")
    count = resid.shape[1] // size

    def shape(*dims, kind=bf16):
        return jax.ShapeDtypeStruct(dims, kind)

    blocks = shape(size, resid.shape[0], count)
    weight = shape(devices, *wg.shape[1:])
    out = [blocks, blocks, shape(size, *small.shape, kind=f32)]
    out += [shape(size, *line.shape) for line in lines]
    out += [shape(size, devices, *line.shape) for line in lines[:2]] + [weight] * 2
    return pl.pallas_call(
        opening_kernel,
        out_shape=out,
        in_specs=[ANY] * 9,
        out_specs=[ANY] * 11,
        scratch_shapes=chain_scratch() * 5 + exchange_scratch() * 2 + spread_scratch(4),
        compiler_params=pltpu.CompilerParams(collective_id=2, has_side_effects=True),
        name="opening",
    )(resid, cot, small, *lines, wg, wu)


FF_CHUNK = 512
PIECES = 4


def spans(total):
    return [(start, min(FF_CHUNK, total - start)) for start in range(0, total, FF_CHUNK)]


def nn(left, right):
    return lax.dot_general(left, right, (((1,), (0,)), ((), ())), preferred_element_type=f32)


def nt(left, right):
    return lax.dot_general(left, right, (((1,), (1,)), ((), ())), preferred_element_type=f32)


def line_pass(own_ref, own, gathered, part, outb, inb, sems, load, finish, peers=(), plan={}):
    own_sem, ag_send, ag_recv, rs_send, rs_recv = sems
    gx, me, size = lax.axis_index("gx"), lax.axis_index("gy"), lax.axis_size("gy")
    rows = own.shape[0]
    piece = rows // PIECES
    last = size - 1
    inner = jnp.logical_and(me > 0, me < last)

    first = pltpu.make_async_copy(own_ref, gathered.at[me], own_sem)
    first.start()
    barrier = pltpu.get_barrier_semaphore()

    @pl.when(me > 0)
    def _():
        pl.semaphore_signal(barrier, inc=1, device_id=(gx, me - 1), device_id_type=MESH)

    @pl.when(me < last)
    def _():
        pl.semaphore_signal(barrier, inc=1, device_id=(gx, me + 1), device_id_type=MESH)

    for peer in peers:
        pl.semaphore_signal(barrier, inc=1, device_id=(peer, me), device_id_type=MESH)
    pl.semaphore_wait(barrier, jnp.where(inner, 2, 1) + len(peers))
    first.wait()

    def planned(name, t):
        for (key, when), act in plan.items():
            if key == name:
                pl.when(t == when)(act)


    def gather_copy(b, s, way):
        here = gathered.at[b, pl.ds(s * piece, piece)]
        return pltpu.make_async_remote_copy(
            src_ref=here,
            dst_ref=here,
            send_sem=ag_send.at[b, way, s],
            recv_sem=ag_recv.at[b, s],
            device_id=(gx, me - 1 + 2 * way),
            device_id_type=MESH,
        )

    def sum_copy(b, s):
        towards = jnp.where(b > me, me + 1, me - 1)
        slot = jnp.where(jnp.logical_and(towards == b, me > b), size, b)
        return pltpu.make_async_remote_copy(
            src_ref=outb.at[b, pl.ds(s * piece, piece)],
            dst_ref=inb.at[slot, pl.ds(s * piece, piece)],
            send_sem=rs_send.at[b, s],
            recv_sem=rs_recv.at[slot, s],
            device_id=(gx, towards),
            device_id_type=MESH,
        )

    def sum_arrived(slot, s):
        here = inb.at[slot, pl.ds(s * piece, piece)]
        pltpu.make_async_copy(here, here, rs_recv.at[slot, s]).wait()

    def step(t, carry):
        b = line_order(t, me, last)
        for s in range(PIECES):

            @pl.when(t > 0)
            def _():
                gather_copy(b, s, 0).wait_recv()

            @pl.when(jnp.logical_and(b <= me, me < last))
            def _():
                gather_copy(b, s, 1).start()

            @pl.when(jnp.logical_and(b >= me, me > 0))
            def _():
                gather_copy(b, s, 0).start()

        @pl.when(t == 0)
        def _():
            load()

        planned("step", t)
        finish(b)

        @pl.when(b == me)
        def _():
            own[...] = part[...]

        @pl.when(b != me)
        def _():
            outb[b] = part[...].astype(bf16)

            @pl.when(jnp.logical_not(inner))
            def _():
                for s in range(PIECES):
                    sum_copy(b, s).start()

        return carry

    lax.fori_loop(0, size, step, 0)

    def relay(t, carry):
        above, below = last - me, me
        low = jnp.where(t < above, me + 1 + t, me - 1 - (t - above))
        high = jnp.where(t < below, me - 1 - t, me + 1 + (t - below))
        b = jnp.where(2 * me < size, low, high)
        planned("hop", t)

        @pl.when(inner)
        def _():
            for s in range(PIECES):
                at = pl.ds(s * piece, piece)
                sum_arrived(b, s)
                outb[b, at] = (outb[b, at].astype(f32) + inb[b, at].astype(f32)).astype(bf16)
                sum_copy(b, s).start()

        return carry

    lax.fori_loop(0, last, relay, 0)

    @pl.when(me > 0)
    def _():
        for s in range(PIECES):
            sum_arrived(me, s)
        own[...] += inb[me].astype(f32)

    @pl.when(me < last)
    def _():
        for s in range(PIECES):
            sum_arrived(size, s)
        own[...] += inb[size].astype(f32)

    def drain(b, carry):
        for s in range(PIECES):

            @pl.when(jnp.logical_and(b <= me, me < last))
            def _():
                gather_copy(b, s, 1).wait_send()

            @pl.when(jnp.logical_and(b >= me, me > 0))
            def _():
                gather_copy(b, s, 0).wait_send()

            @pl.when(b != me)
            def _():
                sum_copy(b, s).wait_send()

        return carry

    lax.fori_loop(0, size, drain, 0)


def line_scratch(size, rows, width):
    return [
        pltpu.VMEM((size, rows, width), bf16),
        pltpu.VMEM((rows, width), f32),
        pltpu.VMEM((size, rows, width), bf16),
        pltpu.VMEM((size + 1, rows, width), bf16),
        pltpu.SemaphoreType.DMA,
        pltpu.SemaphoreType.DMA((size, 2, PIECES)),
        pltpu.SemaphoreType.DMA((size, PIECES)),
        pltpu.SemaphoreType.DMA((size, PIECES)),
        pltpu.SemaphoreType.DMA((size + 1, PIECES)),
    ]


LINE = 9


ORDER = {
    ("step", 0): (("begin", 0), ("begin", 1)),
    ("step", 2): (("begin", 2),),
    ("hop", 0): (("relay", 0), ("relay", 1), ("relay", 2), ("begin", 3)),
    ("hop", 1): (("finish", 0), ("finish", 1), ("finish", 2)),
}
REST = (("relay", 3), ("finish", 3))


def schedule(spread):
    def run(steps):
        def act():
            for verb, i in steps:
                getattr(spread, verb)(i)

        return act

    plan = {key: run(steps) for key, steps in ORDER.items()}
    return plan, REST + tuple(("close", i) for i in range(len(spread.items)))


def forward_kernel(extra, *refs):
    acts_ref, wg_ref, wu_ref, wd_ref = refs[:4]
    shards, refs = refs[4 : 4 + extra], refs[4 + extra :]
    sum_ref, turned_ref, gate_ref, up_ref, hidden_ref = refs[:5]
    wholes, scratch = refs[5 : 5 + extra], refs[5 + extra :]
    gathered, part, outb, inb = scratch[:4]
    sems = scratch[4:LINE]
    wg, wu, wd, gate, up, hidden, turned, w_sem, out_sem = scratch[LINE : LINE + 9]
    peers, spread = [], None
    if extra:
        items = [(r if len(w.shape) == 4 else r.at[1], w) for r, w in zip(shards, wholes)]
        spread = Spread(items, scratch[LINE + 9 :])
        partner, others = places()
        peers = [partner] + (list(square()[:2]) if spread.four else others)

    plan, rest = schedule(spread) if extra else ({}, ())
    loads = [
        pltpu.make_async_copy(src, dst, w_sem.at[k])
        for k, (src, dst) in enumerate(((wg_ref, wg), (wu_ref, wu), (wd_ref, wd)))
    ]
    for copy in loads:
        copy.start()

    def load():
        for copy in loads:
            copy.wait()

    def results(b):
        pairs = ((gate, gate_ref), (up, up_ref), (hidden, hidden_ref))
        return [
            pltpu.make_async_copy(src.at[b], dst.at[b], out_sem.at[b, k])
            for k, (src, dst) in enumerate(pairs)
        ]

    def finish(b):
        block = gathered[b]
        store_turned(block, turned, b)
        for start, width in spans(wg.shape[1]):
            at = slice(start, start + width)
            g = nn(block, wg[:, at])
            u = nn(block, wu[:, at])
            h = (g * lax.logistic(g) * u).astype(bf16)
            gate[b, :, at] = g.astype(bf16)
            up[b, :, at] = u.astype(bf16)
            hidden[b, :, at] = h
            p = nt(h, wd[:, at])
            if start == 0:
                part[...] = p
            else:
                part[...] += p
        for copy in results(b):
            copy.start()

    line_pass(
        acts_ref, sum_ref, gathered, part, outb, inb, sems, load, finish, peers, plan
    )
    keep = pltpu.make_async_copy(turned, turned_ref, w_sem.at[0])
    keep.start()
    for act, i in rest:
        getattr(spread, act)(i)

    def settle(b, carry):
        for copy in results(b):
            copy.wait()
        return carry

    lax.fori_loop(0, gathered.shape[0], settle, 0)
    keep.wait()


def forward_ffn(acts, wg, wu, wd, shards=()):
    rows, width = acts.shape
    devices, size, hidden = lax.axis_size("gx"), lax.axis_size("gy"), wg.shape[1]
    wide = jax.ShapeDtypeStruct((size, rows, hidden), bf16)
    extra = len(shards)
    wholes = [
        jax.ShapeDtypeStruct(
            (size, devices) + s.shape[1:] if k < 2 else (devices,) + s.shape[1:], bf16
        )
        for k, s in enumerate(shards)
    ]
    return pl.pallas_call(
        functools.partial(forward_kernel, extra),
        out_shape=[
            jax.ShapeDtypeStruct((rows, width), f32),
            jax.ShapeDtypeStruct((2, width // 2, size * rows), bf16),
            wide,
            wide,
            wide,
        ]
        + wholes,
        in_specs=[ANY] * (4 + extra),
        out_specs=[pl.BlockSpec(memory_space=pltpu.VMEM)] + [ANY] * (4 + extra),
        scratch_shapes=line_scratch(size, rows, width)
        + [pltpu.VMEM((width, hidden), bf16)] * 3
        + [pltpu.VMEM((size, rows, hidden), bf16)] * 3
        + [pltpu.VMEM((2, width // 2, size * rows), bf16)]
        + [pltpu.SemaphoreType.DMA((3,)), pltpu.SemaphoreType.DMA((size, 3))]
        + (spread_scratch(extra) if extra else []),
        compiler_params=pltpu.CompilerParams(
            collective_id=3 if extra else 0, has_side_effects=True, vmem_limit_bytes=VMEM_LIMIT
        ),
        cost_estimate=pl.CostEstimate(
            flops=6 * size * rows * width * hidden, bytes_accessed=40 << 20, transcendentals=0
        ),
        name="ffn_forward",
    )(acts, wg, wu, wd, *shards)


class Reduce:
    def __init__(self, lhs, rhs, bufs, abuf, fbuf, ftail, a_all, r_all, c_all, outs, late, sems):
        self.late = late
        self.lhs, self.rhs, self.bufs, self.outs = lhs, rhs, bufs, outs
        self.abuf, self.fbuf, self.ftail = abuf, fbuf, ftail
        self.a_all, self.r_all, self.c_all = a_all, r_all, c_all
        (
            self.a_send,
            self.a_recv,
            self.r_send,
            self.r_recv,
            self.c_send,
            self.c_recv,
            self.local,
        ) = sems
        gx, self.gy = lax.axis_index("gx"), lax.axis_index("gy")
        self.chip, self.core = gx // 2, lax.rem(gx, 2)
        self.chips = lax.axis_size("gx") // 2
        self.half, self.wide = bufs[0].shape[0] // 2, bufs[0].shape[1]
        self.r = self.half // self.chips
        self.four = self.chips == 4
        self.partner, self.others = places()
        self.near = list(square()[:2]) if self.four else self.others

    def product(self, m, which, at):
        z, n, _ = self.rhs[m].shape
        right = self.rhs[m][:, :, at].reshape(z * n, at.stop - at.start)
        return nn(self.lhs[which], right)

    def remote(self, src, dst, send, recv, target):
        return pltpu.make_async_remote_copy(
            src_ref=src,
            dst_ref=dst,
            send_sem=send,
            recv_sem=recv,
            device_id=(target, self.gy),
            device_id_type=MESH,
        )

    def columns(self):
        return [(j, slice(s, s + w)) for j, (s, w) in enumerate(spans(self.wide))]

    def swap(self, m, j, at):
        here = (slice(0, self.half), at)
        return self.remote(
            self.bufs[m].at[here],
            self.a_all.at[m, :, at],
            self.a_send.at[m, j],
            self.a_recv.at[m, j],
            self.partner,
        )

    def block(self, m, device, start=0, size=None):
        size = self.r if size is None else size
        first = self.half + (device // 2) * self.r + start
        return self.bufs[m].at[pl.ds(pl.multiple_of(first, 16), size)]

    def first(self, m):
        for j, at in self.columns():
            self.bufs[m][: self.half, at] = self.product(m, 1 - self.core, at).astype(bf16)
            self.swap(m, j, at).start()

    def corner(self, m, h):
        side, along, across = square()
        half = self.r // 2
        return self.remote(
            self.block(m, across, h * half, half),
            self.r_all.at[m, h],
            self.r_send.at[m, h],
            self.r_recv.at[m, h],
            along if h else side,
        )

    def second(self, m):
        for j, at in self.columns():
            self.swap(m, j, at).wait_recv()
            landed = self.abuf.at[:, at]
            fetch = pltpu.make_async_copy(self.a_all.at[m, :, at], landed, self.local.at[0])
            fetch.start()
            mine = self.product(m, self.core, at)
            fetch.wait()
            self.bufs[m][self.half :, at] = (mine + landed[...].astype(f32)).astype(bf16)
        if m in self.late:
            self.keep(m).start()
        elif self.four:
            for h in range(2):
                self.corner(m, h).start()

    def keep(self, m):
        kept = self.outs[m]
        return pltpu.make_async_copy(
            self.bufs[m].at[pl.ds(self.half, self.half)], kept, self.local.at[max(len(self.near), 2)]
        )

    def hand(self, m, k):
        target = self.near[k]
        return self.remote(
            self.block(m, target),
            self.c_all.at[m, k],
            self.c_send.at[m, k],
            self.c_recv.at[m, k],
            target,
        )

    def third(self, m):
        if self.four:
            side, along, _ = square()
            half = self.r // 2
            for h, device in ((0, along), (1, side)):
                self.corner(m, h).wait_recv()
                here = self.block(m, device, h * half, half)
                landed = self.abuf.at[h * half : (h + 1) * half]
                fetch = pltpu.make_async_copy(self.r_all.at[m, h], landed, self.local.at[0])
                fetch.start()
                fetch.wait()
                here[...] = (here[...].astype(f32) + landed[...].astype(f32)).astype(bf16)
        for k in range(len(self.near)):
            self.hand(m, k).start()

    def fourth(self, m):
        for j, at in self.columns():
            self.swap(m, j, at).wait_send()
        fetches = []
        for k in range(len(self.near)):
            self.hand(m, k).wait_recv()
            here = self.bufs[m].at[pl.ds(k * self.r, self.r)]
            fetch = pltpu.make_async_copy(self.c_all.at[m, k], here, self.local.at[k])
            fetch.start()
            fetches.append(fetch)
        for fetch in fetches:
            fetch.wait()
        first = pl.multiple_of(self.half + self.chip * self.r, 16)
        for _, at in self.columns():
            total = self.bufs[m][pl.ds(first, self.r), at].astype(f32)
            for k in range(len(self.near)):
                total = total + self.bufs[m][k * self.r : (k + 1) * self.r, at].astype(f32)
            stage = self.fbuf if total.shape[1] == FF_CHUNK else self.ftail
            stage[...] = total
            store = pltpu.make_async_copy(stage, self.outs[m].at[:, at], self.local.at[0])
            store.start()
            store.wait()

    def drain(self, m):
        if self.four:
            for h in range(2):
                self.corner(m, h).wait_send()
        for k in range(len(self.near)):
            self.hand(m, k).wait_send()


def reduce_scratch(width, hidden, count=3):
    devices = lax.axis_size("gx")
    rows, parts = width // devices, len(spans(hidden))
    near = 2 if devices == 8 else devices // 2 - 1
    dma = pltpu.SemaphoreType.DMA
    return [
        pltpu.VMEM((width // 2, hidden), bf16),
        pltpu.VMEM((rows, FF_CHUNK), f32),
        pltpu.VMEM((rows, hidden % FF_CHUNK), f32),
        dma((count, parts)),
        dma((count, parts)),
        dma((count, 2)),
        dma((count, 2)),
        dma((count, near)),
        dma((count, near)),
        dma((max(near, 2) + 1,)),
    ]


class Tail:
    def __init__(self, b_all, r_all, c_all, outs, abuf, fbuf, ftail, sems):
        self.b_all, self.r_all, self.c_all, self.outs = b_all, r_all, c_all, outs
        self.abuf, self.fbuf, self.ftail = abuf, fbuf, ftail
        self.r_send, self.r_recv, self.c_send, self.c_recv, self.local = sems
        gx, self.gy = lax.axis_index("gx"), lax.axis_index("gy")
        self.chip, chips = gx // 2, lax.axis_size("gx") // 2
        self.r = b_all.shape[1] // chips
        self.part = self.r // 2
        self.space = b_all.shape[1] // b_all.shape[0]
        self.four = chips == 4
        self.near = list(square()[:2]) if self.four else places()[1]

    def remote(self, src, dst, send, recv, target):
        return pltpu.make_async_remote_copy(
            src_ref=src,
            dst_ref=dst,
            send_sem=send,
            recv_sem=recv,
            device_id=(target, self.gy),
            device_id_type=MESH,
        )

    def held(self, i, chip, h):
        first = pl.multiple_of(chip * self.r + h * self.part, 16)
        return self.b_all.at[i, pl.ds(first, self.part)]

    def slot(self, i, k):
        return self.abuf.at[pl.ds(i * self.space + k * self.part, self.part)]

    def corner(self, i, h):
        side, along, across = square()
        return self.remote(
            self.held(i, across // 2, h),
            self.r_all.at[i, h],
            self.r_send.at[i, h],
            self.r_recv.at[i, h],
            along if h else side,
        )

    def hand(self, i, k, h):
        target = self.near[k]
        summed = self.four and k != h
        return self.remote(
            self.slot(i, 2 + h) if summed else self.held(i, target // 2, h),
            self.c_all.at[i, k, h],
            self.c_send.at[i, k, h],
            self.c_recv.at[i, k, h],
            target,
        )

    def hands(self):
        return [(k, h) for k in range(len(self.near)) for h in range(2)]

    def begin(self, i):
        if self.four:
            for h in range(2):
                self.corner(i, h).start()

    def middle(self, i):
        if self.four:
            side, along, _ = square()
            for h, device in ((0, along), (1, side)):
                self.corner(i, h).wait_recv()
                came, mine = self.slot(i, h), self.slot(i, 2 + h)
                fetches = [
                    pltpu.make_async_copy(self.r_all.at[i, h], came, self.local.at[0]),
                    pltpu.make_async_copy(self.held(i, device // 2, h), mine, self.local.at[1]),
                ]
                for fetch in fetches:
                    fetch.start()
                for fetch in fetches:
                    fetch.wait()
                mine[...] = (mine[...].astype(f32) + came[...].astype(f32)).astype(bf16)
        for k, h in self.hands():
            self.hand(i, k, h).start()

    def close(self, i):
        if self.four:
            for h in range(2):
                self.corner(i, h).wait_send()
        for k, h in self.hands():
            self.hand(i, k, h).wait_send()
        count = len(self.near)
        for h in range(2):
            fetches = [
                pltpu.make_async_copy(
                    self.held(i, self.chip, h), self.slot(i, count), self.local.at[count]
                )
            ]
            for k in range(count):
                self.hand(i, k, h).wait_recv()
                fetches.append(
                    pltpu.make_async_copy(
                        self.c_all.at[i, k, h], self.slot(i, k), self.local.at[k]
                    )
                )
            for fetch in fetches:
                fetch.start()
            for fetch in fetches:
                fetch.wait()
            for start, width in spans(self.abuf.shape[1]):
                at = slice(start, start + width)
                total = self.slot(i, 0)[:, at].astype(f32)
                for k in range(1, count + 1):
                    total = total + self.slot(i, k)[:, at].astype(f32)
                stage = self.fbuf if width == FF_CHUNK else self.ftail
                stage[: self.part] = total
                store = pltpu.make_async_copy(
                    stage.at[pl.ds(0, self.part)],
                    self.outs[i].at[pl.ds(h * self.part, self.part), at],
                    self.local.at[0],
                )
                store.start()
                store.wait()


def tail_scratch(count):
    devices = lax.axis_size("gx")
    near = 2 if devices == 8 else devices // 2 - 1
    dma = pltpu.SemaphoreType.DMA
    return [
        dma((count, 2)),
        dma((count, 2)),
        dma((count, near, 2)),
        dma((count, near, 2)),
        dma((near + 1,)),
    ]


def store_turned(block, turned, b):
    count, width = block.shape
    _, chips_rows, _ = turned.shape
    devices = lax.axis_size("gx")
    r = width // devices
    flipped = block.T
    at = pl.ds(pl.multiple_of(b * count, count), count)
    for k in range(devices):
        q = k // 2
        turned[k % 2, q * r : (q + 1) * r, at] = flipped[k * r : (k + 1) * r]


AFTER = {
    0: (("first", 0),),
    1: (("second", 0), ("swap", 0), ("first", 1)),
    2: (("third", 0), ("second", 1)),
}
WHOLE_END = (("first", 2), ("third", 1), ("second", 2), ("fourth", 0), ("third", 2))
WHOLE_END += (("fourth", 1), ("fourth", 2), ("drain", 0), ("drain", 1), ("drain", 2))
LATE_END = (("kept", 1), ("first", 2), ("second", 2), ("fourth", 0), ("kept", 2))
LATE_END += (("sent", 1), ("sent", 2), ("drain", 0))


TAIL_BEGIN, TAIL_MIDDLE = ("step", 0), ("step", 2)


def both(one, other):
    def act():
        one()
        other()

    return act


def backward_kernel(late, tails, *refs):
    grad_ref, gate_ref, up_ref, hidden_ref, turned_ref, wg_ref, wu_ref, wd_ref = refs[:8]
    held, refs = refs[8 : 8 + (tails > 0)], refs[8 + (tails > 0) :]
    sum_ref, refs = refs[0], refs[1:]
    if late:
        od, b_all, a_all, r_all, c_all = refs[:5]
        outs, refs = (od, b_all.at[0], b_all.at[1]), refs[5:]
    else:
        og, ou, od, a_all, r_all, c_all = refs[:6]
        outs, refs = (od, og, ou), refs[6:]
    tail_refs, scratch = refs[: tails + 2 * (tails > 0)], refs[tails + 2 * (tails > 0) :]
    gathered, part, outb, inb = scratch[:4]
    sems = scratch[4:LINE]
    wg, wu, wd, gate, up, hidden, turned, w_sem = scratch[LINE : LINE + 8]
    abuf, fbuf, ftail = scratch[LINE + 8 : LINE + 11]
    operands = (
        (wd_ref, wd),
        (gate_ref, gate),
        (up_ref, up),
        (wg_ref, wg),
        (wu_ref, wu),
        (hidden_ref, hidden),
    )
    loads = [
        pltpu.make_async_copy(src, dst, w_sem.at[k]) for k, (src, dst) in enumerate(operands)
    ]
    for copy in loads:
        copy.start()

    def load():
        for copy in loads:
            copy.wait()

    reduce = Reduce(
        turned,
        (hidden, gate, up),
        (wd, wg, wu),
        abuf,
        fbuf,
        ftail,
        a_all,
        r_all,
        c_all,
        outs,
        late,
        scratch[LINE + 11 : LINE + 18],
    )
    tail = None
    if tails:
        tail = Tail(
            held[0],
            tail_refs[tails],
            tail_refs[tails + 1],
            tail_refs[:tails],
            abuf,
            fbuf,
            ftail,
            scratch[LINE + 18 :],
        )

    def finish(b):
        block = gathered[b]
        store_turned(block, turned, b)
        for start, width in spans(wg.shape[1]):
            at = slice(start, start + width)
            d = nn(block, wd[:, at])
            g = gate[b, :, at].astype(f32)
            u = up[b, :, at].astype(f32)
            sigma = lax.logistic(g)
            ds = d * sigma
            dg = (ds * u * (1.0 + g * (1.0 - sigma))).astype(bf16)
            du = (ds * g).astype(bf16)
            gate[b, :, at] = dg
            up[b, :, at] = du
            p = nt(dg, wg[:, at]) + nt(du, wu[:, at])
            if start == 0:
                part[...] = p
            else:
                part[...] += p

    def run(verb, m):
        if verb == "swap":
            copy = pltpu.make_async_copy(turned_ref, turned, w_sem.at[0])
            copy.start()
            copy.wait()
        elif verb == "kept":
            reduce.keep(m).wait()
        elif verb == "sent":
            for j, at in reduce.columns():
                reduce.swap(m, j, at).wait_send()
        else:
            getattr(reduce, verb)(m)

    def work(t):
        def act():
            if tail is not None and t == 1:
                for i in range(tails):
                    tail.close(i)
            for verb, m in AFTER[t]:
                run(verb, m)

        return act

    def each(verb):
        def act():
            for i in range(tails):
                getattr(tail, verb)(i)

        return act

    peers = [reduce.partner] + reduce.near
    plan = {("hop", t): work(t) for t in range(3)}
    if tails:
        for key, act in ((TAIL_BEGIN, each("begin")), (TAIL_MIDDLE, each("middle"))):
            old = plan.get(key)
            plan[key] = act if old is None else both(act, old)
    line_pass(grad_ref, sum_ref, gathered, part, outb, inb, sems, load, finish, peers, plan)
    for verb, m in LATE_END if late else WHOLE_END:
        run(verb, m)


def backward_ffn(grad, gate, up, hidden, turned, wg, wu, wd, late=False, held=None):
    rows, width = grad.shape
    devices, size, wide = lax.axis_size("gx"), lax.axis_size("gy"), wg.shape[1]
    near = 2 if devices == 8 else devices // 2 - 1
    r = width // devices
    mine = jax.ShapeDtypeStruct((r, wide), f32)

    def between(*dims):
        return jax.ShapeDtypeStruct(dims + (wide,), bf16)

    count = 1 if late else 3
    out = [jax.ShapeDtypeStruct((rows, width), f32)]
    out += [mine, between(2, width // 2)] if late else [mine] * 3
    out += [between(3, width // 2), between(count, 2, r // 2), between(count, near, r)]
    tails = 0 if held is None else held.shape[0]
    if tails:
        out += [mine] * tails
        out += [between(tails, 2, r // 2), between(tails, near, 2, r // 2)]
    extra = [held] if tails else []
    return pl.pallas_call(
        functools.partial(backward_kernel, (1, 2) if late else (), tails),
        out_shape=out,
        in_specs=[ANY] * (8 + len(extra)),
        out_specs=[pl.BlockSpec(memory_space=pltpu.VMEM)] + [ANY] * (len(out) - 1),
        scratch_shapes=line_scratch(size, rows, width)
        + [pltpu.VMEM((width, wide), bf16)] * 3
        + [pltpu.VMEM((size, rows, wide), bf16)] * 3
        + [pltpu.VMEM((2, width // 2, size * rows), bf16), pltpu.SemaphoreType.DMA((6,))]
        + reduce_scratch(width, wide)
        + (tail_scratch(tails) if tails else []),
        compiler_params=pltpu.CompilerParams(
            collective_id=1 if late else 5, has_side_effects=True, vmem_limit_bytes=VMEM_LIMIT
        ),
        cost_estimate=pl.CostEstimate(
            flops=12 * size * rows * width * wide, bytes_accessed=40 << 20, transcendentals=0
        ),
        name="ffn_backward",
    )(grad, gate, up, hidden, turned, wg, wu, wd, *extra)


class Fold:
    def __init__(self, lhs, rhs, bufs, sems):
        self.lhs, self.rhs = lhs, rhs
        self.up, self.low, self.a_in, self.r_in, self.c_in, self.z_out, self.z_in = bufs
        (
            self.a_send,
            self.a_recv,
            self.r_send,
            self.r_recv,
            self.c_send,
            self.c_recv,
            self.z_send,
            self.z_recv,
        ) = sems
        self.gx, self.gy = lax.axis_index("gx"), lax.axis_index("gy")
        self.core, self.size = lax.rem(self.gx, 2), lax.axis_size("gy")
        self.chips = lax.axis_size("gx") // 2
        self.r = self.low.shape[2] // self.chips
        self.four = self.chips == 4
        self.partner, self.others = places()
        self.near = list(square()[:2]) if self.four else self.others

    def product(self, m, which, z):
        return [nn(left[which], right[z]) for left, right in zip(self.lhs[m], self.rhs[m])]

    def remote(self, src, dst, send, recv, gx, gy):
        return pltpu.make_async_remote_copy(
            src_ref=src,
            dst_ref=dst,
            send_sem=send,
            recv_sem=recv,
            device_id=(gx, gy),
            device_id_type=MESH,
        )

    def block(self, m, device, start=0, size=None):
        size = self.r if size is None else size
        first = (device // 2) * self.r + start
        return self.low.at[m, :, pl.ds(pl.multiple_of(first, 16), size)]

    def swap(self, m, z):
        return self.remote(
            self.up.at[m, z],
            self.a_in.at[m, z],
            self.a_send.at[m, z],
            self.a_recv.at[m, z],
            self.partner,
            self.gy,
        )

    def first(self, m):
        for z in range(self.size):
            left, right = self.product(m, 1 - self.core, z)
            edge = left.shape[1]
            self.up[m, z, :, :edge] = left.astype(bf16)
            self.up[m, z, :, edge:] = right.astype(bf16)
            self.swap(m, z).start()

    def corner(self, m, h):
        side, along, across = square()
        half = self.r // 2
        return self.remote(
            self.block(m, across, h * half, half),
            self.r_in.at[m, h],
            self.r_send.at[m, h],
            self.r_recv.at[m, h],
            along if h else side,
            self.gy,
        )

    def second(self, m):
        for z in range(self.size):
            left, right = self.product(m, self.core, z)
            edge = left.shape[1]
            self.swap(m, z).wait_recv()
            came = self.a_in[m, z].astype(f32)
            self.low[m, z, :, :edge] = (left + came[:, :edge]).astype(bf16)
            self.low[m, z, :, edge:] = (right + came[:, edge:]).astype(bf16)
        if self.four:
            for h in range(2):
                self.corner(m, h).start()

    def hand(self, m, k):
        return self.remote(
            self.block(m, self.near[k]),
            self.c_in.at[m, k],
            self.c_send.at[m, k],
            self.c_recv.at[m, k],
            self.near[k],
            self.gy,
        )

    def third(self, m):
        if self.four:
            side, along, _ = square()
            half = self.r // 2
            for h, device in ((0, along), (1, side)):
                self.corner(m, h).wait_recv()
                here = self.block(m, device, h * half, half)
                here[...] = (here[...].astype(f32) + self.r_in[m, h].astype(f32)).astype(bf16)
        for k in range(len(self.near)):
            self.hand(m, k).start()

    def down_line(self, m, d):
        target = lax.rem(self.gy + d, self.size)
        return self.remote(
            self.z_out.at[m, target],
            self.z_in.at[m, self.gy],
            self.z_send.at[m, d],
            self.z_recv.at[m, self.gy],
            self.gx,
            target,
        )

    def fourth(self, m):
        for k in range(len(self.near)):
            self.hand(m, k).wait_recv()
        mine = self.block(m, self.gx)
        for z in range(self.size):
            total = mine[z].astype(f32)
            for k in range(len(self.near)):
                total = total + self.c_in[m, k, z].astype(f32)
            self.z_out[m, z] = total.astype(bf16)
        for d in range(1, self.size):
            self.down_line(m, d).start()

    def fifth(self, m, out):
        total = self.z_out[m, self.gy].astype(f32)
        for d in range(1, self.size):
            z = lax.rem(self.gy + d, self.size)
            wait_for(self.z_in.at[m, z], self.z_recv.at[m, z])
            total = total + self.z_in[m, z].astype(f32)
        out[m] = total

    def drain(self, m):
        for z in range(self.size):
            self.swap(m, z).wait_send()
        if self.four:
            for h in range(2):
                self.corner(m, h).wait_send()
        for k in range(len(self.near)):
            self.hand(m, k).wait_send()
        for d in range(1, self.size):
            self.down_line(m, d).wait_send()


class Total:
    def __init__(self, own, line_in, pair, pair_in, chip_in, sems):
        self.own, self.line_in, self.pair = own, line_in, pair
        self.pair_in, self.chip_in = pair_in, chip_in
        self.l_send, self.l_recv, self.p_send, self.p_recv, self.g_send, self.g_recv = sems
        self.gx, self.gy = lax.axis_index("gx"), lax.axis_index("gy")
        self.size, self.chips = lax.axis_size("gy"), lax.axis_size("gx") // 2
        self.partner, self.others = places()

    def remote(self, src, dst, send, recv, gx, gy):
        return pltpu.make_async_remote_copy(
            src_ref=src,
            dst_ref=dst,
            send_sem=send,
            recv_sem=recv,
            device_id=(gx, gy),
            device_id_type=MESH,
        )

    def line(self, d):
        target = lax.rem(self.gy + d, self.size)
        return self.remote(
            self.own.at[target],
            self.line_in.at[self.gy],
            self.l_send.at[d],
            self.l_recv.at[self.gy],
            self.gx,
            target,
        )

    def across(self):
        return self.remote(
            self.pair.at[0], self.pair_in, self.p_send, self.p_recv, self.partner, self.gy
        )

    def chip(self, k):
        return self.remote(
            self.pair.at[1],
            self.chip_in.at[self.gx // 2],
            self.g_send.at[k],
            self.g_recv.at[self.gx // 2],
            self.others[k],
            self.gy,
        )

    def begin(self):
        for d in range(1, self.size):
            self.line(d).start()

    def middle(self):
        total = self.own[self.gy]
        for d in range(1, self.size):
            z = lax.rem(self.gy + d, self.size)
            wait_for(self.line_in.at[z], self.l_recv.at[z])
            total = total + self.line_in[z]
        self.pair[0] = total
        self.across().start()

    def later(self):
        self.across().wait_recv()
        self.pair[1] = self.pair[0] + self.pair_in[...]
        self.chip_in[self.gx // 2] = self.pair[1]
        for k in range(self.chips - 1):
            self.chip(k).start()

    def close(self, out):
        for k in range(self.chips - 1):
            q = self.others[k] // 2
            wait_for(self.chip_in.at[q], self.g_recv.at[q])
        total = self.chip_in[0]
        for q in range(1, self.chips):
            total = total + self.chip_in[q]
        out[...] = total
        for d in range(1, self.size):
            self.line(d).wait_send()
        self.across().wait_send()
        for k in range(self.chips - 1):
            self.chip(k).wait_send()


def closing_kernel(layers, *refs):
    operands, refs = refs[: 4 * layers], refs[4 * layers :]
    small, out_rows, grad_rows = refs[:3]
    grads, small_out, out_blocks, grad_blocks = refs[3:7]
    scratch = refs[7:]
    lhs = [operands[4 * m : 4 * m + 2] for m in range(layers)]
    rhs = [operands[4 * m + 2 : 4 * m + 4] for m in range(layers)]
    fold = Fold(lhs, rhs, scratch[:7], scratch[7:15])
    total = Total(small, *scratch[15:19], scratch[19:25])
    swaps = [
        Exchange(own, full, scratch[25 + 3 * k : 28 + 3 * k], True)
        for k, (own, full) in enumerate(((grad_rows, grad_blocks), (out_rows, out_blocks)))
    ]
    me, size = lax.axis_index("gy"), lax.axis_size("gy")
    greet([fold.partner] + fold.others, [lax.rem(me + d, size) for d in range(1, size)])
    total.begin()
    for m in range(layers):
        fold.first(m)
    for swap in swaps:
        swap.begin()
    fold.second(0)
    total.middle()
    for m in range(1, layers):
        fold.second(m)
    total.later()
    for m in range(layers):
        fold.third(m)
    for m in range(layers):
        fold.fourth(m)
    total.close(small_out)
    for m in range(layers):
        fold.fifth(m, grads)
    for m in range(layers):
        fold.drain(m)
    for swap in swaps:
        swap.close()


def closing(operands, small, out_rows, grad_rows):
    layers = len(operands) // 4
    devices, size = lax.axis_size("gx"), lax.axis_size("gy")
    half = operands[0].shape[1]
    chips = devices // 2
    r, near = half // chips, 2 if chips == 4 else chips - 1
    c = operands[2].shape[2] + operands[3].shape[2]
    vmem, dma = pltpu.VMEM, pltpu.SemaphoreType.DMA
    row = small.shape[1:]
    local = pl.BlockSpec(memory_space=pltpu.VMEM)
    blocks = jax.ShapeDtypeStruct(out_rows.shape, bf16)
    return pl.pallas_call(
        functools.partial(closing_kernel, layers),
        out_shape=[
            jax.ShapeDtypeStruct((layers, r, c), f32),
            jax.ShapeDtypeStruct(row, f32),
            blocks,
            blocks,
        ],
        in_specs=[local] * (len(operands) + 1) + [ANY] * 2,
        out_specs=[local] * 2 + [ANY] * 2,
        scratch_shapes=[
            vmem((layers, size, half, c), bf16),
            vmem((layers, size, half, c), bf16),
            vmem((layers, size, half, c), bf16),
            vmem((layers, 2, size, r // 2, c), bf16),
            vmem((layers, near, size, r, c), bf16),
            vmem((layers, size, r, c), bf16),
            vmem((layers, size, r, c), bf16),
            dma((layers, size)),
            dma((layers, size)),
            dma((layers, 2)),
            dma((layers, 2)),
            dma((layers, near)),
            dma((layers, near)),
            dma((layers, size)),
            dma((layers, size)),
            vmem((size,) + row, f32),
            vmem((2,) + row, f32),
            vmem(row, f32),
            vmem((chips,) + row, f32),
            dma((size,)),
            dma((size,)),
            dma,
            dma,
            dma((chips,)),
            dma((chips,)),
        ]
        + exchange_scratch() * 2,
        compiler_params=pltpu.CompilerParams(
            collective_id=4, has_side_effects=True, vmem_limit_bytes=VMEM_LIMIT
        ),
        name="closing",
    )(*operands, small, out_rows, grad_rows)


def swing(value, cosine, turned_sine):
    return value * cosine + pltpu.roll(value, HEAD_DIM // 2, 1) * turned_sine


def tile_columns(value, tables):
    heads = value.shape[1] // HEAD_DIM
    parts = [swing(value[:, k * HEAD_DIM : (k + 1) * HEAD_DIM], *tables) for k in range(heads)]
    return jnp.concatenate(parts, axis=1)


def store_split(block, turned):
    width = block.shape[1]
    devices = lax.axis_size("gx")
    r = width // devices
    flipped = block.T
    for k in range(devices):
        q = k // 2
        turned[k % 2, q * r : (q + 1) * r] = flipped[k * r : (k + 1) * r]


def norm_pull(grad, normed, scale, gain):
    row = jnp.sum(grad * normed, axis=0, keepdims=True)
    scaled = grad * gain
    project = jnp.mean(scaled * normed, axis=1, keepdims=True)
    return row, scale * (scaled - normed * project)


def attention_pull_kernel(*refs):
    (grad, grad_ffn, norm_b, scale_b, gain_b, norm_a, scale_a, gain_a) = refs[:8]
    acts, q, k, v, lse, cosine, sine, qkv_ref, out_ref = refs[8:17]
    grad_out, grad_low, acts_turned, branch_turned, gqkv, small = refs[17:23]
    qkv, wout, heads, branch, dq, dk_sum, dv_sum, kv_out, kv_in, total = refs[23:33]
    w_sem, kv_send, kv_recv = refs[33:]
    gx, me, size = lax.axis_index("gx"), lax.axis_index("gy"), lax.axis_size("gy")
    count, rows = q.shape[0], k.shape[0]
    loads = [
        pltpu.make_async_copy(out_ref, wout, w_sem.at[0]),
        pltpu.make_async_copy(qkv_ref, qkv, w_sem.at[1]),
    ]
    for load in loads:
        load.start()
    greet([], [lax.rem(me + d, size) for d in range(1, size)])
    small[...] = jnp.zeros_like(small)
    row, pulled = norm_pull(grad_ffn[...], norm_b[...], scale_b[...], gain_b[...])
    small[1:2] = row
    branch[...] = grad[...] + pulled
    low = branch[...].astype(bf16)
    store_split(low, branch_turned)
    store_split(acts[...], acts_turned)
    loads[0].wait()
    cq = wout.shape[2]
    heads[...] = jnp.concatenate([nn(low, wout[z]) for z in range(size)], axis=1).astype(bf16)

    query = me * count + lax.broadcasted_iota(jnp.int32, (rows, count), 1)
    key = lax.broadcasted_iota(jnp.int32, (rows, count), 0)
    allowed = key <= query
    if rows > LEN:
        allowed = jnp.logical_and(allowed, key // LEN == query // LEN)
    factor = 1.0 / math.sqrt(HEAD_DIM)
    tables = (cosine[...], sine[...])

    def kv_copy(g, d):
        target = lax.rem(me + d, size)
        return pltpu.make_async_remote_copy(
            src_ref=kv_out.at[g, target],
            dst_ref=kv_in.at[g, me],
            send_sem=kv_send.at[g, d],
            recv_sem=kv_recv.at[g, me],
            device_id=(gx, target),
            device_id_type=MESH,
        )

    for g in range(KV_HEADS):
        span = slice(g * HEAD_DIM, (g + 1) * HEAD_DIM)
        kg, vg = k[:, span], v[:, span]
        turned_k = kg.T
        dk_sum[...] = jnp.zeros_like(dk_sum)
        dv_sum[...] = jnp.zeros_like(dv_sum)

        def head(i, carry):
            h = g * GROUP + i
            at = pl.ds(pl.multiple_of(h * HEAD_DIM, HEAD_DIM), HEAD_DIM)
            qh, dh = q[:, at], heads[:, at]
            scores = jnp.where(allowed, nt(kg, qh) * factor, -1e30)
            p = jnp.exp(scores - lse[pl.ds(h, 1), :])
            dp = nt(vg, dh)
            inner = jnp.sum(p * dp, axis=0, keepdims=True)
            ds = (p * (dp - inner)).astype(bf16)
            dv_sum[...] += nn(p.astype(bf16), dh)
            dk_sum[...] += nn(ds, qh)
            dq[:, at] = swing(nn(turned_k, ds).T * factor, *tables).astype(bf16)
            return carry

        lax.fori_loop(0, GROUP, head, 0)
        for z in range(size):
            at = slice(z * count, (z + 1) * count)
            kv_out[g, z, :, :HEAD_DIM] = (dk_sum[at] * factor).astype(bf16)
            kv_out[g, z, :, HEAD_DIM:] = dv_sum[at].astype(bf16)
        for d in range(1, size):
            kv_copy(g, d).start()

    loads[1].wait()
    apart = cq % HEAD_DIM == 0
    if apart:
        for z in range(size):
            p = nt(dq[:, z * cq : (z + 1) * cq], qkv[z, :, :cq])
            if z == 0:
                total[...] = p
            else:
                total[...] += p
    dks, dvs = [], []
    for g in range(KV_HEADS):
        summed = kv_out[g, me].astype(f32)
        for d in range(1, size):
            z = lax.rem(me + d, size)
            wait_for(kv_in.at[g, z], kv_recv.at[g, z])
            summed = summed + kv_in[g, z].astype(f32)
        dks.append(swing(summed[:, :HEAD_DIM], *tables).astype(bf16).astype(f32))
        dvs.append(summed[:, HEAD_DIM:].astype(bf16).astype(f32))
    dk, dv = jnp.concatenate(dks, axis=1), jnp.concatenate(dvs, axis=1)
    ck = dk.shape[1] // size
    for z in range(size):
        at = slice(z * ck, (z + 1) * ck)
        kv = jnp.concatenate([dk[:, at], dv[:, at]], axis=1)
        if apart:
            kv = kv.astype(bf16)
            gqkv[z, :, :cq] = dq[:, z * cq : (z + 1) * cq]
            gqkv[z, :, cq:] = kv
            total[...] += nt(kv, qkv[z, :, cq:])
        else:
            mine = dq[:, z * cq : (z + 1) * cq].astype(f32)
            gqkv[z] = jnp.concatenate([mine, kv], axis=1).astype(bf16)
            p = nt(gqkv[z], qkv[z])
            if z == 0:
                total[...] = p
            else:
                total[...] += p
    row, pulled = norm_pull(total[...], norm_a[...], scale_a[...], gain_a[...])
    small[0:1] = row
    small[2:3] = jnp.sum(dq[...].astype(f32), axis=0, keepdims=True)
    width = dk.shape[1]
    small[3:4, :width] = jnp.sum(dk, axis=0, keepdims=True)
    small[4:5, :width] = jnp.sum(dv, axis=0, keepdims=True)
    final = branch[...] + pulled
    grad_out[...] = final
    grad_low[...] = final.astype(bf16)
    for g in range(KV_HEADS):
        for d in range(1, size):
            kv_copy(g, d).wait_send()


def attention_pull(vectors, acts, q, k, v, lse, tables, qkv, wout):
    count, width = acts.shape
    size, rows = lax.axis_size("gy"), k.shape[0]
    local = pl.BlockSpec(memory_space=pltpu.VMEM)
    vmem, dma = pltpu.VMEM, pltpu.SemaphoreType.DMA
    turned = jax.ShapeDtypeStruct((2, width // 2, count), bf16)
    return pl.pallas_call(
        attention_pull_kernel,
        out_shape=[
            jax.ShapeDtypeStruct((count, width), f32),
            jax.ShapeDtypeStruct((count, width), bf16),
            turned,
            turned,
            jax.ShapeDtypeStruct((size, count, qkv.shape[2]), bf16),
            jax.ShapeDtypeStruct((8, width), f32),
        ],
        in_specs=[local] * 15 + [ANY] * 2,
        out_specs=[local] * 6,
        scratch_shapes=[
            vmem(qkv.shape, bf16),
            vmem(wout.shape, bf16),
            vmem((count, width), bf16),
            vmem((count, width), f32),
            vmem((count, width), bf16),
            vmem((rows, HEAD_DIM), f32),
            vmem((rows, HEAD_DIM), f32),
            vmem((KV_HEADS, size, count, 2 * HEAD_DIM), bf16),
            vmem((KV_HEADS, size, count, 2 * HEAD_DIM), bf16),
            vmem((count, width), f32),
            dma((2,)),
            dma((KV_HEADS, size)),
            dma((KV_HEADS, size)),
        ],
        compiler_params=pltpu.CompilerParams(
            collective_id=6, has_side_effects=True, vmem_limit_bytes=VMEM_LIMIT
        ),
        name="attention_pull",
    )(*vectors, acts, q, k, v, lse, *tables, qkv, wout)


def greet_line(gx_peers=()):
    gx, me, last = lax.axis_index("gx"), lax.axis_index("gy"), lax.axis_size("gy") - 1
    barrier = pltpu.get_barrier_semaphore()

    @pl.when(me > 0)
    def _():
        pl.semaphore_signal(barrier, inc=1, device_id=(gx, me - 1), device_id_type=MESH)

    @pl.when(me < last)
    def _():
        pl.semaphore_signal(barrier, inc=1, device_id=(gx, me + 1), device_id_type=MESH)

    for peer in gx_peers:
        pl.semaphore_signal(barrier, inc=1, device_id=(peer, me), device_id_type=MESH)
    count = jnp.where(jnp.logical_and(me > 0, me < last), 2, 1)
    pl.semaphore_wait(barrier, count + len(gx_peers))


PUSH_PLAN = {
    "chained": ("begin",),
    "group0": ("relay",),
    "group1": ("finish",),
    "end": ("close",),
}


def attention_push_kernel(layer, *refs):
    shard_ref, whole_ref = refs[10], refs[23]
    refs = refs[:10] + refs[11:23] + refs[24:]
    x, gain_a, gain_b, bq, bk, bv, cosine, sine, qkv_ref, out_ref = refs[:10]
    middle, norm_a, scale_a, acts_a, q, k_all, v_all, lse = refs[10:18]
    mixed, norm_b, scale_b, acts_b = refs[18:22]
    qkv, wout, kv_own, kv_all, flat, w_sem = refs[22:28]
    me, size = lax.axis_index("gy"), lax.axis_size("gy")
    count, rows = x.shape[0], k_all.shape[0]
    loads = [
        pltpu.make_async_copy(qkv_ref, qkv, w_sem.at[0]),
        pltpu.make_async_copy(out_ref, wout, w_sem.at[1]),
    ]
    for load in loads:
        load.start()
    chain = Chain(kv_own, kv_all, refs[28:31])
    spread = Spread([(shard_ref.at[layer], whole_ref)], refs[31:34])

    def move(name):
        for verb in PUSH_PLAN.get(name, ()):
            getattr(spread, verb)(0)

    greet_line([spread.partner] + spread.near)
    move("greeted")
    value = x[...]
    scale = lax.rsqrt(jnp.mean(value * value, axis=1, keepdims=True) + epsilon)
    scale_a[...] = scale
    norm_a[...] = value * scale
    acts_a[...] = (norm_a[...] * gain_a[...]).astype(bf16)
    loads[0].wait()
    cq, width = wout.shape[2], k_all.shape[1]
    ck = width // size
    tables = (cosine[...], sine[...])
    apart = cq % HEAD_DIM == 0
    if apart:
        kv = [nn(acts_a[...], qkv[z, :, cq:]) for z in range(size)]
    else:
        both = [nn(acts_a[...], qkv[z]) for z in range(size)]
        kv = [part[:, cq:] for part in both]
    keys = jnp.concatenate([part[:, :ck] for part in kv], axis=1) + bk[...]
    values = jnp.concatenate([part[:, ck:] for part in kv], axis=1) + bv[...]
    kv_own[:, :width] = tile_columns(keys, tables).astype(bf16)
    kv_own[:, width:] = values.astype(bf16)
    chain.begin()
    move("chained")
    if apart:
        for z in range(size):
            at = slice(z * cq, (z + 1) * cq)
            mine = nn(acts_a[...], qkv[z, :, :cq]) + bq[:, at]
            q[:, at] = tile_columns(mine, tables).astype(bf16)
            if z:
                chain.relay(z)
    else:
        mine = jnp.concatenate([part[:, :cq] for part in both], axis=1) + bq[...]
        q[...] = tile_columns(mine, tables).astype(bf16)
        for t in range(1, size):
            chain.relay(t)
    chain.close()
    move("relayed")
    k_all[...] = kv_all[:, :, :width].reshape(rows, width)
    v_all[...] = kv_all[:, :, width:].reshape(rows, width)

    query = me * count + lax.broadcasted_iota(jnp.int32, (rows, count), 1)
    key = lax.broadcasted_iota(jnp.int32, (rows, count), 0)
    allowed = key <= query
    if rows > LEN:
        allowed = jnp.logical_and(allowed, key // LEN == query // LEN)
    factor = 1.0 / math.sqrt(HEAD_DIM)
    for g in range(KV_HEADS):
        span = slice(g * HEAD_DIM, (g + 1) * HEAD_DIM)
        kg, turned_v = k_all[:, span], v_all[:, span].T

        def head(i, carry):
            h = g * GROUP + i
            at = pl.ds(pl.multiple_of(h * HEAD_DIM, HEAD_DIM), HEAD_DIM)
            scores = jnp.where(allowed, nt(kg, q[:, at]) * factor, -1e30)
            top = jnp.max(scores, axis=0, keepdims=True)
            expo = jnp.exp(scores - top)
            total = jnp.sum(expo, axis=0, keepdims=True)
            lse[pl.ds(h, 1), :] = top + jnp.log(total)
            soft = (expo * (1.0 / total)).astype(bf16)
            flat[:, at] = nn(turned_v, soft).T.astype(bf16)
            return carry

        lax.fori_loop(0, GROUP, head, 0)
        move("group%d" % g)
    loads[1].wait()
    middle[...] = x[...]
    for z in range(size):
        at = slice(z * cq, (z + 1) * cq)
        if apart:
            mixed[z] = flat[:, at]
        else:
            mixed[z] = flat[:, at].astype(f32).astype(bf16)
        middle[...] += nt(mixed[z], wout[z])
    value = middle[...]
    scale = lax.rsqrt(jnp.mean(value * value, axis=1, keepdims=True) + epsilon)
    scale_b[...] = scale
    norm_b[...] = value * scale
    acts_b[...] = (norm_b[...] * gain_b[...]).astype(bf16)
    move("end")


def attention_push(x, vectors, tables, qkv, wout, rows, shard, layer):
    count, width = x.shape
    size = lax.axis_size("gy")
    kvd = KV_HEADS * HEAD_DIM
    local = pl.BlockSpec(memory_space=pltpu.VMEM)
    vmem = pltpu.VMEM

    def shape(*dims, kind=bf16):
        return jax.ShapeDtypeStruct(dims, kind)

    normed = [shape(count, width, kind=f32), shape(count, 1, kind=f32), shape(count, width)]
    out = [shape(count, width, kind=f32), *normed, shape(count, HEADS * HEAD_DIM)]
    out += [shape(rows, kvd), shape(rows, kvd), shape(HEADS, count, kind=f32)]
    out += [shape(size, count, wout.shape[2]), *normed]
    out += [shape(lax.axis_size("gx"), *shard.shape[1:])]
    return pl.pallas_call(
        functools.partial(attention_push_kernel, layer),
        out_shape=out,
        in_specs=[local] * 8 + [ANY] * 3,
        out_specs=[local] * 12 + [ANY],
        scratch_shapes=[
            vmem(qkv.shape, bf16),
            vmem(wout.shape, bf16),
            vmem((count, 2 * kvd), bf16),
            vmem((size, count, 2 * kvd), bf16),
            vmem((count, HEADS * HEAD_DIM), bf16),
            pltpu.SemaphoreType.DMA((2,)),
        ]
        + chain_scratch()
        + spread_scratch(1),
        compiler_params=pltpu.CompilerParams(
            collective_id=7 + layer, has_side_effects=True, vmem_limit_bytes=VMEM_LIMIT
        ),
        name="attention_push",
    )(x, *vectors, *tables, qkv, wout, shard)


def on_device(
    residual_in,
    w_query,
    w_key,
    w_value,
    b_query,
    b_key,
    b_value,
    w_output,
    gain_attn,
    gain_ffn,
    w_gate,
    w_up,
    w_down,
    cotangent,
):
    devices_y = lax.axis_size("gy")
    rows_tok = residual_in.shape[1]
    count = rows_tok // devices_y
    q_index = lax.axis_index("gy") * count + jnp.arange(count, dtype=jnp.int32)
    cos_table, sin_table = rope_tables(q_index % LEN, HEAD_DIM)

    small = jnp.concatenate([gain_attn, gain_ffn, b_query, b_key, b_value], axis=1)
    small_sizes = [v.shape[1] for v in (gain_attn, gain_ffn, b_query, b_key, b_value)]
    small = jnp.pad(small.astype(f32), ((0, 8 - LAYERS), (0, 0)))
    lines = []
    for l in range(LAYERS):
        lines += [jnp.concatenate([w_query[l], w_key[l], w_value[l]], axis=1), w_output[l]]
    part_sizes = (w_query.shape[2], w_key.shape[2], w_value.shape[2])
    opened = opening(residual_in, cotangent, small, lines, w_gate, w_up)
    resid, cot, small = opened[:3]
    lines_next = opened[5:7]
    attn_full = [[w.reshape(devices_y, D, -1) for w in opened[7:9]], None]
    ffn_full = [[w.reshape(D, -1) for w in opened[9:]], None]
    small = small[:, :LAYERS].transpose(1, 0, 2)
    vectors, start = [], 0
    for size in small_sizes:
        vectors.append(small[:, :, start : start + size].reshape(LAYERS, -1))
        start += size
    gains_one, gains_two, bias_q, bias_k, bias_v = vectors

    resid = resid.reshape(D, count).astype(f32).T
    cot = cot.reshape(D, count)

    kept = []
    for l in range(LAYERS):
        w_qkv, w_out = attn_full[l]
        vectors = [v[l][None] for v in (gains_one, gains_two, bias_q, bias_k, bias_v)]
        done = attention_push(
            resid, vectors, (cos_table, -sin_table), w_qkv, w_out, rows_tok, w_down, l
        )
        middle, normed_one, scale_one, acts_one, q_rot, k_rot, v_heads, log_total = done[:8]
        mixed, normed_two, scale_two, acts_two = done[8:12]
        wg, wu = ffn_full[l]
        wd = done[12].reshape(D, -1)
        ffn_full[l] = (wg, wu, wd)
        if l == 0:
            shards = (*lines_next, w_gate, w_up)
            done = forward_ffn(acts_two, wg, wu, wd, shards)
            attn_full[1] = [w.reshape(devices_y, D, -1) for w in done[5:7]]
            ffn_full[1] = [w.reshape(D, -1) for w in done[7:]]
        else:
            done = forward_ffn(acts_two, wg, wu, wd)
        part, acts_two, gate, up, hidden = done[:5]
        kept.append(
            (
                normed_one,
                scale_one,
                acts_one,
                q_rot,
                k_rot,
                v_heads,
                log_total,
                mixed,
                normed_two,
                scale_two,
                acts_two,
                gate,
                up,
                hidden,
            )
        )
        resid = middle + part

    grad = cot.astype(f32).T + 2.0 * penalty * resid
    grad_low = grad.astype(bf16)
    attn_grads = [None] * LAYERS
    ffn_grads = [None] * LAYERS
    small_grads = [None] * LAYERS

    for l in reversed(range(LAYERS)):
        (
            normed_one,
            scale_one,
            acts_one,
            q_rot,
            k_rot,
            v_heads,
            log_total,
            mixed,
            normed_two,
            scale_two,
            acts_two,
            gate,
            up,
            hidden,
        ) = kept[l]
        w_qkv, w_out = attn_full[l]
        wg, wu, wd = ffn_full[l]
        operands = (grad_low, gate, up, hidden, acts_two, wg, wu, wd)
        if l == LAYERS - 1:
            done = backward_ffn(*operands, late=True)
            grad_down, held = done[1:3]
        else:
            done = backward_ffn(*operands, held=held)
            ffn_grads[l] = done[1:4]
            ffn_grads[l + 1] = [*done[7:9], grad_down]
        grad_acts_two = done[0]
        vectors = [grad, grad_acts_two, normed_two, scale_two, gains_two[l][None]]
        vectors += [normed_one, scale_one, gains_one[l][None]]
        done = attention_pull(
            vectors, acts_one, q_rot, k_rot, v_heads, log_total, (cos_table, sin_table), w_qkv, w_out
        )
        grad, grad_low = done[:2]
        attn_grads[l] = [*done[2:5], mixed]
        rows = done[5]
        width = k_rot.shape[1]
        small_grads[l] = [
            v.reshape(devices_y, -1)
            for v in (rows[0], rows[1], rows[2], rows[3, :width], rows[4, :width])
        ]
    small = jnp.stack([jnp.concatenate(v, axis=1) for v in small_grads], axis=1)
    small = jnp.pad(small, ((0, 0), (0, 8 - LAYERS), (0, 0)))

    def to_rows(tokens_major):
        return tokens_major.astype(bf16).T.reshape(devices_y, -1, count)

    def from_blocks(blocks):
        return blocks.transpose(1, 0, 2).reshape(-1, rows_tok).astype(f32)

    attn_sums, small, output, grad_input = closing(
        attn_grads[0] + attn_grads[1], small, to_rows(resid), to_rows(grad_low)
    )
    small = small[:LAYERS]
    attn_out, start = [], 0
    for size in part_sizes + (w_output.shape[2],):
        attn_out.append(attn_sums[:, :, start : start + size])
        start += size
    small_out, start = [], 0
    for size in small_sizes:
        small_out.append(small[:, start : start + size])
        start += size

    def stack(parts, k):
        return jnp.stack([part[k] for part in parts])

    return (
        from_blocks(output),
        from_blocks(grad_input),
        attn_out[0],
        attn_out[1],
        attn_out[2],
        small_out[2],
        small_out[3],
        small_out[4],
        attn_out[3],
        small_out[0],
        small_out[1],
        stack(ffn_grads, 0),
        stack(ffn_grads, 1),
        stack(ffn_grads, 2),
    )


def solution(mesh):
    tokens = P("gy", "gx")
    weight = P(None, "gx", "gy")
    vector = P(None, "gy")
    return jax.shard_map(
        on_device,
        mesh=mesh,
        in_specs=(
            tokens,
            weight,
            weight,
            weight,
            vector,
            vector,
            vector,
            weight,
            vector,
            vector,
            weight,
            weight,
            weight,
            tokens,
        ),
        out_specs=(
            tokens,
            tokens,
            weight,
            weight,
            weight,
            vector,
            vector,
            vector,
            weight,
            vector,
            vector,
            weight,
            weight,
            weight,
        ),
        check_vma=False,
    )
```

```python
import functools
import math

import jax
import jax.numpy as jnp
from jax import lax
from jax.experimental import pallas as pl
from jax.experimental.pallas import tpu as pltpu
from jax.sharding import PartitionSpec as P

D = 1536
HEADS = 12
KV_HEADS = 2
HEAD_DIM = 128
LEN = 1024
LAYERS = 2
GROUP = HEADS // KV_HEADS

epsilon = 1e-06
rope_base = 1000000.0
penalty = 0.25
bf16 = jnp.bfloat16
f32 = jnp.float32
MESH = pl.DeviceIdType.MESH
VMEM_LIMIT = 62 << 20
ANY = pl.BlockSpec(memory_space=pl.ANY)


def rope_tables(positions, head_size):
    freqs = rope_base ** (-jnp.arange(0, head_size, 2).astype(f32) / head_size)
    angles = positions.astype(f32)[:, None] * freqs[None, :]
    cosine = jnp.cos(angles)
    sine_table = jnp.sin(angles)
    return (
        jnp.concatenate([cosine, cosine], -1),
        jnp.concatenate([sine_table, -sine_table], -1),
    )


def wait_for(ref, sem):
    pltpu.make_async_copy(ref, ref, sem).wait()


def places():
    gx, devices = lax.axis_index("gx"), lax.axis_size("gx")
    chips = devices // 2
    chip, core = gx // 2, lax.rem(gx, 2)
    partner = gx + 1 - 2 * core
    others = [lax.rem(chip + k, chips) * 2 + core for k in range(1, chips)]
    return partner, others


def square():
    gx = lax.axis_index("gx")
    chip, core = gx // 2, lax.rem(gx, 2)
    side = gx + 2 - 4 * lax.rem(chip, 2)
    along = gx + 4 - 8 * (chip // 2)
    return side, along, (3 - chip) * 2 + core


def spread_slots():
    chips = lax.axis_size("gx") // 2
    return 14 if chips == 4 else 2 * chips + 2 * (chips - 1)


def spread_scratch(count):
    devices = lax.axis_size("gx")
    return [
        pltpu.SemaphoreType.DMA((count,)),
        pltpu.SemaphoreType.DMA((count, spread_slots())),
        pltpu.SemaphoreType.DMA((count, devices, 2)),
    ]


def greet(gx_peers, gy_peers):
    gx, gy = lax.axis_index("gx"), lax.axis_index("gy")
    barrier = pltpu.get_barrier_semaphore()
    for peer in gx_peers:
        pl.semaphore_signal(barrier, inc=1, device_id=(peer, gy), device_id_type=MESH)
    for peer in gy_peers:
        pl.semaphore_signal(barrier, inc=1, device_id=(gx, peer), device_id_type=MESH)
    pl.semaphore_wait(barrier, len(gx_peers) + len(gy_peers))


class Spread:
    def __init__(self, items, sems):
        self.items, (self.local, self.send_sem, self.recv_sem) = items, sems
        self.partner, self.others = places()
        self.four = lax.axis_size("gx") // 2 == 4
        self.near = list(square()[:2]) if self.four else self.others

    def part(self, i, k, h):
        full = self.items[i][1]
        if len(full.shape) == 4:
            half = full.shape[0] // 2
            return full.at[pl.ds(h * half, half), k]
        half = full.shape[1] // 2
        return full.at[k, pl.ds(h * half, half)]

    def send(self, i, k, h, target, slot, first=False):
        here = self.part(i, k, h)
        half = here.shape[0]
        source = self.items[i][0].at[pl.ds(h * half, half)] if first else here
        pltpu.make_async_remote_copy(
            src_ref=source,
            dst_ref=here,
            send_sem=self.send_sem.at[i, slot],
            recv_sem=self.recv_sem.at[i, k, h],
            device_id=(target, lax.axis_index("gy")),
            device_id_type=MESH,
        ).start()

    def arrived(self, i, k, h):
        wait_for(self.part(i, k, h), self.recv_sem.at[i, k, h])

    def place(self, i):
        own, full = self.items[i]
        gx = lax.axis_index("gx")
        here = full.at[:, gx] if len(full.shape) == 4 else full.at[gx]
        return pltpu.make_async_copy(own, here, self.local.at[i])

    def begin(self, i):
        gx = lax.axis_index("gx")
        self.place(i).start()
        slot = 0
        for target in self.near + [self.partner]:
            for h in range(2):
                self.send(i, gx, h, target, slot, True)
                slot += 1

    def relay(self, i):
        slot = 2 * len(self.near) + 2
        if self.four:
            side, along, _ = square()
            steps = [(side, 0, along), (along, 1, side), (side, 1, None), (along, 0, None)]
        else:
            steps = [(k, h, None) for k in self.others for h in range(2)]
        for k, h, target in steps:
            self.arrived(i, k, h)
            for to in [self.partner] if target is None else [target, self.partner]:
                self.send(i, k, h, to, slot)
                slot += 1

    def finish(self, i):
        if self.four:
            for h in range(2):
                self.arrived(i, square()[2], h)
                self.send(i, square()[2], h, self.partner, 12 + h)

    def close(self, i):
        core = lax.rem(lax.axis_index("gx"), 2)
        for k in [self.partner] + [k + 1 - 2 * core for k in self.others]:
            for h in range(2):
                self.arrived(i, k, h)
        for slot in range(spread_slots()):
            wait_for(self.part(i, 0, 0), self.send_sem.at[i, slot])
        self.place(i).wait()


def line_order(t, me, last):
    short = jnp.minimum(me, last - me)
    near = jnp.where(lax.rem(t, 2) == 0, me - t // 2, me + (t + 1) // 2)
    far = jnp.where(me < last - me, me + (t - short), me - (t - short))
    return jnp.where(t <= 2 * short, near, far)


class Chain:
    def __init__(self, own, full, sems):
        self.own, self.full, (self.local, self.send_sem, self.recv_sem) = own, full, sems

    def copy(self, b, way, first=False):
        me = lax.axis_index("gy")
        return pltpu.make_async_remote_copy(
            src_ref=self.own if first else self.full.at[b],
            dst_ref=self.full.at[b],
            send_sem=self.send_sem.at[b, way],
            recv_sem=self.recv_sem.at[b],
            device_id=(lax.axis_index("gx"), me - 1 + 2 * way),
            device_id_type=MESH,
        )

    def each(self, b, act, first=False):
        me, last = lax.axis_index("gy"), lax.axis_size("gy") - 1

        @pl.when(jnp.logical_and(b <= me, me < last))
        def _():
            act(self.copy(b, 1, first))

        @pl.when(jnp.logical_and(b >= me, me > 0))
        def _():
            act(self.copy(b, 0, first))

    def begin(self):
        me = lax.axis_index("gy")
        self.place = pltpu.make_async_copy(self.own, self.full.at[me], self.local)
        self.place.start()
        self.each(me, lambda copy: copy.start(), True)

    def relay(self, t):
        b = line_order(t, lax.axis_index("gy"), lax.axis_size("gy") - 1)
        wait_for(self.full.at[b], self.recv_sem.at[b])
        self.each(b, lambda copy: copy.start())

    def close(self):
        self.place.wait()
        for b in range(lax.axis_size("gy")):
            self.each(b, lambda copy: copy.wait_send())


class Exchange:
    def __init__(self, own, full, sems, apart=False):
        self.own, self.full, (self.local, self.send_sem, self.recv_sem) = own, full, sems
        self.apart = apart

    def begin(self):
        gx, me, size = lax.axis_index("gx"), lax.axis_index("gy"), lax.axis_size("gy")
        width = self.full.shape[2]

        def columns(k):
            if self.apart:
                return self.own.at[k]
            return self.own.at[:, pl.ds(pl.multiple_of(k * width, width), width)]

        self.place = pltpu.make_async_copy(columns(me), self.full.at[me], self.local)
        self.place.start()
        self.sent = []
        for d in range(1, size):
            target = lax.rem(me + d, size)
            copy = pltpu.make_async_remote_copy(
                src_ref=columns(target),
                dst_ref=self.full.at[me],
                send_sem=self.send_sem.at[d],
                recv_sem=self.recv_sem.at[me],
                device_id=(gx, target),
                device_id_type=MESH,
            )
            copy.start()
            self.sent.append(copy)

    def close(self):
        me, size = lax.axis_index("gy"), lax.axis_size("gy")
        self.place.wait()
        for copy in self.sent:
            copy.wait_send()
        for d in range(1, size):
            k = lax.rem(me + d, size)
            wait_for(self.full.at[k], self.recv_sem.at[k])


def chain_scratch():
    size = lax.axis_size("gy")
    return [
        pltpu.SemaphoreType.DMA,
        pltpu.SemaphoreType.DMA((size, 2)),
        pltpu.SemaphoreType.DMA((size,)),
    ]


def exchange_scratch():
    size = lax.axis_size("gy")
    return [
        pltpu.SemaphoreType.DMA,
        pltpu.SemaphoreType.DMA((size,)),
        pltpu.SemaphoreType.DMA((size,)),
    ]


def opening_kernel(*refs):
    ins, outs, sems = refs[:9], refs[9:20], refs[20:]
    resid, cot, small, qkv_a, o_a, qkv_b, o_b, wg, wu = ins
    resid_out, cot_out, small_out = outs[:3]
    lines, (qkv, o, gate, up) = outs[3:7], outs[7:]
    me, size = lax.axis_index("gy"), lax.axis_size("gy")
    owns = (qkv_a, o_a, qkv_b, o_b, small)
    chains = [
        Chain(own, full, sems[3 * k : 3 * k + 3])
        for k, (own, full) in enumerate(zip(owns, list(lines) + [small_out]))
    ]
    swaps = [
        Exchange(own, full, sems[15 + 3 * k : 18 + 3 * k])
        for k, (own, full) in enumerate(((resid, resid_out), (cot, cot_out)))
    ]
    items = [(lines[0], qkv), (lines[1], o), (wg.at[0], gate), (wu.at[0], up)]
    spread = Spread(items, sems[21:24])
    greet([spread.partner] + spread.near, [lax.rem(me + d, size) for d in range(1, size)])
    for k in (0, 1, 4):
        chains[k].begin()
    spread.begin(2)
    for t in range(1, size):
        chains[0].relay(t)
        chains[1].relay(t)
    chains[0].close()
    spread.begin(0)
    chains[1].close()
    spread.begin(1)
    swaps[0].begin()
    for t in range(1, size):
        chains[4].relay(t)
    spread.relay(2)
    spread.begin(3)
    chains[2].begin()
    chains[3].begin()
    for i in (0, 1):
        spread.relay(i)
    swaps[1].begin()
    for t in range(1, size):
        chains[2].relay(t)
        chains[3].relay(t)
    spread.finish(2)
    for i in (0, 1):
        spread.finish(i)
    spread.relay(3)
    spread.finish(3)
    for i in range(4):
        spread.close(i)
    for part in chains[2:] + swaps:
        part.close()


def opening(resid, cot, small, lines, wg, wu):
    devices, size = lax.axis_size("gx"), lax.axis_size("gy")
    count = resid.shape[1] // size

    def shape(*dims, kind=bf16):
        return jax.ShapeDtypeStruct(dims, kind)

    blocks = shape(size, resid.shape[0], count)
    weight = shape(devices, *wg.shape[1:])
    out = [blocks, blocks, shape(size, *small.shape, kind=f32)]
    out += [shape(size, *line.shape) for line in lines]
    out += [shape(size, devices, *line.shape) for line in lines[:2]] + [weight] * 2
    return pl.pallas_call(
        opening_kernel,
        out_shape=out,
        in_specs=[ANY] * 9,
        out_specs=[ANY] * 11,
        scratch_shapes=chain_scratch() * 5 + exchange_scratch() * 2 + spread_scratch(4),
        compiler_params=pltpu.CompilerParams(collective_id=2, has_side_effects=True),
        name="opening",
    )(resid, cot, small, *lines, wg, wu)


FF_CHUNK = 512
PIECES = 4


def spans(total):
    return [(start, min(FF_CHUNK, total - start)) for start in range(0, total, FF_CHUNK)]


def nn(left, right):
    return lax.dot_general(left, right, (((1,), (0,)), ((), ())), preferred_element_type=f32)


def nt(left, right):
    return lax.dot_general(left, right, (((1,), (1,)), ((), ())), preferred_element_type=f32)


def line_pass(own_ref, own, gathered, part, outb, inb, sems, load, finish, peers=(), plan={}):
    own_sem, ag_send, ag_recv, rs_send, rs_recv = sems
    gx, me, size = lax.axis_index("gx"), lax.axis_index("gy"), lax.axis_size("gy")
    rows = own.shape[0]
    piece = rows // PIECES
    last = size - 1
    inner = jnp.logical_and(me > 0, me < last)

    first = pltpu.make_async_copy(own_ref, gathered.at[me], own_sem)
    first.start()
    barrier = pltpu.get_barrier_semaphore()

    @pl.when(me > 0)
    def _():
        pl.semaphore_signal(barrier, inc=1, device_id=(gx, me - 1), device_id_type=MESH)

    @pl.when(me < last)
    def _():
        pl.semaphore_signal(barrier, inc=1, device_id=(gx, me + 1), device_id_type=MESH)

    for peer in peers:
        pl.semaphore_signal(barrier, inc=1, device_id=(peer, me), device_id_type=MESH)
    pl.semaphore_wait(barrier, jnp.where(inner, 2, 1) + len(peers))
    first.wait()

    def planned(name, t):
        for (key, when), act in plan.items():
            if key == name:
                pl.when(t == when)(act)


    def gather_copy(b, s, way):
        here = gathered.at[b, pl.ds(s * piece, piece)]
        return pltpu.make_async_remote_copy(
            src_ref=here,
            dst_ref=here,
            send_sem=ag_send.at[b, way, s],
            recv_sem=ag_recv.at[b, s],
            device_id=(gx, me - 1 + 2 * way),
            device_id_type=MESH,
        )

    def sum_copy(b, s):
        towards = jnp.where(b > me, me + 1, me - 1)
        slot = jnp.where(jnp.logical_and(towards == b, me > b), size, b)
        return pltpu.make_async_remote_copy(
            src_ref=outb.at[b, pl.ds(s * piece, piece)],
            dst_ref=inb.at[slot, pl.ds(s * piece, piece)],
            send_sem=rs_send.at[b, s],
            recv_sem=rs_recv.at[slot, s],
            device_id=(gx, towards),
            device_id_type=MESH,
        )

    def sum_arrived(slot, s):
        here = inb.at[slot, pl.ds(s * piece, piece)]
        pltpu.make_async_copy(here, here, rs_recv.at[slot, s]).wait()

    def step(t, carry):
        b = line_order(t, me, last)
        for s in range(PIECES):

            @pl.when(t > 0)
            def _():
                gather_copy(b, s, 0).wait_recv()

            @pl.when(jnp.logical_and(b <= me, me < last))
            def _():
                gather_copy(b, s, 1).start()

            @pl.when(jnp.logical_and(b >= me, me > 0))
            def _():
                gather_copy(b, s, 0).start()

        @pl.when(t == 0)
        def _():
            load()

        planned("step", t)
        finish(b)

        @pl.when(b == me)
        def _():
            own[...] = part[...]

        @pl.when(b != me)
        def _():
            outb[b] = part[...].astype(bf16)

            @pl.when(jnp.logical_not(inner))
            def _():
                for s in range(PIECES):
                    sum_copy(b, s).start()

        return carry

    lax.fori_loop(0, size, step, 0)

    def relay(t, carry):
        above, below = last - me, me
        low = jnp.where(t < above, me + 1 + t, me - 1 - (t - above))
        high = jnp.where(t < below, me - 1 - t, me + 1 + (t - below))
        b = jnp.where(2 * me < size, low, high)
        planned("hop", t)

        @pl.when(inner)
        def _():
            for s in range(PIECES):
                at = pl.ds(s * piece, piece)
                sum_arrived(b, s)
                outb[b, at] = (outb[b, at].astype(f32) + inb[b, at].astype(f32)).astype(bf16)
                sum_copy(b, s).start()

        return carry

    lax.fori_loop(0, last, relay, 0)

    @pl.when(me > 0)
    def _():
        for s in range(PIECES):
            sum_arrived(me, s)
        own[...] += inb[me].astype(f32)

    @pl.when(me < last)
    def _():
        for s in range(PIECES):
            sum_arrived(size, s)
        own[...] += inb[size].astype(f32)

    def drain(b, carry):
        for s in range(PIECES):

            @pl.when(jnp.logical_and(b <= me, me < last))
            def _():
                gather_copy(b, s, 1).wait_send()

            @pl.when(jnp.logical_and(b >= me, me > 0))
            def _():
                gather_copy(b, s, 0).wait_send()

            @pl.when(b != me)
            def _():
                sum_copy(b, s).wait_send()

        return carry

    lax.fori_loop(0, size, drain, 0)


def line_scratch(size, rows, width):
    return [
        pltpu.VMEM((size, rows, width), bf16),
        pltpu.VMEM((rows, width), f32),
        pltpu.VMEM((size, rows, width), bf16),
        pltpu.VMEM((size + 1, rows, width), bf16),
        pltpu.SemaphoreType.DMA,
        pltpu.SemaphoreType.DMA((size, 2, PIECES)),
        pltpu.SemaphoreType.DMA((size, PIECES)),
        pltpu.SemaphoreType.DMA((size, PIECES)),
        pltpu.SemaphoreType.DMA((size + 1, PIECES)),
    ]


LINE = 9


ORDER = {
    ("step", 0): (("begin", 0), ("begin", 1)),
    ("step", 2): (("begin", 2),),
    ("hop", 0): (("relay", 0), ("relay", 1), ("relay", 2), ("begin", 3)),
    ("hop", 1): (("finish", 0), ("finish", 1), ("finish", 2)),
}
REST = (("relay", 3), ("finish", 3))


def schedule(spread):
    def run(steps):
        def act():
            for verb, i in steps:
                getattr(spread, verb)(i)

        return act

    plan = {key: run(steps) for key, steps in ORDER.items()}
    return plan, REST + tuple(("close", i) for i in range(len(spread.items)))


def forward_kernel(extra, *refs):
    acts_ref, wg_ref, wu_ref, wd_ref = refs[:4]
    shards, refs = refs[4 : 4 + extra], refs[4 + extra :]
    sum_ref, turned_ref, gate_ref, up_ref, hidden_ref = refs[:5]
    wholes, scratch = refs[5 : 5 + extra], refs[5 + extra :]
    gathered, part, outb, inb = scratch[:4]
    sems = scratch[4:LINE]
    wg, wu, wd, gate, up, hidden, turned, w_sem, out_sem = scratch[LINE : LINE + 9]
    peers, spread = [], None
    if extra:
        items = [(r if len(w.shape) == 4 else r.at[1], w) for r, w in zip(shards, wholes)]
        spread = Spread(items, scratch[LINE + 9 :])
        partner, others = places()
        peers = [partner] + (list(square()[:2]) if spread.four else others)

    plan, rest = schedule(spread) if extra else ({}, ())
    loads = [
        pltpu.make_async_copy(src, dst, w_sem.at[k])
        for k, (src, dst) in enumerate(((wg_ref, wg), (wu_ref, wu), (wd_ref, wd)))
    ]
    for copy in loads:
        copy.start()

    def load():
        for copy in loads:
            copy.wait()

    def results(b):
        pairs = ((gate, gate_ref), (up, up_ref), (hidden, hidden_ref))
        return [
            pltpu.make_async_copy(src.at[b], dst.at[b], out_sem.at[b, k])
            for k, (src, dst) in enumerate(pairs)
        ]

    def finish(b):
        block = gathered[b]
        store_turned(block, turned, b)
        for start, width in spans(wg.shape[1]):
            at = slice(start, start + width)
            g = nn(block, wg[:, at])
            u = nn(block, wu[:, at])
            h = (g * lax.logistic(g) * u).astype(bf16)
            gate[b, :, at] = g.astype(bf16)
            up[b, :, at] = u.astype(bf16)
            hidden[b, :, at] = h
            p = nt(h, wd[:, at])
            if start == 0:
                part[...] = p
            else:
                part[...] += p
        for copy in results(b):
            copy.start()

    line_pass(
        acts_ref, sum_ref, gathered, part, outb, inb, sems, load, finish, peers, plan
    )
    keep = pltpu.make_async_copy(turned, turned_ref, w_sem.at[0])
    keep.start()
    for act, i in rest:
        getattr(spread, act)(i)

    def settle(b, carry):
        for copy in results(b):
            copy.wait()
        return carry

    lax.fori_loop(0, gathered.shape[0], settle, 0)
    keep.wait()


def forward_ffn(acts, wg, wu, wd, shards=()):
    rows, width = acts.shape
    devices, size, hidden = lax.axis_size("gx"), lax.axis_size("gy"), wg.shape[1]
    wide = jax.ShapeDtypeStruct((size, rows, hidden), bf16)
    extra = len(shards)
    wholes = [
        jax.ShapeDtypeStruct(
            (size, devices) + s.shape[1:] if k < 2 else (devices,) + s.shape[1:], bf16
        )
        for k, s in enumerate(shards)
    ]
    return pl.pallas_call(
        functools.partial(forward_kernel, extra),
        out_shape=[
            jax.ShapeDtypeStruct((rows, width), f32),
            jax.ShapeDtypeStruct((2, width // 2, size * rows), bf16),
            wide,
            wide,
            wide,
        ]
        + wholes,
        in_specs=[ANY] * (4 + extra),
        out_specs=[pl.BlockSpec(memory_space=pltpu.VMEM)] + [ANY] * (4 + extra),
        scratch_shapes=line_scratch(size, rows, width)
        + [pltpu.VMEM((width, hidden), bf16)] * 3
        + [pltpu.VMEM((size, rows, hidden), bf16)] * 3
        + [pltpu.VMEM((2, width // 2, size * rows), bf16)]
        + [pltpu.SemaphoreType.DMA((3,)), pltpu.SemaphoreType.DMA((size, 3))]
        + (spread_scratch(extra) if extra else []),
        compiler_params=pltpu.CompilerParams(
            collective_id=3 if extra else 0, has_side_effects=True, vmem_limit_bytes=VMEM_LIMIT
        ),
        cost_estimate=pl.CostEstimate(
            flops=6 * size * rows * width * hidden, bytes_accessed=40 << 20, transcendentals=0
        ),
        name="ffn_forward",
    )(acts, wg, wu, wd, *shards)


class Reduce:
    def __init__(self, lhs, rhs, bufs, abuf, fbuf, ftail, a_all, r_all, c_all, outs, late, sems):
        self.late = late
        self.lhs, self.rhs, self.bufs, self.outs = lhs, rhs, bufs, outs
        self.abuf, self.fbuf, self.ftail = abuf, fbuf, ftail
        self.a_all, self.r_all, self.c_all = a_all, r_all, c_all
        (
            self.a_send,
            self.a_recv,
            self.r_send,
            self.r_recv,
            self.c_send,
            self.c_recv,
            self.local,
        ) = sems
        gx, self.gy = lax.axis_index("gx"), lax.axis_index("gy")
        self.chip, self.core = gx // 2, lax.rem(gx, 2)
        self.chips = lax.axis_size("gx") // 2
        self.half, self.wide = bufs[0].shape[0] // 2, bufs[0].shape[1]
        self.r = self.half // self.chips
        self.four = self.chips == 4
        self.partner, self.others = places()
        self.near = list(square()[:2]) if self.four else self.others

    def product(self, m, which, at):
        z, n, _ = self.rhs[m].shape
        right = self.rhs[m][:, :, at].reshape(z * n, at.stop - at.start)
        return nn(self.lhs[which], right)

    def remote(self, src, dst, send, recv, target):
        return pltpu.make_async_remote_copy(
            src_ref=src,
            dst_ref=dst,
            send_sem=send,
            recv_sem=recv,
            device_id=(target, self.gy),
            device_id_type=MESH,
        )

    def columns(self):
        return [(j, slice(s, s + w)) for j, (s, w) in enumerate(spans(self.wide))]

    def swap(self, m, j, at):
        here = (slice(0, self.half), at)
        return self.remote(
            self.bufs[m].at[here],
            self.a_all.at[m, :, at],
            self.a_send.at[m, j],
            self.a_recv.at[m, j],
            self.partner,
        )

    def block(self, m, device, start=0, size=None):
        size = self.r if size is None else size
        first = self.half + (device // 2) * self.r + start
        return self.bufs[m].at[pl.ds(pl.multiple_of(first, 16), size)]

    def first(self, m):
        for j, at in self.columns():
            self.bufs[m][: self.half, at] = self.product(m, 1 - self.core, at).astype(bf16)
            self.swap(m, j, at).start()

    def corner(self, m, h):
        side, along, across = square()
        half = self.r // 2
        return self.remote(
            self.block(m, across, h * half, half),
            self.r_all.at[m, h],
            self.r_send.at[m, h],
            self.r_recv.at[m, h],
            along if h else side,
        )

    def second(self, m):
        for j, at in self.columns():
            self.swap(m, j, at).wait_recv()
            landed = self.abuf.at[:, at]
            fetch = pltpu.make_async_copy(self.a_all.at[m, :, at], landed, self.local.at[0])
            fetch.start()
            mine = self.product(m, self.core, at)
            fetch.wait()
            self.bufs[m][self.half :, at] = (mine + landed[...].astype(f32)).astype(bf16)
        if m in self.late:
            self.keep(m).start()
        elif self.four:
            for h in range(2):
                self.corner(m, h).start()

    def keep(self, m):
        kept = self.outs[m].at[0]
        return pltpu.make_async_copy(
            self.bufs[m].at[pl.ds(self.half, self.half)], kept, self.local.at[max(len(self.near), 2)]
        )

    def hand(self, m, k):
        target = self.near[k]
        return self.remote(
            self.block(m, target),
            self.c_all.at[m, k],
            self.c_send.at[m, k],
            self.c_recv.at[m, k],
            target,
        )

    def third(self, m):
        if self.four:
            side, along, _ = square()
            half = self.r // 2
            for h, device in ((0, along), (1, side)):
                self.corner(m, h).wait_recv()
                here = self.block(m, device, h * half, half)
                landed = self.abuf.at[h * half : (h + 1) * half]
                fetch = pltpu.make_async_copy(self.r_all.at[m, h], landed, self.local.at[0])
                fetch.start()
                fetch.wait()
                here[...] = (here[...].astype(f32) + landed[...].astype(f32)).astype(bf16)
        for k in range(len(self.near)):
            self.hand(m, k).start()

    def fourth(self, m):
        for j, at in self.columns():
            self.swap(m, j, at).wait_send()
        fetches = []
        for k in range(len(self.near)):
            self.hand(m, k).wait_recv()
            here = self.bufs[m].at[pl.ds(k * self.r, self.r)]
            fetch = pltpu.make_async_copy(self.c_all.at[m, k], here, self.local.at[k])
            fetch.start()
            fetches.append(fetch)
        for fetch in fetches:
            fetch.wait()
        first = pl.multiple_of(self.half + self.chip * self.r, 16)
        for _, at in self.columns():
            total = self.bufs[m][pl.ds(first, self.r), at].astype(f32)
            for k in range(len(self.near)):
                total = total + self.bufs[m][k * self.r : (k + 1) * self.r, at].astype(f32)
            stage = self.fbuf if total.shape[1] == FF_CHUNK else self.ftail
            stage[...] = total
            store = pltpu.make_async_copy(stage, self.outs[m].at[:, at], self.local.at[0])
            store.start()
            store.wait()

    def drain(self, m):
        if self.four:
            for h in range(2):
                self.corner(m, h).wait_send()
        for k in range(len(self.near)):
            self.hand(m, k).wait_send()


def reduce_scratch(width, hidden, count=3):
    devices = lax.axis_size("gx")
    rows, parts = width // devices, len(spans(hidden))
    near = 2 if devices == 8 else devices // 2 - 1
    dma = pltpu.SemaphoreType.DMA
    return [
        pltpu.VMEM((width // 2, hidden), bf16),
        pltpu.VMEM((rows, FF_CHUNK), f32),
        pltpu.VMEM((rows, hidden % FF_CHUNK), f32),
        dma((count, parts)),
        dma((count, parts)),
        dma((count, 2)),
        dma((count, 2)),
        dma((count, near)),
        dma((count, near)),
        dma((max(near, 2) + 1,)),
    ]


class Tail:
    def __init__(self, b_all, r_all, c_all, outs, abuf, fbuf, ftail, sems):
        self.b_all, self.r_all, self.c_all, self.outs = b_all, r_all, c_all, outs
        self.abuf, self.fbuf, self.ftail = abuf, fbuf, ftail
        self.r_send, self.r_recv, self.c_send, self.c_recv, self.local = sems
        gx, self.gy = lax.axis_index("gx"), lax.axis_index("gy")
        self.chip, chips = gx // 2, lax.axis_size("gx") // 2
        self.r = b_all.shape[1] // chips
        self.part = self.r // 2
        self.space = b_all.shape[1] // b_all.shape[0]
        self.four = chips == 4
        self.near = list(square()[:2]) if self.four else places()[1]

    def remote(self, src, dst, send, recv, target):
        return pltpu.make_async_remote_copy(
            src_ref=src,
            dst_ref=dst,
            send_sem=send,
            recv_sem=recv,
            device_id=(target, self.gy),
            device_id_type=MESH,
        )

    def held(self, i, chip, h):
        first = pl.multiple_of(chip * self.r + h * self.part, 16)
        return self.b_all.at[i, pl.ds(first, self.part)]

    def slot(self, i, k):
        return self.abuf.at[pl.ds(i * self.space + k * self.part, self.part)]

    def corner(self, i, h):
        side, along, across = square()
        return self.remote(
            self.held(i, across // 2, h),
            self.r_all.at[i, h],
            self.r_send.at[i, h],
            self.r_recv.at[i, h],
            along if h else side,
        )

    def hand(self, i, k, h):
        target = self.near[k]
        summed = self.four and k != h
        return self.remote(
            self.slot(i, 2 + h) if summed else self.held(i, target // 2, h),
            self.c_all.at[i, k, h],
            self.c_send.at[i, k, h],
            self.c_recv.at[i, k, h],
            target,
        )

    def hands(self):
        return [(k, h) for k in range(len(self.near)) for h in range(2)]

    def begin(self, i):
        if self.four:
            for h in range(2):
                self.corner(i, h).start()

    def middle(self, i):
        if self.four:
            side, along, _ = square()
            for h, device in ((0, along), (1, side)):
                self.corner(i, h).wait_recv()
                came, mine = self.slot(i, h), self.slot(i, 2 + h)
                fetches = [
                    pltpu.make_async_copy(self.r_all.at[i, h], came, self.local.at[0]),
                    pltpu.make_async_copy(self.held(i, device // 2, h), mine, self.local.at[1]),
                ]
                for fetch in fetches:
                    fetch.start()
                for fetch in fetches:
                    fetch.wait()
                mine[...] = (mine[...].astype(f32) + came[...].astype(f32)).astype(bf16)
        for k, h in self.hands():
            self.hand(i, k, h).start()

    def close(self, i):
        if self.four:
            for h in range(2):
                self.corner(i, h).wait_send()
        for k, h in self.hands():
            self.hand(i, k, h).wait_send()
        count = len(self.near)
        for h in range(2):
            fetches = [
                pltpu.make_async_copy(
                    self.held(i, self.chip, h), self.slot(i, count), self.local.at[count]
                )
            ]
            for k in range(count):
                self.hand(i, k, h).wait_recv()
                fetches.append(
                    pltpu.make_async_copy(
                        self.c_all.at[i, k, h], self.slot(i, k), self.local.at[k]
                    )
                )
            for fetch in fetches:
                fetch.start()
            for fetch in fetches:
                fetch.wait()
            for start, width in spans(self.abuf.shape[1]):
                at = slice(start, start + width)
                total = self.slot(i, 0)[:, at].astype(f32)
                for k in range(1, count + 1):
                    total = total + self.slot(i, k)[:, at].astype(f32)
                stage = self.fbuf if width == FF_CHUNK else self.ftail
                stage[: self.part] = total
                store = pltpu.make_async_copy(
                    stage.at[pl.ds(0, self.part)],
                    self.outs[i].at[pl.ds(h * self.part, self.part), at],
                    self.local.at[0],
                )
                store.start()
                store.wait()


def tail_scratch(count):
    devices = lax.axis_size("gx")
    near = 2 if devices == 8 else devices // 2 - 1
    dma = pltpu.SemaphoreType.DMA
    return [
        dma((count, 2)),
        dma((count, 2)),
        dma((count, near, 2)),
        dma((count, near, 2)),
        dma((near + 1,)),
    ]


def store_turned(block, turned, b):
    count, width = block.shape
    _, chips_rows, _ = turned.shape
    devices = lax.axis_size("gx")
    r = width // devices
    flipped = block.T
    at = pl.ds(pl.multiple_of(b * count, count), count)
    for k in range(devices):
        q = k // 2
        turned[k % 2, q * r : (q + 1) * r, at] = flipped[k * r : (k + 1) * r]


AFTER = {
    0: (("first", 0),),
    1: (("second", 0), ("swap", 0), ("first", 1)),
    2: (("third", 0), ("second", 1)),
}
ENDS = {
    (1, 2): (
        ("kept", 1),
        ("first", 2),
        ("second", 2),
        ("fourth", 0),
        ("kept", 2),
        ("sent", 1),
        ("sent", 2),
        ("drain", 0),
    ),
    (2,): (
        ("first", 2),
        ("third", 1),
        ("second", 2),
        ("fourth", 0),
        ("kept", 2),
        ("fourth", 1),
        ("sent", 2),
        ("drain", 0),
        ("drain", 1),
    ),
}
TAIL_BEGIN, TAIL_MIDDLE = ("step", 0), ("step", 2)


def both(one, other):
    def act():
        one()
        other()

    return act


def backward_kernel(late, tails, *refs):
    grad_ref, gate_ref, up_ref, hidden_ref, turned_ref, wg_ref, wu_ref, wd_ref = refs[:8]
    held, refs = refs[8 : 8 + (tails > 0)], refs[8 + (tails > 0) :]
    sum_ref, refs = refs[0], refs[1:]
    outs, (a_all, r_all, c_all), refs = refs[:3], refs[3:6], refs[6:]
    tail_refs, scratch = refs[: tails + 2 * (tails > 0)], refs[tails + 2 * (tails > 0) :]
    gathered, part, outb, inb = scratch[:4]
    sems = scratch[4:LINE]
    wg, wu, wd, gate, up, hidden, turned, w_sem = scratch[LINE : LINE + 8]
    abuf, fbuf, ftail = scratch[LINE + 8 : LINE + 11]
    operands = (
        (wd_ref, wd),
        (gate_ref, gate),
        (up_ref, up),
        (wg_ref, wg),
        (wu_ref, wu),
        (hidden_ref, hidden),
    )
    loads = [
        pltpu.make_async_copy(src, dst, w_sem.at[k]) for k, (src, dst) in enumerate(operands)
    ]
    for copy in loads:
        copy.start()

    def load():
        for copy in loads:
            copy.wait()

    reduce = Reduce(
        turned,
        (hidden, gate, up),
        (wd, wg, wu),
        abuf,
        fbuf,
        ftail,
        a_all,
        r_all,
        c_all,
        outs,
        late,
        scratch[LINE + 11 : LINE + 18],
    )
    tail = None
    if tails:
        tail = Tail(
            held[0],
            tail_refs[tails],
            tail_refs[tails + 1],
            tail_refs[:tails],
            abuf,
            fbuf,
            ftail,
            scratch[LINE + 18 :],
        )

    def finish(b):
        block = gathered[b]
        store_turned(block, turned, b)
        for start, width in spans(wg.shape[1]):
            at = slice(start, start + width)
            d = nn(block, wd[:, at])
            g = gate[b, :, at].astype(f32)
            u = up[b, :, at].astype(f32)
            sigma = lax.logistic(g)
            ds = d * sigma
            dg = (ds * u * (1.0 + g * (1.0 - sigma))).astype(bf16)
            du = (ds * g).astype(bf16)
            gate[b, :, at] = dg
            up[b, :, at] = du
            p = nt(dg, wg[:, at]) + nt(du, wu[:, at])
            if start == 0:
                part[...] = p
            else:
                part[...] += p

    def run(verb, m):
        if verb == "swap":
            copy = pltpu.make_async_copy(turned_ref, turned, w_sem.at[0])
            copy.start()
            copy.wait()
        elif verb == "kept":
            reduce.keep(m).wait()
        elif verb == "sent":
            for j, at in reduce.columns():
                reduce.swap(m, j, at).wait_send()
        else:
            getattr(reduce, verb)(m)

    def work(t):
        def act():
            if tail is not None and t == 1:
                for i in range(tails):
                    tail.close(i)
            for verb, m in AFTER[t]:
                run(verb, m)

        return act

    def each(verb):
        def act():
            for i in range(tails):
                getattr(tail, verb)(i)

        return act

    peers = [reduce.partner] + reduce.near
    plan = {("hop", t): work(t) for t in range(3)}
    if tails:
        for key, act in ((TAIL_BEGIN, each("begin")), (TAIL_MIDDLE, each("middle"))):
            old = plan.get(key)
            plan[key] = act if old is None else both(act, old)
    line_pass(grad_ref, sum_ref, gathered, part, outb, inb, sems, load, finish, peers, plan)
    for verb, m in ENDS[late]:
        run(verb, m)


def backward_ffn(grad, gate, up, hidden, turned, wg, wu, wd, late, held=None):
    rows, width = grad.shape
    devices, size, wide = lax.axis_size("gx"), lax.axis_size("gy"), wg.shape[1]
    near = 2 if devices == 8 else devices // 2 - 1
    r = width // devices
    mine = jax.ShapeDtypeStruct((r, wide), f32)

    def between(*dims):
        return jax.ShapeDtypeStruct(dims + (wide,), bf16)

    count = 3 - len(late)
    out = [jax.ShapeDtypeStruct((rows, width), f32)]
    out += [between(1, width // 2) if m in late else mine for m in range(3)]
    out += [between(3, width // 2), between(count, 2, r // 2), between(count, near, r)]
    tails = 0 if held is None else held.shape[0]
    if tails:
        out += [mine] * tails
        out += [between(tails, 2, r // 2), between(tails, near, 2, r // 2)]
    extra = [held] if tails else []
    return pl.pallas_call(
        functools.partial(backward_kernel, late, tails),
        out_shape=out,
        in_specs=[ANY] * (8 + len(extra)),
        out_specs=[pl.BlockSpec(memory_space=pltpu.VMEM)] + [ANY] * (len(out) - 1),
        scratch_shapes=line_scratch(size, rows, width)
        + [pltpu.VMEM((width, wide), bf16)] * 3
        + [pltpu.VMEM((size, rows, wide), bf16)] * 3
        + [pltpu.VMEM((2, width // 2, size * rows), bf16), pltpu.SemaphoreType.DMA((6,))]
        + reduce_scratch(width, wide)
        + (tail_scratch(tails) if tails else []),
        compiler_params=pltpu.CompilerParams(
            collective_id=1 if held is None else 5, has_side_effects=True, vmem_limit_bytes=VMEM_LIMIT
        ),
        cost_estimate=pl.CostEstimate(
            flops=12 * size * rows * width * wide, bytes_accessed=40 << 20, transcendentals=0
        ),
        name="ffn_backward",
    )(grad, gate, up, hidden, turned, wg, wu, wd, *extra)


class Fold:
    def __init__(self, lhs, rhs, bufs, sems):
        self.lhs, self.rhs = lhs, rhs
        self.up, self.low, self.a_in, self.r_in, self.c_in, self.z_out, self.z_in = bufs
        (
            self.a_send,
            self.a_recv,
            self.r_send,
            self.r_recv,
            self.c_send,
            self.c_recv,
            self.z_send,
            self.z_recv,
        ) = sems
        self.gx, self.gy = lax.axis_index("gx"), lax.axis_index("gy")
        self.core, self.size = lax.rem(self.gx, 2), lax.axis_size("gy")
        self.chips = lax.axis_size("gx") // 2
        self.r = self.low.shape[2] // self.chips
        self.four = self.chips == 4
        self.partner, self.others = places()
        self.near = list(square()[:2]) if self.four else self.others

    def product(self, m, which, z):
        return [nn(left[which], right[z]) for left, right in zip(self.lhs[m], self.rhs[m])]

    def remote(self, src, dst, send, recv, gx, gy):
        return pltpu.make_async_remote_copy(
            src_ref=src,
            dst_ref=dst,
            send_sem=send,
            recv_sem=recv,
            device_id=(gx, gy),
            device_id_type=MESH,
        )

    def block(self, m, device, start=0, size=None):
        size = self.r if size is None else size
        first = (device // 2) * self.r + start
        return self.low.at[m, :, pl.ds(pl.multiple_of(first, 16), size)]

    def swap(self, m, z):
        return self.remote(
            self.up.at[m, z],
            self.a_in.at[m, z],
            self.a_send.at[m, z],
            self.a_recv.at[m, z],
            self.partner,
            self.gy,
        )

    def first(self, m):
        for z in range(self.size):
            left, right = self.product(m, 1 - self.core, z)
            edge = left.shape[1]
            self.up[m, z, :, :edge] = left.astype(bf16)
            self.up[m, z, :, edge:] = right.astype(bf16)
            self.swap(m, z).start()

    def corner(self, m, h):
        side, along, across = square()
        half = self.r // 2
        return self.remote(
            self.block(m, across, h * half, half),
            self.r_in.at[m, h],
            self.r_send.at[m, h],
            self.r_recv.at[m, h],
            along if h else side,
            self.gy,
        )

    def second(self, m):
        for z in range(self.size):
            left, right = self.product(m, self.core, z)
            edge = left.shape[1]
            self.swap(m, z).wait_recv()
            came = self.a_in[m, z].astype(f32)
            self.low[m, z, :, :edge] = (left + came[:, :edge]).astype(bf16)
            self.low[m, z, :, edge:] = (right + came[:, edge:]).astype(bf16)
        if self.four:
            for h in range(2):
                self.corner(m, h).start()

    def hand(self, m, k):
        return self.remote(
            self.block(m, self.near[k]),
            self.c_in.at[m, k],
            self.c_send.at[m, k],
            self.c_recv.at[m, k],
            self.near[k],
            self.gy,
        )

    def third(self, m):
        if self.four:
            side, along, _ = square()
            half = self.r // 2
            for h, device in ((0, along), (1, side)):
                self.corner(m, h).wait_recv()
                here = self.block(m, device, h * half, half)
                here[...] = (here[...].astype(f32) + self.r_in[m, h].astype(f32)).astype(bf16)
        for k in range(len(self.near)):
            self.hand(m, k).start()

    def down_line(self, m, d):
        target = lax.rem(self.gy + d, self.size)
        return self.remote(
            self.z_out.at[m, target],
            self.z_in.at[m, self.gy],
            self.z_send.at[m, d],
            self.z_recv.at[m, self.gy],
            self.gx,
            target,
        )

    def fourth(self, m):
        for k in range(len(self.near)):
            self.hand(m, k).wait_recv()
        mine = self.block(m, self.gx)
        for z in range(self.size):
            total = mine[z].astype(f32)
            for k in range(len(self.near)):
                total = total + self.c_in[m, k, z].astype(f32)
            self.z_out[m, z] = total.astype(bf16)
        for d in range(1, self.size):
            self.down_line(m, d).start()

    def fifth(self, m, out):
        total = self.z_out[m, self.gy].astype(f32)
        for d in range(1, self.size):
            z = lax.rem(self.gy + d, self.size)
            wait_for(self.z_in.at[m, z], self.z_recv.at[m, z])
            total = total + self.z_in[m, z].astype(f32)
        out[m] = total

    def drain(self, m):
        for z in range(self.size):
            self.swap(m, z).wait_send()
        if self.four:
            for h in range(2):
                self.corner(m, h).wait_send()
        for k in range(len(self.near)):
            self.hand(m, k).wait_send()
        for d in range(1, self.size):
            self.down_line(m, d).wait_send()


class Total:
    def __init__(self, own, line_in, pair, pair_in, chip_in, sems):
        self.own, self.line_in, self.pair = own, line_in, pair
        self.pair_in, self.chip_in = pair_in, chip_in
        self.l_send, self.l_recv, self.p_send, self.p_recv, self.g_send, self.g_recv = sems
        self.gx, self.gy = lax.axis_index("gx"), lax.axis_index("gy")
        self.size, self.chips = lax.axis_size("gy"), lax.axis_size("gx") // 2
        self.partner, self.others = places()

    def remote(self, src, dst, send, recv, gx, gy):
        return pltpu.make_async_remote_copy(
            src_ref=src,
            dst_ref=dst,
            send_sem=send,
            recv_sem=recv,
            device_id=(gx, gy),
            device_id_type=MESH,
        )

    def line(self, d):
        target = lax.rem(self.gy + d, self.size)
        return self.remote(
            self.own.at[target],
            self.line_in.at[self.gy],
            self.l_send.at[d],
            self.l_recv.at[self.gy],
            self.gx,
            target,
        )

    def across(self):
        return self.remote(
            self.pair.at[0], self.pair_in, self.p_send, self.p_recv, self.partner, self.gy
        )

    def chip(self, k):
        return self.remote(
            self.pair.at[1],
            self.chip_in.at[self.gx // 2],
            self.g_send.at[k],
            self.g_recv.at[self.gx // 2],
            self.others[k],
            self.gy,
        )

    def begin(self):
        for d in range(1, self.size):
            self.line(d).start()

    def middle(self):
        total = self.own[self.gy]
        for d in range(1, self.size):
            z = lax.rem(self.gy + d, self.size)
            wait_for(self.line_in.at[z], self.l_recv.at[z])
            total = total + self.line_in[z]
        self.pair[0] = total
        self.across().start()

    def later(self):
        self.across().wait_recv()
        self.pair[1] = self.pair[0] + self.pair_in[...]
        self.chip_in[self.gx // 2] = self.pair[1]
        for k in range(self.chips - 1):
            self.chip(k).start()

    def close(self, out):
        for k in range(self.chips - 1):
            q = self.others[k] // 2
            wait_for(self.chip_in.at[q], self.g_recv.at[q])
        total = self.chip_in[0]
        for q in range(1, self.chips):
            total = total + self.chip_in[q]
        out[...] = total
        for d in range(1, self.size):
            self.line(d).wait_send()
        self.across().wait_send()
        for k in range(self.chips - 1):
            self.chip(k).wait_send()


def closing_kernel(layers, *refs):
    operands, refs = refs[: 4 * layers], refs[4 * layers :]
    small, out_rows, grad_rows = refs[:3]
    grads, small_out, out_blocks, grad_blocks = refs[3:7]
    scratch = refs[7:]
    lhs = [operands[4 * m : 4 * m + 2] for m in range(layers)]
    rhs = [operands[4 * m + 2 : 4 * m + 4] for m in range(layers)]
    fold = Fold(lhs, rhs, scratch[:7], scratch[7:15])
    total = Total(small, *scratch[15:19], scratch[19:25])
    swaps = [
        Exchange(own, full, scratch[25 + 3 * k : 28 + 3 * k], True)
        for k, (own, full) in enumerate(((grad_rows, grad_blocks), (out_rows, out_blocks)))
    ]
    me, size = lax.axis_index("gy"), lax.axis_size("gy")
    greet([fold.partner] + fold.others, [lax.rem(me + d, size) for d in range(1, size)])
    total.begin()
    for m in range(layers):
        fold.first(m)
    for swap in swaps:
        swap.begin()
    fold.second(0)
    total.middle()
    for m in range(1, layers):
        fold.second(m)
    total.later()
    for m in range(layers):
        fold.third(m)
    for m in range(layers):
        fold.fourth(m)
    total.close(small_out)
    for m in range(layers):
        fold.fifth(m, grads)
    for m in range(layers):
        fold.drain(m)
    for swap in swaps:
        swap.close()


def closing(operands, small, out_rows, grad_rows):
    layers = len(operands) // 4
    devices, size = lax.axis_size("gx"), lax.axis_size("gy")
    half = operands[0].shape[1]
    chips = devices // 2
    r, near = half // chips, 2 if chips == 4 else chips - 1
    c = operands[2].shape[2] + operands[3].shape[2]
    vmem, dma = pltpu.VMEM, pltpu.SemaphoreType.DMA
    row = small.shape[1:]
    local = pl.BlockSpec(memory_space=pltpu.VMEM)
    blocks = jax.ShapeDtypeStruct(out_rows.shape, bf16)
    return pl.pallas_call(
        functools.partial(closing_kernel, layers),
        out_shape=[
            jax.ShapeDtypeStruct((layers, r, c), f32),
            jax.ShapeDtypeStruct(row, f32),
            blocks,
            blocks,
        ],
        in_specs=[local] * (len(operands) + 1) + [ANY] * 2,
        out_specs=[local] * 2 + [ANY] * 2,
        scratch_shapes=[
            vmem((layers, size, half, c), bf16),
            vmem((layers, size, half, c), bf16),
            vmem((layers, size, half, c), bf16),
            vmem((layers, 2, size, r // 2, c), bf16),
            vmem((layers, near, size, r, c), bf16),
            vmem((layers, size, r, c), bf16),
            vmem((layers, size, r, c), bf16),
            dma((layers, size)),
            dma((layers, size)),
            dma((layers, 2)),
            dma((layers, 2)),
            dma((layers, near)),
            dma((layers, near)),
            dma((layers, size)),
            dma((layers, size)),
            vmem((size,) + row, f32),
            vmem((2,) + row, f32),
            vmem(row, f32),
            vmem((chips,) + row, f32),
            dma((size,)),
            dma((size,)),
            dma,
            dma,
            dma((chips,)),
            dma((chips,)),
        ]
        + exchange_scratch() * 2,
        compiler_params=pltpu.CompilerParams(
            collective_id=4, has_side_effects=True, vmem_limit_bytes=VMEM_LIMIT
        ),
        name="closing",
    )(*operands, small, out_rows, grad_rows)


def swing(value, cosine, turned_sine):
    return value * cosine + pltpu.roll(value, HEAD_DIM // 2, 1) * turned_sine


def tile_columns(value, tables):
    heads = value.shape[1] // HEAD_DIM
    parts = [swing(value[:, k * HEAD_DIM : (k + 1) * HEAD_DIM], *tables) for k in range(heads)]
    return jnp.concatenate(parts, axis=1)


def store_split(block, turned):
    width = block.shape[1]
    devices = lax.axis_size("gx")
    r = width // devices
    flipped = block.T
    for k in range(devices):
        q = k // 2
        turned[k % 2, q * r : (q + 1) * r] = flipped[k * r : (k + 1) * r]


def norm_pull(grad, normed, scale, gain):
    row = jnp.sum(grad * normed, axis=0, keepdims=True)
    scaled = grad * gain
    project = jnp.mean(scaled * normed, axis=1, keepdims=True)
    return row, scale * (scaled - normed * project)


def attention_pull_kernel(*refs):
    held, (late_grad, r_all, c_all) = refs[17], refs[24:27]
    refs = refs[:17] + refs[18:24] + refs[27:]
    (grad, grad_ffn, norm_b, scale_b, gain_b, norm_a, scale_a, gain_a) = refs[:8]
    acts, q, k, v, lse, cosine, sine, qkv_ref, out_ref = refs[8:17]
    grad_out, grad_low, acts_turned, branch_turned, gqkv, small = refs[17:23]
    qkv, wout, heads, branch, dq, dk_sum, dv_sum, kv_out, kv_in, total = refs[23:33]
    w_sem, kv_send, kv_recv, abuf, fbuf, ftail = refs[33:39]
    tail = Tail(held, r_all, c_all, [late_grad], abuf, fbuf, ftail, refs[39:])
    gx, me, size = lax.axis_index("gx"), lax.axis_index("gy"), lax.axis_size("gy")
    count, rows = q.shape[0], k.shape[0]
    loads = [
        pltpu.make_async_copy(out_ref, wout, w_sem.at[0]),
        pltpu.make_async_copy(qkv_ref, qkv, w_sem.at[1]),
    ]
    for load in loads:
        load.start()
    greet(tail.near, [lax.rem(me + d, size) for d in range(1, size)])
    tail.begin(0)
    small[...] = jnp.zeros_like(small)
    row, pulled = norm_pull(grad_ffn[...], norm_b[...], scale_b[...], gain_b[...])
    small[1:2] = row
    branch[...] = grad[...] + pulled
    low = branch[...].astype(bf16)
    store_split(low, branch_turned)
    store_split(acts[...], acts_turned)
    loads[0].wait()
    cq = wout.shape[2]
    heads[...] = jnp.concatenate([nn(low, wout[z]) for z in range(size)], axis=1).astype(bf16)

    tail.middle(0)
    query = me * count + lax.broadcasted_iota(jnp.int32, (rows, count), 1)
    key = lax.broadcasted_iota(jnp.int32, (rows, count), 0)
    allowed = key <= query
    if rows > LEN:
        allowed = jnp.logical_and(allowed, key // LEN == query // LEN)
    factor = 1.0 / math.sqrt(HEAD_DIM)
    tables = (cosine[...], sine[...])

    def kv_copy(g, d):
        target = lax.rem(me + d, size)
        return pltpu.make_async_remote_copy(
            src_ref=kv_out.at[g, target],
            dst_ref=kv_in.at[g, me],
            send_sem=kv_send.at[g, d],
            recv_sem=kv_recv.at[g, me],
            device_id=(gx, target),
            device_id_type=MESH,
        )

    for g in range(KV_HEADS):
        span = slice(g * HEAD_DIM, (g + 1) * HEAD_DIM)
        kg, vg = k[:, span], v[:, span]
        turned_k = kg.T
        dk_sum[...] = jnp.zeros_like(dk_sum)
        dv_sum[...] = jnp.zeros_like(dv_sum)

        def head(i, carry):
            h = g * GROUP + i
            at = pl.ds(pl.multiple_of(h * HEAD_DIM, HEAD_DIM), HEAD_DIM)
            qh, dh = q[:, at], heads[:, at]
            scores = jnp.where(allowed, nt(kg, qh) * factor, -1e30)
            p = jnp.exp(scores - lse[pl.ds(h, 1), :])
            dp = nt(vg, dh)
            inner = jnp.sum(p * dp, axis=0, keepdims=True)
            ds = (p * (dp - inner)).astype(bf16)
            dv_sum[...] += nn(p.astype(bf16), dh)
            dk_sum[...] += nn(ds, qh)
            dq[:, at] = swing(nn(turned_k, ds).T * factor, *tables).astype(bf16)
            return carry

        lax.fori_loop(0, GROUP, head, 0)
        for z in range(size):
            at = slice(z * count, (z + 1) * count)
            kv_out[g, z, :, :HEAD_DIM] = (dk_sum[at] * factor).astype(bf16)
            kv_out[g, z, :, HEAD_DIM:] = dv_sum[at].astype(bf16)
        for d in range(1, size):
            kv_copy(g, d).start()

    loads[1].wait()
    apart = cq % HEAD_DIM == 0
    if apart:
        for z in range(size):
            p = nt(dq[:, z * cq : (z + 1) * cq], qkv[z, :, :cq])
            if z == 0:
                total[...] = p
            else:
                total[...] += p
    dks, dvs = [], []
    for g in range(KV_HEADS):
        summed = kv_out[g, me].astype(f32)
        for d in range(1, size):
            z = lax.rem(me + d, size)
            wait_for(kv_in.at[g, z], kv_recv.at[g, z])
            summed = summed + kv_in[g, z].astype(f32)
        dks.append(swing(summed[:, :HEAD_DIM], *tables).astype(bf16).astype(f32))
        dvs.append(summed[:, HEAD_DIM:].astype(bf16).astype(f32))
    dk, dv = jnp.concatenate(dks, axis=1), jnp.concatenate(dvs, axis=1)
    ck = dk.shape[1] // size
    for z in range(size):
        at = slice(z * ck, (z + 1) * ck)
        kv = jnp.concatenate([dk[:, at], dv[:, at]], axis=1)
        if apart:
            kv = kv.astype(bf16)
            gqkv[z, :, :cq] = dq[:, z * cq : (z + 1) * cq]
            gqkv[z, :, cq:] = kv
            total[...] += nt(kv, qkv[z, :, cq:])
        else:
            mine = dq[:, z * cq : (z + 1) * cq].astype(f32)
            gqkv[z] = jnp.concatenate([mine, kv], axis=1).astype(bf16)
            p = nt(gqkv[z], qkv[z])
            if z == 0:
                total[...] = p
            else:
                total[...] += p
    row, pulled = norm_pull(total[...], norm_a[...], scale_a[...], gain_a[...])
    small[0:1] = row
    small[2:3] = jnp.sum(dq[...].astype(f32), axis=0, keepdims=True)
    width = dk.shape[1]
    small[3:4, :width] = jnp.sum(dk, axis=0, keepdims=True)
    small[4:5, :width] = jnp.sum(dv, axis=0, keepdims=True)
    final = branch[...] + pulled
    grad_out[...] = final
    grad_low[...] = final.astype(bf16)
    tail.close(0)
    for g in range(KV_HEADS):
        for d in range(1, size):
            kv_copy(g, d).wait_send()


def attention_pull(vectors, acts, q, k, v, lse, tables, qkv, wout, held):
    count, width = acts.shape
    size, rows = lax.axis_size("gy"), k.shape[0]
    local = pl.BlockSpec(memory_space=pltpu.VMEM)
    vmem, dma = pltpu.VMEM, pltpu.SemaphoreType.DMA
    turned = jax.ShapeDtypeStruct((2, width // 2, count), bf16)
    devices, wide = lax.axis_size("gx"), held.shape[2]
    near = 2 if devices == 8 else devices // 2 - 1
    r = width // devices
    return pl.pallas_call(
        attention_pull_kernel,
        out_shape=[
            jax.ShapeDtypeStruct((count, width), f32),
            jax.ShapeDtypeStruct((count, width), bf16),
            turned,
            turned,
            jax.ShapeDtypeStruct((size, count, qkv.shape[2]), bf16),
            jax.ShapeDtypeStruct((8, width), f32),
            jax.ShapeDtypeStruct((r, wide), f32),
            jax.ShapeDtypeStruct((1, 2, r // 2, wide), bf16),
            jax.ShapeDtypeStruct((1, near, 2, r // 2, wide), bf16),
        ],
        in_specs=[local] * 15 + [ANY] * 3,
        out_specs=[local] * 6 + [ANY] * 3,
        scratch_shapes=[
            vmem(qkv.shape, bf16),
            vmem(wout.shape, bf16),
            vmem((count, width), bf16),
            vmem((count, width), f32),
            vmem((count, width), bf16),
            vmem((rows, HEAD_DIM), f32),
            vmem((rows, HEAD_DIM), f32),
            vmem((KV_HEADS, size, count, 2 * HEAD_DIM), bf16),
            vmem((KV_HEADS, size, count, 2 * HEAD_DIM), bf16),
            vmem((count, width), f32),
            dma((2,)),
            dma((KV_HEADS, size)),
            dma((KV_HEADS, size)),
            vmem((width // 4, wide), bf16),
            vmem((r, FF_CHUNK), f32),
            vmem((r, wide % FF_CHUNK), f32),
        ]
        + tail_scratch(1),
        compiler_params=pltpu.CompilerParams(
            collective_id=6, has_side_effects=True, vmem_limit_bytes=VMEM_LIMIT
        ),
        name="attention_pull",
    )(*vectors, acts, q, k, v, lse, *tables, qkv, wout, held)


def greet_line(gx_peers=()):
    gx, me, last = lax.axis_index("gx"), lax.axis_index("gy"), lax.axis_size("gy") - 1
    barrier = pltpu.get_barrier_semaphore()

    @pl.when(me > 0)
    def _():
        pl.semaphore_signal(barrier, inc=1, device_id=(gx, me - 1), device_id_type=MESH)

    @pl.when(me < last)
    def _():
        pl.semaphore_signal(barrier, inc=1, device_id=(gx, me + 1), device_id_type=MESH)

    for peer in gx_peers:
        pl.semaphore_signal(barrier, inc=1, device_id=(peer, me), device_id_type=MESH)
    count = jnp.where(jnp.logical_and(me > 0, me < last), 2, 1)
    pl.semaphore_wait(barrier, count + len(gx_peers))


PUSH_PLAN = {
    "chained": ("begin",),
    "group0": ("relay",),
    "group1": ("finish",),
    "end": ("close",),
}


def attention_push_kernel(layer, *refs):
    shard_ref, whole_ref = refs[10], refs[23]
    refs = refs[:10] + refs[11:23] + refs[24:]
    x, gain_a, gain_b, bq, bk, bv, cosine, sine, qkv_ref, out_ref = refs[:10]
    middle, norm_a, scale_a, acts_a, q, k_all, v_all, lse = refs[10:18]
    mixed, norm_b, scale_b, acts_b = refs[18:22]
    qkv, wout, kv_own, kv_all, flat, w_sem = refs[22:28]
    me, size = lax.axis_index("gy"), lax.axis_size("gy")
    count, rows = x.shape[0], k_all.shape[0]
    loads = [
        pltpu.make_async_copy(qkv_ref, qkv, w_sem.at[0]),
        pltpu.make_async_copy(out_ref, wout, w_sem.at[1]),
    ]
    for load in loads:
        load.start()
    chain = Chain(kv_own, kv_all, refs[28:31])
    spread = Spread([(shard_ref.at[layer], whole_ref)], refs[31:34])

    def move(name):
        for verb in PUSH_PLAN.get(name, ()):
            getattr(spread, verb)(0)

    greet_line([spread.partner] + spread.near)
    move("greeted")
    value = x[...]
    scale = lax.rsqrt(jnp.mean(value * value, axis=1, keepdims=True) + epsilon)
    scale_a[...] = scale
    norm_a[...] = value * scale
    acts_a[...] = (norm_a[...] * gain_a[...]).astype(bf16)
    loads[0].wait()
    cq, width = wout.shape[2], k_all.shape[1]
    ck = width // size
    tables = (cosine[...], sine[...])
    apart = cq % HEAD_DIM == 0
    if apart:
        kv = [nn(acts_a[...], qkv[z, :, cq:]) for z in range(size)]
    else:
        both = [nn(acts_a[...], qkv[z]) for z in range(size)]
        kv = [part[:, cq:] for part in both]
    keys = jnp.concatenate([part[:, :ck] for part in kv], axis=1) + bk[...]
    values = jnp.concatenate([part[:, ck:] for part in kv], axis=1) + bv[...]
    kv_own[:, :width] = tile_columns(keys, tables).astype(bf16)
    kv_own[:, width:] = values.astype(bf16)
    chain.begin()
    move("chained")
    if apart:
        for z in range(size):
            at = slice(z * cq, (z + 1) * cq)
            mine = nn(acts_a[...], qkv[z, :, :cq]) + bq[:, at]
            q[:, at] = tile_columns(mine, tables).astype(bf16)
            if z:
                chain.relay(z)
    else:
        mine = jnp.concatenate([part[:, :cq] for part in both], axis=1) + bq[...]
        q[...] = tile_columns(mine, tables).astype(bf16)
        for t in range(1, size):
            chain.relay(t)
    chain.close()
    move("relayed")
    k_all[...] = kv_all[:, :, :width].reshape(rows, width)
    v_all[...] = kv_all[:, :, width:].reshape(rows, width)

    query = me * count + lax.broadcasted_iota(jnp.int32, (rows, count), 1)
    key = lax.broadcasted_iota(jnp.int32, (rows, count), 0)
    allowed = key <= query
    if rows > LEN:
        allowed = jnp.logical_and(allowed, key // LEN == query // LEN)
    factor = 1.0 / math.sqrt(HEAD_DIM)
    for g in range(KV_HEADS):
        span = slice(g * HEAD_DIM, (g + 1) * HEAD_DIM)
        kg, turned_v = k_all[:, span], v_all[:, span].T

        def head(i, carry):
            h = g * GROUP + i
            at = pl.ds(pl.multiple_of(h * HEAD_DIM, HEAD_DIM), HEAD_DIM)
            scores = jnp.where(allowed, nt(kg, q[:, at]) * factor, -1e30)
            top = jnp.max(scores, axis=0, keepdims=True)
            expo = jnp.exp(scores - top)
            total = jnp.sum(expo, axis=0, keepdims=True)
            lse[pl.ds(h, 1), :] = top + jnp.log(total)
            soft = (expo * (1.0 / total)).astype(bf16)
            flat[:, at] = nn(turned_v, soft).T.astype(bf16)
            return carry

        lax.fori_loop(0, GROUP, head, 0)
        move("group%d" % g)
    loads[1].wait()
    middle[...] = x[...]
    for z in range(size):
        at = slice(z * cq, (z + 1) * cq)
        if apart:
            mixed[z] = flat[:, at]
        else:
            mixed[z] = flat[:, at].astype(f32).astype(bf16)
        middle[...] += nt(mixed[z], wout[z])
    value = middle[...]
    scale = lax.rsqrt(jnp.mean(value * value, axis=1, keepdims=True) + epsilon)
    scale_b[...] = scale
    norm_b[...] = value * scale
    acts_b[...] = (norm_b[...] * gain_b[...]).astype(bf16)
    move("end")


def attention_push(x, vectors, tables, qkv, wout, rows, shard, layer):
    count, width = x.shape
    size = lax.axis_size("gy")
    kvd = KV_HEADS * HEAD_DIM
    local = pl.BlockSpec(memory_space=pltpu.VMEM)
    vmem = pltpu.VMEM

    def shape(*dims, kind=bf16):
        return jax.ShapeDtypeStruct(dims, kind)

    normed = [shape(count, width, kind=f32), shape(count, 1, kind=f32), shape(count, width)]
    out = [shape(count, width, kind=f32), *normed, shape(count, HEADS * HEAD_DIM)]
    out += [shape(rows, kvd), shape(rows, kvd), shape(HEADS, count, kind=f32)]
    out += [shape(size, count, wout.shape[2]), *normed]
    out += [shape(lax.axis_size("gx"), *shard.shape[1:])]
    return pl.pallas_call(
        functools.partial(attention_push_kernel, layer),
        out_shape=out,
        in_specs=[local] * 8 + [ANY] * 3,
        out_specs=[local] * 12 + [ANY],
        scratch_shapes=[
            vmem(qkv.shape, bf16),
            vmem(wout.shape, bf16),
            vmem((count, 2 * kvd), bf16),
            vmem((size, count, 2 * kvd), bf16),
            vmem((count, HEADS * HEAD_DIM), bf16),
            pltpu.SemaphoreType.DMA((2,)),
        ]
        + chain_scratch()
        + spread_scratch(1),
        compiler_params=pltpu.CompilerParams(
            collective_id=7 + layer, has_side_effects=True, vmem_limit_bytes=VMEM_LIMIT
        ),
        name="attention_push",
    )(x, *vectors, *tables, qkv, wout, shard)


def on_device(
    residual_in,
    w_query,
    w_key,
    w_value,
    b_query,
    b_key,
    b_value,
    w_output,
    gain_attn,
    gain_ffn,
    w_gate,
    w_up,
    w_down,
    cotangent,
):
    devices_y = lax.axis_size("gy")
    rows_tok = residual_in.shape[1]
    count = rows_tok // devices_y
    q_index = lax.axis_index("gy") * count + jnp.arange(count, dtype=jnp.int32)
    cos_table, sin_table = rope_tables(q_index % LEN, HEAD_DIM)

    small = jnp.concatenate([gain_attn, gain_ffn, b_query, b_key, b_value], axis=1)
    small_sizes = [v.shape[1] for v in (gain_attn, gain_ffn, b_query, b_key, b_value)]
    small = jnp.pad(small.astype(f32), ((0, 8 - LAYERS), (0, 0)))
    lines = []
    for l in range(LAYERS):
        lines += [jnp.concatenate([w_query[l], w_key[l], w_value[l]], axis=1), w_output[l]]
    part_sizes = (w_query.shape[2], w_key.shape[2], w_value.shape[2])
    opened = opening(residual_in, cotangent, small, lines, w_gate, w_up)
    resid, cot, small = opened[:3]
    lines_next = opened[5:7]
    attn_full = [[w.reshape(devices_y, D, -1) for w in opened[7:9]], None]
    ffn_full = [[w.reshape(D, -1) for w in opened[9:]], None]
    small = small[:, :LAYERS].transpose(1, 0, 2)
    vectors, start = [], 0
    for size in small_sizes:
        vectors.append(small[:, :, start : start + size].reshape(LAYERS, -1))
        start += size
    gains_one, gains_two, bias_q, bias_k, bias_v = vectors

    resid = resid.reshape(D, count).astype(f32).T
    cot = cot.reshape(D, count)

    kept = []
    for l in range(LAYERS):
        w_qkv, w_out = attn_full[l]
        vectors = [v[l][None] for v in (gains_one, gains_two, bias_q, bias_k, bias_v)]
        done = attention_push(
            resid, vectors, (cos_table, -sin_table), w_qkv, w_out, rows_tok, w_down, l
        )
        middle, normed_one, scale_one, acts_one, q_rot, k_rot, v_heads, log_total = done[:8]
        mixed, normed_two, scale_two, acts_two = done[8:12]
        wg, wu = ffn_full[l]
        wd = done[12].reshape(D, -1)
        ffn_full[l] = (wg, wu, wd)
        if l == 0:
            shards = (*lines_next, w_gate, w_up)
            done = forward_ffn(acts_two, wg, wu, wd, shards)
            attn_full[1] = [w.reshape(devices_y, D, -1) for w in done[5:7]]
            ffn_full[1] = [w.reshape(D, -1) for w in done[7:]]
        else:
            done = forward_ffn(acts_two, wg, wu, wd)
        part, acts_two, gate, up, hidden = done[:5]
        kept.append(
            (
                normed_one,
                scale_one,
                acts_one,
                q_rot,
                k_rot,
                v_heads,
                log_total,
                mixed,
                normed_two,
                scale_two,
                acts_two,
                gate,
                up,
                hidden,
            )
        )
        resid = middle + part

    grad = cot.astype(f32).T + 2.0 * penalty * resid
    grad_low = grad.astype(bf16)
    attn_grads = [None] * LAYERS
    ffn_grads = [None] * LAYERS
    small_grads = [None] * LAYERS

    for l in reversed(range(LAYERS)):
        (
            normed_one,
            scale_one,
            acts_one,
            q_rot,
            k_rot,
            v_heads,
            log_total,
            mixed,
            normed_two,
            scale_two,
            acts_two,
            gate,
            up,
            hidden,
        ) = kept[l]
        w_qkv, w_out = attn_full[l]
        wg, wu, wd = ffn_full[l]
        operands = (grad_low, gate, up, hidden, acts_two, wg, wu, wd)
        if l == LAYERS - 1:
            done = backward_ffn(*operands, (1, 2))
            held = done[2]
            ffn_grads[l] = [None, None, done[1]]
        else:
            done = backward_ffn(*operands, (2,), held_next)
            ffn_grads[l] = [done[2], None, done[1]]
            ffn_grads[l + 1][1] = done[7]
            held = done[3]
        held_next = done[3]
        grad_acts_two = done[0]
        vectors = [grad, grad_acts_two, normed_two, scale_two, gains_two[l][None]]
        vectors += [normed_one, scale_one, gains_one[l][None]]
        done = attention_pull(
            vectors, acts_one, q_rot, k_rot, v_heads, log_total, (cos_table, sin_table), w_qkv, w_out, held
        )
        ffn_grads[l][0 if l == LAYERS - 1 else 1] = done[6]
        grad, grad_low = done[:2]
        attn_grads[l] = [*done[2:5], mixed]
        rows = done[5]
        width = k_rot.shape[1]
        small_grads[l] = [
            v.reshape(devices_y, -1)
            for v in (rows[0], rows[1], rows[2], rows[3, :width], rows[4, :width])
        ]
    small = jnp.stack([jnp.concatenate(v, axis=1) for v in small_grads], axis=1)
    small = jnp.pad(small, ((0, 0), (0, 8 - LAYERS), (0, 0)))

    def to_rows(tokens_major):
        return tokens_major.astype(bf16).T.reshape(devices_y, -1, count)

    def from_blocks(blocks):
        return blocks.transpose(1, 0, 2).reshape(-1, rows_tok).astype(f32)

    attn_sums, small, output, grad_input = closing(
        attn_grads[0] + attn_grads[1], small, to_rows(resid), to_rows(grad_low)
    )
    small = small[:LAYERS]
    attn_out, start = [], 0
    for size in part_sizes + (w_output.shape[2],):
        attn_out.append(attn_sums[:, :, start : start + size])
        start += size
    small_out, start = [], 0
    for size in small_sizes:
        small_out.append(small[:, start : start + size])
        start += size

    def stack(parts, k):
        return jnp.stack([part[k] for part in parts])

    return (
        from_blocks(output),
        from_blocks(grad_input),
        attn_out[0],
        attn_out[1],
        attn_out[2],
        small_out[2],
        small_out[3],
        small_out[4],
        attn_out[3],
        small_out[0],
        small_out[1],
        stack(ffn_grads, 0),
        stack(ffn_grads, 1),
        stack(ffn_grads, 2),
    )


def solution(mesh):
    tokens = P("gy", "gx")
    weight = P(None, "gx", "gy")
    vector = P(None, "gy")
    return jax.shard_map(
        on_device,
        mesh=mesh,
        in_specs=(
            tokens,
            weight,
            weight,
            weight,
            vector,
            vector,
            vector,
            weight,
            vector,
            vector,
            weight,
            weight,
            weight,
            tokens,
        ),
        out_specs=(
            tokens,
            tokens,
            weight,
            weight,
            weight,
            vector,
            vector,
            vector,
            weight,
            vector,
            vector,
            weight,
            weight,
            weight,
        ),
        check_vma=False,
    )
```

```python
import functools
import math

import jax
import jax.numpy as jnp
from jax import lax
from jax.experimental import pallas as pl
from jax.experimental.pallas import tpu as pltpu
from jax.sharding import PartitionSpec as P

D = 1536
HEADS = 12
KV_HEADS = 2
HEAD_DIM = 128
LEN = 1024
LAYERS = 2
GROUP = HEADS // KV_HEADS

epsilon = 1e-06
rope_base = 1000000.0
penalty = 0.25
bf16 = jnp.bfloat16
f32 = jnp.float32
MESH = pl.DeviceIdType.MESH
VMEM_LIMIT = 62 << 20
ANY = pl.BlockSpec(memory_space=pl.ANY)


def rope_tables(positions, head_size):
    freqs = rope_base ** (-jnp.arange(0, head_size, 2).astype(f32) / head_size)
    angles = positions.astype(f32)[:, None] * freqs[None, :]
    cosine = jnp.cos(angles)
    sine_table = jnp.sin(angles)
    return (
        jnp.concatenate([cosine, cosine], -1),
        jnp.concatenate([sine_table, -sine_table], -1),
    )


def wait_for(ref, sem):
    pltpu.make_async_copy(ref, ref, sem).wait()


def places():
    gx, devices = lax.axis_index("gx"), lax.axis_size("gx")
    chips = devices // 2
    chip, core = gx // 2, lax.rem(gx, 2)
    partner = gx + 1 - 2 * core
    others = [lax.rem(chip + k, chips) * 2 + core for k in range(1, chips)]
    return partner, others


def square():
    gx = lax.axis_index("gx")
    chip, core = gx // 2, lax.rem(gx, 2)
    side = gx + 2 - 4 * lax.rem(chip, 2)
    along = gx + 4 - 8 * (chip // 2)
    return side, along, (3 - chip) * 2 + core


def spread_slots():
    chips = lax.axis_size("gx") // 2
    return 14 if chips == 4 else 2 * chips + 2 * (chips - 1)


def spread_scratch(count):
    devices = lax.axis_size("gx")
    return [
        pltpu.SemaphoreType.DMA((count,)),
        pltpu.SemaphoreType.DMA((count, spread_slots())),
        pltpu.SemaphoreType.DMA((count, devices, 2)),
    ]


def greet(gx_peers, gy_peers):
    gx, gy = lax.axis_index("gx"), lax.axis_index("gy")
    barrier = pltpu.get_barrier_semaphore()
    for peer in gx_peers:
        pl.semaphore_signal(barrier, inc=1, device_id=(peer, gy), device_id_type=MESH)
    for peer in gy_peers:
        pl.semaphore_signal(barrier, inc=1, device_id=(gx, peer), device_id_type=MESH)
    pl.semaphore_wait(barrier, len(gx_peers) + len(gy_peers))


class Spread:
    def __init__(self, items, sems):
        self.items, (self.local, self.send_sem, self.recv_sem) = items, sems
        self.partner, self.others = places()
        self.four = lax.axis_size("gx") // 2 == 4
        self.near = list(square()[:2]) if self.four else self.others

    def part(self, i, k, h):
        full = self.items[i][1]
        if len(full.shape) == 4:
            half = full.shape[0] // 2
            return full.at[pl.ds(h * half, half), k]
        half = full.shape[1] // 2
        return full.at[k, pl.ds(h * half, half)]

    def send(self, i, k, h, target, slot, first=False):
        here = self.part(i, k, h)
        half = here.shape[0]
        source = self.items[i][0].at[pl.ds(h * half, half)] if first else here
        pltpu.make_async_remote_copy(
            src_ref=source,
            dst_ref=here,
            send_sem=self.send_sem.at[i, slot],
            recv_sem=self.recv_sem.at[i, k, h],
            device_id=(target, lax.axis_index("gy")),
            device_id_type=MESH,
        ).start()

    def arrived(self, i, k, h):
        wait_for(self.part(i, k, h), self.recv_sem.at[i, k, h])

    def place(self, i):
        own, full = self.items[i]
        gx = lax.axis_index("gx")
        here = full.at[:, gx] if len(full.shape) == 4 else full.at[gx]
        return pltpu.make_async_copy(own, here, self.local.at[i])

    def begin(self, i):
        gx = lax.axis_index("gx")
        self.place(i).start()
        slot = 0
        for target in self.near + [self.partner]:
            for h in range(2):
                self.send(i, gx, h, target, slot, True)
                slot += 1

    def relay(self, i):
        slot = 2 * len(self.near) + 2
        if self.four:
            side, along, _ = square()
            steps = [(side, 0, along), (along, 1, side), (side, 1, None), (along, 0, None)]
        else:
            steps = [(k, h, None) for k in self.others for h in range(2)]
        for k, h, target in steps:
            self.arrived(i, k, h)
            for to in [self.partner] if target is None else [target, self.partner]:
                self.send(i, k, h, to, slot)
                slot += 1

    def finish(self, i):
        if self.four:
            for h in range(2):
                self.arrived(i, square()[2], h)
                self.send(i, square()[2], h, self.partner, 12 + h)

    def close(self, i):
        core = lax.rem(lax.axis_index("gx"), 2)
        for k in [self.partner] + [k + 1 - 2 * core for k in self.others]:
            for h in range(2):
                self.arrived(i, k, h)
        for slot in range(spread_slots()):
            wait_for(self.part(i, 0, 0), self.send_sem.at[i, slot])
        self.place(i).wait()


def line_order(t, me, last):
    short = jnp.minimum(me, last - me)
    near = jnp.where(lax.rem(t, 2) == 0, me - t // 2, me + (t + 1) // 2)
    far = jnp.where(me < last - me, me + (t - short), me - (t - short))
    return jnp.where(t <= 2 * short, near, far)


class Chain:
    def __init__(self, own, full, sems):
        self.own, self.full, (self.local, self.send_sem, self.recv_sem) = own, full, sems

    def copy(self, b, way, first=False):
        me = lax.axis_index("gy")
        return pltpu.make_async_remote_copy(
            src_ref=self.own if first else self.full.at[b],
            dst_ref=self.full.at[b],
            send_sem=self.send_sem.at[b, way],
            recv_sem=self.recv_sem.at[b],
            device_id=(lax.axis_index("gx"), me - 1 + 2 * way),
            device_id_type=MESH,
        )

    def each(self, b, act, first=False):
        me, last = lax.axis_index("gy"), lax.axis_size("gy") - 1

        @pl.when(jnp.logical_and(b <= me, me < last))
        def _():
            act(self.copy(b, 1, first))

        @pl.when(jnp.logical_and(b >= me, me > 0))
        def _():
            act(self.copy(b, 0, first))

    def begin(self):
        me = lax.axis_index("gy")
        self.place = pltpu.make_async_copy(self.own, self.full.at[me], self.local)
        self.place.start()
        self.each(me, lambda copy: copy.start(), True)

    def relay(self, t):
        b = line_order(t, lax.axis_index("gy"), lax.axis_size("gy") - 1)
        wait_for(self.full.at[b], self.recv_sem.at[b])
        self.each(b, lambda copy: copy.start())

    def close(self):
        self.place.wait()
        for b in range(lax.axis_size("gy")):
            self.each(b, lambda copy: copy.wait_send())


class Exchange:
    def __init__(self, own, full, sems, apart=False):
        self.own, self.full, (self.local, self.send_sem, self.recv_sem) = own, full, sems
        self.apart = apart

    def begin(self):
        gx, me, size = lax.axis_index("gx"), lax.axis_index("gy"), lax.axis_size("gy")
        width = self.full.shape[2]

        def columns(k):
            if self.apart:
                return self.own.at[k]
            return self.own.at[:, pl.ds(pl.multiple_of(k * width, width), width)]

        self.place = pltpu.make_async_copy(columns(me), self.full.at[me], self.local)
        self.place.start()
        self.sent = []
        for d in range(1, size):
            target = lax.rem(me + d, size)
            copy = pltpu.make_async_remote_copy(
                src_ref=columns(target),
                dst_ref=self.full.at[me],
                send_sem=self.send_sem.at[d],
                recv_sem=self.recv_sem.at[me],
                device_id=(gx, target),
                device_id_type=MESH,
            )
            copy.start()
            self.sent.append(copy)

    def close(self):
        me, size = lax.axis_index("gy"), lax.axis_size("gy")
        self.place.wait()
        for copy in self.sent:
            copy.wait_send()
        for d in range(1, size):
            k = lax.rem(me + d, size)
            wait_for(self.full.at[k], self.recv_sem.at[k])


def chain_scratch():
    size = lax.axis_size("gy")
    return [
        pltpu.SemaphoreType.DMA,
        pltpu.SemaphoreType.DMA((size, 2)),
        pltpu.SemaphoreType.DMA((size,)),
    ]


def exchange_scratch():
    size = lax.axis_size("gy")
    return [
        pltpu.SemaphoreType.DMA,
        pltpu.SemaphoreType.DMA((size,)),
        pltpu.SemaphoreType.DMA((size,)),
    ]


def opening_kernel(*refs):
    ins, outs, sems = refs[:9], refs[9:20], refs[20:]
    resid, cot, small, qkv_a, o_a, qkv_b, o_b, wg, wu = ins
    resid_out, cot_out, small_out = outs[:3]
    lines, (qkv, o, gate, up) = outs[3:7], outs[7:]
    me, size = lax.axis_index("gy"), lax.axis_size("gy")
    owns = (qkv_a, o_a, qkv_b, o_b, small)
    chains = [
        Chain(own, full, sems[3 * k : 3 * k + 3])
        for k, (own, full) in enumerate(zip(owns, list(lines) + [small_out]))
    ]
    swaps = [
        Exchange(own, full, sems[15 + 3 * k : 18 + 3 * k])
        for k, (own, full) in enumerate(((resid, resid_out), (cot, cot_out)))
    ]
    items = [(lines[0], qkv), (lines[1], o), (wg.at[0], gate), (wu.at[0], up)]
    spread = Spread(items, sems[21:24])
    greet([spread.partner] + spread.near, [lax.rem(me + d, size) for d in range(1, size)])
    for k in (0, 1, 4):
        chains[k].begin()
    spread.begin(2)
    for t in range(1, size):
        chains[0].relay(t)
        chains[1].relay(t)
    chains[0].close()
    spread.begin(0)
    chains[1].close()
    spread.begin(1)
    swaps[0].begin()
    for t in range(1, size):
        chains[4].relay(t)
    spread.relay(2)
    spread.begin(3)
    chains[2].begin()
    chains[3].begin()
    for i in (0, 1):
        spread.relay(i)
    swaps[1].begin()
    for t in range(1, size):
        chains[2].relay(t)
        chains[3].relay(t)
    spread.finish(2)
    for i in (0, 1):
        spread.finish(i)
    spread.relay(3)
    spread.finish(3)
    for i in range(4):
        spread.close(i)
    for part in chains[2:] + swaps:
        part.close()


def opening(resid, cot, small, lines, wg, wu):
    devices, size = lax.axis_size("gx"), lax.axis_size("gy")
    count = resid.shape[1] // size

    def shape(*dims, kind=bf16):
        return jax.ShapeDtypeStruct(dims, kind)

    blocks = shape(size, resid.shape[0], count)
    weight = shape(devices, *wg.shape[1:])
    out = [blocks, blocks, shape(size, *small.shape, kind=f32)]
    out += [shape(size, *line.shape) for line in lines]
    out += [shape(size, devices, *line.shape) for line in lines[:2]] + [weight] * 2
    return pl.pallas_call(
        opening_kernel,
        out_shape=out,
        in_specs=[ANY] * 9,
        out_specs=[ANY] * 11,
        scratch_shapes=chain_scratch() * 5 + exchange_scratch() * 2 + spread_scratch(4),
        compiler_params=pltpu.CompilerParams(collective_id=2, has_side_effects=True),
        name="opening",
    )(resid, cot, small, *lines, wg, wu)


FF_CHUNK = 512
PIECES = 4


def spans(total):
    return [(start, min(FF_CHUNK, total - start)) for start in range(0, total, FF_CHUNK)]


def nn(left, right):
    return lax.dot_general(left, right, (((1,), (0,)), ((), ())), preferred_element_type=f32)


def nt(left, right):
    return lax.dot_general(left, right, (((1,), (1,)), ((), ())), preferred_element_type=f32)


def line_pass(own_ref, own, gathered, part, outb, inb, sems, load, finish, peers=(), plan={}):
    own_sem, ag_send, ag_recv, rs_send, rs_recv = sems
    gx, me, size = lax.axis_index("gx"), lax.axis_index("gy"), lax.axis_size("gy")
    rows = own.shape[0]
    piece = rows // PIECES
    last = size - 1
    inner = jnp.logical_and(me > 0, me < last)

    first = pltpu.make_async_copy(own_ref, gathered.at[me], own_sem)
    first.start()
    barrier = pltpu.get_barrier_semaphore()

    @pl.when(me > 0)
    def _():
        pl.semaphore_signal(barrier, inc=1, device_id=(gx, me - 1), device_id_type=MESH)

    @pl.when(me < last)
    def _():
        pl.semaphore_signal(barrier, inc=1, device_id=(gx, me + 1), device_id_type=MESH)

    for peer in peers:
        pl.semaphore_signal(barrier, inc=1, device_id=(peer, me), device_id_type=MESH)
    pl.semaphore_wait(barrier, jnp.where(inner, 2, 1) + len(peers))
    first.wait()

    def planned(name, t):
        for (key, when), act in plan.items():
            if key == name:
                pl.when(t == when)(act)


    def gather_copy(b, s, way):
        here = gathered.at[b, pl.ds(s * piece, piece)]
        return pltpu.make_async_remote_copy(
            src_ref=here,
            dst_ref=here,
            send_sem=ag_send.at[b, way, s],
            recv_sem=ag_recv.at[b, s],
            device_id=(gx, me - 1 + 2 * way),
            device_id_type=MESH,
        )

    def sum_copy(b, s):
        towards = jnp.where(b > me, me + 1, me - 1)
        slot = jnp.where(jnp.logical_and(towards == b, me > b), size, b)
        return pltpu.make_async_remote_copy(
            src_ref=outb.at[b, pl.ds(s * piece, piece)],
            dst_ref=inb.at[slot, pl.ds(s * piece, piece)],
            send_sem=rs_send.at[b, s],
            recv_sem=rs_recv.at[slot, s],
            device_id=(gx, towards),
            device_id_type=MESH,
        )

    def sum_arrived(slot, s):
        here = inb.at[slot, pl.ds(s * piece, piece)]
        pltpu.make_async_copy(here, here, rs_recv.at[slot, s]).wait()

    def step(t, carry):
        b = line_order(t, me, last)
        for s in range(PIECES):

            @pl.when(t > 0)
            def _():
                gather_copy(b, s, 0).wait_recv()

            @pl.when(jnp.logical_and(b <= me, me < last))
            def _():
                gather_copy(b, s, 1).start()

            @pl.when(jnp.logical_and(b >= me, me > 0))
            def _():
                gather_copy(b, s, 0).start()

        @pl.when(t == 0)
        def _():
            load()

        planned("step", t)
        finish(b)

        @pl.when(b == me)
        def _():
            own[...] = part[...]

        @pl.when(b != me)
        def _():
            outb[b] = part[...].astype(bf16)

            @pl.when(jnp.logical_not(inner))
            def _():
                for s in range(PIECES):
                    sum_copy(b, s).start()

        return carry

    lax.fori_loop(0, size, step, 0)

    def relay(t, carry):
        above, below = last - me, me
        low = jnp.where(t < above, me + 1 + t, me - 1 - (t - above))
        high = jnp.where(t < below, me - 1 - t, me + 1 + (t - below))
        b = jnp.where(2 * me < size, low, high)
        planned("hop", t)

        @pl.when(inner)
        def _():
            for s in range(PIECES):
                at = pl.ds(s * piece, piece)
                sum_arrived(b, s)
                outb[b, at] = (outb[b, at].astype(f32) + inb[b, at].astype(f32)).astype(bf16)
                sum_copy(b, s).start()

        return carry

    lax.fori_loop(0, last, relay, 0)

    @pl.when(me > 0)
    def _():
        for s in range(PIECES):
            sum_arrived(me, s)
        own[...] += inb[me].astype(f32)

    @pl.when(me < last)
    def _():
        for s in range(PIECES):
            sum_arrived(size, s)
        own[...] += inb[size].astype(f32)

    def drain(b, carry):
        for s in range(PIECES):

            @pl.when(jnp.logical_and(b <= me, me < last))
            def _():
                gather_copy(b, s, 1).wait_send()

            @pl.when(jnp.logical_and(b >= me, me > 0))
            def _():
                gather_copy(b, s, 0).wait_send()

            @pl.when(b != me)
            def _():
                sum_copy(b, s).wait_send()

        return carry

    lax.fori_loop(0, size, drain, 0)


def line_scratch(size, rows, width):
    return [
        pltpu.VMEM((size, rows, width), bf16),
        pltpu.VMEM((rows, width), f32),
        pltpu.VMEM((size, rows, width), bf16),
        pltpu.VMEM((size + 1, rows, width), bf16),
        pltpu.SemaphoreType.DMA,
        pltpu.SemaphoreType.DMA((size, 2, PIECES)),
        pltpu.SemaphoreType.DMA((size, PIECES)),
        pltpu.SemaphoreType.DMA((size, PIECES)),
        pltpu.SemaphoreType.DMA((size + 1, PIECES)),
    ]


LINE = 9


ORDER = {
    ("step", 0): (("begin", 0), ("begin", 1)),
    ("step", 2): (("begin", 2),),
    ("hop", 0): (("relay", 0), ("relay", 1), ("relay", 2), ("begin", 3)),
    ("hop", 1): (("finish", 0), ("finish", 1), ("finish", 2)),
}
REST = (("relay", 3), ("finish", 3))


def schedule(spread):
    def run(steps):
        def act():
            for verb, i in steps:
                getattr(spread, verb)(i)

        return act

    plan = {key: run(steps) for key, steps in ORDER.items()}
    return plan, REST + tuple(("close", i) for i in range(len(spread.items)))


def forward_kernel(extra, *refs):
    acts_ref, wg_ref, wu_ref, wd_ref = refs[:4]
    shards, refs = refs[4 : 4 + extra], refs[4 + extra :]
    sum_ref, turned_ref, gate_ref, up_ref, hidden_ref = refs[:5]
    wholes, scratch = refs[5 : 5 + extra], refs[5 + extra :]
    gathered, part, outb, inb = scratch[:4]
    sems = scratch[4:LINE]
    wg, wu, wd, gate, up, hidden, turned, w_sem, out_sem = scratch[LINE : LINE + 9]
    peers, spread = [], None
    if extra:
        items = [(r if len(w.shape) == 4 else r.at[1], w) for r, w in zip(shards, wholes)]
        spread = Spread(items, scratch[LINE + 9 :])
        partner, others = places()
        peers = [partner] + (list(square()[:2]) if spread.four else others)

    plan, rest = schedule(spread) if extra else ({}, ())
    loads = [
        pltpu.make_async_copy(src, dst, w_sem.at[k])
        for k, (src, dst) in enumerate(((wg_ref, wg), (wu_ref, wu), (wd_ref, wd)))
    ]
    for copy in loads:
        copy.start()

    def load():
        for copy in loads:
            copy.wait()

    def results(b):
        pairs = ((gate, gate_ref), (up, up_ref), (hidden, hidden_ref))
        return [
            pltpu.make_async_copy(src.at[b], dst.at[b], out_sem.at[b, k])
            for k, (src, dst) in enumerate(pairs)
        ]

    def finish(b):
        block = gathered[b]
        store_turned(block, turned, b)
        for start, width in spans(wg.shape[1]):
            at = slice(start, start + width)
            g = nn(block, wg[:, at])
            u = nn(block, wu[:, at])
            h = (g * lax.logistic(g) * u).astype(bf16)
            gate[b, :, at] = g.astype(bf16)
            up[b, :, at] = u.astype(bf16)
            hidden[b, :, at] = h
            p = nt(h, wd[:, at])
            if start == 0:
                part[...] = p
            else:
                part[...] += p
        for copy in results(b):
            copy.start()

    line_pass(
        acts_ref, sum_ref, gathered, part, outb, inb, sems, load, finish, peers, plan
    )
    keep = pltpu.make_async_copy(turned, turned_ref, w_sem.at[0])
    keep.start()
    for act, i in rest:
        getattr(spread, act)(i)

    def settle(b, carry):
        for copy in results(b):
            copy.wait()
        return carry

    lax.fori_loop(0, gathered.shape[0], settle, 0)
    keep.wait()


def forward_ffn(acts, wg, wu, wd, shards=()):
    rows, width = acts.shape
    devices, size, hidden = lax.axis_size("gx"), lax.axis_size("gy"), wg.shape[1]
    wide = jax.ShapeDtypeStruct((size, rows, hidden), bf16)
    extra = len(shards)
    wholes = [
        jax.ShapeDtypeStruct(
            (size, devices) + s.shape[1:] if k < 2 else (devices,) + s.shape[1:], bf16
        )
        for k, s in enumerate(shards)
    ]
    return pl.pallas_call(
        functools.partial(forward_kernel, extra),
        out_shape=[
            jax.ShapeDtypeStruct((rows, width), f32),
            jax.ShapeDtypeStruct((2, width // 2, size * rows), bf16),
            wide,
            wide,
            wide,
        ]
        + wholes,
        in_specs=[ANY] * (4 + extra),
        out_specs=[pl.BlockSpec(memory_space=pltpu.VMEM)] + [ANY] * (4 + extra),
        scratch_shapes=line_scratch(size, rows, width)
        + [pltpu.VMEM((width, hidden), bf16)] * 3
        + [pltpu.VMEM((size, rows, hidden), bf16)] * 3
        + [pltpu.VMEM((2, width // 2, size * rows), bf16)]
        + [pltpu.SemaphoreType.DMA((3,)), pltpu.SemaphoreType.DMA((size, 3))]
        + (spread_scratch(extra) if extra else []),
        compiler_params=pltpu.CompilerParams(
            collective_id=3 if extra else 0, has_side_effects=True, vmem_limit_bytes=VMEM_LIMIT
        ),
        cost_estimate=pl.CostEstimate(
            flops=6 * size * rows * width * hidden, bytes_accessed=40 << 20, transcendentals=0
        ),
        name="ffn_forward",
    )(acts, wg, wu, wd, *shards)


def put_rows(totals, out, row, fbuf, ftail, sems, lanes):
    stores, edge, wide = [], 0, 0
    for j, make in enumerate(totals):
        total = make()
        part, width = total.shape
        full = width == FF_CHUNK
        wide += full
        if full and j >= 2:
            stores[j - 2].wait()
        stage = fbuf.at[pl.ds((j % 2) * part, part)] if full else ftail.at[pl.ds(0, part)]
        stage[...] = total
        store = pltpu.make_async_copy(
            stage,
            out.at[pl.ds(row, part), edge : edge + width],
            sems.at[lanes[j % 2 if full else 2]],
        )
        store.start()
        stores.append(store)
        edge += width
    for store in stores[max(wide - 2, 0) :]:
        store.wait()


class Reduce:
    def __init__(self, lhs, rhs, bufs, abuf, fbuf, ftail, a_all, r_all, c_all, outs, late, sems):
        self.late = late
        self.lhs, self.rhs, self.bufs, self.outs = lhs, rhs, bufs, outs
        self.abuf, self.fbuf, self.ftail = abuf, fbuf, ftail
        self.a_all, self.r_all, self.c_all = a_all, r_all, c_all
        (
            self.a_send,
            self.a_recv,
            self.r_send,
            self.r_recv,
            self.c_send,
            self.c_recv,
            self.local,
        ) = sems
        gx, self.gy = lax.axis_index("gx"), lax.axis_index("gy")
        self.chip, self.core = gx // 2, lax.rem(gx, 2)
        self.chips = lax.axis_size("gx") // 2
        self.half, self.wide = bufs[0].shape[0] // 2, bufs[0].shape[1]
        self.r = self.half // self.chips
        self.four = self.chips == 4
        self.partner, self.others = places()
        self.near = list(square()[:2]) if self.four else self.others

    def product(self, m, which, at):
        z, n, _ = self.rhs[m].shape
        right = self.rhs[m][:, :, at].reshape(z * n, at.stop - at.start)
        return nn(self.lhs[which], right)

    def remote(self, src, dst, send, recv, target):
        return pltpu.make_async_remote_copy(
            src_ref=src,
            dst_ref=dst,
            send_sem=send,
            recv_sem=recv,
            device_id=(target, self.gy),
            device_id_type=MESH,
        )

    def columns(self):
        return [(j, slice(s, s + w)) for j, (s, w) in enumerate(spans(self.wide))]

    def swap(self, m, j, at):
        here = (slice(0, self.half), at)
        return self.remote(
            self.bufs[m].at[here],
            self.a_all.at[m, :, at],
            self.a_send.at[m, j],
            self.a_recv.at[m, j],
            self.partner,
        )

    def block(self, m, device, start=0, size=None):
        size = self.r if size is None else size
        first = self.half + (device // 2) * self.r + start
        return self.bufs[m].at[pl.ds(pl.multiple_of(first, 16), size)]

    def first(self, m):
        for j, at in self.columns():
            self.bufs[m][: self.half, at] = self.product(m, 1 - self.core, at).astype(bf16)
            self.swap(m, j, at).start()

    def corner(self, m, h):
        side, along, across = square()
        half = self.r // 2
        return self.remote(
            self.block(m, across, h * half, half),
            self.r_all.at[m, h],
            self.r_send.at[m, h],
            self.r_recv.at[m, h],
            along if h else side,
        )

    def second(self, m):
        for j, at in self.columns():
            self.swap(m, j, at).wait_recv()
            landed = self.abuf.at[:, at]
            fetch = pltpu.make_async_copy(self.a_all.at[m, :, at], landed, self.local.at[0])
            fetch.start()
            mine = self.product(m, self.core, at)
            fetch.wait()
            self.bufs[m][self.half :, at] = (mine + landed[...].astype(f32)).astype(bf16)
        if m in self.late:
            self.keep(m).start()
        elif self.four:
            for h in range(2):
                self.corner(m, h).start()

    def keep(self, m):
        kept = self.outs[m].at[0]
        return pltpu.make_async_copy(
            self.bufs[m].at[pl.ds(self.half, self.half)], kept, self.local.at[max(len(self.near), 2)]
        )

    def hand(self, m, k):
        target = self.near[k]
        return self.remote(
            self.block(m, target),
            self.c_all.at[m, k],
            self.c_send.at[m, k],
            self.c_recv.at[m, k],
            target,
        )

    def third(self, m):
        if self.four:
            side, along, _ = square()
            half = self.r // 2
            for h, device in ((0, along), (1, side)):
                self.corner(m, h).wait_recv()
                here = self.block(m, device, h * half, half)
                landed = self.abuf.at[h * half : (h + 1) * half]
                fetch = pltpu.make_async_copy(self.r_all.at[m, h], landed, self.local.at[0])
                fetch.start()
                fetch.wait()
                here[...] = (here[...].astype(f32) + landed[...].astype(f32)).astype(bf16)
        for k in range(len(self.near)):
            self.hand(m, k).start()

    def fourth(self, m):
        for j, at in self.columns():
            self.swap(m, j, at).wait_send()
        fetches = []
        for k in range(len(self.near)):
            self.hand(m, k).wait_recv()
            here = self.bufs[m].at[pl.ds(k * self.r, self.r)]
            fetch = pltpu.make_async_copy(self.c_all.at[m, k], here, self.local.at[k])
            fetch.start()
            fetches.append(fetch)
        for fetch in fetches:
            fetch.wait()
        part = self.r // 2
        for h in range(2):
            first = pl.multiple_of(self.half + self.chip * self.r + h * part, 16)
            totals = []
            for _, at in self.columns():

                def make(at=at, first=first, h=h):
                    total = self.bufs[m][pl.ds(first, part), at].astype(f32)
                    for k in range(len(self.near)):
                        start = k * self.r + h * part
                        total = total + self.bufs[m][start : start + part, at].astype(f32)
                    return total

                totals.append(make)
            lanes = (0, 1, max(len(self.near), 2) + 1)
            put_rows(totals, self.outs[m], h * part, self.fbuf, self.ftail, self.local, lanes)

    def drain(self, m):
        if self.four:
            for h in range(2):
                self.corner(m, h).wait_send()
        for k in range(len(self.near)):
            self.hand(m, k).wait_send()


def reduce_scratch(width, hidden, count=3):
    devices = lax.axis_size("gx")
    rows, parts = width // devices, len(spans(hidden))
    near = 2 if devices == 8 else devices // 2 - 1
    dma = pltpu.SemaphoreType.DMA
    return [
        pltpu.VMEM((width // 2, hidden), bf16),
        pltpu.VMEM((rows, FF_CHUNK), f32),
        pltpu.VMEM((rows, hidden % FF_CHUNK), f32),
        dma((count, parts)),
        dma((count, parts)),
        dma((count, 2)),
        dma((count, 2)),
        dma((count, near)),
        dma((count, near)),
        dma((max(near, 2) + 2,)),
    ]


class Tail:
    def __init__(self, b_all, r_all, c_all, outs, abuf, fbuf, ftail, sems, direct=False):
        self.direct = direct
        self.b_all, self.r_all, self.c_all, self.outs = b_all, r_all, c_all, outs
        self.abuf, self.fbuf, self.ftail = abuf, fbuf, ftail
        self.r_send, self.r_recv, self.c_send, self.c_recv, self.local = sems
        gx, self.gy = lax.axis_index("gx"), lax.axis_index("gy")
        self.chip, chips = gx // 2, lax.axis_size("gx") // 2
        self.r = b_all.shape[1] // chips
        self.part = self.r // 2
        self.space = b_all.shape[1] // b_all.shape[0]
        self.four = chips == 4
        self.near = list(square()[:2]) if self.four else places()[1]

    def remote(self, src, dst, send, recv, target):
        return pltpu.make_async_remote_copy(
            src_ref=src,
            dst_ref=dst,
            send_sem=send,
            recv_sem=recv,
            device_id=(target, self.gy),
            device_id_type=MESH,
        )

    def held(self, i, chip, h):
        first = pl.multiple_of(chip * self.r + h * self.part, 16)
        return self.b_all.at[i, pl.ds(first, self.part)]

    def slot(self, i, k):
        return self.abuf.at[pl.ds(i * self.space + k * self.part, self.part)]

    def corner(self, i, h):
        side, along, across = square()
        return self.remote(
            self.held(i, across // 2, h),
            self.r_all.at[i, h],
            self.r_send.at[i, h],
            self.r_recv.at[i, h],
            along if h else side,
        )

    def hand(self, i, k, h):
        target = self.near[k]
        summed = self.four and k != h
        return self.remote(
            self.slot(i, 2 + h) if summed else self.held(i, target // 2, h),
            self.c_all.at[i, k, h],
            self.c_send.at[i, k, h],
            self.c_recv.at[i, k, h],
            target,
        )

    def hands(self):
        return [(k, h) for k in range(len(self.near)) for h in range(2)]

    def begin(self, i):
        if self.four:
            for h in range(2):
                self.corner(i, h).start()

    def middle(self, i):
        if self.four:
            side, along, _ = square()
            for h, device in ((0, along), (1, side)):
                self.corner(i, h).wait_recv()
                came, mine = self.slot(i, h), self.slot(i, 2 + h)
                fetches = [
                    pltpu.make_async_copy(self.r_all.at[i, h], came, self.local.at[0]),
                    pltpu.make_async_copy(self.held(i, device // 2, h), mine, self.local.at[1]),
                ]
                for fetch in fetches:
                    fetch.start()
                for fetch in fetches:
                    fetch.wait()
                mine[...] = (mine[...].astype(f32) + came[...].astype(f32)).astype(bf16)
        for k, h in self.hands():
            self.hand(i, k, h).start()

    def close(self, i):
        if self.four:
            for h in range(2):
                self.corner(i, h).wait_send()
        for k, h in self.hands():
            self.hand(i, k, h).wait_send()
        count = len(self.near)
        for h in range(2):
            fetches = [
                pltpu.make_async_copy(
                    self.held(i, self.chip, h), self.slot(i, count), self.local.at[count]
                )
            ]
            for k in range(count):
                self.hand(i, k, h).wait_recv()
                fetches.append(
                    pltpu.make_async_copy(
                        self.c_all.at[i, k, h], self.slot(i, k), self.local.at[k]
                    )
                )
            for fetch in fetches:
                fetch.start()
            for fetch in fetches:
                fetch.wait()
            totals = []
            for start, width in spans(self.abuf.shape[1]):
                at = slice(start, start + width)

                def make(at=at):
                    total = self.slot(i, 0)[:, at].astype(f32)
                    for k in range(1, count + 1):
                        total = total + self.slot(i, k)[:, at].astype(f32)
                    return total

                if self.direct:
                    self.outs[i][h * self.part : (h + 1) * self.part, at] = make()
                else:
                    totals.append(make)
            put_rows(
                totals, self.outs[i], h * self.part, self.fbuf, self.ftail, self.local, (0, 1, 2)
            )


def tail_scratch(count):
    devices = lax.axis_size("gx")
    near = 2 if devices == 8 else devices // 2 - 1
    dma = pltpu.SemaphoreType.DMA
    return [
        dma((count, 2)),
        dma((count, 2)),
        dma((count, near, 2)),
        dma((count, near, 2)),
        dma((near + 1,)),
    ]


def store_turned(block, turned, b):
    count, width = block.shape
    _, chips_rows, _ = turned.shape
    devices = lax.axis_size("gx")
    r = width // devices
    flipped = block.T
    at = pl.ds(pl.multiple_of(b * count, count), count)
    for k in range(devices):
        q = k // 2
        turned[k % 2, q * r : (q + 1) * r, at] = flipped[k * r : (k + 1) * r]


AFTER = {
    0: (("first", 0),),
    1: (("second", 0), ("swap", 0), ("first", 1)),
    2: (("third", 0), ("second", 1)),
}
ENDS = {
    (1, 2): (
        ("kept", 1),
        ("first", 2),
        ("second", 2),
        ("fourth", 0),
        ("kept", 2),
        ("sent", 1),
        ("sent", 2),
        ("drain", 0),
    ),
    (2,): (
        ("first", 2),
        ("third", 1),
        ("second", 2),
        ("fourth", 0),
        ("kept", 2),
        ("fourth", 1),
        ("sent", 2),
        ("drain", 0),
        ("drain", 1),
    ),
}
TAIL_BEGIN, TAIL_MIDDLE = ("step", 0), ("step", 2)


def both(one, other):
    def act():
        one()
        other()

    return act


def backward_kernel(late, tails, *refs):
    grad_ref, gate_ref, up_ref, hidden_ref, turned_ref, wg_ref, wu_ref, wd_ref = refs[:8]
    held, refs = refs[8 : 8 + (tails > 0)], refs[8 + (tails > 0) :]
    sum_ref, refs = refs[0], refs[1:]
    outs, (a_all, r_all, c_all), refs = refs[:3], refs[3:6], refs[6:]
    tail_refs, scratch = refs[: tails + 2 * (tails > 0)], refs[tails + 2 * (tails > 0) :]
    gathered, part, outb, inb = scratch[:4]
    sems = scratch[4:LINE]
    wg, wu, wd, gate, up, hidden, turned, w_sem = scratch[LINE : LINE + 8]
    abuf, fbuf, ftail = scratch[LINE + 8 : LINE + 11]
    operands = (
        (wd_ref, wd),
        (gate_ref, gate),
        (up_ref, up),
        (wg_ref, wg),
        (wu_ref, wu),
        (hidden_ref, hidden),
    )
    loads = [
        pltpu.make_async_copy(src, dst, w_sem.at[k]) for k, (src, dst) in enumerate(operands)
    ]
    for copy in loads:
        copy.start()

    def load():
        for copy in loads:
            copy.wait()

    reduce = Reduce(
        turned,
        (hidden, gate, up),
        (wd, wg, wu),
        abuf,
        fbuf,
        ftail,
        a_all,
        r_all,
        c_all,
        outs,
        late,
        scratch[LINE + 11 : LINE + 18],
    )
    tail = None
    if tails:
        tail = Tail(
            held[0],
            tail_refs[tails],
            tail_refs[tails + 1],
            tail_refs[:tails],
            abuf,
            fbuf,
            ftail,
            scratch[LINE + 18 :],
        )

    def finish(b):
        block = gathered[b]
        store_turned(block, turned, b)
        for start, width in spans(wg.shape[1]):
            at = slice(start, start + width)
            d = nn(block, wd[:, at])
            g = gate[b, :, at].astype(f32)
            u = up[b, :, at].astype(f32)
            sigma = lax.logistic(g)
            ds = d * sigma
            dg = (ds * u * (1.0 + g * (1.0 - sigma))).astype(bf16)
            du = (ds * g).astype(bf16)
            gate[b, :, at] = dg
            up[b, :, at] = du
            p = nt(dg, wg[:, at]) + nt(du, wu[:, at])
            if start == 0:
                part[...] = p
            else:
                part[...] += p

    def run(verb, m):
        if verb == "swap":
            copy = pltpu.make_async_copy(turned_ref, turned, w_sem.at[0])
            copy.start()
            copy.wait()
        elif verb == "kept":
            reduce.keep(m).wait()
        elif verb == "sent":
            for j, at in reduce.columns():
                reduce.swap(m, j, at).wait_send()
        else:
            getattr(reduce, verb)(m)

    def work(t):
        def act():
            if tail is not None and t == 1:
                for i in range(tails):
                    tail.close(i)
            for verb, m in AFTER[t]:
                run(verb, m)

        return act

    def each(verb):
        def act():
            for i in range(tails):
                getattr(tail, verb)(i)

        return act

    peers = [reduce.partner] + reduce.near
    plan = {("hop", t): work(t) for t in range(3)}
    if tails:
        for key, act in ((TAIL_BEGIN, each("begin")), (TAIL_MIDDLE, each("middle"))):
            old = plan.get(key)
            plan[key] = act if old is None else both(act, old)
    line_pass(grad_ref, sum_ref, gathered, part, outb, inb, sems, load, finish, peers, plan)
    for verb, m in ENDS[late]:
        run(verb, m)


def backward_ffn(grad, gate, up, hidden, turned, wg, wu, wd, late, held=None):
    rows, width = grad.shape
    devices, size, wide = lax.axis_size("gx"), lax.axis_size("gy"), wg.shape[1]
    near = 2 if devices == 8 else devices // 2 - 1
    r = width // devices
    mine = jax.ShapeDtypeStruct((r, wide), f32)

    def between(*dims):
        return jax.ShapeDtypeStruct(dims + (wide,), bf16)

    count = 3 - len(late)
    out = [jax.ShapeDtypeStruct((rows, width), f32)]
    out += [between(1, width // 2) if m in late else mine for m in range(3)]
    out += [between(3, width // 2), between(count, 2, r // 2), between(count, near, r)]
    tails = 0 if held is None else held.shape[0]
    if tails:
        out += [mine] * tails
        out += [between(tails, 2, r // 2), between(tails, near, 2, r // 2)]
    extra = [held] if tails else []
    return pl.pallas_call(
        functools.partial(backward_kernel, late, tails),
        out_shape=out,
        in_specs=[ANY] * (8 + len(extra)),
        out_specs=[pl.BlockSpec(memory_space=pltpu.VMEM)] + [ANY] * (len(out) - 1),
        scratch_shapes=line_scratch(size, rows, width)
        + [pltpu.VMEM((width, wide), bf16)] * 3
        + [pltpu.VMEM((size, rows, wide), bf16)] * 3
        + [pltpu.VMEM((2, width // 2, size * rows), bf16), pltpu.SemaphoreType.DMA((6,))]
        + reduce_scratch(width, wide)
        + (tail_scratch(tails) if tails else []),
        compiler_params=pltpu.CompilerParams(
            collective_id=1 if held is None else 5, has_side_effects=True, vmem_limit_bytes=VMEM_LIMIT
        ),
        cost_estimate=pl.CostEstimate(
            flops=12 * size * rows * width * wide, bytes_accessed=40 << 20, transcendentals=0
        ),
        name="ffn_backward",
    )(grad, gate, up, hidden, turned, wg, wu, wd, *extra)


class Fold:
    def __init__(self, lhs, rhs, bufs, sems):
        self.lhs, self.rhs = lhs, rhs
        self.up, self.low, self.a_in, self.r_in, self.c_in, self.z_out, self.z_in = bufs
        (
            self.a_send,
            self.a_recv,
            self.r_send,
            self.r_recv,
            self.c_send,
            self.c_recv,
            self.z_send,
            self.z_recv,
        ) = sems
        self.gx, self.gy = lax.axis_index("gx"), lax.axis_index("gy")
        self.core, self.size = lax.rem(self.gx, 2), lax.axis_size("gy")
        self.chips = lax.axis_size("gx") // 2
        self.r = self.low.shape[2] // self.chips
        self.four = self.chips == 4
        self.partner, self.others = places()
        self.near = list(square()[:2]) if self.four else self.others

    def product(self, m, which, z):
        return [nn(left[which], right[z]) for left, right in zip(self.lhs[m], self.rhs[m])]

    def remote(self, src, dst, send, recv, gx, gy):
        return pltpu.make_async_remote_copy(
            src_ref=src,
            dst_ref=dst,
            send_sem=send,
            recv_sem=recv,
            device_id=(gx, gy),
            device_id_type=MESH,
        )

    def block(self, m, device, start=0, size=None):
        size = self.r if size is None else size
        first = (device // 2) * self.r + start
        return self.low.at[m, :, pl.ds(pl.multiple_of(first, 16), size)]

    def swap(self, m, z):
        return self.remote(
            self.up.at[m, z],
            self.a_in.at[m, z],
            self.a_send.at[m, z],
            self.a_recv.at[m, z],
            self.partner,
            self.gy,
        )

    def first(self, m):
        for z in range(self.size):
            left, right = self.product(m, 1 - self.core, z)
            edge = left.shape[1]
            self.up[m, z, :, :edge] = left.astype(bf16)
            self.up[m, z, :, edge:] = right.astype(bf16)
            self.swap(m, z).start()

    def corner(self, m, h):
        side, along, across = square()
        half = self.r // 2
        return self.remote(
            self.block(m, across, h * half, half),
            self.r_in.at[m, h],
            self.r_send.at[m, h],
            self.r_recv.at[m, h],
            along if h else side,
            self.gy,
        )

    def second(self, m):
        for z in range(self.size):
            left, right = self.product(m, self.core, z)
            edge = left.shape[1]
            self.swap(m, z).wait_recv()
            came = self.a_in[m, z].astype(f32)
            self.low[m, z, :, :edge] = (left + came[:, :edge]).astype(bf16)
            self.low[m, z, :, edge:] = (right + came[:, edge:]).astype(bf16)
        if self.four:
            for h in range(2):
                self.corner(m, h).start()

    def hand(self, m, k):
        return self.remote(
            self.block(m, self.near[k]),
            self.c_in.at[m, k],
            self.c_send.at[m, k],
            self.c_recv.at[m, k],
            self.near[k],
            self.gy,
        )

    def third(self, m):
        if self.four:
            side, along, _ = square()
            half = self.r // 2
            for h, device in ((0, along), (1, side)):
                self.corner(m, h).wait_recv()
                here = self.block(m, device, h * half, half)
                here[...] = (here[...].astype(f32) + self.r_in[m, h].astype(f32)).astype(bf16)
        for k in range(len(self.near)):
            self.hand(m, k).start()

    def down_line(self, m, d):
        target = lax.rem(self.gy + d, self.size)
        return self.remote(
            self.z_out.at[m, target],
            self.z_in.at[m, self.gy],
            self.z_send.at[m, d],
            self.z_recv.at[m, self.gy],
            self.gx,
            target,
        )

    def fourth(self, m):
        for k in range(len(self.near)):
            self.hand(m, k).wait_recv()
        mine = self.block(m, self.gx)
        for z in range(self.size):
            total = mine[z].astype(f32)
            for k in range(len(self.near)):
                total = total + self.c_in[m, k, z].astype(f32)
            self.z_out[m, z] = total.astype(bf16)
        for d in range(1, self.size):
            self.down_line(m, d).start()

    def fifth(self, m, out):
        total = self.z_out[m, self.gy].astype(f32)
        for d in range(1, self.size):
            z = lax.rem(self.gy + d, self.size)
            wait_for(self.z_in.at[m, z], self.z_recv.at[m, z])
            total = total + self.z_in[m, z].astype(f32)
        out[m] = total

    def drain(self, m):
        for z in range(self.size):
            self.swap(m, z).wait_send()
        if self.four:
            for h in range(2):
                self.corner(m, h).wait_send()
        for k in range(len(self.near)):
            self.hand(m, k).wait_send()
        for d in range(1, self.size):
            self.down_line(m, d).wait_send()


class Total:
    def __init__(self, own, line_in, pair, pair_in, chip_in, sems):
        self.own, self.line_in, self.pair = own, line_in, pair
        self.pair_in, self.chip_in = pair_in, chip_in
        self.l_send, self.l_recv, self.p_send, self.p_recv, self.g_send, self.g_recv = sems
        self.gx, self.gy = lax.axis_index("gx"), lax.axis_index("gy")
        self.size, self.chips = lax.axis_size("gy"), lax.axis_size("gx") // 2
        self.partner, self.others = places()

    def remote(self, src, dst, send, recv, gx, gy):
        return pltpu.make_async_remote_copy(
            src_ref=src,
            dst_ref=dst,
            send_sem=send,
            recv_sem=recv,
            device_id=(gx, gy),
            device_id_type=MESH,
        )

    def line(self, d):
        target = lax.rem(self.gy + d, self.size)
        return self.remote(
            self.own.at[target],
            self.line_in.at[self.gy],
            self.l_send.at[d],
            self.l_recv.at[self.gy],
            self.gx,
            target,
        )

    def across(self):
        return self.remote(
            self.pair.at[0], self.pair_in, self.p_send, self.p_recv, self.partner, self.gy
        )

    def chip(self, k):
        return self.remote(
            self.pair.at[1],
            self.chip_in.at[self.gx // 2],
            self.g_send.at[k],
            self.g_recv.at[self.gx // 2],
            self.others[k],
            self.gy,
        )

    def begin(self):
        for d in range(1, self.size):
            self.line(d).start()

    def middle(self):
        total = self.own[self.gy]
        for d in range(1, self.size):
            z = lax.rem(self.gy + d, self.size)
            wait_for(self.line_in.at[z], self.l_recv.at[z])
            total = total + self.line_in[z]
        self.pair[0] = total
        self.across().start()

    def later(self):
        self.across().wait_recv()
        self.pair[1] = self.pair[0] + self.pair_in[...]
        self.chip_in[self.gx // 2] = self.pair[1]
        for k in range(self.chips - 1):
            self.chip(k).start()

    def close(self, out):
        for k in range(self.chips - 1):
            q = self.others[k] // 2
            wait_for(self.chip_in.at[q], self.g_recv.at[q])
        total = self.chip_in[0]
        for q in range(1, self.chips):
            total = total + self.chip_in[q]
        out[...] = total
        for d in range(1, self.size):
            self.line(d).wait_send()
        self.across().wait_send()
        for k in range(self.chips - 1):
            self.chip(k).wait_send()


def closing_kernel(layers, *refs):
    operands, refs = refs[: 4 * layers], refs[4 * layers :]
    small, out_rows, grad_rows = refs[:3]
    grads, small_out, out_blocks, grad_blocks = refs[3:7]
    scratch = refs[7:]
    lhs = [operands[4 * m : 4 * m + 2] for m in range(layers)]
    rhs = [operands[4 * m + 2 : 4 * m + 4] for m in range(layers)]
    fold = Fold(lhs, rhs, scratch[:7], scratch[7:15])
    total = Total(small, *scratch[15:19], scratch[19:25])
    swaps = [
        Exchange(own, full, scratch[25 + 3 * k : 28 + 3 * k], True)
        for k, (own, full) in enumerate(((grad_rows, grad_blocks), (out_rows, out_blocks)))
    ]
    me, size = lax.axis_index("gy"), lax.axis_size("gy")
    greet([fold.partner] + fold.others, [lax.rem(me + d, size) for d in range(1, size)])
    total.begin()
    for m in range(layers):
        fold.first(m)
    for swap in swaps:
        swap.begin()
    fold.second(0)
    total.middle()
    for m in range(1, layers):
        fold.second(m)
    total.later()
    for m in range(layers):
        fold.third(m)
    for m in range(layers):
        fold.fourth(m)
    total.close(small_out)
    for m in range(layers):
        fold.fifth(m, grads)
    for m in range(layers):
        fold.drain(m)
    for swap in swaps:
        swap.close()


def closing(operands, small, out_rows, grad_rows):
    layers = len(operands) // 4
    devices, size = lax.axis_size("gx"), lax.axis_size("gy")
    half = operands[0].shape[1]
    chips = devices // 2
    r, near = half // chips, 2 if chips == 4 else chips - 1
    c = operands[2].shape[2] + operands[3].shape[2]
    vmem, dma = pltpu.VMEM, pltpu.SemaphoreType.DMA
    row = small.shape[1:]
    local = pl.BlockSpec(memory_space=pltpu.VMEM)
    blocks = jax.ShapeDtypeStruct(out_rows.shape, bf16)
    return pl.pallas_call(
        functools.partial(closing_kernel, layers),
        out_shape=[
            jax.ShapeDtypeStruct((layers, r, c), f32),
            jax.ShapeDtypeStruct(row, f32),
            blocks,
            blocks,
        ],
        in_specs=[local] * (len(operands) + 1) + [ANY] * 2,
        out_specs=[local] * 2 + [ANY] * 2,
        scratch_shapes=[
            vmem((layers, size, half, c), bf16),
            vmem((layers, size, half, c), bf16),
            vmem((layers, size, half, c), bf16),
            vmem((layers, 2, size, r // 2, c), bf16),
            vmem((layers, near, size, r, c), bf16),
            vmem((layers, size, r, c), bf16),
            vmem((layers, size, r, c), bf16),
            dma((layers, size)),
            dma((layers, size)),
            dma((layers, 2)),
            dma((layers, 2)),
            dma((layers, near)),
            dma((layers, near)),
            dma((layers, size)),
            dma((layers, size)),
            vmem((size,) + row, f32),
            vmem((2,) + row, f32),
            vmem(row, f32),
            vmem((chips,) + row, f32),
            dma((size,)),
            dma((size,)),
            dma,
            dma,
            dma((chips,)),
            dma((chips,)),
        ]
        + exchange_scratch() * 2,
        compiler_params=pltpu.CompilerParams(
            collective_id=4, has_side_effects=True, vmem_limit_bytes=VMEM_LIMIT
        ),
        name="closing",
    )(*operands, small, out_rows, grad_rows)


def swing(value, cosine, turned_sine):
    return value * cosine + pltpu.roll(value, HEAD_DIM // 2, 1) * turned_sine


def tile_columns(value, tables):
    heads = value.shape[1] // HEAD_DIM
    parts = [swing(value[:, k * HEAD_DIM : (k + 1) * HEAD_DIM], *tables) for k in range(heads)]
    return jnp.concatenate(parts, axis=1)


def store_split(block, turned):
    width = block.shape[1]
    devices = lax.axis_size("gx")
    r = width // devices
    flipped = block.T
    for k in range(devices):
        q = k // 2
        turned[k % 2, q * r : (q + 1) * r] = flipped[k * r : (k + 1) * r]


def norm_pull(grad, normed, scale, gain):
    row = jnp.sum(grad * normed, axis=0, keepdims=True)
    scaled = grad * gain
    project = jnp.mean(scaled * normed, axis=1, keepdims=True)
    return row, scale * (scaled - normed * project)


def attention_pull_kernel(*refs):
    held, (late_grad, r_all, c_all) = refs[17], refs[24:27]
    refs = refs[:17] + refs[18:24] + refs[27:]
    (grad, grad_ffn, norm_b, scale_b, gain_b, norm_a, scale_a, gain_a) = refs[:8]
    acts, q, k, v, lse, cosine, sine, qkv_ref, out_ref = refs[8:17]
    grad_out, grad_low, acts_turned, branch_turned, gqkv, small = refs[17:23]
    qkv, wout, heads, branch, dq, dk_sum, dv_sum, kv_out, kv_in, total = refs[23:33]
    w_sem, kv_send, kv_recv, abuf = refs[33:37]
    tail = Tail(held, r_all, c_all, [late_grad], abuf, None, None, refs[37:], True)
    gx, me, size = lax.axis_index("gx"), lax.axis_index("gy"), lax.axis_size("gy")
    count, rows = q.shape[0], k.shape[0]
    loads = [
        pltpu.make_async_copy(out_ref, wout, w_sem.at[0]),
        pltpu.make_async_copy(qkv_ref, qkv, w_sem.at[1]),
    ]
    for load in loads:
        load.start()
    greet(tail.near, [lax.rem(me + d, size) for d in range(1, size)])
    tail.begin(0)
    small[...] = jnp.zeros_like(small)
    row, pulled = norm_pull(grad_ffn[...], norm_b[...], scale_b[...], gain_b[...])
    small[1:2] = row
    branch[...] = grad[...] + pulled
    low = branch[...].astype(bf16)
    store_split(low, branch_turned)
    store_split(acts[...], acts_turned)
    loads[0].wait()
    cq = wout.shape[2]
    heads[...] = jnp.concatenate([nn(low, wout[z]) for z in range(size)], axis=1).astype(bf16)

    tail.middle(0)
    query = me * count + lax.broadcasted_iota(jnp.int32, (rows, count), 1)
    key = lax.broadcasted_iota(jnp.int32, (rows, count), 0)
    allowed = key <= query
    if rows > LEN:
        allowed = jnp.logical_and(allowed, key // LEN == query // LEN)
    factor = 1.0 / math.sqrt(HEAD_DIM)
    tables = (cosine[...], sine[...])

    def kv_copy(g, d):
        target = lax.rem(me + d, size)
        return pltpu.make_async_remote_copy(
            src_ref=kv_out.at[g, target],
            dst_ref=kv_in.at[g, me],
            send_sem=kv_send.at[g, d],
            recv_sem=kv_recv.at[g, me],
            device_id=(gx, target),
            device_id_type=MESH,
        )

    for g in range(KV_HEADS):
        span = slice(g * HEAD_DIM, (g + 1) * HEAD_DIM)
        kg, vg = k[:, span], v[:, span]
        turned_k = kg.T
        dk_sum[...] = jnp.zeros_like(dk_sum)
        dv_sum[...] = jnp.zeros_like(dv_sum)

        def head(i, carry):
            h = g * GROUP + i
            at = pl.ds(pl.multiple_of(h * HEAD_DIM, HEAD_DIM), HEAD_DIM)
            qh, dh = q[:, at], heads[:, at]
            scores = jnp.where(allowed, nt(kg, qh) * factor, -1e30)
            p = jnp.exp(scores - lse[pl.ds(h, 1), :])
            dp = nt(vg, dh)
            inner = jnp.sum(p * dp, axis=0, keepdims=True)
            ds = (p * (dp - inner)).astype(bf16)
            dv_sum[...] += nn(p.astype(bf16), dh)
            dk_sum[...] += nn(ds, qh)
            dq[:, at] = swing(nn(turned_k, ds).T * factor, *tables).astype(bf16)
            return carry

        lax.fori_loop(0, GROUP, head, 0)
        for z in range(size):
            at = slice(z * count, (z + 1) * count)
            kv_out[g, z, :, :HEAD_DIM] = (dk_sum[at] * factor).astype(bf16)
            kv_out[g, z, :, HEAD_DIM:] = dv_sum[at].astype(bf16)
        for d in range(1, size):
            kv_copy(g, d).start()

    loads[1].wait()
    apart = cq % HEAD_DIM == 0
    if apart:
        for z in range(size):
            p = nt(dq[:, z * cq : (z + 1) * cq], qkv[z, :, :cq])
            if z == 0:
                total[...] = p
            else:
                total[...] += p
    dks, dvs = [], []
    for g in range(KV_HEADS):
        summed = kv_out[g, me].astype(f32)
        for d in range(1, size):
            z = lax.rem(me + d, size)
            wait_for(kv_in.at[g, z], kv_recv.at[g, z])
            summed = summed + kv_in[g, z].astype(f32)
        dks.append(swing(summed[:, :HEAD_DIM], *tables).astype(bf16).astype(f32))
        dvs.append(summed[:, HEAD_DIM:].astype(bf16).astype(f32))
    dk, dv = jnp.concatenate(dks, axis=1), jnp.concatenate(dvs, axis=1)
    ck = dk.shape[1] // size
    for z in range(size):
        at = slice(z * ck, (z + 1) * ck)
        kv = jnp.concatenate([dk[:, at], dv[:, at]], axis=1)
        if apart:
            kv = kv.astype(bf16)
            gqkv[z, :, :cq] = dq[:, z * cq : (z + 1) * cq]
            gqkv[z, :, cq:] = kv
            total[...] += nt(kv, qkv[z, :, cq:])
        else:
            mine = dq[:, z * cq : (z + 1) * cq].astype(f32)
            gqkv[z] = jnp.concatenate([mine, kv], axis=1).astype(bf16)
            p = nt(gqkv[z], qkv[z])
            if z == 0:
                total[...] = p
            else:
                total[...] += p
    row, pulled = norm_pull(total[...], norm_a[...], scale_a[...], gain_a[...])
    small[0:1] = row
    small[2:3] = jnp.sum(dq[...].astype(f32), axis=0, keepdims=True)
    width = dk.shape[1]
    small[3:4, :width] = jnp.sum(dk, axis=0, keepdims=True)
    small[4:5, :width] = jnp.sum(dv, axis=0, keepdims=True)
    final = branch[...] + pulled
    grad_out[...] = final
    grad_low[...] = final.astype(bf16)
    tail.close(0)
    for g in range(KV_HEADS):
        for d in range(1, size):
            kv_copy(g, d).wait_send()


def attention_pull(vectors, acts, q, k, v, lse, tables, qkv, wout, held):
    count, width = acts.shape
    size, rows = lax.axis_size("gy"), k.shape[0]
    local = pl.BlockSpec(memory_space=pltpu.VMEM)
    vmem, dma = pltpu.VMEM, pltpu.SemaphoreType.DMA
    turned = jax.ShapeDtypeStruct((2, width // 2, count), bf16)
    devices, wide = lax.axis_size("gx"), held.shape[2]
    near = 2 if devices == 8 else devices // 2 - 1
    r = width // devices
    return pl.pallas_call(
        attention_pull_kernel,
        out_shape=[
            jax.ShapeDtypeStruct((count, width), f32),
            jax.ShapeDtypeStruct((count, width), bf16),
            turned,
            turned,
            jax.ShapeDtypeStruct((size, count, qkv.shape[2]), bf16),
            jax.ShapeDtypeStruct((8, width), f32),
            jax.ShapeDtypeStruct((r, wide), f32),
            jax.ShapeDtypeStruct((1, 2, r // 2, wide), bf16),
            jax.ShapeDtypeStruct((1, near, 2, r // 2, wide), bf16),
        ],
        in_specs=[local] * 15 + [ANY] * 3,
        out_specs=[local] * 7 + [ANY] * 2,
        scratch_shapes=[
            vmem(qkv.shape, bf16),
            vmem(wout.shape, bf16),
            vmem((count, width), bf16),
            vmem((count, width), f32),
            vmem((count, width), bf16),
            vmem((rows, HEAD_DIM), f32),
            vmem((rows, HEAD_DIM), f32),
            vmem((KV_HEADS, size, count, 2 * HEAD_DIM), bf16),
            vmem((KV_HEADS, size, count, 2 * HEAD_DIM), bf16),
            vmem((count, width), f32),
            dma((2,)),
            dma((KV_HEADS, size)),
            dma((KV_HEADS, size)),
            vmem((width // 4, wide), bf16),
        ]
        + tail_scratch(1),
        compiler_params=pltpu.CompilerParams(
            collective_id=6, has_side_effects=True, vmem_limit_bytes=VMEM_LIMIT
        ),
        name="attention_pull",
    )(*vectors, acts, q, k, v, lse, *tables, qkv, wout, held)


def greet_line(gx_peers=()):
    gx, me, last = lax.axis_index("gx"), lax.axis_index("gy"), lax.axis_size("gy") - 1
    barrier = pltpu.get_barrier_semaphore()

    @pl.when(me > 0)
    def _():
        pl.semaphore_signal(barrier, inc=1, device_id=(gx, me - 1), device_id_type=MESH)

    @pl.when(me < last)
    def _():
        pl.semaphore_signal(barrier, inc=1, device_id=(gx, me + 1), device_id_type=MESH)

    for peer in gx_peers:
        pl.semaphore_signal(barrier, inc=1, device_id=(peer, me), device_id_type=MESH)
    count = jnp.where(jnp.logical_and(me > 0, me < last), 2, 1)
    pl.semaphore_wait(barrier, count + len(gx_peers))


PUSH_PLAN = {
    "chained": ("begin",),
    "group0": ("relay",),
    "group1": ("finish",),
    "end": ("close",),
}


def attention_push_kernel(layer, *refs):
    shard_ref, whole_ref = refs[10], refs[23]
    refs = refs[:10] + refs[11:23] + refs[24:]
    x, gain_a, gain_b, bq, bk, bv, cosine, sine, qkv_ref, out_ref = refs[:10]
    middle, norm_a, scale_a, acts_a, q, k_all, v_all, lse = refs[10:18]
    mixed, norm_b, scale_b, acts_b = refs[18:22]
    qkv, wout, kv_own, kv_all, flat, w_sem = refs[22:28]
    me, size = lax.axis_index("gy"), lax.axis_size("gy")
    count, rows = x.shape[0], k_all.shape[0]
    loads = [
        pltpu.make_async_copy(qkv_ref, qkv, w_sem.at[0]),
        pltpu.make_async_copy(out_ref, wout, w_sem.at[1]),
    ]
    for load in loads:
        load.start()
    chain = Chain(kv_own, kv_all, refs[28:31])
    spread = Spread([(shard_ref.at[layer], whole_ref)], refs[31:34])

    def move(name):
        for verb in PUSH_PLAN.get(name, ()):
            getattr(spread, verb)(0)

    greet_line([spread.partner] + spread.near)
    move("greeted")
    value = x[...]
    scale = lax.rsqrt(jnp.mean(value * value, axis=1, keepdims=True) + epsilon)
    scale_a[...] = scale
    norm_a[...] = value * scale
    acts_a[...] = (norm_a[...] * gain_a[...]).astype(bf16)
    loads[0].wait()
    cq, width = wout.shape[2], k_all.shape[1]
    ck = width // size
    tables = (cosine[...], sine[...])
    apart = cq % HEAD_DIM == 0
    if apart:
        kv = [nn(acts_a[...], qkv[z, :, cq:]) for z in range(size)]
    else:
        both = [nn(acts_a[...], qkv[z]) for z in range(size)]
        kv = [part[:, cq:] for part in both]
    keys = jnp.concatenate([part[:, :ck] for part in kv], axis=1) + bk[...]
    values = jnp.concatenate([part[:, ck:] for part in kv], axis=1) + bv[...]
    kv_own[:, :width] = tile_columns(keys, tables).astype(bf16)
    kv_own[:, width:] = values.astype(bf16)
    chain.begin()
    move("chained")
    if apart:
        for z in range(size):
            at = slice(z * cq, (z + 1) * cq)
            mine = nn(acts_a[...], qkv[z, :, :cq]) + bq[:, at]
            q[:, at] = tile_columns(mine, tables).astype(bf16)
            if z:
                chain.relay(z)
    else:
        mine = jnp.concatenate([part[:, :cq] for part in both], axis=1) + bq[...]
        q[...] = tile_columns(mine, tables).astype(bf16)
        for t in range(1, size):
            chain.relay(t)
    chain.close()
    move("relayed")
    k_all[...] = kv_all[:, :, :width].reshape(rows, width)
    v_all[...] = kv_all[:, :, width:].reshape(rows, width)

    query = me * count + lax.broadcasted_iota(jnp.int32, (rows, count), 1)
    key = lax.broadcasted_iota(jnp.int32, (rows, count), 0)
    allowed = key <= query
    if rows > LEN:
        allowed = jnp.logical_and(allowed, key // LEN == query // LEN)
    factor = 1.0 / math.sqrt(HEAD_DIM)
    for g in range(KV_HEADS):
        span = slice(g * HEAD_DIM, (g + 1) * HEAD_DIM)
        kg, turned_v = k_all[:, span], v_all[:, span].T

        def head(i, carry):
            h = g * GROUP + i
            at = pl.ds(pl.multiple_of(h * HEAD_DIM, HEAD_DIM), HEAD_DIM)
            scores = jnp.where(allowed, nt(kg, q[:, at]) * factor, -1e30)
            top = jnp.max(scores, axis=0, keepdims=True)
            expo = jnp.exp(scores - top)
            total = jnp.sum(expo, axis=0, keepdims=True)
            lse[pl.ds(h, 1), :] = top + jnp.log(total)
            soft = (expo * (1.0 / total)).astype(bf16)
            flat[:, at] = nn(turned_v, soft).T.astype(bf16)
            return carry

        lax.fori_loop(0, GROUP, head, 0)
        move("group%d" % g)
    loads[1].wait()
    middle[...] = x[...]
    for z in range(size):
        at = slice(z * cq, (z + 1) * cq)
        if apart:
            mixed[z] = flat[:, at]
        else:
            mixed[z] = flat[:, at].astype(f32).astype(bf16)
        middle[...] += nt(mixed[z], wout[z])
    value = middle[...]
    scale = lax.rsqrt(jnp.mean(value * value, axis=1, keepdims=True) + epsilon)
    scale_b[...] = scale
    norm_b[...] = value * scale
    acts_b[...] = (norm_b[...] * gain_b[...]).astype(bf16)
    move("end")


def attention_push(x, vectors, tables, qkv, wout, rows, shard, layer):
    count, width = x.shape
    size = lax.axis_size("gy")
    kvd = KV_HEADS * HEAD_DIM
    local = pl.BlockSpec(memory_space=pltpu.VMEM)
    vmem = pltpu.VMEM

    def shape(*dims, kind=bf16):
        return jax.ShapeDtypeStruct(dims, kind)

    normed = [shape(count, width, kind=f32), shape(count, 1, kind=f32), shape(count, width)]
    out = [shape(count, width, kind=f32), *normed, shape(count, HEADS * HEAD_DIM)]
    out += [shape(rows, kvd), shape(rows, kvd), shape(HEADS, count, kind=f32)]
    out += [shape(size, count, wout.shape[2]), *normed]
    out += [shape(lax.axis_size("gx"), *shard.shape[1:])]
    return pl.pallas_call(
        functools.partial(attention_push_kernel, layer),
        out_shape=out,
        in_specs=[local] * 8 + [ANY] * 3,
        out_specs=[local] * 12 + [ANY],
        scratch_shapes=[
            vmem(qkv.shape, bf16),
            vmem(wout.shape, bf16),
            vmem((count, 2 * kvd), bf16),
            vmem((size, count, 2 * kvd), bf16),
            vmem((count, HEADS * HEAD_DIM), bf16),
            pltpu.SemaphoreType.DMA((2,)),
        ]
        + chain_scratch()
        + spread_scratch(1),
        compiler_params=pltpu.CompilerParams(
            collective_id=7 + layer, has_side_effects=True, vmem_limit_bytes=VMEM_LIMIT
        ),
        name="attention_push",
    )(x, *vectors, *tables, qkv, wout, shard)


def on_device(
    residual_in,
    w_query,
    w_key,
    w_value,
    b_query,
    b_key,
    b_value,
    w_output,
    gain_attn,
    gain_ffn,
    w_gate,
    w_up,
    w_down,
    cotangent,
):
    devices_y = lax.axis_size("gy")
    rows_tok = residual_in.shape[1]
    count = rows_tok // devices_y
    q_index = lax.axis_index("gy") * count + jnp.arange(count, dtype=jnp.int32)
    cos_table, sin_table = rope_tables(q_index % LEN, HEAD_DIM)

    small = jnp.concatenate([gain_attn, gain_ffn, b_query, b_key, b_value], axis=1)
    small_sizes = [v.shape[1] for v in (gain_attn, gain_ffn, b_query, b_key, b_value)]
    small = jnp.pad(small.astype(f32), ((0, 8 - LAYERS), (0, 0)))
    lines = []
    for l in range(LAYERS):
        lines += [jnp.concatenate([w_query[l], w_key[l], w_value[l]], axis=1), w_output[l]]
    part_sizes = (w_query.shape[2], w_key.shape[2], w_value.shape[2])
    opened = opening(residual_in, cotangent, small, lines, w_gate, w_up)
    resid, cot, small = opened[:3]
    lines_next = opened[5:7]
    attn_full = [[w.reshape(devices_y, D, -1) for w in opened[7:9]], None]
    ffn_full = [[w.reshape(D, -1) for w in opened[9:]], None]
    small = small[:, :LAYERS].transpose(1, 0, 2)
    vectors, start = [], 0
    for size in small_sizes:
        vectors.append(small[:, :, start : start + size].reshape(LAYERS, -1))
        start += size
    gains_one, gains_two, bias_q, bias_k, bias_v = vectors

    resid = resid.reshape(D, count).astype(f32).T
    cot = cot.reshape(D, count)

    kept = []
    for l in range(LAYERS):
        w_qkv, w_out = attn_full[l]
        vectors = [v[l][None] for v in (gains_one, gains_two, bias_q, bias_k, bias_v)]
        done = attention_push(
            resid, vectors, (cos_table, -sin_table), w_qkv, w_out, rows_tok, w_down, l
        )
        middle, normed_one, scale_one, acts_one, q_rot, k_rot, v_heads, log_total = done[:8]
        mixed, normed_two, scale_two, acts_two = done[8:12]
        wg, wu = ffn_full[l]
        wd = done[12].reshape(D, -1)
        ffn_full[l] = (wg, wu, wd)
        if l == 0:
            shards = (*lines_next, w_gate, w_up)
            done = forward_ffn(acts_two, wg, wu, wd, shards)
            attn_full[1] = [w.reshape(devices_y, D, -1) for w in done[5:7]]
            ffn_full[1] = [w.reshape(D, -1) for w in done[7:]]
        else:
            done = forward_ffn(acts_two, wg, wu, wd)
        part, acts_two, gate, up, hidden = done[:5]
        kept.append(
            (
                normed_one,
                scale_one,
                acts_one,
                q_rot,
                k_rot,
                v_heads,
                log_total,
                mixed,
                normed_two,
                scale_two,
                acts_two,
                gate,
                up,
                hidden,
            )
        )
        resid = middle + part

    grad = cot.astype(f32).T + 2.0 * penalty * resid
    grad_low = grad.astype(bf16)
    attn_grads = [None] * LAYERS
    ffn_grads = [None] * LAYERS
    small_grads = [None] * LAYERS

    for l in reversed(range(LAYERS)):
        (
            normed_one,
            scale_one,
            acts_one,
            q_rot,
            k_rot,
            v_heads,
            log_total,
            mixed,
            normed_two,
            scale_two,
            acts_two,
            gate,
            up,
            hidden,
        ) = kept[l]
        w_qkv, w_out = attn_full[l]
        wg, wu, wd = ffn_full[l]
        operands = (grad_low, gate, up, hidden, acts_two, wg, wu, wd)
        if l == LAYERS - 1:
            done = backward_ffn(*operands, (1, 2))
            held = done[2]
            ffn_grads[l] = [None, None, done[1]]
        else:
            done = backward_ffn(*operands, (2,), held_next)
            ffn_grads[l] = [done[2], None, done[1]]
            ffn_grads[l + 1][1] = done[7]
            held = done[3]
        held_next = done[3]
        grad_acts_two = done[0]
        vectors = [grad, grad_acts_two, normed_two, scale_two, gains_two[l][None]]
        vectors += [normed_one, scale_one, gains_one[l][None]]
        done = attention_pull(
            vectors, acts_one, q_rot, k_rot, v_heads, log_total, (cos_table, sin_table), w_qkv, w_out, held
        )
        ffn_grads[l][0 if l == LAYERS - 1 else 1] = done[6]
        grad, grad_low = done[:2]
        attn_grads[l] = [*done[2:5], mixed]
        rows = done[5]
        width = k_rot.shape[1]
        small_grads[l] = [
            v.reshape(devices_y, -1)
            for v in (rows[0], rows[1], rows[2], rows[3, :width], rows[4, :width])
        ]
    small = jnp.stack([jnp.concatenate(v, axis=1) for v in small_grads], axis=1)
    small = jnp.pad(small, ((0, 0), (0, 8 - LAYERS), (0, 0)))

    def to_rows(tokens_major):
        return tokens_major.astype(bf16).T.reshape(devices_y, -1, count)

    def from_blocks(blocks):
        return blocks.transpose(1, 0, 2).reshape(-1, rows_tok).astype(f32)

    attn_sums, small, output, grad_input = closing(
        attn_grads[0] + attn_grads[1], small, to_rows(resid), to_rows(grad_low)
    )
    small = small[:LAYERS]
    attn_out, start = [], 0
    for size in part_sizes + (w_output.shape[2],):
        attn_out.append(attn_sums[:, :, start : start + size])
        start += size
    small_out, start = [], 0
    for size in small_sizes:
        small_out.append(small[:, start : start + size])
        start += size

    def stack(parts, k):
        return jnp.stack([part[k] for part in parts])

    return (
        from_blocks(output),
        from_blocks(grad_input),
        attn_out[0],
        attn_out[1],
        attn_out[2],
        small_out[2],
        small_out[3],
        small_out[4],
        attn_out[3],
        small_out[0],
        small_out[1],
        stack(ffn_grads, 0),
        stack(ffn_grads, 1),
        stack(ffn_grads, 2),
    )


def solution(mesh):
    tokens = P("gy", "gx")
    weight = P(None, "gx", "gy")
    vector = P(None, "gy")
    return jax.shard_map(
        on_device,
        mesh=mesh,
        in_specs=(
            tokens,
            weight,
            weight,
            weight,
            vector,
            vector,
            vector,
            weight,
            vector,
            vector,
            weight,
            weight,
            weight,
            tokens,
        ),
        out_specs=(
            tokens,
            tokens,
            weight,
            weight,
            weight,
            vector,
            vector,
            vector,
            weight,
            vector,
            vector,
            weight,
            weight,
            weight,
        ),
        check_vma=False,
    )
```

```python
import functools
import math

import jax
import jax.numpy as jnp
from jax import lax
from jax.experimental import pallas as pl
from jax.experimental.pallas import tpu as pltpu
from jax.sharding import PartitionSpec as P

D = 1536
HEADS = 12
KV_HEADS = 2
HEAD_DIM = 128
LEN = 1024
LAYERS = 2
GROUP = HEADS // KV_HEADS

epsilon = 1e-06
rope_base = 1000000.0
penalty = 0.25
bf16 = jnp.bfloat16
f32 = jnp.float32
MESH = pl.DeviceIdType.MESH
VMEM_LIMIT = 62 << 20
ANY = pl.BlockSpec(memory_space=pl.ANY)


def rope_tables(positions, head_size):
    freqs = rope_base ** (-jnp.arange(0, head_size, 2).astype(f32) / head_size)
    angles = positions.astype(f32)[:, None] * freqs[None, :]
    cosine = jnp.cos(angles)
    sine_table = jnp.sin(angles)
    return (
        jnp.concatenate([cosine, cosine], -1),
        jnp.concatenate([sine_table, -sine_table], -1),
    )


def wait_for(ref, sem):
    pltpu.make_async_copy(ref, ref, sem).wait()


def places():
    gx, devices = lax.axis_index("gx"), lax.axis_size("gx")
    chips = devices // 2
    chip, core = gx // 2, lax.rem(gx, 2)
    partner = gx + 1 - 2 * core
    others = [lax.rem(chip + k, chips) * 2 + core for k in range(1, chips)]
    return partner, others


def square():
    gx = lax.axis_index("gx")
    chip, core = gx // 2, lax.rem(gx, 2)
    side = gx + 2 - 4 * lax.rem(chip, 2)
    along = gx + 4 - 8 * (chip // 2)
    return side, along, (3 - chip) * 2 + core


def spread_slots():
    chips = lax.axis_size("gx") // 2
    return 14 if chips == 4 else 2 * chips + 2 * (chips - 1)


def spread_scratch(count):
    devices = lax.axis_size("gx")
    return [
        pltpu.SemaphoreType.DMA((count,)),
        pltpu.SemaphoreType.DMA((count, spread_slots())),
        pltpu.SemaphoreType.DMA((count, devices, 2)),
    ]


def greet(gx_peers, gy_peers):
    gx, gy = lax.axis_index("gx"), lax.axis_index("gy")
    barrier = pltpu.get_barrier_semaphore()
    for peer in gx_peers:
        pl.semaphore_signal(barrier, inc=1, device_id=(peer, gy), device_id_type=MESH)
    for peer in gy_peers:
        pl.semaphore_signal(barrier, inc=1, device_id=(gx, peer), device_id_type=MESH)
    pl.semaphore_wait(barrier, len(gx_peers) + len(gy_peers))


class Spread:
    def __init__(self, items, sems):
        self.items, (self.local, self.send_sem, self.recv_sem) = items, sems
        self.partner, self.others = places()
        self.four = lax.axis_size("gx") // 2 == 4
        self.near = list(square()[:2]) if self.four else self.others

    def part(self, i, k, h):
        full = self.items[i][1]
        if len(full.shape) == 4:
            half = full.shape[0] // 2
            return full.at[pl.ds(h * half, half), k]
        half = full.shape[1] // 2
        return full.at[k, pl.ds(h * half, half)]

    def send(self, i, k, h, target, slot, first=False):
        here = self.part(i, k, h)
        half = here.shape[0]
        source = self.items[i][0].at[pl.ds(h * half, half)] if first else here
        pltpu.make_async_remote_copy(
            src_ref=source,
            dst_ref=here,
            send_sem=self.send_sem.at[i, slot],
            recv_sem=self.recv_sem.at[i, k, h],
            device_id=(target, lax.axis_index("gy")),
            device_id_type=MESH,
        ).start()

    def arrived(self, i, k, h):
        wait_for(self.part(i, k, h), self.recv_sem.at[i, k, h])

    def place(self, i):
        own, full = self.items[i]
        gx = lax.axis_index("gx")
        here = full.at[:, gx] if len(full.shape) == 4 else full.at[gx]
        return pltpu.make_async_copy(own, here, self.local.at[i])

    def begin(self, i):
        gx = lax.axis_index("gx")
        self.place(i).start()
        slot = 0
        for target in self.near + [self.partner]:
            for h in range(2):
                self.send(i, gx, h, target, slot, True)
                slot += 1

    def relay(self, i):
        slot = 2 * len(self.near) + 2
        if self.four:
            side, along, _ = square()
            steps = [(side, 0, along), (along, 1, side), (side, 1, None), (along, 0, None)]
        else:
            steps = [(k, h, None) for k in self.others for h in range(2)]
        for k, h, target in steps:
            self.arrived(i, k, h)
            for to in [self.partner] if target is None else [target, self.partner]:
                self.send(i, k, h, to, slot)
                slot += 1

    def finish(self, i):
        if self.four:
            for h in range(2):
                self.arrived(i, square()[2], h)
                self.send(i, square()[2], h, self.partner, 12 + h)

    def close(self, i):
        core = lax.rem(lax.axis_index("gx"), 2)
        for k in [self.partner] + [k + 1 - 2 * core for k in self.others]:
            for h in range(2):
                self.arrived(i, k, h)
        for slot in range(spread_slots()):
            wait_for(self.part(i, 0, 0), self.send_sem.at[i, slot])
        self.place(i).wait()


def line_order(t, me, last):
    short = jnp.minimum(me, last - me)
    near = jnp.where(lax.rem(t, 2) == 0, me - t // 2, me + (t + 1) // 2)
    far = jnp.where(me < last - me, me + (t - short), me - (t - short))
    return jnp.where(t <= 2 * short, near, far)


class Chain:
    def __init__(self, own, full, sems):
        self.own, self.full, (self.local, self.send_sem, self.recv_sem) = own, full, sems

    def copy(self, b, way, first=False):
        me = lax.axis_index("gy")
        return pltpu.make_async_remote_copy(
            src_ref=self.own if first else self.full.at[b],
            dst_ref=self.full.at[b],
            send_sem=self.send_sem.at[b, way],
            recv_sem=self.recv_sem.at[b],
            device_id=(lax.axis_index("gx"), me - 1 + 2 * way),
            device_id_type=MESH,
        )

    def each(self, b, act, first=False):
        me, last = lax.axis_index("gy"), lax.axis_size("gy") - 1

        @pl.when(jnp.logical_and(b <= me, me < last))
        def _():
            act(self.copy(b, 1, first))

        @pl.when(jnp.logical_and(b >= me, me > 0))
        def _():
            act(self.copy(b, 0, first))

    def begin(self):
        me = lax.axis_index("gy")
        self.place = pltpu.make_async_copy(self.own, self.full.at[me], self.local)
        self.place.start()
        self.each(me, lambda copy: copy.start(), True)

    def relay(self, t):
        b = line_order(t, lax.axis_index("gy"), lax.axis_size("gy") - 1)
        wait_for(self.full.at[b], self.recv_sem.at[b])
        self.each(b, lambda copy: copy.start())

    def close(self):
        self.place.wait()
        for b in range(lax.axis_size("gy")):
            self.each(b, lambda copy: copy.wait_send())


class Exchange:
    def __init__(self, own, full, sems, apart=False):
        self.own, self.full, (self.local, self.send_sem, self.recv_sem) = own, full, sems
        self.apart = apart

    def begin(self):
        gx, me, size = lax.axis_index("gx"), lax.axis_index("gy"), lax.axis_size("gy")
        width = self.full.shape[2]

        def columns(k):
            if self.apart:
                return self.own.at[k]
            return self.own.at[:, pl.ds(pl.multiple_of(k * width, width), width)]

        self.place = pltpu.make_async_copy(columns(me), self.full.at[me], self.local)
        self.place.start()
        self.sent = []
        for d in range(1, size):
            target = lax.rem(me + d, size)
            copy = pltpu.make_async_remote_copy(
                src_ref=columns(target),
                dst_ref=self.full.at[me],
                send_sem=self.send_sem.at[d],
                recv_sem=self.recv_sem.at[me],
                device_id=(gx, target),
                device_id_type=MESH,
            )
            copy.start()
            self.sent.append(copy)

    def close(self):
        me, size = lax.axis_index("gy"), lax.axis_size("gy")
        self.place.wait()
        for copy in self.sent:
            copy.wait_send()
        for d in range(1, size):
            k = lax.rem(me + d, size)
            wait_for(self.full.at[k], self.recv_sem.at[k])


def chain_scratch():
    size = lax.axis_size("gy")
    return [
        pltpu.SemaphoreType.DMA,
        pltpu.SemaphoreType.DMA((size, 2)),
        pltpu.SemaphoreType.DMA((size,)),
    ]


def exchange_scratch():
    size = lax.axis_size("gy")
    return [
        pltpu.SemaphoreType.DMA,
        pltpu.SemaphoreType.DMA((size,)),
        pltpu.SemaphoreType.DMA((size,)),
    ]


def opening_kernel(*refs):
    ins, outs, sems = refs[:9], refs[9:20], refs[20:]
    resid, cot, small, qkv_a, o_a, qkv_b, o_b, wg, wu = ins
    resid_out, cot_out, small_out = outs[:3]
    lines, (qkv, o, gate, up) = outs[3:7], outs[7:]
    me, size = lax.axis_index("gy"), lax.axis_size("gy")
    owns = (qkv_a, o_a, qkv_b, o_b, small)
    chains = [
        Chain(own, full, sems[3 * k : 3 * k + 3])
        for k, (own, full) in enumerate(zip(owns, list(lines) + [small_out]))
    ]
    swaps = [
        Exchange(own, full, sems[15 + 3 * k : 18 + 3 * k])
        for k, (own, full) in enumerate(((resid, resid_out), (cot, cot_out)))
    ]
    items = [(lines[0], qkv), (lines[1], o), (wg.at[0], gate), (wu.at[0], up)]
    spread = Spread(items, sems[21:24])
    greet([spread.partner] + spread.near, [lax.rem(me + d, size) for d in range(1, size)])
    for k in (0, 1, 4):
        chains[k].begin()
    spread.begin(2)
    for t in range(1, size):
        chains[0].relay(t)
        chains[1].relay(t)
    chains[0].close()
    spread.begin(0)
    chains[1].close()
    spread.begin(1)
    swaps[0].begin()
    for t in range(1, size):
        chains[4].relay(t)
    spread.relay(2)
    spread.begin(3)
    chains[2].begin()
    chains[3].begin()
    for i in (0, 1):
        spread.relay(i)
    swaps[1].begin()
    for t in range(1, size):
        chains[2].relay(t)
        chains[3].relay(t)
    spread.finish(2)
    for i in (0, 1):
        spread.finish(i)
    spread.relay(3)
    spread.finish(3)
    for i in range(4):
        spread.close(i)
    for part in chains[2:] + swaps:
        part.close()


def opening(resid, cot, small, lines, wg, wu):
    devices, size = lax.axis_size("gx"), lax.axis_size("gy")
    count = resid.shape[1] // size

    def shape(*dims, kind=bf16):
        return jax.ShapeDtypeStruct(dims, kind)

    blocks = shape(size, resid.shape[0], count)
    weight = shape(devices, *wg.shape[1:])
    out = [blocks, blocks, shape(size, *small.shape, kind=f32)]
    out += [shape(size, *line.shape) for line in lines]
    out += [shape(size, devices, *line.shape) for line in lines[:2]] + [weight] * 2
    return pl.pallas_call(
        opening_kernel,
        out_shape=out,
        in_specs=[ANY] * 9,
        out_specs=[ANY] * 11,
        scratch_shapes=chain_scratch() * 5 + exchange_scratch() * 2 + spread_scratch(4),
        compiler_params=pltpu.CompilerParams(collective_id=2, has_side_effects=True),
        name="opening",
    )(resid, cot, small, *lines, wg, wu)


FF_CHUNK = 512
PIECES = 4


def spans(total):
    return [(start, min(FF_CHUNK, total - start)) for start in range(0, total, FF_CHUNK)]


def nn(left, right):
    return lax.dot_general(left, right, (((1,), (0,)), ((), ())), preferred_element_type=f32)


def nt(left, right):
    return lax.dot_general(left, right, (((1,), (1,)), ((), ())), preferred_element_type=f32)


def line_pass(own_ref, own, gathered, part, outb, inb, sems, load, finish, peers=(), plan={}):
    own_sem, ag_send, ag_recv, rs_send, rs_recv = sems
    gx, me, size = lax.axis_index("gx"), lax.axis_index("gy"), lax.axis_size("gy")
    rows = own.shape[0]
    piece = rows // PIECES
    last = size - 1
    inner = jnp.logical_and(me > 0, me < last)

    first = pltpu.make_async_copy(own_ref, gathered.at[me], own_sem)
    first.start()
    barrier = pltpu.get_barrier_semaphore()

    @pl.when(me > 0)
    def _():
        pl.semaphore_signal(barrier, inc=1, device_id=(gx, me - 1), device_id_type=MESH)

    @pl.when(me < last)
    def _():
        pl.semaphore_signal(barrier, inc=1, device_id=(gx, me + 1), device_id_type=MESH)

    for peer in peers:
        pl.semaphore_signal(barrier, inc=1, device_id=(peer, me), device_id_type=MESH)
    pl.semaphore_wait(barrier, jnp.where(inner, 2, 1) + len(peers))
    first.wait()

    def planned(name, t):
        for (key, when), act in plan.items():
            if key == name:
                pl.when(t == when)(act)


    def gather_copy(b, s, way):
        here = gathered.at[b, pl.ds(s * piece, piece)]
        return pltpu.make_async_remote_copy(
            src_ref=here,
            dst_ref=here,
            send_sem=ag_send.at[b, way, s],
            recv_sem=ag_recv.at[b, s],
            device_id=(gx, me - 1 + 2 * way),
            device_id_type=MESH,
        )

    def sum_copy(b, s):
        towards = jnp.where(b > me, me + 1, me - 1)
        slot = jnp.where(jnp.logical_and(towards == b, me > b), size, b)
        return pltpu.make_async_remote_copy(
            src_ref=outb.at[b, pl.ds(s * piece, piece)],
            dst_ref=inb.at[slot, pl.ds(s * piece, piece)],
            send_sem=rs_send.at[b, s],
            recv_sem=rs_recv.at[slot, s],
            device_id=(gx, towards),
            device_id_type=MESH,
        )

    def sum_arrived(slot, s):
        here = inb.at[slot, pl.ds(s * piece, piece)]
        pltpu.make_async_copy(here, here, rs_recv.at[slot, s]).wait()

    def step(t, carry):
        b = line_order(t, me, last)
        for s in range(PIECES):

            @pl.when(t > 0)
            def _():
                gather_copy(b, s, 0).wait_recv()

            @pl.when(jnp.logical_and(b <= me, me < last))
            def _():
                gather_copy(b, s, 1).start()

            @pl.when(jnp.logical_and(b >= me, me > 0))
            def _():
                gather_copy(b, s, 0).start()

        @pl.when(t == 0)
        def _():
            load()

        planned("step", t)
        finish(b)

        @pl.when(b == me)
        def _():
            own[...] = part[...]

        @pl.when(b != me)
        def _():
            outb[b] = part[...].astype(bf16)

            @pl.when(jnp.logical_not(inner))
            def _():
                for s in range(PIECES):
                    sum_copy(b, s).start()

        return carry

    lax.fori_loop(0, size, step, 0)

    def relay(t, carry):
        above, below = last - me, me
        low = jnp.where(t < above, me + 1 + t, me - 1 - (t - above))
        high = jnp.where(t < below, me - 1 - t, me + 1 + (t - below))
        b = jnp.where(2 * me < size, low, high)
        planned("hop", t)

        @pl.when(inner)
        def _():
            for s in range(PIECES):
                at = pl.ds(s * piece, piece)
                sum_arrived(b, s)
                outb[b, at] = (outb[b, at].astype(f32) + inb[b, at].astype(f32)).astype(bf16)
                sum_copy(b, s).start()

        return carry

    lax.fori_loop(0, last, relay, 0)

    @pl.when(me > 0)
    def _():
        for s in range(PIECES):
            sum_arrived(me, s)
        own[...] += inb[me].astype(f32)

    @pl.when(me < last)
    def _():
        for s in range(PIECES):
            sum_arrived(size, s)
        own[...] += inb[size].astype(f32)

    def drain(b, carry):
        for s in range(PIECES):

            @pl.when(jnp.logical_and(b <= me, me < last))
            def _():
                gather_copy(b, s, 1).wait_send()

            @pl.when(jnp.logical_and(b >= me, me > 0))
            def _():
                gather_copy(b, s, 0).wait_send()

            @pl.when(b != me)
            def _():
                sum_copy(b, s).wait_send()

        return carry

    lax.fori_loop(0, size, drain, 0)


def line_scratch(size, rows, width):
    return [
        pltpu.VMEM((size, rows, width), bf16),
        pltpu.VMEM((rows, width), f32),
        pltpu.VMEM((size, rows, width), bf16),
        pltpu.VMEM((size + 1, rows, width), bf16),
        pltpu.SemaphoreType.DMA,
        pltpu.SemaphoreType.DMA((size, 2, PIECES)),
        pltpu.SemaphoreType.DMA((size, PIECES)),
        pltpu.SemaphoreType.DMA((size, PIECES)),
        pltpu.SemaphoreType.DMA((size + 1, PIECES)),
    ]


LINE = 9


ORDER = {
    ("step", 0): (("begin", 0), ("begin", 1)),
    ("step", 2): (("begin", 2),),
    ("hop", 0): (("relay", 0), ("relay", 1), ("relay", 2), ("begin", 3)),
    ("hop", 1): (("finish", 0), ("finish", 1), ("finish", 2)),
}
REST = (("relay", 3), ("finish", 3))


def schedule(spread):
    def run(steps):
        def act():
            for verb, i in steps:
                getattr(spread, verb)(i)

        return act

    plan = {key: run(steps) for key, steps in ORDER.items()}
    return plan, REST + tuple(("close", i) for i in range(len(spread.items)))


def forward_kernel(extra, *refs):
    acts_ref, wg_ref, wu_ref, wd_ref = refs[:4]
    shards, refs = refs[4 : 4 + extra], refs[4 + extra :]
    sum_ref, turned_ref, gate_ref, up_ref, hidden_ref = refs[:5]
    wholes, scratch = refs[5 : 5 + extra], refs[5 + extra :]
    gathered, part, outb, inb = scratch[:4]
    sems = scratch[4:LINE]
    wg, wu, wd, gate, up, hidden, turned, w_sem, out_sem = scratch[LINE : LINE + 9]
    peers, spread = [], None
    if extra:
        items = [(r if len(w.shape) == 4 else r.at[1], w) for r, w in zip(shards, wholes)]
        spread = Spread(items, scratch[LINE + 9 :])
        partner, others = places()
        peers = [partner] + (list(square()[:2]) if spread.four else others)

    plan, rest = schedule(spread) if extra else ({}, ())
    loads = [
        pltpu.make_async_copy(src, dst, w_sem.at[k])
        for k, (src, dst) in enumerate(((wg_ref, wg), (wu_ref, wu), (wd_ref, wd)))
    ]
    for copy in loads:
        copy.start()

    def load():
        for copy in loads:
            copy.wait()

    def results(b):
        pairs = ((gate, gate_ref), (up, up_ref), (hidden, hidden_ref))
        return [
            pltpu.make_async_copy(src.at[b], dst.at[b], out_sem.at[b, k])
            for k, (src, dst) in enumerate(pairs)
        ]

    def finish(b):
        block = gathered[b]
        store_turned(block, turned, b)
        for start, width in spans(wg.shape[1]):
            at = slice(start, start + width)
            g = nn(block, wg[:, at])
            u = nn(block, wu[:, at])
            h = (g * lax.logistic(g) * u).astype(bf16)
            gate[b, :, at] = g.astype(bf16)
            up[b, :, at] = u.astype(bf16)
            hidden[b, :, at] = h
            p = nt(h, wd[:, at])
            if start == 0:
                part[...] = p
            else:
                part[...] += p
        for copy in results(b):
            copy.start()

    line_pass(
        acts_ref, sum_ref, gathered, part, outb, inb, sems, load, finish, peers, plan
    )
    keep = pltpu.make_async_copy(turned, turned_ref, w_sem.at[0])
    keep.start()
    for act, i in rest:
        getattr(spread, act)(i)

    def settle(b, carry):
        for copy in results(b):
            copy.wait()
        return carry

    lax.fori_loop(0, gathered.shape[0], settle, 0)
    keep.wait()


def forward_ffn(acts, wg, wu, wd, shards=()):
    rows, width = acts.shape
    devices, size, hidden = lax.axis_size("gx"), lax.axis_size("gy"), wg.shape[1]
    wide = jax.ShapeDtypeStruct((size, rows, hidden), bf16)
    extra = len(shards)
    wholes = [
        jax.ShapeDtypeStruct(
            (size, devices) + s.shape[1:] if k < 2 else (devices,) + s.shape[1:], bf16
        )
        for k, s in enumerate(shards)
    ]
    return pl.pallas_call(
        functools.partial(forward_kernel, extra),
        out_shape=[
            jax.ShapeDtypeStruct((rows, width), f32),
            jax.ShapeDtypeStruct((2, width // 2, size * rows), bf16),
            wide,
            wide,
            wide,
        ]
        + wholes,
        in_specs=[ANY] * (4 + extra),
        out_specs=[pl.BlockSpec(memory_space=pltpu.VMEM)] + [ANY] * (4 + extra),
        scratch_shapes=line_scratch(size, rows, width)
        + [pltpu.VMEM((width, hidden), bf16)] * 3
        + [pltpu.VMEM((size, rows, hidden), bf16)] * 3
        + [pltpu.VMEM((2, width // 2, size * rows), bf16)]
        + [pltpu.SemaphoreType.DMA((3,)), pltpu.SemaphoreType.DMA((size, 3))]
        + (spread_scratch(extra) if extra else []),
        compiler_params=pltpu.CompilerParams(
            collective_id=3 if extra else 0, has_side_effects=True, vmem_limit_bytes=VMEM_LIMIT
        ),
        cost_estimate=pl.CostEstimate(
            flops=6 * size * rows * width * hidden, bytes_accessed=40 << 20, transcendentals=0
        ),
        name="ffn_forward",
    )(acts, wg, wu, wd, *shards)


def put_rows(totals, out, row, fbuf, ftail, sems, lanes):
    stores, edge, wide = [], 0, 0
    for j, make in enumerate(totals):
        total = make()
        part, width = total.shape
        full = width == FF_CHUNK
        wide += full
        if full and j >= 2:
            stores[j - 2].wait()
        stage = fbuf.at[pl.ds((j % 2) * part, part)] if full else ftail.at[pl.ds(0, part)]
        stage[...] = total
        store = pltpu.make_async_copy(
            stage,
            out.at[pl.ds(row, part), edge : edge + width],
            sems.at[lanes[j % 2 if full else 2]],
        )
        store.start()
        stores.append(store)
        edge += width
    for store in stores[max(wide - 2, 0) :]:
        store.wait()


class Reduce:
    def __init__(self, lhs, rhs, bufs, abuf, fbuf, ftail, a_all, r_all, c_all, outs, late, sems):
        self.late = late
        self.lhs, self.rhs, self.bufs, self.outs = lhs, rhs, bufs, outs
        self.abuf, self.fbuf, self.ftail = abuf, fbuf, ftail
        self.a_all, self.r_all, self.c_all = a_all, r_all, c_all
        (
            self.a_send,
            self.a_recv,
            self.r_send,
            self.r_recv,
            self.c_send,
            self.c_recv,
            self.local,
        ) = sems
        gx, self.gy = lax.axis_index("gx"), lax.axis_index("gy")
        self.chip, self.core = gx // 2, lax.rem(gx, 2)
        self.chips = lax.axis_size("gx") // 2
        self.half, self.wide = bufs[0].shape[0] // 2, bufs[0].shape[1]
        self.r = self.half // self.chips
        self.four = self.chips == 4
        self.partner, self.others = places()
        self.near = list(square()[:2]) if self.four else self.others

    def product(self, m, which, at):
        z, n, _ = self.rhs[m].shape
        right = self.rhs[m][:, :, at].reshape(z * n, at.stop - at.start)
        return nn(self.lhs[which], right)

    def remote(self, src, dst, send, recv, target):
        return pltpu.make_async_remote_copy(
            src_ref=src,
            dst_ref=dst,
            send_sem=send,
            recv_sem=recv,
            device_id=(target, self.gy),
            device_id_type=MESH,
        )

    def columns(self):
        return [(j, slice(s, s + w)) for j, (s, w) in enumerate(spans(self.wide))]

    def swap(self, m, j, at):
        here = (slice(0, self.half), at)
        return self.remote(
            self.bufs[m].at[here],
            self.a_all.at[m, :, at],
            self.a_send.at[m, j],
            self.a_recv.at[m, j],
            self.partner,
        )

    def block(self, m, device, start=0, size=None):
        size = self.r if size is None else size
        first = self.half + (device // 2) * self.r + start
        return self.bufs[m].at[pl.ds(pl.multiple_of(first, 16), size)]

    def first(self, m):
        for j, at in self.columns():
            self.bufs[m][: self.half, at] = self.product(m, 1 - self.core, at).astype(bf16)
            self.swap(m, j, at).start()

    def corner(self, m, h):
        side, along, across = square()
        half = self.r // 2
        return self.remote(
            self.block(m, across, h * half, half),
            self.r_all.at[m, h],
            self.r_send.at[m, h],
            self.r_recv.at[m, h],
            along if h else side,
        )

    def second(self, m):
        for j, at in self.columns():
            self.swap(m, j, at).wait_recv()
            landed = self.abuf.at[:, at]
            fetch = pltpu.make_async_copy(self.a_all.at[m, :, at], landed, self.local.at[0])
            fetch.start()
            mine = self.product(m, self.core, at)
            fetch.wait()
            self.bufs[m][self.half :, at] = (mine + landed[...].astype(f32)).astype(bf16)
        if m in self.late:
            self.keep(m).start()
        elif self.four:
            for h in range(2):
                self.corner(m, h).start()

    def keep(self, m):
        kept = self.outs[m].at[0]
        return pltpu.make_async_copy(
            self.bufs[m].at[pl.ds(self.half, self.half)], kept, self.local.at[max(len(self.near), 2)]
        )

    def hand(self, m, k):
        target = self.near[k]
        return self.remote(
            self.block(m, target),
            self.c_all.at[m, k],
            self.c_send.at[m, k],
            self.c_recv.at[m, k],
            target,
        )

    def third(self, m):
        if self.four:
            side, along, _ = square()
            half = self.r // 2
            for h, device in ((0, along), (1, side)):
                self.corner(m, h).wait_recv()
                here = self.block(m, device, h * half, half)
                landed = self.abuf.at[h * half : (h + 1) * half]
                fetch = pltpu.make_async_copy(self.r_all.at[m, h], landed, self.local.at[0])
                fetch.start()
                fetch.wait()
                here[...] = (here[...].astype(f32) + landed[...].astype(f32)).astype(bf16)
        for k in range(len(self.near)):
            self.hand(m, k).start()

    def fourth(self, m):
        for j, at in self.columns():
            self.swap(m, j, at).wait_send()
        fetches = []
        for k in range(len(self.near)):
            self.hand(m, k).wait_recv()
            here = self.bufs[m].at[pl.ds(k * self.r, self.r)]
            fetch = pltpu.make_async_copy(self.c_all.at[m, k], here, self.local.at[k])
            fetch.start()
            fetches.append(fetch)
        for fetch in fetches:
            fetch.wait()
        part = self.r // 2
        for h in range(2):
            first = pl.multiple_of(self.half + self.chip * self.r + h * part, 16)
            totals = []
            for _, at in self.columns():

                def make(at=at, first=first, h=h):
                    total = self.bufs[m][pl.ds(first, part), at].astype(f32)
                    for k in range(len(self.near)):
                        start = k * self.r + h * part
                        total = total + self.bufs[m][start : start + part, at].astype(f32)
                    return total

                totals.append(make)
            lanes = (0, 1, max(len(self.near), 2) + 1)
            put_rows(totals, self.outs[m], h * part, self.fbuf, self.ftail, self.local, lanes)

    def drain(self, m):
        if self.four:
            for h in range(2):
                self.corner(m, h).wait_send()
        for k in range(len(self.near)):
            self.hand(m, k).wait_send()


def reduce_scratch(width, hidden, count=3):
    devices = lax.axis_size("gx")
    rows, parts = width // devices, len(spans(hidden))
    near = 2 if devices == 8 else devices // 2 - 1
    dma = pltpu.SemaphoreType.DMA
    return [
        pltpu.VMEM((width // 2, hidden), bf16),
        pltpu.VMEM((rows, FF_CHUNK), f32),
        pltpu.VMEM((rows, hidden % FF_CHUNK), f32),
        dma((count, parts)),
        dma((count, parts)),
        dma((count, 2)),
        dma((count, 2)),
        dma((count, near)),
        dma((count, near)),
        dma((max(near, 2) + 2,)),
    ]


class Tail:
    def __init__(self, b_all, r_all, c_all, outs, abuf, fbuf, ftail, sems, direct=False):
        self.direct = direct
        self.b_all, self.r_all, self.c_all, self.outs = b_all, r_all, c_all, outs
        self.abuf, self.fbuf, self.ftail = abuf, fbuf, ftail
        self.r_send, self.r_recv, self.c_send, self.c_recv, self.local = sems
        gx, self.gy = lax.axis_index("gx"), lax.axis_index("gy")
        self.chip, chips = gx // 2, lax.axis_size("gx") // 2
        self.r = b_all.shape[1] // chips
        self.part = self.r // 2
        self.space = b_all.shape[1] // b_all.shape[0]
        self.four = chips == 4
        self.near = list(square()[:2]) if self.four else places()[1]

    def remote(self, src, dst, send, recv, target):
        return pltpu.make_async_remote_copy(
            src_ref=src,
            dst_ref=dst,
            send_sem=send,
            recv_sem=recv,
            device_id=(target, self.gy),
            device_id_type=MESH,
        )

    def held(self, i, chip, h):
        first = pl.multiple_of(chip * self.r + h * self.part, 16)
        return self.b_all.at[i, pl.ds(first, self.part)]

    def slot(self, i, k):
        return self.abuf.at[pl.ds(i * self.space + k * self.part, self.part)]

    def corner(self, i, h):
        side, along, across = square()
        return self.remote(
            self.held(i, across // 2, h),
            self.r_all.at[i, h],
            self.r_send.at[i, h],
            self.r_recv.at[i, h],
            along if h else side,
        )

    def hand(self, i, k, h):
        target = self.near[k]
        summed = self.four and k != h
        return self.remote(
            self.slot(i, 2 + h) if summed else self.held(i, target // 2, h),
            self.c_all.at[i, k, h],
            self.c_send.at[i, k, h],
            self.c_recv.at[i, k, h],
            target,
        )

    def hands(self):
        return [(k, h) for k in range(len(self.near)) for h in range(2)]

    def begin(self, i):
        if self.four:
            for h in range(2):
                self.corner(i, h).start()

    def middle(self, i):
        if self.four:
            side, along, _ = square()
            for h, device in ((0, along), (1, side)):
                self.corner(i, h).wait_recv()
                came, mine = self.slot(i, h), self.slot(i, 2 + h)
                fetches = [
                    pltpu.make_async_copy(self.r_all.at[i, h], came, self.local.at[0]),
                    pltpu.make_async_copy(self.held(i, device // 2, h), mine, self.local.at[1]),
                ]
                for fetch in fetches:
                    fetch.start()
                for fetch in fetches:
                    fetch.wait()
                mine[...] = (mine[...].astype(f32) + came[...].astype(f32)).astype(bf16)
        for k, h in self.hands():
            self.hand(i, k, h).start()

    def close(self, i):
        if self.four:
            for h in range(2):
                self.corner(i, h).wait_send()
        for k, h in self.hands():
            self.hand(i, k, h).wait_send()
        count = len(self.near)
        for h in range(2):
            fetches = [
                pltpu.make_async_copy(
                    self.held(i, self.chip, h), self.slot(i, count), self.local.at[count]
                )
            ]
            for k in range(count):
                self.hand(i, k, h).wait_recv()
                fetches.append(
                    pltpu.make_async_copy(
                        self.c_all.at[i, k, h], self.slot(i, k), self.local.at[k]
                    )
                )
            for fetch in fetches:
                fetch.start()
            for fetch in fetches:
                fetch.wait()
            totals = []
            for start, width in spans(self.abuf.shape[1]):
                at = slice(start, start + width)

                def make(at=at):
                    total = self.slot(i, 0)[:, at].astype(f32)
                    for k in range(1, count + 1):
                        total = total + self.slot(i, k)[:, at].astype(f32)
                    return total

                if self.direct:
                    self.outs[i][h * self.part : (h + 1) * self.part, at] = make()
                else:
                    totals.append(make)
            put_rows(
                totals, self.outs[i], h * self.part, self.fbuf, self.ftail, self.local, (0, 1, 2)
            )


def tail_scratch(count):
    devices = lax.axis_size("gx")
    near = 2 if devices == 8 else devices // 2 - 1
    dma = pltpu.SemaphoreType.DMA
    return [
        dma((count, 2)),
        dma((count, 2)),
        dma((count, near, 2)),
        dma((count, near, 2)),
        dma((near + 1,)),
    ]


def store_turned(block, turned, b):
    count, width = block.shape
    _, chips_rows, _ = turned.shape
    devices = lax.axis_size("gx")
    r = width // devices
    flipped = block.T
    at = pl.ds(pl.multiple_of(b * count, count), count)
    for k in range(devices):
        q = k // 2
        turned[k % 2, q * r : (q + 1) * r, at] = flipped[k * r : (k + 1) * r]


AFTER = {
    0: (("first", 0),),
    1: (("second", 0), ("swap", 0), ("first", 1)),
    2: (("third", 0), ("second", 1)),
}
ENDS = {
    (1, 2): (
        ("kept", 1),
        ("first", 2),
        ("second", 2),
        ("fourth", 0),
        ("kept", 2),
        ("sent", 1),
        ("sent", 2),
        ("drain", 0),
    ),
    (2,): (
        ("first", 2),
        ("third", 1),
        ("second", 2),
        ("fourth", 0),
        ("kept", 2),
        ("fourth", 1),
        ("sent", 2),
        ("drain", 0),
        ("drain", 1),
    ),
}
TAIL_BEGIN, TAIL_MIDDLE = ("step", 0), ("step", 2)


def both(one, other):
    def act():
        one()
        other()

    return act


def backward_kernel(late, tails, *refs):
    grad_ref, gate_ref, up_ref, hidden_ref, turned_ref, wg_ref, wu_ref, wd_ref = refs[:8]
    held, refs = refs[8 : 8 + (tails > 0)], refs[8 + (tails > 0) :]
    sum_ref, refs = refs[0], refs[1:]
    outs, (a_all, r_all, c_all), refs = refs[:3], refs[3:6], refs[6:]
    tail_refs, scratch = refs[: tails + 2 * (tails > 0)], refs[tails + 2 * (tails > 0) :]
    gathered, part, outb, inb = scratch[:4]
    sems = scratch[4:LINE]
    wg, wu, wd, gate, up, hidden, turned, w_sem = scratch[LINE : LINE + 8]
    abuf, fbuf, ftail = scratch[LINE + 8 : LINE + 11]
    operands = (
        (wd_ref, wd),
        (gate_ref, gate),
        (up_ref, up),
        (wg_ref, wg),
        (wu_ref, wu),
        (hidden_ref, hidden),
    )
    loads = [
        pltpu.make_async_copy(src, dst, w_sem.at[k]) for k, (src, dst) in enumerate(operands)
    ]
    for copy in loads:
        copy.start()

    def load():
        for copy in loads:
            copy.wait()

    reduce = Reduce(
        turned,
        (hidden, gate, up),
        (wd, wg, wu),
        abuf,
        fbuf,
        ftail,
        a_all,
        r_all,
        c_all,
        outs,
        late,
        scratch[LINE + 11 : LINE + 18],
    )
    tail = None
    if tails:
        tail = Tail(
            held[0],
            tail_refs[tails],
            tail_refs[tails + 1],
            tail_refs[:tails],
            abuf,
            fbuf,
            ftail,
            scratch[LINE + 18 :],
        )

    def finish(b):
        block = gathered[b]
        store_turned(block, turned, b)
        for start, width in spans(wg.shape[1]):
            at = slice(start, start + width)
            d = nn(block, wd[:, at])
            g = gate[b, :, at].astype(f32)
            u = up[b, :, at].astype(f32)
            sigma = lax.logistic(g)
            ds = d * sigma
            dg = (ds * u * (1.0 + g * (1.0 - sigma))).astype(bf16)
            du = (ds * g).astype(bf16)
            gate[b, :, at] = dg
            up[b, :, at] = du
            p = nt(dg, wg[:, at]) + nt(du, wu[:, at])
            if start == 0:
                part[...] = p
            else:
                part[...] += p

    def run(verb, m):
        if verb == "swap":
            copy = pltpu.make_async_copy(turned_ref, turned, w_sem.at[0])
            copy.start()
            copy.wait()
        elif verb == "kept":
            reduce.keep(m).wait()
        elif verb == "sent":
            for j, at in reduce.columns():
                reduce.swap(m, j, at).wait_send()
        else:
            getattr(reduce, verb)(m)

    def work(t):
        def act():
            if tail is not None and t == 1:
                for i in range(tails):
                    tail.close(i)
            for verb, m in AFTER[t]:
                run(verb, m)

        return act

    def each(verb):
        def act():
            for i in range(tails):
                getattr(tail, verb)(i)

        return act

    peers = [reduce.partner] + reduce.near
    plan = {("hop", t): work(t) for t in range(3)}
    if tails:
        for key, act in ((TAIL_BEGIN, each("begin")), (TAIL_MIDDLE, each("middle"))):
            old = plan.get(key)
            plan[key] = act if old is None else both(act, old)
    line_pass(grad_ref, sum_ref, gathered, part, outb, inb, sems, load, finish, peers, plan)
    for verb, m in ENDS[late]:
        run(verb, m)


def backward_ffn(grad, gate, up, hidden, turned, wg, wu, wd, late, held=None):
    rows, width = grad.shape
    devices, size, wide = lax.axis_size("gx"), lax.axis_size("gy"), wg.shape[1]
    near = 2 if devices == 8 else devices // 2 - 1
    r = width // devices
    mine = jax.ShapeDtypeStruct((r, wide), f32)

    def between(*dims):
        return jax.ShapeDtypeStruct(dims + (wide,), bf16)

    count = 3 - len(late)
    out = [jax.ShapeDtypeStruct((rows, width), f32)]
    out += [between(1, width // 2) if m in late else mine for m in range(3)]
    out += [between(3, width // 2), between(count, 2, r // 2), between(count, near, r)]
    tails = 0 if held is None else held.shape[0]
    if tails:
        out += [mine] * tails
        out += [between(tails, 2, r // 2), between(tails, near, 2, r // 2)]
    extra = [held] if tails else []
    return pl.pallas_call(
        functools.partial(backward_kernel, late, tails),
        out_shape=out,
        in_specs=[ANY] * (8 + len(extra)),
        out_specs=[pl.BlockSpec(memory_space=pltpu.VMEM)] + [ANY] * (len(out) - 1),
        scratch_shapes=line_scratch(size, rows, width)
        + [pltpu.VMEM((width, wide), bf16)] * 3
        + [pltpu.VMEM((size, rows, wide), bf16)] * 3
        + [pltpu.VMEM((2, width // 2, size * rows), bf16), pltpu.SemaphoreType.DMA((6,))]
        + reduce_scratch(width, wide)
        + (tail_scratch(tails) if tails else []),
        compiler_params=pltpu.CompilerParams(
            collective_id=1 if held is None else 5, has_side_effects=True, vmem_limit_bytes=VMEM_LIMIT
        ),
        cost_estimate=pl.CostEstimate(
            flops=12 * size * rows * width * wide, bytes_accessed=40 << 20, transcendentals=0
        ),
        name="ffn_backward",
    )(grad, gate, up, hidden, turned, wg, wu, wd, *extra)


class Fold:
    def __init__(self, lhs, rhs, bufs, sems):
        self.lhs, self.rhs = lhs, rhs
        self.up, self.low, self.a_in, self.r_in, self.c_in, self.z_out, self.z_in = bufs
        (
            self.a_send,
            self.a_recv,
            self.r_send,
            self.r_recv,
            self.c_send,
            self.c_recv,
            self.z_send,
            self.z_recv,
        ) = sems
        self.gx, self.gy = lax.axis_index("gx"), lax.axis_index("gy")
        self.core, self.size = lax.rem(self.gx, 2), lax.axis_size("gy")
        self.chips = lax.axis_size("gx") // 2
        self.r = self.low.shape[2] // self.chips
        self.four = self.chips == 4
        self.partner, self.others = places()
        self.near = list(square()[:2]) if self.four else self.others

    def product(self, m, which, z):
        return [nn(left[which], right[z]) for left, right in zip(self.lhs[m], self.rhs[m])]

    def remote(self, src, dst, send, recv, gx, gy):
        return pltpu.make_async_remote_copy(
            src_ref=src,
            dst_ref=dst,
            send_sem=send,
            recv_sem=recv,
            device_id=(gx, gy),
            device_id_type=MESH,
        )

    def block(self, m, device, start=0, size=None):
        size = self.r if size is None else size
        first = (device // 2) * self.r + start
        return self.low.at[m, :, pl.ds(pl.multiple_of(first, 16), size)]

    def swap(self, m, z):
        return self.remote(
            self.up.at[m, z],
            self.a_in.at[m, z],
            self.a_send.at[m, z],
            self.a_recv.at[m, z],
            self.partner,
            self.gy,
        )

    def first(self, m):
        for z in range(self.size):
            left, right = self.product(m, 1 - self.core, z)
            edge = left.shape[1]
            self.up[m, z, :, :edge] = left.astype(bf16)
            self.up[m, z, :, edge:] = right.astype(bf16)
            self.swap(m, z).start()

    def corner(self, m, h):
        side, along, across = square()
        half = self.r // 2
        return self.remote(
            self.block(m, across, h * half, half),
            self.r_in.at[m, h],
            self.r_send.at[m, h],
            self.r_recv.at[m, h],
            along if h else side,
            self.gy,
        )

    def second(self, m):
        for z in range(self.size):
            left, right = self.product(m, self.core, z)
            edge = left.shape[1]
            self.swap(m, z).wait_recv()
            came = self.a_in[m, z].astype(f32)
            self.low[m, z, :, :edge] = (left + came[:, :edge]).astype(bf16)
            self.low[m, z, :, edge:] = (right + came[:, edge:]).astype(bf16)
        if self.four:
            for h in range(2):
                self.corner(m, h).start()

    def hand(self, m, k):
        return self.remote(
            self.block(m, self.near[k]),
            self.c_in.at[m, k],
            self.c_send.at[m, k],
            self.c_recv.at[m, k],
            self.near[k],
            self.gy,
        )

    def third(self, m):
        if self.four:
            side, along, _ = square()
            half = self.r // 2
            for h, device in ((0, along), (1, side)):
                self.corner(m, h).wait_recv()
                here = self.block(m, device, h * half, half)
                here[...] = (here[...].astype(f32) + self.r_in[m, h].astype(f32)).astype(bf16)
        for k in range(len(self.near)):
            self.hand(m, k).start()

    def down_line(self, m, d):
        target = lax.rem(self.gy + d, self.size)
        return self.remote(
            self.z_out.at[m, target],
            self.z_in.at[m, self.gy],
            self.z_send.at[m, d],
            self.z_recv.at[m, self.gy],
            self.gx,
            target,
        )

    def fourth(self, m):
        for k in range(len(self.near)):
            self.hand(m, k).wait_recv()
        mine = self.block(m, self.gx)
        for z in range(self.size):
            total = mine[z].astype(f32)
            for k in range(len(self.near)):
                total = total + self.c_in[m, k, z].astype(f32)
            self.z_out[m, z] = total.astype(bf16)
        for d in range(1, self.size):
            self.down_line(m, d).start()

    def fifth(self, m, out):
        total = self.z_out[m, self.gy].astype(f32)
        for d in range(1, self.size):
            z = lax.rem(self.gy + d, self.size)
            wait_for(self.z_in.at[m, z], self.z_recv.at[m, z])
            total = total + self.z_in[m, z].astype(f32)
        out[m] = total

    def drain(self, m):
        for z in range(self.size):
            self.swap(m, z).wait_send()
        if self.four:
            for h in range(2):
                self.corner(m, h).wait_send()
        for k in range(len(self.near)):
            self.hand(m, k).wait_send()
        for d in range(1, self.size):
            self.down_line(m, d).wait_send()


class Total:
    def __init__(self, own, line_in, pair, pair_in, chip_in, sems):
        self.own, self.line_in, self.pair = own, line_in, pair
        self.pair_in, self.chip_in = pair_in, chip_in
        self.l_send, self.l_recv, self.p_send, self.p_recv, self.g_send, self.g_recv = sems
        self.gx, self.gy = lax.axis_index("gx"), lax.axis_index("gy")
        self.size, self.chips = lax.axis_size("gy"), lax.axis_size("gx") // 2
        self.partner, self.others = places()

    def remote(self, src, dst, send, recv, gx, gy):
        return pltpu.make_async_remote_copy(
            src_ref=src,
            dst_ref=dst,
            send_sem=send,
            recv_sem=recv,
            device_id=(gx, gy),
            device_id_type=MESH,
        )

    def line(self, d):
        target = lax.rem(self.gy + d, self.size)
        return self.remote(
            self.own.at[target],
            self.line_in.at[self.gy],
            self.l_send.at[d],
            self.l_recv.at[self.gy],
            self.gx,
            target,
        )

    def across(self):
        return self.remote(
            self.pair.at[0], self.pair_in, self.p_send, self.p_recv, self.partner, self.gy
        )

    def chip(self, k):
        return self.remote(
            self.pair.at[1],
            self.chip_in.at[self.gx // 2],
            self.g_send.at[k],
            self.g_recv.at[self.gx // 2],
            self.others[k],
            self.gy,
        )

    def begin(self):
        for d in range(1, self.size):
            self.line(d).start()

    def middle(self):
        total = self.own[self.gy]
        for d in range(1, self.size):
            z = lax.rem(self.gy + d, self.size)
            wait_for(self.line_in.at[z], self.l_recv.at[z])
            total = total + self.line_in[z]
        self.pair[0] = total
        self.across().start()

    def later(self):
        self.across().wait_recv()
        self.pair[1] = self.pair[0] + self.pair_in[...]
        self.chip_in[self.gx // 2] = self.pair[1]
        for k in range(self.chips - 1):
            self.chip(k).start()

    def close(self, out):
        for k in range(self.chips - 1):
            q = self.others[k] // 2
            wait_for(self.chip_in.at[q], self.g_recv.at[q])
        total = self.chip_in[0]
        for q in range(1, self.chips):
            total = total + self.chip_in[q]
        out[...] = total
        for d in range(1, self.size):
            self.line(d).wait_send()
        self.across().wait_send()
        for k in range(self.chips - 1):
            self.chip(k).wait_send()


def closing_kernel(layers, *refs):
    operands, refs = refs[: 4 * layers], refs[4 * layers :]
    small, out_rows, grad_rows = refs[:3]
    grads, small_out, out_blocks, grad_blocks = refs[3:7]
    scratch = refs[7:]
    lhs = [operands[4 * m : 4 * m + 2] for m in range(layers)]
    rhs = [operands[4 * m + 2 : 4 * m + 4] for m in range(layers)]
    fold = Fold(lhs, rhs, scratch[:7], scratch[7:15])
    total = Total(small, *scratch[15:19], scratch[19:25])
    swaps = [
        Exchange(own, full, scratch[25 + 3 * k : 28 + 3 * k], True)
        for k, (own, full) in enumerate(((grad_rows, grad_blocks), (out_rows, out_blocks)))
    ]
    me, size = lax.axis_index("gy"), lax.axis_size("gy")
    greet([fold.partner] + fold.others, [lax.rem(me + d, size) for d in range(1, size)])
    total.begin()
    for m in range(layers):
        fold.first(m)
    fold.second(0)
    total.middle()
    for m in range(1, layers):
        fold.second(m)
    total.later()
    for m in range(layers):
        fold.third(m)
        if m == 0:
            for swap in swaps:
                swap.begin()
    for m in range(layers):
        fold.fourth(m)
    total.close(small_out)
    for m in range(layers):
        fold.fifth(m, grads)
    for m in range(layers):
        fold.drain(m)
    for swap in swaps:
        swap.close()


def closing(operands, small, out_rows, grad_rows):
    layers = len(operands) // 4
    devices, size = lax.axis_size("gx"), lax.axis_size("gy")
    half = operands[0].shape[1]
    chips = devices // 2
    r, near = half // chips, 2 if chips == 4 else chips - 1
    c = operands[2].shape[2] + operands[3].shape[2]
    vmem, dma = pltpu.VMEM, pltpu.SemaphoreType.DMA
    row = small.shape[1:]
    local = pl.BlockSpec(memory_space=pltpu.VMEM)
    blocks = jax.ShapeDtypeStruct(out_rows.shape, bf16)
    return pl.pallas_call(
        functools.partial(closing_kernel, layers),
        out_shape=[
            jax.ShapeDtypeStruct((layers, r, c), f32),
            jax.ShapeDtypeStruct(row, f32),
            blocks,
            blocks,
        ],
        in_specs=[local] * (len(operands) + 1) + [ANY] * 2,
        out_specs=[local] * 2 + [ANY] * 2,
        scratch_shapes=[
            vmem((layers, size, half, c), bf16),
            vmem((layers, size, half, c), bf16),
            vmem((layers, size, half, c), bf16),
            vmem((layers, 2, size, r // 2, c), bf16),
            vmem((layers, near, size, r, c), bf16),
            vmem((layers, size, r, c), bf16),
            vmem((layers, size, r, c), bf16),
            dma((layers, size)),
            dma((layers, size)),
            dma((layers, 2)),
            dma((layers, 2)),
            dma((layers, near)),
            dma((layers, near)),
            dma((layers, size)),
            dma((layers, size)),
            vmem((size,) + row, f32),
            vmem((2,) + row, f32),
            vmem(row, f32),
            vmem((chips,) + row, f32),
            dma((size,)),
            dma((size,)),
            dma,
            dma,
            dma((chips,)),
            dma((chips,)),
        ]
        + exchange_scratch() * 2,
        compiler_params=pltpu.CompilerParams(
            collective_id=4, has_side_effects=True, vmem_limit_bytes=VMEM_LIMIT
        ),
        name="closing",
    )(*operands, small, out_rows, grad_rows)


def swing(value, cosine, turned_sine):
    return value * cosine + pltpu.roll(value, HEAD_DIM // 2, 1) * turned_sine


def tile_columns(value, tables):
    heads = value.shape[1] // HEAD_DIM
    parts = [swing(value[:, k * HEAD_DIM : (k + 1) * HEAD_DIM], *tables) for k in range(heads)]
    return jnp.concatenate(parts, axis=1)


def store_split(block, turned):
    width = block.shape[1]
    devices = lax.axis_size("gx")
    r = width // devices
    flipped = block.T
    for k in range(devices):
        q = k // 2
        turned[k % 2, q * r : (q + 1) * r] = flipped[k * r : (k + 1) * r]


def norm_pull(grad, normed, scale, gain):
    row = jnp.sum(grad * normed, axis=0, keepdims=True)
    scaled = grad * gain
    project = jnp.mean(scaled * normed, axis=1, keepdims=True)
    return row, scale * (scaled - normed * project)


def attention_pull_kernel(*refs):
    held, (late_grad, r_all, c_all) = refs[17], refs[24:27]
    refs = refs[:17] + refs[18:24] + refs[27:]
    (grad, grad_ffn, norm_b, scale_b, gain_b, norm_a, scale_a, gain_a) = refs[:8]
    acts, q, k, v, lse, cosine, sine, qkv_ref, out_ref = refs[8:17]
    grad_out, grad_low, acts_turned, branch_turned, gqkv, small = refs[17:23]
    qkv, wout, heads, branch, dq, dk_sum, dv_sum, kv_out, kv_in, total = refs[23:33]
    w_sem, kv_send, kv_recv, abuf = refs[33:37]
    tail = Tail(held, r_all, c_all, [late_grad], abuf, None, None, refs[37:], True)
    gx, me, size = lax.axis_index("gx"), lax.axis_index("gy"), lax.axis_size("gy")
    count, rows = q.shape[0], k.shape[0]
    loads = [
        pltpu.make_async_copy(out_ref, wout, w_sem.at[0]),
        pltpu.make_async_copy(qkv_ref, qkv, w_sem.at[1]),
    ]
    for load in loads:
        load.start()
    greet(tail.near, [lax.rem(me + d, size) for d in range(1, size)])
    tail.begin(0)
    small[...] = jnp.zeros_like(small)
    row, pulled = norm_pull(grad_ffn[...], norm_b[...], scale_b[...], gain_b[...])
    small[1:2] = row
    branch[...] = grad[...] + pulled
    low = branch[...].astype(bf16)
    store_split(low, branch_turned)
    store_split(acts[...], acts_turned)
    loads[0].wait()
    cq = wout.shape[2]
    heads[...] = jnp.concatenate([nn(low, wout[z]) for z in range(size)], axis=1).astype(bf16)

    tail.middle(0)
    query = me * count + lax.broadcasted_iota(jnp.int32, (rows, count), 1)
    key = lax.broadcasted_iota(jnp.int32, (rows, count), 0)
    allowed = key <= query
    if rows > LEN:
        allowed = jnp.logical_and(allowed, key // LEN == query // LEN)
    factor = 1.0 / math.sqrt(HEAD_DIM)
    tables = (cosine[...], sine[...])

    def kv_copy(g, d):
        target = lax.rem(me + d, size)
        return pltpu.make_async_remote_copy(
            src_ref=kv_out.at[g, target],
            dst_ref=kv_in.at[g, me],
            send_sem=kv_send.at[g, d],
            recv_sem=kv_recv.at[g, me],
            device_id=(gx, target),
            device_id_type=MESH,
        )

    for g in range(KV_HEADS):
        span = slice(g * HEAD_DIM, (g + 1) * HEAD_DIM)
        kg, vg = k[:, span], v[:, span]
        turned_k = kg.T
        dk_sum[...] = jnp.zeros_like(dk_sum)
        dv_sum[...] = jnp.zeros_like(dv_sum)

        def head(i, carry):
            h = g * GROUP + i
            at = pl.ds(pl.multiple_of(h * HEAD_DIM, HEAD_DIM), HEAD_DIM)
            qh, dh = q[:, at], heads[:, at]
            scores = jnp.where(allowed, nt(kg, qh) * factor, -1e30)
            p = jnp.exp(scores - lse[pl.ds(h, 1), :])
            dp = nt(vg, dh)
            inner = jnp.sum(p * dp, axis=0, keepdims=True)
            ds = (p * (dp - inner)).astype(bf16)
            dv_sum[...] += nn(p.astype(bf16), dh)
            dk_sum[...] += nn(ds, qh)
            dq[:, at] = swing(nn(turned_k, ds).T * factor, *tables).astype(bf16)
            return carry

        lax.fori_loop(0, GROUP, head, 0)
        for z in range(size):
            at = slice(z * count, (z + 1) * count)
            kv_out[g, z, :, :HEAD_DIM] = (dk_sum[at] * factor).astype(bf16)
            kv_out[g, z, :, HEAD_DIM:] = dv_sum[at].astype(bf16)
        for d in range(1, size):
            kv_copy(g, d).start()

    loads[1].wait()
    apart = cq % HEAD_DIM == 0
    if apart:
        for z in range(size):
            p = nt(dq[:, z * cq : (z + 1) * cq], qkv[z, :, :cq])
            if z == 0:
                total[...] = p
            else:
                total[...] += p
    dks, dvs = [], []
    for g in range(KV_HEADS):
        summed = kv_out[g, me].astype(f32)
        for d in range(1, size):
            z = lax.rem(me + d, size)
            wait_for(kv_in.at[g, z], kv_recv.at[g, z])
            summed = summed + kv_in[g, z].astype(f32)
        dks.append(swing(summed[:, :HEAD_DIM], *tables).astype(bf16).astype(f32))
        dvs.append(summed[:, HEAD_DIM:].astype(bf16).astype(f32))
    dk, dv = jnp.concatenate(dks, axis=1), jnp.concatenate(dvs, axis=1)
    ck = dk.shape[1] // size
    for z in range(size):
        at = slice(z * ck, (z + 1) * ck)
        kv = jnp.concatenate([dk[:, at], dv[:, at]], axis=1)
        if apart:
            kv = kv.astype(bf16)
            gqkv[z, :, :cq] = dq[:, z * cq : (z + 1) * cq]
            gqkv[z, :, cq:] = kv
            total[...] += nt(kv, qkv[z, :, cq:])
        else:
            mine = dq[:, z * cq : (z + 1) * cq].astype(f32)
            gqkv[z] = jnp.concatenate([mine, kv], axis=1).astype(bf16)
            p = nt(gqkv[z], qkv[z])
            if z == 0:
                total[...] = p
            else:
                total[...] += p
    row, pulled = norm_pull(total[...], norm_a[...], scale_a[...], gain_a[...])
    small[0:1] = row
    small[2:3] = jnp.sum(dq[...].astype(f32), axis=0, keepdims=True)
    width = dk.shape[1]
    small[3:4, :width] = jnp.sum(dk, axis=0, keepdims=True)
    small[4:5, :width] = jnp.sum(dv, axis=0, keepdims=True)
    final = branch[...] + pulled
    grad_out[...] = final
    grad_low[...] = final.astype(bf16)
    tail.close(0)
    for g in range(KV_HEADS):
        for d in range(1, size):
            kv_copy(g, d).wait_send()


def attention_pull(vectors, acts, q, k, v, lse, tables, qkv, wout, held):
    count, width = acts.shape
    size, rows = lax.axis_size("gy"), k.shape[0]
    local = pl.BlockSpec(memory_space=pltpu.VMEM)
    vmem, dma = pltpu.VMEM, pltpu.SemaphoreType.DMA
    turned = jax.ShapeDtypeStruct((2, width // 2, count), bf16)
    devices, wide = lax.axis_size("gx"), held.shape[2]
    near = 2 if devices == 8 else devices // 2 - 1
    r = width // devices
    return pl.pallas_call(
        attention_pull_kernel,
        out_shape=[
            jax.ShapeDtypeStruct((count, width), f32),
            jax.ShapeDtypeStruct((count, width), bf16),
            turned,
            turned,
            jax.ShapeDtypeStruct((size, count, qkv.shape[2]), bf16),
            jax.ShapeDtypeStruct((8, width), f32),
            jax.ShapeDtypeStruct((r, wide), f32),
            jax.ShapeDtypeStruct((1, 2, r // 2, wide), bf16),
            jax.ShapeDtypeStruct((1, near, 2, r // 2, wide), bf16),
        ],
        in_specs=[local] * 15 + [ANY] * 3,
        out_specs=[local] * 7 + [ANY] * 2,
        scratch_shapes=[
            vmem(qkv.shape, bf16),
            vmem(wout.shape, bf16),
            vmem((count, width), bf16),
            vmem((count, width), f32),
            vmem((count, width), bf16),
            vmem((rows, HEAD_DIM), f32),
            vmem((rows, HEAD_DIM), f32),
            vmem((KV_HEADS, size, count, 2 * HEAD_DIM), bf16),
            vmem((KV_HEADS, size, count, 2 * HEAD_DIM), bf16),
            vmem((count, width), f32),
            dma((2,)),
            dma((KV_HEADS, size)),
            dma((KV_HEADS, size)),
            vmem((width // 4, wide), bf16),
        ]
        + tail_scratch(1),
        compiler_params=pltpu.CompilerParams(
            collective_id=6, has_side_effects=True, vmem_limit_bytes=VMEM_LIMIT
        ),
        name="attention_pull",
    )(*vectors, acts, q, k, v, lse, *tables, qkv, wout, held)


def greet_line(gx_peers=()):
    gx, me, last = lax.axis_index("gx"), lax.axis_index("gy"), lax.axis_size("gy") - 1
    barrier = pltpu.get_barrier_semaphore()

    @pl.when(me > 0)
    def _():
        pl.semaphore_signal(barrier, inc=1, device_id=(gx, me - 1), device_id_type=MESH)

    @pl.when(me < last)
    def _():
        pl.semaphore_signal(barrier, inc=1, device_id=(gx, me + 1), device_id_type=MESH)

    for peer in gx_peers:
        pl.semaphore_signal(barrier, inc=1, device_id=(peer, me), device_id_type=MESH)
    count = jnp.where(jnp.logical_and(me > 0, me < last), 2, 1)
    pl.semaphore_wait(barrier, count + len(gx_peers))


PUSH_PLAN = {
    "chained": ("begin",),
    "group0": ("relay",),
    "group1": ("finish",),
    "end": ("close",),
}


def attention_push_kernel(layer, *refs):
    shard_ref, whole_ref = refs[10], refs[23]
    refs = refs[:10] + refs[11:23] + refs[24:]
    x, gain_a, gain_b, bq, bk, bv, cosine, sine, qkv_ref, out_ref = refs[:10]
    middle, norm_a, scale_a, acts_a, q, k_all, v_all, lse = refs[10:18]
    mixed, norm_b, scale_b, acts_b = refs[18:22]
    qkv, wout, kv_own, kv_all, flat, w_sem = refs[22:28]
    me, size = lax.axis_index("gy"), lax.axis_size("gy")
    count, rows = x.shape[0], k_all.shape[0]
    loads = [
        pltpu.make_async_copy(qkv_ref, qkv, w_sem.at[0]),
        pltpu.make_async_copy(out_ref, wout, w_sem.at[1]),
    ]
    for load in loads:
        load.start()
    chain = Chain(kv_own, kv_all, refs[28:31])
    spread = Spread([(shard_ref.at[layer], whole_ref)], refs[31:34])

    def move(name):
        for verb in PUSH_PLAN.get(name, ()):
            getattr(spread, verb)(0)

    greet_line([spread.partner] + spread.near)
    move("greeted")
    value = x[...]
    scale = lax.rsqrt(jnp.mean(value * value, axis=1, keepdims=True) + epsilon)
    scale_a[...] = scale
    norm_a[...] = value * scale
    acts_a[...] = (norm_a[...] * gain_a[...]).astype(bf16)
    loads[0].wait()
    cq, width = wout.shape[2], k_all.shape[1]
    ck = width // size
    tables = (cosine[...], sine[...])
    apart = cq % HEAD_DIM == 0
    if apart:
        kv = [nn(acts_a[...], qkv[z, :, cq:]) for z in range(size)]
    else:
        both = [nn(acts_a[...], qkv[z]) for z in range(size)]
        kv = [part[:, cq:] for part in both]
    keys = jnp.concatenate([part[:, :ck] for part in kv], axis=1) + bk[...]
    values = jnp.concatenate([part[:, ck:] for part in kv], axis=1) + bv[...]
    kv_own[:, :width] = tile_columns(keys, tables).astype(bf16)
    kv_own[:, width:] = values.astype(bf16)
    chain.begin()
    move("chained")
    if apart:
        for z in range(size):
            at = slice(z * cq, (z + 1) * cq)
            mine = nn(acts_a[...], qkv[z, :, :cq]) + bq[:, at]
            q[:, at] = tile_columns(mine, tables).astype(bf16)
            if z:
                chain.relay(z)
    else:
        mine = jnp.concatenate([part[:, :cq] for part in both], axis=1) + bq[...]
        q[...] = tile_columns(mine, tables).astype(bf16)
        for t in range(1, size):
            chain.relay(t)
    chain.close()
    move("relayed")
    k_all[...] = kv_all[:, :, :width].reshape(rows, width)
    v_all[...] = kv_all[:, :, width:].reshape(rows, width)

    query = me * count + lax.broadcasted_iota(jnp.int32, (rows, count), 1)
    key = lax.broadcasted_iota(jnp.int32, (rows, count), 0)
    allowed = key <= query
    if rows > LEN:
        allowed = jnp.logical_and(allowed, key // LEN == query // LEN)
    factor = 1.0 / math.sqrt(HEAD_DIM)
    for g in range(KV_HEADS):
        span = slice(g * HEAD_DIM, (g + 1) * HEAD_DIM)
        kg, turned_v = k_all[:, span], v_all[:, span].T

        def head(i, carry):
            h = g * GROUP + i
            at = pl.ds(pl.multiple_of(h * HEAD_DIM, HEAD_DIM), HEAD_DIM)
            scores = jnp.where(allowed, nt(kg, q[:, at]) * factor, -1e30)
            top = jnp.max(scores, axis=0, keepdims=True)
            expo = jnp.exp(scores - top)
            total = jnp.sum(expo, axis=0, keepdims=True)
            lse[pl.ds(h, 1), :] = top + jnp.log(total)
            soft = (expo * (1.0 / total)).astype(bf16)
            flat[:, at] = nn(turned_v, soft).T.astype(bf16)
            return carry

        lax.fori_loop(0, GROUP, head, 0)
        move("group%d" % g)
    loads[1].wait()
    middle[...] = x[...]
    for z in range(size):
        at = slice(z * cq, (z + 1) * cq)
        if apart:
            mixed[z] = flat[:, at]
        else:
            mixed[z] = flat[:, at].astype(f32).astype(bf16)
        middle[...] += nt(mixed[z], wout[z])
    value = middle[...]
    scale = lax.rsqrt(jnp.mean(value * value, axis=1, keepdims=True) + epsilon)
    scale_b[...] = scale
    norm_b[...] = value * scale
    acts_b[...] = (norm_b[...] * gain_b[...]).astype(bf16)
    move("end")


def attention_push(x, vectors, tables, qkv, wout, rows, shard, layer):
    count, width = x.shape
    size = lax.axis_size("gy")
    kvd = KV_HEADS * HEAD_DIM
    local = pl.BlockSpec(memory_space=pltpu.VMEM)
    vmem = pltpu.VMEM

    def shape(*dims, kind=bf16):
        return jax.ShapeDtypeStruct(dims, kind)

    normed = [shape(count, width, kind=f32), shape(count, 1, kind=f32), shape(count, width)]
    out = [shape(count, width, kind=f32), *normed, shape(count, HEADS * HEAD_DIM)]
    out += [shape(rows, kvd), shape(rows, kvd), shape(HEADS, count, kind=f32)]
    out += [shape(size, count, wout.shape[2]), *normed]
    out += [shape(lax.axis_size("gx"), *shard.shape[1:])]
    return pl.pallas_call(
        functools.partial(attention_push_kernel, layer),
        out_shape=out,
        in_specs=[local] * 8 + [ANY] * 3,
        out_specs=[local] * 12 + [ANY],
        scratch_shapes=[
            vmem(qkv.shape, bf16),
            vmem(wout.shape, bf16),
            vmem((count, 2 * kvd), bf16),
            vmem((size, count, 2 * kvd), bf16),
            vmem((count, HEADS * HEAD_DIM), bf16),
            pltpu.SemaphoreType.DMA((2,)),
        ]
        + chain_scratch()
        + spread_scratch(1),
        compiler_params=pltpu.CompilerParams(
            collective_id=7 + layer, has_side_effects=True, vmem_limit_bytes=VMEM_LIMIT
        ),
        name="attention_push",
    )(x, *vectors, *tables, qkv, wout, shard)


def on_device(
    residual_in,
    w_query,
    w_key,
    w_value,
    b_query,
    b_key,
    b_value,
    w_output,
    gain_attn,
    gain_ffn,
    w_gate,
    w_up,
    w_down,
    cotangent,
):
    devices_y = lax.axis_size("gy")
    rows_tok = residual_in.shape[1]
    count = rows_tok // devices_y
    q_index = lax.axis_index("gy") * count + jnp.arange(count, dtype=jnp.int32)
    cos_table, sin_table = rope_tables(q_index % LEN, HEAD_DIM)

    small = jnp.concatenate([gain_attn, gain_ffn, b_query, b_key, b_value], axis=1)
    small_sizes = [v.shape[1] for v in (gain_attn, gain_ffn, b_query, b_key, b_value)]
    small = jnp.pad(small.astype(f32), ((0, 8 - LAYERS), (0, 0)))
    lines = []
    for l in range(LAYERS):
        lines += [jnp.concatenate([w_query[l], w_key[l], w_value[l]], axis=1), w_output[l]]
    part_sizes = (w_query.shape[2], w_key.shape[2], w_value.shape[2])
    opened = opening(residual_in, cotangent, small, lines, w_gate, w_up)
    resid, cot, small = opened[:3]
    lines_next = opened[5:7]
    attn_full = [[w.reshape(devices_y, D, -1) for w in opened[7:9]], None]
    ffn_full = [[w.reshape(D, -1) for w in opened[9:]], None]
    small = small[:, :LAYERS].transpose(1, 0, 2)
    vectors, start = [], 0
    for size in small_sizes:
        vectors.append(small[:, :, start : start + size].reshape(LAYERS, -1))
        start += size
    gains_one, gains_two, bias_q, bias_k, bias_v = vectors

    resid = resid.reshape(D, count).astype(f32).T
    cot = cot.reshape(D, count)

    kept = []
    for l in range(LAYERS):
        w_qkv, w_out = attn_full[l]
        vectors = [v[l][None] for v in (gains_one, gains_two, bias_q, bias_k, bias_v)]
        done = attention_push(
            resid, vectors, (cos_table, -sin_table), w_qkv, w_out, rows_tok, w_down, l
        )
        middle, normed_one, scale_one, acts_one, q_rot, k_rot, v_heads, log_total = done[:8]
        mixed, normed_two, scale_two, acts_two = done[8:12]
        wg, wu = ffn_full[l]
        wd = done[12].reshape(D, -1)
        ffn_full[l] = (wg, wu, wd)
        if l == 0:
            shards = (*lines_next, w_gate, w_up)
            done = forward_ffn(acts_two, wg, wu, wd, shards)
            attn_full[1] = [w.reshape(devices_y, D, -1) for w in done[5:7]]
            ffn_full[1] = [w.reshape(D, -1) for w in done[7:]]
        else:
            done = forward_ffn(acts_two, wg, wu, wd)
        part, acts_two, gate, up, hidden = done[:5]
        kept.append(
            (
                normed_one,
                scale_one,
                acts_one,
                q_rot,
                k_rot,
                v_heads,
                log_total,
                mixed,
                normed_two,
                scale_two,
                acts_two,
                gate,
                up,
                hidden,
            )
        )
        resid = middle + part

    grad = cot.astype(f32).T + 2.0 * penalty * resid
    grad_low = grad.astype(bf16)
    attn_grads = [None] * LAYERS
    ffn_grads = [None] * LAYERS
    small_grads = [None] * LAYERS

    for l in reversed(range(LAYERS)):
        (
            normed_one,
            scale_one,
            acts_one,
            q_rot,
            k_rot,
            v_heads,
            log_total,
            mixed,
            normed_two,
            scale_two,
            acts_two,
            gate,
            up,
            hidden,
        ) = kept[l]
        w_qkv, w_out = attn_full[l]
        wg, wu, wd = ffn_full[l]
        operands = (grad_low, gate, up, hidden, acts_two, wg, wu, wd)
        if l == LAYERS - 1:
            done = backward_ffn(*operands, (1, 2))
            held = done[2]
            ffn_grads[l] = [None, None, done[1]]
        else:
            done = backward_ffn(*operands, (2,), held_next)
            ffn_grads[l] = [done[2], None, done[1]]
            ffn_grads[l + 1][1] = done[7]
            held = done[3]
        held_next = done[3]
        grad_acts_two = done[0]
        vectors = [grad, grad_acts_two, normed_two, scale_two, gains_two[l][None]]
        vectors += [normed_one, scale_one, gains_one[l][None]]
        done = attention_pull(
            vectors, acts_one, q_rot, k_rot, v_heads, log_total, (cos_table, sin_table), w_qkv, w_out, held
        )
        ffn_grads[l][0 if l == LAYERS - 1 else 1] = done[6]
        grad, grad_low = done[:2]
        attn_grads[l] = [*done[2:5], mixed]
        rows = done[5]
        width = k_rot.shape[1]
        small_grads[l] = [
            v.reshape(devices_y, -1)
            for v in (rows[0], rows[1], rows[2], rows[3, :width], rows[4, :width])
        ]
    small = jnp.stack([jnp.concatenate(v, axis=1) for v in small_grads], axis=1)
    small = jnp.pad(small, ((0, 0), (0, 8 - LAYERS), (0, 0)))

    def to_rows(tokens_major):
        return tokens_major.astype(bf16).T.reshape(devices_y, -1, count)

    def from_blocks(blocks):
        return blocks.transpose(1, 0, 2).reshape(-1, rows_tok).astype(f32)

    attn_sums, small, output, grad_input = closing(
        attn_grads[0] + attn_grads[1], small, to_rows(resid), to_rows(grad_low)
    )
    small = small[:LAYERS]
    attn_out, start = [], 0
    for size in part_sizes + (w_output.shape[2],):
        attn_out.append(attn_sums[:, :, start : start + size])
        start += size
    small_out, start = [], 0
    for size in small_sizes:
        small_out.append(small[:, start : start + size])
        start += size

    def stack(parts, k):
        return jnp.stack([part[k] for part in parts])

    return (
        from_blocks(output),
        from_blocks(grad_input),
        attn_out[0],
        attn_out[1],
        attn_out[2],
        small_out[2],
        small_out[3],
        small_out[4],
        attn_out[3],
        small_out[0],
        small_out[1],
        stack(ffn_grads, 0),
        stack(ffn_grads, 1),
        stack(ffn_grads, 2),
    )


def solution(mesh):
    tokens = P("gy", "gx")
    weight = P(None, "gx", "gy")
    vector = P(None, "gy")
    return jax.shard_map(
        on_device,
        mesh=mesh,
        in_specs=(
            tokens,
            weight,
            weight,
            weight,
            vector,
            vector,
            vector,
            weight,
            vector,
            vector,
            weight,
            weight,
            weight,
            tokens,
        ),
        out_specs=(
            tokens,
            tokens,
            weight,
            weight,
            weight,
            vector,
            vector,
            vector,
            weight,
            vector,
            vector,
            weight,
            weight,
            weight,
        ),
        check_vma=False,
    )
```
